32 devices in a mesh: rep: 4 (over x, core), shard: 8 (over z, y).
Axes of the slice: x: 2, y: 2, z: 4, core: 2. Of those that a mesh axis runs over, the one named last changes fastest.
Arguments:
- activations: bfloat16 [8, 2048, 1280], P('rep', 'shard'), may hold values from -6 to 6
- cotangent: bfloat16 [8, 2048, 1280], P('rep', 'shard'), may hold values from -6 to 6
- doc_lengths: int32 [8, 16], P('rep'), may hold values from 1 to 1024, 2048 in all within a row
- gain_attn: bfloat16 [1280], P('shard'), may hold values from 0.25 to 1.75
- query_weight: bfloat16 [1280, 1280], P('shard'), may hold values from -0.15625 to 0.15625
- query_bias: bfloat16 [1280], P('shard'), may hold values from -3 to 3
- key_weight: bfloat16 [1280, 1280], P('shard'), may hold values from -0.15625 to 0.15625
- value_weight: bfloat16 [1280, 1280], P('shard'), may hold values from -0.15625 to 0.15625
- value_bias: bfloat16 [1280], P('shard'), may hold values from -3 to 3
- dim_scale: float32 [80], replicated, may hold values from -0.5 to 1.5
- out_weight: bfloat16 [1280, 1280], P('shard'), may hold values from -1 to 1
- gain_mlp: bfloat16 [1280], P('shard'), may hold values from 0.25 to 1.75
- up_weight: bfloat16 [1280, 1280], P('shard'), may hold values from -0.15625 to 0.15625
- down_weight: bfloat16 [1280, 1280], P('shard'), may hold values from -0.15625 to 0.15625
Outputs:
- output: bfloat16 [8, 2048, 1280], P('rep', 'shard')
- input_grad: bfloat16 [8, 2048, 1280], P('rep', 'shard')
- grad_gain_attn: float32 [1280], P('shard')
- grad_query: float32 [1280, 1280], P('shard')
- grad_query_bias: float32 [1280], P('shard')
- grad_key: float32 [1280, 1280], P('shard')
- grad_value: float32 [1280, 1280], P('shard')
- grad_value_bias: float32 [1280], P('shard')
- grad_scale: float32 [80], replicated
- grad_out: float32 [1280, 1280], P('shard')
- grad_gain_mlp: float32 [1280], P('shard')
- grad_up: float32 [1280, 1280], P('shard')
- grad_down: float32 [1280, 1280], P('shard')
The draws below stay inside these ranges and needn't reach their ends.
Inputs may be any that keep to these rules, and one draw needn't show every extreme that they name: `doc_lengths`: each row of 16 lengths sums to 2048, and its longest document has exactly 1024 tokens.
All inputs are finite; a program needn't handle non-finite values.
Results may differ from the reference program's by a relative error of at most 0.03.
Values may be sent and summed in bfloat16 or wider, within the bound.
No kernel may reach another device: no remote copies, remote signals or barrier semaphores. Data moves between devices by JAX's collectives and lax.ppermute only.
A program may use at most 192 MiB of HBM per device.

```python
import math
import jax
import jax.numpy as jnp
import numpy as np
from jax import lax

D = 1280
FF = 1280
HEADS = 16
HEAD_DIM = 80
DOCS = 16
BLOCK = 512
LENGTH = 2048
SEQS = 8


def block_levels(own_key, shape, split, least, top_value):
    def one(dim, blocks):
        steps = jax.random.uniform(jax.random.fold_in(jax.random.fold_in(own_key, 6), dim), (blocks,), jnp.float32, least / len(split), top_value / len(split))
        return jnp.repeat(jnp.exp(steps), shape[dim] // blocks).reshape((-1,) + (1,) * (len(shape) - dim - 1))

    loudness = one(*split[0])
    for cut in split[1:]:
        loudness = loudness * one(*cut)
    return loudness


def split_up(count, total, limit, lean):
    loads = [(1 << 20) // math.isqrt(rank ** lean) + 1 for rank in range(2, count + 1)]
    rest, given = total - limit - (count - 1), [1] * (count - 1)
    while rest > 0:
        movable = [i for i in range(count - 1) if given[i] < limit]
        whole, budget = sum([loads[i] for i in movable]), rest
        for i in movable:
            addition = min(limit - given[i], max(1, budget * loads[i] // whole), rest)
            given[i] = given[i] + addition
            rest = rest - addition
    return np.array([limit] + given)


def ragged_sizes(key, count, total, most, lean):
    if count == 2:
        one = jax.random.randint(key, (), max(1, total - most), min(most, total - 1) + 1)
        return jnp.stack([one, total - one])
    sizes = jnp.asarray(split_up(count, total, most, lean), jnp.int32)
    couples = (count - 1) // 2
    donor, taker = sizes[1:1 + 2 * couples:2], sizes[2:2 + 2 * couples:2]
    slack = jnp.minimum(donor - 1, most - taker)
    passed = jax.random.randint(jax.random.fold_in(key, 1), (couples,), 0, 1 << 20) % (slack + 1)
    sizes = sizes.at[1:1 + 2 * couples:2].set(donor - passed).at[2:2 + 2 * couples:2].set(taker + passed)
    return sizes[jax.random.permutation(jax.random.fold_in(key, 2), count)]


def noise(stream_key, dims, scale, reach, shards=(), kind=jnp.bfloat16):
    drawn = scale * jax.random.normal(stream_key, dims, jnp.float32)
    if shards:
        drawn = drawn * block_levels(stream_key, dims, shards, -0.22, 0.18)
    return jnp.clip(drawn, -reach, reach).astype(kind)


def setup_inputs(seed: int = 0) -> dict:
    streams_of = jax.random.split(jax.random.key(seed), 15)
    activations = noise(streams_of[0], (SEQS, LENGTH, D), 1.0, 6.0, ((0, 4), (1, 8)))
    cotangent = noise(streams_of[1], (SEQS, LENGTH, D), 1.0, 6.0, ((0, 4), (1, 8)))
    doc_lengths = jax.vmap(lambda own: ragged_sizes(own, DOCS, LENGTH, LENGTH // 2, 2))(jax.random.split(streams_of[2], SEQS)).reshape((SEQS, DOCS)).astype(jnp.int32)
    gain_attn = jnp.clip(1.0 + 0.15 * jax.random.normal(streams_of[3], (D,), jnp.float32), 0.25, 1.75).astype(jnp.bfloat16)
    query_weight = noise(streams_of[4], (D, D), D ** -0.5, 0.15625, ((0, 8),))
    query_bias = noise(streams_of[5], (D,), 0.5, 3.0, ((0, 8),))
    key_weight = noise(streams_of[6], (D, D), D ** -0.5, 0.15625, ((0, 8),))
    value_weight = noise(streams_of[7], (D, D), D ** -0.5, 0.15625, ((0, 8),))
    value_bias = noise(streams_of[8], (D,), 0.5, 3.0, ((0, 8),))
    dim_scale = jnp.clip(jax.random.uniform(streams_of[9], (HEAD_DIM,), jnp.float32, -0.5, 1.5), -0.5, 1.5)
    out_weight = noise(streams_of[10], (D, D), (D // 32) ** -0.5, 1.0, ((0, 8),))
    gain_mlp = jnp.clip(1.0 + 0.15 * jax.random.normal(streams_of[11], (D,), jnp.float32), 0.25, 1.75).astype(jnp.bfloat16)
    up_weight = noise(streams_of[12], (D, FF), D ** -0.5, 0.15625, ((0, 8),))
    down_weight = noise(streams_of[13], (FF, D), FF ** -0.5, 0.15625, ((0, 8),))
    return {"activations": activations, "cotangent": cotangent, "doc_lengths": doc_lengths, "gain_attn": gain_attn, "query_weight": query_weight, "query_bias": query_bias, "key_weight": key_weight, "value_weight": value_weight, "value_bias": value_bias, "dim_scale": dim_scale, "out_weight": out_weight, "gain_mlp": gain_mlp, "up_weight": up_weight, "down_weight": down_weight}


NORM_EPS = 1e-06
LOG_BASE = 1.442695041
MASK_FILL = -1e+30

@jax.custom_vjp
def low(v):
    return lax.optimization_barrier(v.astype(jnp.bfloat16)).astype(jnp.float32)

@jax.custom_vjp
def low_back(v):
    return v

def low_keep(v):
    return (low(v), None)

def low_pass(kept, grad):
    return (grad,)

def back_keep(v):
    return (v, None)

def back_low(kept, grad):
    return (low(grad),)
low.defvjp(low_keep, low_pass)
low_back.defvjp(back_keep, back_low)

def matmul(left_side, right_side):
    return jnp.dot(left_side, right_side, precision=lax.Precision.HIGHEST, preferred_element_type=jnp.float32)

def rms_norm(values, gain_vec):
    return values * lax.rsqrt(lax.optimization_barrier(jnp.mean(values * values, axis=-1, keepdims=True)) + NORM_EPS) * gain_vec

def doc_numbers(lengths, total_len):
    doc_ends = jnp.cumsum(lengths, axis=-1).astype(jnp.int32)
    places = jnp.arange(total_len, dtype=jnp.int32)
    return lax.optimization_barrier(jnp.sum((places[None, :, None] >= doc_ends[:, None, :]).astype(jnp.int32), axis=-1)).astype(jnp.int32)

def attend_reference(queries, key_rows, value_rows, seq_docs):
    length = queries.shape[0]
    block_count = length // BLOCK
    places = jnp.arange(length, dtype=jnp.int32)

    def one_block(query_index):
        row_start = (query_index * BLOCK).astype(jnp.int32)
        query_block = lax.dynamic_slice_in_dim(queries, row_start, BLOCK, 0)
        query_docs = lax.dynamic_slice_in_dim(seq_docs, row_start, BLOCK, 0)
        query_places = row_start + jnp.arange(BLOCK, dtype=jnp.int32)
        scores = jnp.einsum('qhe,khe->hqk', query_block, key_rows, precision=lax.Precision.HIGHEST)
        scores = low_back(scores)
        allowed = ((query_docs[:, None] == seq_docs[None, :]) & (places[None, :] <= query_places[:, None]))[None]
        masked = jnp.where(allowed, scores, MASK_FILL)
        log_total = jax.nn.logsumexp(masked, axis=-1, keepdims=True)
        prob_low = low(jnp.where(allowed, jnp.exp(masked - log_total), 0.0))
        return jnp.einsum('hqk,khe->qhe', prob_low, value_rows, precision=lax.Precision.HIGHEST)
    mixed_blocks = lax.map(jax.checkpoint(one_block), jnp.arange(block_count, dtype=jnp.int32))
    return mixed_blocks.reshape(length, HEADS * HEAD_DIM)

def layer_sequence(params, hidden_in, seq_docs):
    gain_attn, query_weight, query_bias, key_weight, value_weight, value_bias, dim_scale, out_weight, gain_mlp, up_weight, down_weight = params
    length = hidden_in.shape[0]
    normed = low(rms_norm(hidden_in, gain_attn))
    query_full = low_back(matmul(normed, query_weight) + query_bias)
    scale_vec = jnp.tile(LOG_BASE / math.sqrt(HEAD_DIM) * jax.nn.softplus(dim_scale), HEADS)
    scaled = low_back(low(query_full * scale_vec))
    key_rows = low_back(low(matmul(normed, key_weight)))
    value_rows = low_back(low(matmul(normed, value_weight) + value_bias))
    head_shape = (length, HEADS, HEAD_DIM)
    mixed_rows = low_back(low(attend_reference(scaled.reshape(head_shape), key_rows.reshape(head_shape), value_rows.reshape(head_shape), seq_docs)))
    residual = hidden_in + low_back(matmul(mixed_rows, out_weight))
    normed_mlp = low(rms_norm(residual, gain_mlp))
    upward = low_back(matmul(normed_mlp, up_weight))
    activated = low(jax.nn.silu(upward))
    return residual + matmul(activated, down_weight)

def reference(activations, cotangent, doc_lengths, gain_attn, query_weight, query_bias, key_weight, value_weight, value_bias, dim_scale, out_weight, gain_mlp, up_weight, down_weight):
    seq_docs = doc_numbers(doc_lengths, LENGTH)
    params = tuple((array_in.astype(jnp.float32) for array_in in (gain_attn, query_weight, query_bias, key_weight, value_weight, value_bias, dim_scale, out_weight, gain_mlp, up_weight, down_weight)))

    def forward(hidden, weights):

        def per_sequence(carry_value, bundle):
            return (carry_value, layer_sequence(weights, bundle[0], bundle[1]))
        return lax.scan(per_sequence, jnp.zeros((), jnp.float32), (hidden, seq_docs))[1]
    outputs, pull_back = jax.vjp(forward, activations.astype(jnp.float32), params)
    input_grad, gradients = pull_back(cotangent.astype(jnp.float32))
    g_gain_attn, g_query, g_query_bias, g_key, g_value, g_value_bias, g_scale, g_out, g_gain_mlp, g_up, g_down = gradients
    return (outputs.astype(jnp.bfloat16), input_grad.astype(jnp.bfloat16), g_gain_attn, g_query, g_query_bias, g_key, g_value, g_value_bias, g_scale, g_out, g_gain_mlp, g_up, g_down)
```

```python
import functools
import math

import jax
import jax.numpy as jnp
from jax import lax
from jax.experimental import pallas as pl
from jax.experimental.pallas import tpu as pltpu
from jax.sharding import PartitionSpec as P

HEAD_DIM = 80
LANES = 128
CORES = 2
NORM_EPS = 1e-06
LOG_BASE = 1.442695041
MASK_FILL = -1e30
AXES = ("rep", "shard")
F32 = jnp.float32
BF16 = jnp.bfloat16


def dot(left, right, left_dim=1, right_dim=0):
    return lax.dot_general(
        left, right, (((left_dim,), (right_dim,)), ((), ())), preferred_element_type=F32
    )


class Place:
    def __init__(self, reps, shards, seqs):
        self.x_size = reps // CORES
        self.a_size = CORES * seqs
        self.b_size = shards // self.a_size
        self.seqs = seqs
        rep, shard = lax.axis_index("rep"), lax.axis_index("shard")
        self.x, self.c = rep // CORES, rep % CORES
        self.a, self.b = shard // self.b_size, shard % self.b_size
        self.shard = shard

    def route(self, move):
        pairs = []
        for x in range(self.x_size):
            for c in range(CORES):
                for a in range(self.a_size):
                    for b in range(self.b_size):
                        pairs.append((self.number(x, c, a, b), self.number(*move(x, c, a, b))))
        return pairs

    def number(self, x, c, a, b):
        return ((x * CORES + c) * self.a_size + a) * self.b_size + b

    def send(self, value, dx=0, dc=0, da=0, db=0):
        return lax.ppermute(
            value,
            AXES,
            self.route(
                lambda x, c, a, b: (
                    (x + dx) % self.x_size,
                    (c + dc) % CORES,
                    (a + da) % self.a_size,
                    (b + db) % self.b_size,
                )
            ),
        )

    def peers(self):
        return [(db, dc) for db in range(self.b_size) for dc in range(CORES)]

    def to_cluster(self, tokens):
        seqs, count, width = tokens.shape
        half = count // CORES
        received = []
        for m in range(self.a_size):
            t = m ^ self.a
            part = lax.dynamic_slice(
                tokens, (t % seqs, (t // seqs) * half, 0), (1, half, width)
            ).reshape(half, width)
            received.append(lax.ppermute(part, AXES, self.route(self._match(m))))
        u = self.a % seqs + seqs * self.c
        return place(received, [m ^ u for m in range(self.a_size)])

    def from_cluster(self, chunks):
        half, width = chunks.shape[1:]
        u = self.a % self.seqs + self.seqs * self.c
        received = []
        for m in range(self.a_size):
            part = lax.dynamic_index_in_dim(chunks, m ^ u, 0, keepdims=False)
            back = [(j, i) for i, j in self.route(self._match(m))]
            received.append(lax.ppermute(part, AXES, back))
        spots = []
        for m in range(self.a_size):
            t = m ^ self.a
            spots.append((t % self.seqs) * CORES + t // self.seqs)
        return place(received, spots).reshape(self.seqs, CORES * half, width)

    def _match(self, m):
        def move(x, c, a, b):
            t = m ^ a
            return x, t // self.seqs, self.seqs * c + t % self.seqs, b

        return move

    def ring(self, value):
        up = self.send(value, da=-1)
        down = self.send(value, da=1)
        cut = value.shape[0] // 2
        far_low = self.send(up[:cut], da=-1)
        far_high = self.send(down[cut:], da=1)
        return [value, up, jnp.concatenate([far_low, far_high]), down]


def place_body(count, spots, *refs):
    pieces, target, sems = refs[:count], refs[count], refs[count + 1]
    copies = [
        pltpu.make_async_copy(pieces[k], target.at[spots[k]], sems.at[k]) for k in range(count)
    ]
    for copy in copies:
        copy.start()
    for copy in copies:
        copy.wait()


def place(pieces, spots):
    count = len(pieces)
    return pl.pallas_call(
        functools.partial(place_body, count),
        out_shape=jax.ShapeDtypeStruct((count, *pieces[0].shape), pieces[0].dtype),
        grid_spec=pltpu.PrefetchScalarGridSpec(
            num_scalar_prefetch=1,
            grid=(1,),
            in_specs=[pl.BlockSpec(memory_space=pltpu.VMEM)] * count,
            out_specs=pl.BlockSpec(memory_space=pl.ANY),
            scratch_shapes=[pltpu.SemaphoreType.DMA((count,))],
        ),
        compiler_params=pltpu.CompilerParams(vmem_limit_bytes=32 * 1024 * 1024),
        name="place",
    )(jnp.stack([jnp.asarray(s, jnp.int32) for s in spots]), *pieces)


def forward_body(heads, block, low, starts, query, key, value, mixed, query_aug, total, top):
    index = pl.program_id(0)
    total[...] = jnp.zeros_like(total)
    top[...] = jnp.full_like(top, MASK_FILL)
    rows = index * block + lax.broadcasted_iota(jnp.int32, (block, block), 0)
    begin = starts[...][:, :1]

    def step(j, carry):
        spot = pl.multiple_of(j * block, block)
        columns = spot + lax.broadcasted_iota(jnp.int32, (block, block), 1)
        bias = jnp.where((columns >= begin) & (columns <= rows), 0.0, MASK_FILL)
        for h in range(heads):
            lanes = slice(h * LANES, (h + 1) * LANES)
            score = dot(query[:, lanes], key[pl.ds(spot, block), lanes], 1, 1) + bias
            old = top[h]
            new = jnp.maximum(old, jnp.max(score, axis=1, keepdims=True))
            weight = jnp.exp(score - jnp.concatenate([new] * (block // LANES), axis=1))
            total[h] = total[h] * jnp.exp(old - new) + dot(
                weight.astype(BF16), value[pl.ds(spot, block), lanes]
            )
            top[h] = new
        return carry

    lax.fori_loop(low[index], index + 1, step, 0)
    lane = lax.broadcasted_iota(jnp.int32, (block, LANES), 1)
    for h in range(heads):
        lanes = slice(h * LANES, (h + 1) * LANES)
        acc = total[h]
        weight_sum = acc[:, HEAD_DIM : HEAD_DIM + 1]
        mixed[:, h * HEAD_DIM : (h + 1) * HEAD_DIM] = (acc / weight_sum)[:, :HEAD_DIM].astype(BF16)
        rest = -(top[h] + jnp.log(weight_sum))
        aug = query[:, lanes].astype(F32)
        for k in range(3):
            term = rest.astype(BF16).astype(F32)
            aug = jnp.where(lane == HEAD_DIM + k, term, aug)
            rest = rest - term
        query_aug[:, lanes] = aug.astype(BF16)


def attend_forward(low, starts, qkv, heads, block):
    length = qkv.shape[0]
    wide = heads * LANES
    return pl.pallas_call(
        functools.partial(forward_body, heads, block),
        out_shape=[
            jax.ShapeDtypeStruct((length, heads * HEAD_DIM), BF16),
            jax.ShapeDtypeStruct((length, wide), BF16),
        ],
        grid_spec=pltpu.PrefetchScalarGridSpec(
            num_scalar_prefetch=1,
            grid=(length // block,),
            in_specs=[
                pl.BlockSpec((block, LANES), lambda i, low: (i, 0)),
                pl.BlockSpec((block, wide), lambda i, low: (i, 0)),
                pl.BlockSpec((length, wide), lambda i, low: (0, 1)),
                pl.BlockSpec((length, wide), lambda i, low: (0, 2)),
            ],
            out_specs=[
                pl.BlockSpec((block, heads * HEAD_DIM), lambda i, low: (i, 0)),
                pl.BlockSpec((block, wide), lambda i, low: (i, 0)),
            ],
            scratch_shapes=[
                pltpu.VMEM((heads, block, LANES), F32),
                pltpu.VMEM((heads, block, LANES), F32),
            ],
        ),
        compiler_params=pltpu.CompilerParams(vmem_limit_bytes=48 * 1024 * 1024),
        name="attend_forward",
    )(low, starts, qkv, qkv, qkv)


def backward_body(
    heads,
    block,
    low,
    starts,
    scale,
    query,
    key,
    value,
    grad,
    mixed,
    grads,
    scale_sum,
    bias_sum,
    grad_aug,
    d_query,
    d_key,
    d_value,
):
    index = pl.num_programs(0) - 1 - pl.program_id(0)
    width = heads * HEAD_DIM

    @pl.when(pl.program_id(0) == 0)
    def clear():
        d_key[...] = jnp.zeros_like(d_key)
        d_value[...] = jnp.zeros_like(d_value)
        scale_sum[...] = jnp.zeros_like(scale_sum)
        bias_sum[...] = jnp.zeros_like(bias_sum)

    lane = lax.broadcasted_iota(jnp.int32, (block, LANES), 1)
    for h in range(heads):
        part = slice(h * HEAD_DIM, (h + 1) * HEAD_DIM)
        grad_h = grad[:, part].astype(F32)
        delta = jnp.sum(grad_h * mixed[:, part].astype(F32), axis=1, keepdims=True)
        aug = jnp.concatenate([grad_h, jnp.zeros((block, LANES - HEAD_DIM), F32)], axis=1)
        high = (-delta).astype(BF16).astype(F32)
        aug = jnp.where(lane == HEAD_DIM, high, aug)
        aug = jnp.where(lane == HEAD_DIM + 1, -delta - high, aug)
        grad_aug[:, h * LANES : (h + 1) * LANES] = aug.astype(BF16)
    d_query[...] = jnp.zeros_like(d_query)
    columns = index * block + lax.broadcasted_iota(jnp.int32, (block, block), 1)
    begin = starts[0:1, :]

    def step(j, carry):
        spot = pl.multiple_of(j * block, block)
        rows = spot + lax.broadcasted_iota(jnp.int32, (block, block), 0)
        allowed = (rows >= begin) & (rows <= columns)
        for h in range(heads):
            lanes = slice(h * LANES, (h + 1) * LANES)
            key_h = key[pl.ds(spot, block), lanes]
            query_h = query[:, lanes]
            grad_h = grad_aug[:, lanes]
            prob = jnp.where(allowed, jnp.exp(dot(key_h, query_h, 1, 1)), 0.0)
            d_prob = dot(value[pl.ds(spot, block), lanes], grad_h, 1, 1)
            d_score = (prob * d_prob).astype(BF16)
            d_value[pl.ds(spot, block), lanes] += dot(prob.astype(BF16), grad_h)
            d_key[pl.ds(spot, block), lanes] += dot(d_score, query_h)
            d_query[:, lanes] += dot(d_score, key_h, 0, 0)
        return carry

    lax.fori_loop(low[index], index + 1, step, 0)
    here = pl.ds(pl.multiple_of(index * block, block), block)
    for h in range(heads):
        lanes = slice(h * LANES, (h + 1) * LANES)
        d_scaled = d_query[:, lanes].astype(BF16).astype(F32)
        scale_sum[...] += jnp.sum(d_scaled * query[:, lanes].astype(F32), axis=0, keepdims=True)
        d_q = (d_scaled * scale[0:1, lanes]).astype(BF16)
        for k, term in enumerate((d_q, d_key[here, lanes], d_value[here, lanes])):
            spot = k * width + h * HEAD_DIM
            term = term.astype(BF16)
            grads[:, spot : spot + HEAD_DIM] = term[:, :HEAD_DIM]
            bias_sum[:, (k * heads + h) * LANES : (k * heads + h + 1) * LANES] += jnp.sum(
                term.astype(F32), axis=0, keepdims=True
            )


def attend_backward(low, starts, scale, query_aug, qkv, grad, mixed, heads, block):
    length = qkv.shape[0]
    wide = heads * LANES
    width = heads * HEAD_DIM
    count = length // block
    return pl.pallas_call(
        functools.partial(backward_body, heads, block),
        out_shape=[
            jax.ShapeDtypeStruct((length, 3 * width), BF16),
            jax.ShapeDtypeStruct((8, LANES), F32),
            jax.ShapeDtypeStruct((8, 3 * wide), F32),
        ],
        grid_spec=pltpu.PrefetchScalarGridSpec(
            num_scalar_prefetch=1,
            grid=(count,),
            in_specs=[
                pl.BlockSpec((8, block), lambda i, low: (0, count - 1 - i)),
                pl.BlockSpec((8, wide), lambda i, low: (0, 0)),
                pl.BlockSpec((block, wide), lambda i, low: (count - 1 - i, 0)),
                pl.BlockSpec((length, wide), lambda i, low: (0, 1)),
                pl.BlockSpec((length, wide), lambda i, low: (0, 2)),
                pl.BlockSpec((block, width), lambda i, low: (count - 1 - i, 0)),
                pl.BlockSpec((block, width), lambda i, low: (count - 1 - i, 0)),
            ],
            out_specs=[
                pl.BlockSpec((block, 3 * width), lambda i, low: (count - 1 - i, 0)),
                pl.BlockSpec((8, LANES), lambda i, low: (0, 0)),
                pl.BlockSpec((8, 3 * wide), lambda i, low: (0, 0)),
            ],
            scratch_shapes=[
                pltpu.VMEM((block, wide), BF16),
                pltpu.VMEM((block, wide), F32),
                pltpu.VMEM((length, wide), F32),
                pltpu.VMEM((length, wide), F32),
            ],
        ),
        compiler_params=pltpu.CompilerParams(vmem_limit_bytes=48 * 1024 * 1024),
        name="attend_backward",
    )(low, starts, scale, query_aug, qkv, qkv, grad, mixed)


def pick(stacked, index):
    return lax.dynamic_index_in_dim(stacked, index, 0, keepdims=False)


def gather_rows(at, pieces, cores):
    rows, width = pieces[0].shape
    split = at.x_size == 2
    if split:
        rows //= 2
        pieces = [pick(p.reshape(2, rows, width), at.x) for p in pieces]
    if cores:
        width //= CORES
        pieces = [pick(p.reshape(rows, CORES, width).swapaxes(0, 1), at.c) for p in pieces]
    near = [pieces[0]] + [at.send(pieces[db], db=db) for db in range(1, at.b_size)]
    rings = [at.ring(p) for p in near]
    found = {}
    for db, ring in enumerate(rings):
        for da, part in enumerate(ring):
            found[(0, da, db)] = part
            if split:
                found[(1, da, db)] = at.send(part, dx=1)
    x_count = 2 if split else 1
    spots, parts = [], []
    for (dx, da, db), part in found.items():
        spot = ((at.a + da) % at.a_size) * at.b_size + (at.b - db) % at.b_size
        spots.append(spot * x_count + ((at.x + dx) % 2 if split else 0))
        parts.append(part)
    whole = place(parts, spots).reshape(-1, width)
    if not cores:
        return whole
    other = at.send(whole, dc=1)
    flip = at.c == 1
    return jnp.concatenate(
        [jnp.where(flip, other, whole), jnp.where(flip, whole, other)], axis=1
    )


def sum_over(at, value, axis, size):
    spot = getattr(at, axis[1])
    total = pick(value, spot).astype(F32)
    for d in range(1, size):
        total = total + at.send(pick(value, (spot + d) % size), **{axis: d}).astype(F32)
    return total


def all_sum(at, value, axis, size):
    total = value
    for d in range(1, size):
        total = total + at.send(value, **{axis: d}).astype(value.dtype)
    return total


def both_cores(at, part):
    other = at.send(part, dc=1)
    flip = at.c == 1
    return jnp.concatenate([jnp.where(flip, other, part), jnp.where(flip, part, other)], axis=1)


def finish_rows(at, part):
    split = at.x_size == 2
    part = sum_over(at, part, "db", at.b_size)
    if not split:
        part = all_sum(at, part.astype(BF16), "dx", at.x_size)
        return part.reshape(-1, part.shape[-1])
    part = part[0].astype(BF16)
    other = at.send(part, dx=1)
    flip = at.x == 1
    return jnp.concatenate([jnp.where(flip, other, part), jnp.where(flip, part, other)], axis=0)


def reduce_full(at, grad):
    rows, width = grad.shape
    split = at.x_size == 2
    x_count = 2 if split else 1
    grad = grad.astype(BF16).reshape(rows, CORES, width // CORES).swapaxes(0, 1)
    part = sum_over(at, grad, "dc", CORES).astype(BF16)
    part = part.reshape(at.a_size, at.b_size, x_count, -1, width // CORES)
    if split:
        part = jnp.moveaxis(part, 2, 0)
        part = sum_over(at, part, "dx", 2).astype(BF16)[:, :, None]
    part = sum_over(at, part, "da", at.a_size).astype(BF16)
    part = finish_rows(at, part)
    return both_cores(at, part).astype(F32)


def reduce_heads(at, grad):
    rows, width = grad.shape
    split = at.x_size == 2
    x_count = 2 if split else 1
    part = grad.astype(BF16).reshape(at.a_size, at.b_size, x_count, -1, width)
    part = sum_over(at, part, "da", at.a_size).astype(BF16)
    if split:
        part = jnp.moveaxis(part, 1, 0)
        part = sum_over(at, part, "dx", 2).astype(BF16)
    else:
        part = all_sum(at, part, "dx", at.x_size)[:, 0]
    pieces, spots = [], []
    for db in range(at.b_size):
        piece = pick(part, (at.b + db) % at.b_size)
        piece = at.send(piece, db=db) if db else piece
        if split:
            other = at.send(piece, dx=1)
            flip = at.x == 1
            piece = jnp.concatenate(
                [jnp.where(flip, other, piece), jnp.where(flip, piece, other)], axis=0
            )
        for dc in range(CORES):
            pieces.append(at.send(piece, dc=dc) if dc else piece)
            spots.append(((at.b - db) % at.b_size) * CORES + (at.c + dc) % CORES)
    stacked = place(pieces, spots)
    count, rows = stacked.shape[:2]
    stacked = stacked.reshape(count, rows, 3, width // 3)
    return stacked.transpose(2, 1, 0, 3).reshape(3, rows, count * width // 3).astype(F32)


def local(
    reps,
    shards,
    activations,
    cotangent,
    doc_lengths,
    gain_attn,
    query_weight,
    query_bias,
    key_weight,
    value_weight,
    value_bias,
    dim_scale,
    out_weight,
    gain_mlp,
    up_weight,
    down_weight,
):
    seqs, tok_count, model = activations.shape
    at = Place(reps, shards, seqs)
    half = tok_count // CORES
    length = tok_count * shards
    peer_count = at.b_size * CORES
    heads = model // HEAD_DIM // peer_count
    width = heads * HEAD_DIM
    wide = heads * LANES
    own_rows = at.a_size * half
    block = min(256, length)
    mine = at.b * CORES + at.c

    vectors = jnp.stack([gain_attn, gain_mlp, query_bias, value_bias])
    vectors = lax.dynamic_update_slice(
        jnp.zeros((4, model), BF16), vectors, (0, at.shard * gain_attn.shape[0])
    )
    vectors = all_sum(at, vectors, "db", at.b_size)
    vectors = all_sum(at, vectors, "da", at.a_size).astype(F32)
    g_attn, g_mlp, b_query, b_value = vectors[0], vectors[1], vectors[2], vectors[3]

    other_lengths = at.send(doc_lengths, dc=1)
    lengths = pick(jnp.where(at.c == at.a // seqs, doc_lengths, other_lengths), at.a % seqs)
    ends = jnp.cumsum(lengths)
    places = jnp.arange(length, dtype=jnp.int32)
    starts = jnp.max(jnp.where(ends[None, :] <= places[:, None], ends[None, :], 0), axis=1)
    starts_row = jnp.broadcast_to(starts[None, :], (8, length))
    starts_col = jnp.broadcast_to(starts[:, None], (length, LANES))
    low = starts[::block] // block

    chunks = at.to_cluster(activations)
    hidden = chunks.reshape(own_rows, model).astype(F32)
    rate_attn = lax.rsqrt(jnp.mean(hidden * hidden, axis=-1, keepdims=True) + NORM_EPS)
    normed_own = (hidden * rate_attn * g_attn).astype(BF16).reshape(at.a_size, half, model)

    stack3 = jnp.stack([query_weight, key_weight, value_weight], axis=1)
    stack3 = stack3.reshape(-1, 3, peer_count, width)
    pieces = [
        lax.dynamic_index_in_dim(
            stack3, ((at.b + db) % at.b_size) * CORES + at.c, 2, keepdims=False
        ).reshape(-1, 3 * width)
        for db in range(at.b_size)
    ]
    w_heads = gather_rows(at, pieces, False)

    parts, spots = [], []
    for db in range(at.b_size):
        near = at.send(normed_own, db=db) if db else normed_own
        for dc in range(CORES):
            part = at.send(near, dc=dc) if dc else near
            for a in range(at.a_size):
                parts.append(part[a])
                spots.append(
                    a * peer_count + ((at.b - db) % at.b_size) * CORES + (at.c + dc) % CORES
                )
    normed = place(parts, spots).reshape(length, model)

    scale_dim = LOG_BASE / math.sqrt(HEAD_DIM) * jax.nn.softplus(dim_scale)
    scale_pad = jnp.tile(jnp.pad(scale_dim, (0, LANES - HEAD_DIM)), heads)
    lane = jnp.arange(LANES)
    ones_key = ((lane >= HEAD_DIM) & (lane < HEAD_DIM + 3)).astype(F32)
    ones_value = ((lane >= HEAD_DIM) & (lane < HEAD_DIM + 2)).astype(F32)

    def pad_heads(vec):
        part = lax.dynamic_slice_in_dim(vec, mine * width, width, 0).reshape(heads, HEAD_DIM)
        return jnp.pad(part, ((0, 0), (0, LANES - HEAD_DIM))).reshape(wide)

    bias_pad = jnp.concatenate(
        [
            pad_heads(b_query),
            jnp.tile(ones_key, heads),
            pad_heads(b_value) + jnp.tile(ones_value, heads),
        ]
    )
    times = jnp.concatenate([scale_pad, jnp.ones((2 * wide,), F32)])
    w_pad = jnp.pad(
        w_heads.reshape(model, 3 * heads, HEAD_DIM), ((0, 0), (0, 0), (0, LANES - HEAD_DIM))
    ).reshape(model, 3 * wide)
    qkv = ((dot(normed, w_pad) + bias_pad) * times).astype(BF16)

    mixed_heads, query_aug = attend_forward(low, starts_col, qkv, heads, block)

    w_out = gather_rows(at, [out_weight] * at.b_size, True)
    w_up = gather_rows(at, [up_weight] * at.b_size, True)
    w_down = gather_rows(at, [down_weight] * at.b_size, True)
    d_out = at.to_cluster(cotangent).reshape(own_rows, model)

    by_peer = mixed_heads.reshape(at.a_size, peer_count, half, width)
    parts, spots = [], []
    for db, dc in at.peers():
        peer = ((at.b + db) % at.b_size) * CORES + (at.c + dc) % CORES
        part = lax.dynamic_index_in_dim(by_peer, peer, 1, keepdims=False)
        part = at.send(part, db=db, dc=dc) if db or dc else part
        parts.append(part.reshape(own_rows, width))
        spots.append(((at.b - db) % at.b_size) * CORES + (at.c + dc) % CORES)
    mixed = place(parts, spots).transpose(1, 0, 2).reshape(own_rows, model)

    residual = hidden + dot(mixed, w_out)
    rate_mlp = lax.rsqrt(jnp.mean(residual * residual, axis=-1, keepdims=True) + NORM_EPS)
    normed_mlp = (residual * rate_mlp * g_mlp).astype(BF16)
    upward = dot(normed_mlp, w_up)
    gate = jax.nn.sigmoid(upward)
    activated = (upward * gate).astype(BF16)
    output = (residual + dot(activated, w_down)).astype(BF16)
    output = at.from_cluster(output.reshape(at.a_size, half, model))

    d_activated = dot(d_out, w_down, 1, 1)
    d_up = (d_activated * gate * (1 + upward * (1 - gate))).astype(BF16)
    d_normed_mlp = dot(d_up, w_up, 1, 1)

    def norm_back(values, rate, gain, grad):
        scaled = grad * gain
        inner = jnp.mean(values * scaled, axis=-1, keepdims=True)
        return (
            rate * scaled - values * (rate * rate * rate * inner),
            jnp.sum(grad * values * rate, axis=0),
        )

    d_norm, grad_gain_mlp = norm_back(residual, rate_mlp, g_mlp, d_normed_mlp)
    d_residual = d_out.astype(F32) + d_norm
    d_proj = d_residual.astype(BF16)
    d_mixed = dot(d_proj, w_out, 1, 1).astype(BF16)

    by_peer = d_mixed.reshape(at.a_size, half, peer_count, width)
    parts, spots = [], []
    for db, dc in at.peers():
        peer = ((at.b + db) % at.b_size) * CORES + (at.c + dc) % CORES
        part = lax.dynamic_index_in_dim(by_peer, peer, 2, keepdims=False)
        part = at.send(part, db=db, dc=dc) if db or dc else part
        source = ((at.b - db) % at.b_size) * CORES + (at.c + dc) % CORES
        for a in range(at.a_size):
            parts.append(part[a])
            spots.append(a * peer_count + source)
    grad_heads = place(parts, spots).reshape(length, width)

    grad_down = reduce_full(at, dot(activated, d_out, 0, 0))
    grad_up = reduce_full(at, dot(normed_mlp, d_up, 0, 0))
    grad_out = reduce_full(at, dot(mixed, d_proj, 0, 0))

    scale_rows = jnp.broadcast_to(scale_pad[None, :], (8, wide))
    d_heads, scale_sum, bias_sum = attend_backward(
        low, starts_row, scale_rows, query_aug, qkv, grad_heads, mixed_heads, heads, block
    )

    partial = dot(d_heads, w_heads, 1, 1).astype(BF16)
    partial = partial.reshape(at.a_size, at.b_size, CORES, half, model)
    partial = sum_over(at, jnp.moveaxis(partial, 2, 0), "dc", CORES).astype(BF16)
    d_normed = sum_over(at, jnp.moveaxis(partial, 1, 0), "db", at.b_size)
    d_normed = d_normed.reshape(own_rows, model)
    d_norm, grad_gain_attn = norm_back(hidden, rate_attn, g_attn, d_normed)
    input_grad = (d_residual + d_norm).astype(BF16)
    input_grad = at.from_cluster(input_grad.reshape(at.a_size, half, model))

    grads = reduce_heads(at, dot(normed, d_heads, 0, 0))

    bias_sum = bias_sum[0].reshape(3, heads, LANES)[:, :, :HEAD_DIM].reshape(3, width)

    def spread(vec):
        return lax.dynamic_update_slice(jnp.zeros((model,), F32), vec, (mine * width,))

    scale_part = jnp.where(scale_dim > 0, scale_sum[0, :HEAD_DIM] / scale_dim, 0.0)
    scale_part = scale_part * (LOG_BASE / math.sqrt(HEAD_DIM)) * jax.nn.sigmoid(dim_scale)
    small = jnp.stack(
        [
            grad_gain_attn,
            grad_gain_mlp,
            spread(bias_sum[0]),
            spread(bias_sum[2]),
            jnp.pad(scale_part, (0, model - HEAD_DIM)),
        ]
    )
    small = all_sum(at, small, "dc", CORES)
    small = all_sum(at, small, "dx", at.x_size)
    small = all_sum(at, small, "db", at.b_size)
    small = all_sum(at, small, "da", at.a_size)
    rows = gain_attn.shape[0]
    owned = lax.dynamic_slice(small, (0, at.shard * rows), (5, rows))
    return (
        output,
        input_grad,
        owned[0],
        grads[0],
        owned[2],
        grads[1],
        grads[2],
        owned[3],
        small[4, :HEAD_DIM],
        grad_out,
        owned[1],
        grad_up,
        grad_down,
    )


def solution(mesh):
    in_specs = (
        P("rep", "shard", None),
        P("rep", "shard", None),
        P("rep", None),
        P("shard"),
        P("shard", None),
        P("shard"),
        P("shard", None),
        P("shard", None),
        P("shard"),
        P(),
        P("shard", None),
        P("shard"),
        P("shard", None),
        P("shard", None),
    )
    out_specs = (
        P("rep", "shard", None),
        P("rep", "shard", None),
        P("shard"),
        P("shard", None),
        P("shard"),
        P("shard", None),
        P("shard", None),
        P("shard"),
        P(),
        P("shard", None),
        P("shard"),
        P("shard", None),
        P("shard", None),
    )
    body = functools.partial(local, mesh.shape["rep"], mesh.shape["shard"])
    return jax.shard_map(body, mesh=mesh, in_specs=in_specs, out_specs=out_specs, check_vma=False)
```

```python
import functools
import math

import jax
import jax.numpy as jnp
from jax import lax
from jax.experimental import pallas as pl
from jax.experimental.pallas import tpu as pltpu
from jax.sharding import PartitionSpec as P

HEAD_DIM = 80
LANES = 128
CORES = 2
NORM_EPS = 1e-06
LOG_BASE = 1.442695041
MASK_FILL = -1e30
AXES = ("rep", "shard")
F32 = jnp.float32
BF16 = jnp.bfloat16


def dot(left, right, left_dim=1, right_dim=0):
    return lax.dot_general(
        left, right, (((left_dim,), (right_dim,)), ((), ())), preferred_element_type=F32
    )


class Place:
    def __init__(self, reps, shards, seqs):
        self.x_size = reps // CORES
        self.x_split = 2 if self.x_size == 2 else 1
        self.a_size = CORES * seqs
        self.b_size = shards // self.a_size
        self.even = self.x_size == 2 and self.b_size == 2
        self.peer_count = self.b_size * CORES
        self.seqs = seqs
        rep, shard = lax.axis_index("rep"), lax.axis_index("shard")
        self.x, self.c = rep // CORES, rep % CORES
        self.a, self.b = shard // self.b_size, shard % self.b_size
        self.shard = shard

    def route(self, move):
        pairs = []
        for x in range(self.x_size):
            for c in range(CORES):
                for a in range(self.a_size):
                    for b in range(self.b_size):
                        pairs.append((self.number(x, c, a, b), self.number(*move(x, c, a, b))))
        return pairs

    def number(self, x, c, a, b):
        return ((x * CORES + c) * self.a_size + a) * self.b_size + b

    def send(self, value, dx=0, dc=0, da=0, db=0):
        return lax.ppermute(
            value,
            AXES,
            self.route(
                lambda x, c, a, b: (
                    (x + dx) % self.x_size,
                    (c + dc) % CORES,
                    (a + da) % self.a_size,
                    (b + db) % self.b_size,
                )
            ),
        )

    def peers(self):
        return [(db, dc) for db in range(self.b_size) for dc in range(CORES)]

    def source(self, db, dc):
        return ((self.b - db) % self.b_size) * CORES + (self.c + dc) % CORES

    def to_cluster(self, tokens):
        seqs, count, width = tokens.shape
        half = count // CORES
        halves = tokens.reshape(seqs, CORES, half, width)
        shape = (seqs, half, width)
        moves = []
        for i in range(seqs):
            moves += [(0, (i, self.c), 0, i), (0, (i, 1 - self.c), 1, i)]
        own, give = shuffle([halves], [(shape, BF16)] * 2, moves)
        got = self.send(give, dc=1)
        after = yield
        parts = route_parts(self, own, got, after or ())
        received = [parts[0]] + [self.send(parts[d], da=d) for d in range(1, self.a_size)]
        moves = [(d, None, 0, (self.a - d) % self.a_size) for d in range(self.a_size)]
        after = yield
        yield shuffle(received, [((self.a_size, half, width), BF16)], moves, after or ())[0]

    def from_cluster(self, chunks):
        half, width = chunks.shape[1:]
        picks = [(0, (self.a + d) % self.a_size, d, None) for d in range(self.a_size)]
        parts = shuffle([chunks], [((half, width), BF16)] * self.a_size, picks)
        received = [parts[0]] + [self.send(parts[d], da=d) for d in range(1, self.a_size)]
        yield
        own, give = route_back(self, received)
        got = self.send(give, dc=1)
        moves = []
        for i in range(self.seqs):
            moves += [(0, i, 0, i * CORES + self.c), (1, i, 0, i * CORES + 1 - self.c)]
        yield
        whole = shuffle([own, got], [((self.a_size, half, width), BF16)], moves)[0]
        yield whole.reshape(self.seqs, CORES * half, width)

    def send_back(self, part, m):
        return lax.ppermute(part, AXES, [(j, i) for i, j in self.route(self._match(m))])

    def place_back(self, received):
        half, width = received[0].shape
        moves = []
        for m in range(self.a_size):
            t = m ^ self.a
            moves.append((m, None, 0, (t % self.seqs) * CORES + t // self.seqs))
        whole = shuffle(received, [((self.a_size, half, width), BF16)], moves)[0]
        return whole.reshape(self.seqs, CORES * half, width)

    def _match(self, m):
        def move(x, c, a, b):
            t = m ^ a
            return x, t // self.seqs, self.seqs * c + t % self.seqs, b

        return move


VMEM = pl.BlockSpec(memory_space=pltpu.VMEM)
ANY = pl.BlockSpec(memory_space=pl.ANY)


LAST = []
SCALE = 0.25
COST = {
    "project": 14.5,
    "attend_forward": 26.0,
    "middle": 20.0,
    "outer": 7.0,
    "outer_give": 0.1,
    "attend_backward": 25.0,
    "heads_outer": 5.5,
    "back_project": 3.5,
    "pad_weights": 3.5,
    "norm_back": 3.0,
    "finish_heads": 4.0,
    "finish_full": 3.5,
}


def call(name, body, scalars, inputs, outputs, grid=(1,), scratch=(), after=(), vmem=40):
    deps = [*LAST[-1:], *after]
    count, skip = len(inputs), len(deps)

    def run(spots, *refs):
        body(spots, *refs[:count], *refs[count + skip :])

    results = pl.pallas_call(
        run,
        out_shape=[jax.ShapeDtypeStruct(shape, kind) for shape, kind, _ in outputs],
        grid_spec=pltpu.PrefetchScalarGridSpec(
            num_scalar_prefetch=1,
            grid=grid,
            in_specs=[spec for _, spec in inputs] + [ANY] * skip,
            out_specs=[spec for _, _, spec in outputs],
            scratch_shapes=list(scratch),
        ),
        cost_estimate=pl.CostEstimate(
            flops=int(COST.get(name, 1.5) * SCALE * 1.1e9),
            bytes_accessed=int(COST.get(name, 1.5) * SCALE * 3.3e6),
            transcendentals=0,
        ),
        compiler_params=pltpu.CompilerParams(vmem_limit_bytes=vmem * 1024 * 1024),
        name=name,
    )(scalars_of(scalars), *[value for value, _ in inputs], *deps)
    LAST.append(results[0])
    return results


def scalars_of(values):
    if isinstance(values, (list, tuple)):
        return jnp.stack([jnp.asarray(v, jnp.int32) for v in values])
    return values


def shuffle_body(moves, counts, spots, *refs):
    sources, targets, sems = refs[: counts[0]], refs[counts[0] : -1], refs[-1]
    copies, n = [], 0
    for src, src_rank, dst, dst_rank in moves:
        ends = []
        for ref, rank in ((sources[src], src_rank), (targets[dst], dst_rank)):
            ends.append(ref.at[tuple(spots[n + k] for k in range(rank))] if rank else ref)
            n += rank
        copies.append(pltpu.make_async_copy(*ends, sems.at[len(copies)]))
    for copy in copies:
        copy.start()
    for copy in copies:
        copy.wait()


def shuffle(sources, shapes, moves, after=()):
    spots, shape_of = [], []
    for src, src_spot, dst, dst_spot in moves:
        ranks = []
        for spot in (src_spot, dst_spot):
            spot = () if spot is None else spot if isinstance(spot, tuple) else (spot,)
            ranks.append(len(spot))
            spots += spot
        shape_of.append((src, ranks[0], dst, ranks[1]))
    return call(
        "shuffle",
        functools.partial(shuffle_body, shape_of, (len(sources), len(shapes))),
        spots or [0],
        [(source, VMEM) for source in sources],
        [(*shape, ANY) for shape in shapes],
        scratch=[pltpu.SemaphoreType.DMA((len(moves),))],
        after=after,
    )


def route_parts_body(seqs, info, own, got, *outs):
    for d, out in enumerate(outs):
        target = info[1 + d]

        @pl.when(target // seqs == info[0])
        def near():
            out[...] = own[target % seqs]

        @pl.when(target // seqs != info[0])
        def far():
            out[...] = got[target % seqs]


def route_parts(at, own, got, after=()):
    return call(
        "route_parts",
        functools.partial(route_parts_body, at.seqs),
        [at.c, *ahead(at.a, at.a_size)],
        [(own, VMEM), (got, VMEM)],
        [(own.shape[1:], BF16, VMEM)] * at.a_size,
        after=after,
    )


def route_back_body(seqs, info, *refs):
    parts, own, give = refs[:-2], refs[-2], refs[-1]
    for d, part in enumerate(parts):
        source = info[1 + d]

        @pl.when(source // seqs == info[0])
        def near():
            own[source % seqs] = part[...]

        @pl.when(source // seqs != info[0])
        def far():
            give[source % seqs] = part[...]


def route_back(at, parts):
    shape = (at.seqs, *parts[0].shape)
    return call(
        "route_back",
        functools.partial(route_back_body, at.seqs),
        [at.c, *[(at.a - d) % at.a_size for d in range(at.a_size)]],
        [(part, VMEM) for part in parts],
        [(shape, BF16, VMEM)] * 2,
    )


def add_body(counts, spots, *refs):
    terms = sum(counts)
    ins, outs, n = refs[:terms], refs[terms:], 0
    for count, out in zip(counts, outs):
        total = ins[n][...].astype(F32)
        for k in range(1, count):
            total = total + ins[n + k][...].astype(F32)
        out[...] = total.reshape(out.shape).astype(out.dtype)
        n += count


def add_blocks(groups):
    spots, inputs, outputs = [], [], []
    for terms in groups:
        for value, dim, index in terms:
            block = [1 if k == dim else size for k, size in enumerate(value.shape)]

            def spot(i, s, dim=dim, n=len(spots), rank=value.ndim):
                return tuple(s[n] if k == dim else 0 for k in range(rank))

            spots.append(index)
            inputs.append((value, pl.BlockSpec(tuple(block), spot)))
        shape = tuple(size for k, size in enumerate(value.shape) if k != dim)
        outputs.append((shape, BF16, VMEM))
    return call(
        "add_blocks",
        functools.partial(add_body, [len(terms) for terms in groups]),
        spots,
        inputs,
        outputs,
    )


def later(value, *done):
    return lax.optimization_barrier((value, *done))[0]


def pick(stacked, index, axis=0):
    return lax.dynamic_index_in_dim(stacked, index, axis, keepdims=False)


def ring_gather(at, piece):
    up = at.send(piece, da=-1)
    down = at.send(piece, da=1)
    cut = max(1, piece.shape[0] // 2)
    far = [at.send(up[:cut], da=-1), at.send(down[cut:], da=1)]
    yield
    shape = (3, *piece.shape)
    yield shuffle([piece, up, down], [(shape, BF16)], [(k, None, 0, k) for k in range(3)])[0]
    moves = []
    for k in range(piece.shape[0]):
        moves.append((0, k, 0, k) if k < cut else (1, k - cut, 0, k))
    yield shuffle(far, [(piece.shape, BF16)], moves)[0]


def by_order(own, others, axis_size, spot):
    moves = [(d, None, 0, (spot - d) % axis_size) for d in range(axis_size)]
    return shuffle([own, *others], [((axis_size, *own.shape), own.dtype)], moves)[0]


def heads_part_body(count, groups, info, query, key, value, vectors, *outs):
    width = query.shape[1] // count // groups
    rows = outs[0].shape[0]
    down = pl.ds(pl.multiple_of(info[len(outs)] * rows, rows), rows)
    for n, out in enumerate(outs):
        for peer in range(count):

            @pl.when(info[n] == peer)
            def copy():
                for g in range(groups):
                    for k, source in enumerate((query, key, value)):
                        spot = (g * 3 + k) * width
                        first = (peer * groups + g) * width
                        out[:, spot : spot + width] = source[down, first : first + width]

        out[:, 3 * groups * width :] = vectors[down, :]


def heads_parts(at, weights, vectors, groups):
    rows, model = weights[0].shape
    count = at.peer_count
    shape = (rows // at.x_split, 3 * model // count + vectors.shape[1])
    targets = [((at.b + db) % at.b_size) * CORES + at.c for db in range(at.b_size)]
    return call(
        "heads_parts",
        functools.partial(heads_part_body, count, groups),
        [*targets, at.x if at.x_split == 2 else 0],
        [(w, VMEM) for w in (*weights, vectors)],
        [(shape, BF16, VMEM)] * at.b_size,
    )


def quarter_body(info, *refs):
    out, sem = refs[3], refs[4]
    rows, half = out.shape[1:]
    down = pl.ds(pl.multiple_of(info[0] * rows, rows), rows)
    right = pl.ds(pl.multiple_of(info[1] * half, half), half)
    copies = [pltpu.make_async_copy(refs[w].at[down, right], out.at[w], sem.at[w]) for w in range(3)]
    for copy in copies:
        copy.start()
    for copy in copies:
        copy.wait()


def quarter_of(at, weights, after):
    rows, model = weights[0].shape
    return call(
        "quarter",
        quarter_body,
        [at.x if at.x_split == 2 else 0, at.c],
        [(w, VMEM) for w in weights],
        [((3, rows // at.x_split, model // CORES), BF16, ANY)],
        scratch=[pltpu.SemaphoreType.DMA((3,))],
        after=after,
    )[0]


def pad_body(heads, groups, x_split, info, *refs):
    sources, outs = refs[: 2 * x_split], refs[2 * x_split :]
    compact, (padded, vectors) = outs[:groups], outs[groups:]
    b_size, rows, width = sources[1].shape
    used = 3 * heads * HEAD_DIM
    part = heads // groups
    padded[...] = jnp.zeros_like(padded)
    for n in range(x_split):
        for a in range(4):
            for b in range(b_size):
                piece = sources[2 * n][a, b] if a < 3 else sources[2 * n + 1][b]
                spot = (info[1 + a] * b_size + b) * x_split
                spot = (spot + (info[0] ^ n if x_split == 2 else 0)) * rows
                spot = pl.ds(pl.multiple_of(spot, rows), rows)
                for g in range(groups):
                    step = used // groups
                    compact[g][spot, :] = piece[:, g * step : (g + 1) * step]
                vectors[spot, :] = piece[:, used:]
                for k in range(3):
                    for h in range(heads):
                        first = (((h // part) * 3 + k) * part + h % part) * HEAD_DIM
                        lane = (k * heads + h) * LANES
                        padded[spot, lane : lane + HEAD_DIM] = piece[:, first : first + HEAD_DIM]


def pad_weights(at, sources, heads, groups, after):
    b_size, rows, width = sources[1].shape
    total = at.a_size * b_size * rows * at.x_split
    used = 3 * heads * HEAD_DIM
    return call(
        "pad_weights",
        functools.partial(pad_body, heads, groups, at.x_split),
        [at.x, at.a, (at.a + 1) % 4, (at.a + 3) % 4, (at.a + 2) % 4],
        [(source, VMEM) for source in sources],
        [
            *[((total, used // groups), BF16, VMEM)] * groups,
            ((total, 3 * heads * LANES), BF16, VMEM),
            ((total, width - used), BF16, VMEM),
        ],
        after=after,
    )


def project_body(count, spots, *refs):
    tokens, (gain, weight, bias, times, qkv, normed) = refs[:count], refs[count:]
    rows = tokens[0].shape[1]
    for p in range(count):
        value = tokens[p][0].astype(F32)
        rate = lax.rsqrt(jnp.mean(value * value, axis=-1, keepdims=True) + NORM_EPS)
        spot = pl.multiple_of(spots[p] * rows, rows)
        normed[pl.ds(spot, rows), :] = (value * rate * gain[...]).astype(BF16)
    step = qkv.shape[1] // 3
    for k in range(3):
        lanes = slice(k * step, (k + 1) * step)
        acc = dot(normed[...], weight[:, lanes])
        qkv[:, lanes] = ((acc + bias[:, lanes]) * times[:, lanes]).astype(BF16)


def project(at, parts, gain, weight, bias, times):
    a_size, half, model = parts[0].shape
    count = len(parts)
    cols = weight.shape[1]
    fixed = lambda a, s: (0, 0)
    return call(
        "project",
        functools.partial(project_body, count),
        [at.source(db, dc) for db, dc in at.peers()],
        [(part, pl.BlockSpec((1, half, model), lambda a, s: (a, 0, 0))) for part in parts]
        + [
            (gain, pl.BlockSpec((1, model), fixed)),
            (weight, pl.BlockSpec((model, cols), fixed)),
            (bias, pl.BlockSpec((1, cols), fixed)),
            (times, pl.BlockSpec((1, cols), fixed)),
        ],
        [
            (
                (a_size * count * half, cols),
                BF16,
                pl.BlockSpec((count * half, cols), lambda a, s: (a, 0)),
            ),
            (
                (a_size * count * half, model),
                BF16,
                pl.BlockSpec((count * half, model), lambda a, s: (a, 0)),
            ),
        ],
        grid=(a_size,),
    )


def forward_body(heads, block, info, starts, query, key, value, mixed, query_aug, total, top):
    index = pl.program_id(0)
    half = block // CORES
    core = info[pl.num_programs(0) + 1]
    total[...] = jnp.zeros_like(total)
    top[...] = jnp.full_like(top, MASK_FILL)
    rows = index * block + lax.broadcasted_iota(jnp.int32, (block, block), 0)
    begin = starts[...][:, :1]

    def step(j, carry):
        spot = pl.multiple_of(j * block, block)
        columns = spot + lax.broadcasted_iota(jnp.int32, (block, block), 1)
        bias = jnp.where((columns >= begin) & (columns <= rows), 0.0, MASK_FILL)
        for h in range(heads):
            lanes = slice(h * LANES, (h + 1) * LANES)
            score = dot(query[:, lanes], key[pl.ds(spot, block), lanes], 1, 1) + bias
            old = top[h]
            new = jnp.maximum(old, jnp.max(score, axis=1, keepdims=True))
            weight = jnp.exp(score - jnp.concatenate([new] * (block // LANES), axis=1))
            total[h] = total[h] * jnp.exp(old - new) + dot(
                weight.astype(BF16), value[pl.ds(spot, block), lanes]
            )
            top[h] = new
        return carry

    lax.fori_loop(info[index], index + 1, step, 0)
    lane = lax.broadcasted_iota(jnp.int32, (block, LANES), 1)
    for h in range(heads):
        lanes = slice(h * LANES, (h + 1) * LANES)
        acc = total[h]
        weight_sum = acc[:, HEAD_DIM : HEAD_DIM + 1]
        result = (acc / weight_sum)[:, :HEAD_DIM].astype(BF16)
        for k in range(CORES):
            mixed[0, core ^ k, 0, :, h * HEAD_DIM : (h + 1) * HEAD_DIM] = result[
                k * half : (k + 1) * half
            ]
        rest = -(top[h] + jnp.log(weight_sum))
        aug = query[:, lanes].astype(F32)
        for k in range(3):
            term = rest.astype(BF16).astype(F32)
            aug = jnp.where(lane == HEAD_DIM + k, term, aug)
            rest = rest - term
        query_aug[:, lanes] = aug.astype(BF16)


def attend_forward(at, info, starts, qkv, heads, block):
    length = qkv.shape[0]
    wide = heads * LANES
    width = heads * HEAD_DIM
    count = length // block
    b_size = at.b_size
    return call(
        "attend_forward",
        functools.partial(forward_body, heads, block),
        info,
        [
            (starts, pl.BlockSpec((block, LANES), lambda i, s: (i, 0))),
            (qkv, pl.BlockSpec((block, wide), lambda i, s: (i, 0))),
            (qkv, pl.BlockSpec((length, wide), lambda i, s: (0, 1))),
            (qkv, pl.BlockSpec((length, wide), lambda i, s: (0, 2))),
        ],
        [
            (
                (b_size, CORES, at.a_size, block // CORES, width),
                BF16,
                pl.BlockSpec(
                    (1, CORES, 1, block // CORES, width),
                    lambda i, s: ((i + b_size - s[count]) % b_size, 0, i // b_size, 0, 0),
                ),
            ),
            ((length, wide), BF16, pl.BlockSpec((block, wide), lambda i, s: (i, 0))),
        ],
        grid=(count,),
        scratch=[
            pltpu.VMEM((heads, block, LANES), F32),
            pltpu.VMEM((heads, block, LANES), F32),
        ],
    )


def backward_body(
    heads,
    first,
    block,
    count,
    info,
    starts,
    scale,
    query,
    key,
    value,
    mixed,
    *rest,
):
    grad_refs = rest[:count]
    grads, scale_sum, bias_sum, grad, grad_aug, d_query, d_key, d_value = rest[count:]
    index = pl.num_programs(0) - 1 - pl.program_id(0)
    b_own, core = info[pl.num_programs(0)], info[pl.num_programs(0) + 1]
    b_size = count // CORES
    width = heads * HEAD_DIM

    @pl.when(pl.program_id(0) == 0)
    def clear():
        d_key[...] = jnp.zeros_like(d_key)
        d_value[...] = jnp.zeros_like(d_value)
        scale_sum[...] = jnp.zeros_like(scale_sum)
        bias_sum[...] = jnp.zeros_like(bias_sum)

    half = block // CORES
    lane = lax.broadcasted_iota(jnp.int32, (half, LANES), 1)
    for k in range(CORES):
        peer = ((b_own + b_size - index % b_size) % b_size) * CORES + (core ^ k)
        for p in range(count):

            @pl.when(peer == p)
            def fetch():
                grad[...] = grad_refs[p][index // b_size]

        for h in range(heads):
            part = slice((first + h) * HEAD_DIM, (first + h + 1) * HEAD_DIM)
            grad_h = grad[:, part].astype(F32)
            mixed_h = mixed[0, core ^ k, 0, :, part].astype(F32)
            delta = jnp.sum(grad_h * mixed_h, axis=1, keepdims=True)
            aug = jnp.concatenate([grad_h, jnp.zeros((half, LANES - HEAD_DIM), F32)], axis=1)
            high = (-delta).astype(BF16).astype(F32)
            aug = jnp.where(lane == HEAD_DIM, high, aug)
            aug = jnp.where(lane == HEAD_DIM + 1, -delta - high, aug)
            grad_aug[k * half : (k + 1) * half, h * LANES : (h + 1) * LANES] = aug.astype(BF16)
    d_query[...] = jnp.zeros_like(d_query)
    columns = index * block + lax.broadcasted_iota(jnp.int32, (block, block), 1)
    begin = starts[0:1, :]

    def step(j, carry):
        spot = pl.multiple_of(j * block, block)
        rows = spot + lax.broadcasted_iota(jnp.int32, (block, block), 0)
        allowed = (rows >= begin) & (rows <= columns)
        for h in range(heads):
            lanes = slice(h * LANES, (h + 1) * LANES)
            key_h = key[pl.ds(spot, block), lanes]
            query_h = query[:, lanes]
            grad_h = grad_aug[:, lanes]
            prob = jnp.where(allowed, jnp.exp(dot(key_h, query_h, 1, 1)), 0.0)
            d_prob = dot(value[pl.ds(spot, block), lanes], grad_h, 1, 1)
            d_score = (prob * d_prob).astype(BF16)
            d_value[pl.ds(spot, block), lanes] += dot(prob.astype(BF16), grad_h)
            d_key[pl.ds(spot, block), lanes] += dot(d_score, query_h)
            d_query[:, lanes] += dot(d_score, key_h, 0, 0)
        return carry

    lax.fori_loop(info[index], index + 1, step, 0)
    here = pl.ds(pl.multiple_of(index * block, block), block)
    for h in range(heads):
        lanes = slice(h * LANES, (h + 1) * LANES)
        d_scaled = d_query[:, lanes].astype(BF16).astype(F32)
        scale_sum[...] += jnp.sum(d_scaled * query[:, lanes].astype(F32), axis=0, keepdims=True)
        d_q = (d_scaled * scale[0:1, lanes]).astype(BF16)
        for k, term in enumerate((d_q, d_key[here, lanes], d_value[here, lanes])):
            spot = k * width + h * HEAD_DIM
            term = term.astype(BF16)
            grads[:, spot : spot + HEAD_DIM] = term[:, :HEAD_DIM]
            bias_sum[:, (k * heads + h) * LANES : (k * heads + h + 1) * LANES] += jnp.sum(
                term.astype(F32), axis=0, keepdims=True
            )


def attend_backward(
    at, info, starts, scale, query_aug, qkv, grads, mixed, heads, groups, group, block
):
    length = qkv.shape[0]
    wide = heads * LANES
    width = heads * HEAD_DIM
    count = length // block
    b_size = at.b_size
    half = block // CORES

    def mixed_spot(i, s):
        i = count - 1 - i
        return (i + b_size - s[count]) % b_size, 0, i // b_size, 0, 0

    fixed = lambda i, s: (0, 0)
    return call(
        "attend_backward",
        functools.partial(backward_body, heads, group * heads, block, len(grads)),
        info,
        [
            (starts, pl.BlockSpec((8, block), lambda i, s: (0, count - 1 - i))),
            (scale, pl.BlockSpec((8, wide), fixed)),
            (query_aug, pl.BlockSpec((block, wide), lambda i, s: (count - 1 - i, group))),
            (qkv, pl.BlockSpec((length, wide), lambda i, s: (0, groups + group))),
            (qkv, pl.BlockSpec((length, wide), lambda i, s: (0, 2 * groups + group))),
            (mixed, pl.BlockSpec((1, CORES, 1, half, mixed.shape[4]), mixed_spot)),
        ]
        + [(grad, VMEM) for grad in grads],
        [
            (
                (length, 3 * width),
                BF16,
                pl.BlockSpec((block, 3 * width), lambda i, s: (count - 1 - i, 0)),
            ),
            ((8, LANES), F32, pl.BlockSpec((8, LANES), fixed)),
            ((8, 3 * wide), F32, pl.BlockSpec((8, 3 * wide), fixed)),
        ],
        grid=(count,),
        scratch=[
            pltpu.VMEM((half, mixed.shape[4]), BF16),
            pltpu.VMEM((block, wide), BF16),
            pltpu.VMEM((block, wide), F32),
            pltpu.VMEM((length, wide), F32),
            pltpu.VMEM((length, wide), F32),
        ],
    )


def concat_body(info, *refs):
    parts, out = refs[:-1], refs[-1]
    width = parts[0].shape[1]
    for p, part in enumerate(parts):
        out[:, p * width : (p + 1) * width] = part[...]


def concat(parts, after):
    rows, width = parts[0].shape
    return call(
        "concat",
        concat_body,
        [0],
        [(part, VMEM) for part in parts],
        [((rows, width * len(parts)), BF16, VMEM)],
        after=after,
    )[0]


def middle_body(count, source_count, moves, info, *refs):
    mixed, tokens, d_out, gain = refs[:4]
    sources = refs[4 : 4 + source_count]
    outs = refs[4 + source_count :]
    output, d_residual, d_proj, normed, activated, d_up = outs[:6]
    d_parts = outs[6:-4]
    weights, sems = outs[-4:-1], outs[-1]
    w_out, w_up, w_down = weights
    rows, half = sources[0].shape[2:]
    width = d_parts[0].shape[1]

    def copies(w):
        for n, (src, s, k) in enumerate(moves):
            if k == w:
                down = pl.ds(pl.multiple_of(info[2 * n] * rows, rows), rows)
                right = pl.ds(pl.multiple_of(info[2 * n + 1] * half, half), half)
                yield pltpu.make_async_copy(
                    sources[src].at[s, w], weights[w].at[down, right], sems.at[n]
                )

    def arrived(w):
        @pl.when(pl.program_id(0) == 0)
        def wait():
            for copy in copies(w):
                copy.wait()

    @pl.when(pl.program_id(0) == 0)
    def start():
        for w in range(3):
            for copy in copies(w):
                copy.start()

    arrived(0)
    residual = tokens[...].astype(F32) + dot(mixed[...], w_out[...])
    rate = lax.rsqrt(jnp.mean(residual * residual, axis=-1, keepdims=True) + NORM_EPS)
    normed[...] = (residual * rate * gain[...]).astype(BF16)
    arrived(1)
    upward = dot(normed[...], w_up[...])
    gate = 1.0 / (1.0 + jnp.exp(-upward))
    activated[...] = (upward * gate).astype(BF16)
    arrived(2)
    output[...] = (residual + dot(activated[...], w_down[...])).astype(BF16)
    d_activated = dot(d_out[...], w_down[...], 1, 1)
    d_up[...] = (d_activated * gate * (1 + upward * (1 - gate))).astype(BF16)
    scaled = dot(d_up[...], w_up[...], 1, 1) * gain[...]
    inner = jnp.mean(residual * scaled, axis=-1, keepdims=True)
    d_norm = rate * scaled - residual * (rate * rate * rate * inner)
    d_total = d_out[...].astype(F32) + d_norm
    d_residual[...] = d_total
    d_proj[...] = d_total.astype(BF16)
    d_mixed = dot(d_proj[...], w_out[...], 1, 1).astype(BF16)
    for p in range(count):
        d_parts[p][...] = d_mixed[:, p * width : (p + 1) * width]


def middle(at, mixed, tokens, d_out, gain, sources):
    count = at.peer_count
    rows, model = tokens.shape
    width = model // count
    arrays = list(sources.values())
    a_size, _, piece, half = arrays[0].shape
    group = model // at.peer_count // piece
    moves, spots = [], []
    for n, (dx, db, dc) in enumerate(sources):
        for a in range(a_size):
            for w in range(3):
                row = a * at.b_size + (at.b - db) % at.b_size
                if at.x_split == 2:
                    row = row * 2 + (at.x + dx) % 2
                if w == 0:
                    peer, rest = row // group, row % group
                    far = (at.b - peer // CORES) % at.b_size
                    row = (far * CORES + ((peer % CORES) ^ at.c)) * group + rest
                moves.append((n, a, w))
                spots += [row, (at.c + dc) % CORES]
    block = min(256, rows)
    row = lambda i, s: (i, 0)
    rows_of = pl.BlockSpec((block, model), row)
    part = pl.BlockSpec((block, width), row)
    types = [BF16, F32, BF16, BF16, BF16, BF16]
    return call(
        "middle",
        functools.partial(middle_body, count, len(arrays), moves),
        spots,
        [(mixed, rows_of), (tokens, rows_of), (d_out, rows_of)]
        + [(gain, pl.BlockSpec(gain.shape, lambda i, s: (0, 0)))]
        + [(source, ANY) for source in arrays],
        [((rows, model), kind, rows_of) for kind in types]
        + [((rows, width), BF16, part)] * count,
        grid=(rows // block,),
        scratch=[pltpu.VMEM((model, model), BF16)] * 3
        + [pltpu.SemaphoreType.DMA((len(moves),))],
    )


def outer_body(count, split, add, info, *refs):
    pairs, rest = refs[:6], refs[6:]
    for w in range(3):

        @pl.when(pl.program_id(0) == w)
        def product():
            value = dot(pairs[2 * w][...], pairs[2 * w + 1][...], 0, 0)
            target = rest[-1] if split else rest[-1].at[0]
            width = value.shape[0] // count
            for p in range(count):
                spot = p * width
                if w == 0:
                    spot = pl.multiple_of(info[3 + p] * width, width)
                part = value[p * width : (p + 1) * width]
                if add:
                    part = part + rest[0][0, pl.ds(spot, width)].astype(F32)
                target[pl.ds(spot, width)] = part.astype(BF16)

    if split:
        keep_x, give_x, keep_b, give_b, total = rest[1:]
        pairs_a, b_size, rows = keep_x.shape[1:4]
        for k in range(pairs_a):
            for b in range(b_size):
                for half, out in ((info[1], keep_x), (1 - info[1], give_x)):
                    spot = pl.multiple_of((k * b_size + b) * 2 * rows + half * rows, rows)
                    out[0, k, b] = total[pl.ds(spot, rows)]
            for b, out in ((info[2], keep_b), (1 - info[2], give_b)):
                for half in range(2):
                    spot = (((k + pairs_a) * b_size) * 2 + half) * rows + b * 2 * rows
                    out[0, k, half] = total[pl.ds(pl.multiple_of(spot, rows), rows)]


def outer(at, pairs, cols, add=None, after=()):
    rows, model = pairs[0][0].shape
    half = model // CORES
    count = at.peer_count
    split = add is not None and at.even
    info = [cols, at.x if at.even else 0, at.b, *[at.source(db, dc) for db, dc in at.peers()]]
    inputs = []
    for left, right in pairs:
        inputs.append((left, pl.BlockSpec((rows, model), lambda w, s: (0, 0))))
        inputs.append((right, pl.BlockSpec((rows, half), lambda w, s: (0, s[0]))))
    block = pl.BlockSpec((1, model, half), lambda w, s: (w, 0, 0))
    outputs = [((3, model, half), BF16, block)]
    scratch = []
    if add is not None:
        inputs.append((add, block))
    if split:
        shape = (at.a_size // 2, 2, model // at.a_size // 4, half)
        part = pl.BlockSpec((1, *shape), lambda w, s: (w, 0, 0, 0, 0))
        outputs = [((3, *shape), BF16, part)] * 4
        scratch = [pltpu.VMEM((model, half), BF16)]
    return call(
        "outer_give" if add is None else "outer",
        functools.partial(outer_body, count, split, add is not None),
        info,
        inputs,
        outputs,
        grid=(3,),
        scratch=scratch,
        after=after,
        vmem=60,
    )


def give_body(groups, info, *refs):
    grads, weights, out = refs[:groups], refs[groups : 2 * groups], refs[-1]
    value = back_product(grads, weights)
    out[...] = value.astype(BF16).reshape(out.shape)


def back_product(grads, weights):
    total = 0.0
    for grad, weight in zip(grads, weights):
        total = total + dot(grad[...].reshape(-1, grad.shape[-1]), weight[...], 1, 1)
    return total


def keep_body(groups, info, *refs):
    grads, weights, got = refs[:groups], refs[groups : 2 * groups], refs[2 * groups]
    outs = refs[2 * groups + 1 :]
    pairs, b_size, half = got.shape[:3]
    value = back_product(grads, weights).reshape(got.shape) + got[...].astype(F32)
    for b in range(b_size):
        for n, out in enumerate(outs):

            @pl.when(info[2 + n] == b)
            def copy():
                out[...] = value[:, b].astype(out.dtype)


def back_project(at, grads, weights, half, which, got=None):
    model = weights[0].shape[0]
    pair = at.a_size // 2
    groups = len(grads)
    width = grads[0].shape[1]
    shape = (pair, at.b_size, half, model)
    grads = [g.reshape(at.a_size, at.b_size, CORES, half, width) for g in grads]
    block = pl.BlockSpec((pair, at.b_size, 1, half, width), lambda i, s: (s[0], 0, s[1], 0, 0))
    core = at.c if got is not None else 1 - at.c
    inputs = [(g, block) for g in grads]
    inputs += [(weight, VMEM) for weight in weights]
    if got is None:
        body, outputs = give_body, [(shape, BF16, VMEM)]
    else:
        body = keep_body
        inputs.append((got, VMEM))
        outputs = [((pair, half, model), F32 if db == 0 else BF16, VMEM) for db in range(at.b_size)]
    return call(
        "back_project",
        functools.partial(body, groups),
        [which ^ core, core, *ahead(at.b, at.b_size)],
        inputs,
        outputs,
    )


def norm_back_body(count, info, *refs):
    own, others = refs[0], refs[1:count]
    tokens, d_residual, gain = refs[count : count + 3]
    for n, out in enumerate(refs[count + 3 :]):
        k = info[1 + n]
        grad = own[k]
        for other in others:
            grad = grad + other[k].astype(F32)
        value = tokens[k].astype(F32)
        rate = lax.rsqrt(jnp.mean(value * value, axis=-1, keepdims=True) + NORM_EPS)
        scaled = grad * gain[...]
        inner = jnp.mean(value * scaled, axis=-1, keepdims=True)
        d_norm = rate * scaled - value * (rate * rate * rate * inner)
        out[...] = (d_residual[k] + d_norm).astype(BF16)


def norm_back(at, terms, chunks, d_residual, gain, which):
    pair, half, model = terms[0].shape
    block = pl.BlockSpec((pair, half, model), lambda i, s: (s[0], 0, 0))
    order = [k ^ (at.a % pair) for k in range(pair)]
    return call(
        "norm_back",
        functools.partial(norm_back_body, len(terms)),
        [which ^ at.c, *order],
        [(t, VMEM) for t in terms] + [(chunks, block), (d_residual, block), (gain, VMEM)],
        [((half, model), BF16, VMEM)] * pair,
    )


def heads_outer_body(steps, info, normed, grads, extra, *rest):
    outs, acc = rest[:-1], rest[-1]
    value = dot(normed[...], grads[...], 0, 0)

    @pl.when(pl.program_id(0) == 0)
    def first():
        acc[...] = value

    @pl.when(pl.program_id(0) != 0)
    def later():
        acc[...] += value

    @pl.when(pl.program_id(0) == steps - 1)
    def last():
        used = acc.shape[1]
        pairs, b_size, rows = outs[0].shape[:3]
        split = len(outs)
        for n, out in enumerate(outs):
            for s in range(pairs * b_size):
                spot = (s * split + (info[0] ^ n if split == 2 else 0)) * rows
                spot = pl.ds(pl.multiple_of(spot, rows), rows)
                out[s // b_size, s % b_size, :, :used] = acc[spot, :].astype(BF16)
                out[s // b_size, s % b_size, :, used:] = extra[spot, :]


def heads_outer(at, normed, grads, extra):
    length, model = normed.shape
    used = grads.shape[1]
    block = min(512, length)
    steps = length // block
    rows = model // at.a_size // at.b_size // at.x_split
    shape = (at.a_size, at.b_size, rows, used + extra.shape[1])
    return call(
        "heads_outer",
        functools.partial(heads_outer_body, steps),
        [at.x],
        [
            (normed, pl.BlockSpec((block, model), lambda i, s: (i, 0))),
            (grads, pl.BlockSpec((block, used), lambda i, s: (i, 0))),
            (extra, pl.BlockSpec(extra.shape, lambda i, s: (0, 0))),
        ],
        [(shape, BF16, pl.BlockSpec(shape, lambda i, s: (0, 0, 0, 0)))] * at.x_split,
        grid=(steps,),
        scratch=[pltpu.VMEM((model, used), F32)],
    )


def all_sum(at, value, axis, size):
    total = value
    for d in range(1, size):
        total = total + at.send(value, **{axis: d}).astype(value.dtype)
    return total


def ahead(spot, size):
    return [(spot + d) % size for d in range(size)]


def cat_body(info, first, first_got, second, second_got, out):
    pair = first.shape[1]
    out[:, :pair] = (first[...].astype(F32) + first_got[...].astype(F32)).astype(BF16)
    out[:, pair:] = (second[...].astype(F32) + second_got[...].astype(F32)).astype(BF16)


class FullReduce:
    def __init__(self, at, parts):
        self.at = at
        if at.even:
            keep_x, give_x, keep_b, give_b = parts
            self.first = keep_x, at.send(give_x, dx=1)
            self.second = keep_b, at.send(give_b, db=1)
        else:
            self.part = parts[0].reshape(3, at.a_size, at.b_size, -1, parts[0].shape[-1])

    def next(self):
        at = self.at
        if not at.even:
            return
        groups = [[(t, 2, b) for t in self.first] for b in ahead(at.b, 2)]
        groups += [[(t, 2, x) for t in self.second] for x in ahead(at.x, 2)]
        keep_b, give_b, keep_x, give_x = add_blocks(groups)
        self.first = keep_b, at.send(give_b, db=1)
        self.second = keep_x, at.send(give_x, dx=1)

    def over_a(self):
        at = self.at
        part = None
        if at.even:
            shape = self.first[0].shape
            part = call(
                "cat",
                cat_body,
                [0],
                [(t, VMEM) for t in (*self.first, *self.second)],
                [((3, at.a_size, *shape[2:]), BF16, VMEM)],
            )[0]
        else:
            part = self.part
        parts = add_blocks([[(part, 1, a)] for a in ahead(at.a, at.a_size)])
        self.got = [parts[0]] + [at.send(parts[d], da=d) for d in range(1, at.a_size)]

    def end(self):
        at = self.at
        if at.even:
            part = add_blocks([[(t[None], 0, 0) for t in self.got]])[0]
            far = at.send(part, dx=1)
            return [part, far, at.send(part, dc=1), at.send(far, dc=1)]
        parts = add_blocks([[(t, 1, b) for t in self.got] for b in ahead(at.b, at.b_size)])
        got = [parts[0]] + [at.send(parts[d], db=d) for d in range(1, at.b_size)]
        part = add_blocks([[(t[None], 0, 0) for t in got]])[0]
        part = all_sum(at, part, "dx", at.x_size)
        return [part, at.send(part, dc=1)]


class HeadsReduce:
    def __init__(self, at, parts):
        self.at = at
        self.got = [parts[0]]
        if at.x_split == 2:
            self.got.append(at.send(parts[1], dx=1))

    def over_a(self):
        at = self.at
        parts = add_blocks([[(t, 0, a) for t in self.got] for a in ahead(at.a, at.a_size)])
        self.got = [parts[0]] + [at.send(parts[d], da=d) for d in range(1, at.a_size)]
        return parts

    def to_peers(self):
        at = self.at
        if at.x_split == 1:
            total = add_blocks([[(t[None], 0, 0) for t in self.got]])[0]
            self.got = [all_sum(at, total, "dx", at.x_size)]
        parts = add_blocks([[(t, 0, b) for t in self.got] for b in ahead(at.b, at.b_size)])
        parts = [
            at.send(parts[db], db=db, dc=dc) if db or dc else parts[0] for db, dc in at.peers()
        ]
        if at.x_split == 1:
            return [parts]
        return [parts, at.send(jnp.stack(parts), dx=1)]


def in_order(info, refs, split, half, core, spot):
    near = [r[spot] for r in refs]
    if split == 2:
        near = [jnp.where(info[0] == half, near[2 * k], near[2 * k + 1]) for k in range(2)]
    return jnp.where(info[1] == core, near[0], near[1])


def finish_full_body(split, info, *refs):
    count = CORES * split
    parts, (weight, gain), outs = refs[:count], refs[count : count + 2], refs[count + 2 :]
    rows, half = parts[0].shape[1:]
    for x in range(split):
        spot = slice(x * rows, (x + 1) * rows)
        for w in range(3):
            for c in range(CORES):
                outs[w][spot, c * half : (c + 1) * half] = in_order(
                    info, parts, split, x, c, w
                ).astype(F32)
    total = jnp.sum(outs[1][...] * weight[...].astype(F32), axis=1, keepdims=True)
    outs[3][...] = total / gain[...].astype(F32)


def finish_full(at, parts, weight, gain, after):
    rows, model = weight.shape
    return call(
        "finish_full",
        functools.partial(finish_full_body, 2 if at.even else 1),
        [at.x, at.c],
        [(p, VMEM) for p in parts] + [(weight, VMEM), (gain[:, None], VMEM)],
        [((rows, model), F32, VMEM)] * 3 + [((rows, 1), F32, VMEM)],
        after=after,
    )


def finish_heads_body(count, groups, split, info, *refs):
    parts, refs = refs[: groups * count], refs[groups * count :]
    far, refs = refs[: groups * (split - 1)], refs[groups * (split - 1) :]
    weights, gain, outs = refs[:3], refs[3], refs[4:]
    few = outs[4].shape[1]
    rows, width = parts[0].shape
    width = (width - few) // 3
    for n in range(split):
        down = pl.ds(pl.multiple_of((info[count] ^ n if split == 2 else 0) * rows, rows), rows)
        total = jnp.zeros((rows, few), F32)
        for p in range(count):
            for g in range(groups):
                source = far[g].at[p] if n else parts[g * count + p]
                total = total + source[:, 3 * width :].astype(F32)
                for peer in range(count):

                    @pl.when(info[p] == peer)
                    def copy():
                        for k in range(3):
                            spot = (peer * groups + g) * width
                            piece = source[:, k * width : (k + 1) * width]
                            outs[k][down, spot : spot + width] = piece.astype(F32)

        outs[4][down, :] = total
    total = jnp.zeros(outs[3].shape, F32)
    for k in range(3):
        total = total + jnp.sum(outs[k][...] * weights[k][...].astype(F32), axis=1, keepdims=True)
    outs[3][...] = total / gain[...].astype(F32)


def finish_heads(at, parts, weights, gain, few):
    rows, model = weights[0].shape
    flat = [part for group in parts for part in group[0]]
    flat += [group[1] for group in parts if at.x_split == 2]
    return call(
        "finish_heads",
        functools.partial(finish_heads_body, at.peer_count, len(parts), at.x_split),
        [*[at.source(db, dc) for db, dc in at.peers()], at.x],
        [(p, VMEM) for p in flat] + [(w, VMEM) for w in weights] + [(gain[:, None], VMEM)],
        [((rows, model), F32, VMEM)] * 3 + [((rows, 1), F32, VMEM), ((rows, few), F32, VMEM)],
    )


def local(
    reps,
    shards,
    activations,
    cotangent,
    doc_lengths,
    gain_attn,
    query_weight,
    query_bias,
    key_weight,
    value_weight,
    value_bias,
    dim_scale,
    out_weight,
    gain_mlp,
    up_weight,
    down_weight,
):
    seqs, tok_count, model = activations.shape
    at = Place(reps, shards, seqs)
    half = tok_count // CORES
    length = tok_count * shards
    peer_count = at.peer_count
    heads = model // HEAD_DIM // peer_count
    width = heads * HEAD_DIM
    wide = heads * LANES
    own_rows = at.a_size * half
    rows = gain_attn.shape[0]
    groups = 2
    block = CORES * half
    mine = at.b * CORES + at.c

    LAST.clear()
    stage = at.to_cluster(activations)
    next(stage)
    vectors = jnp.stack([gain_attn, gain_mlp, query_bias, value_bias], axis=1)
    own, *sent = heads_parts(at, (query_weight, key_weight, value_weight), vectors, groups)
    sent = [at.send(part, db=db + 1) for db, part in enumerate(sent)]
    next(stage)
    near = by_order(own, sent, at.b_size, at.b)
    ring = ring_gather(at, near)
    next(ring)
    chunks = next(stage)
    nears = [at.send(chunks, db=db) if db else chunks for db in range(at.b_size)]
    most = next(ring)
    sources = [most, None]
    if at.x_split == 2:
        sources += [at.send(most, dx=1), None]
    far = next(ring)
    parts = []
    for near in nears:
        parts += [near, at.send(later(near, far), dc=1)]
    sources[1] = far
    if at.x_split == 2:
        sources[3] = at.send(far, dx=1)
    quarter = quarter_of(at, (out_weight, up_weight, down_weight), parts[1:])
    stage = at.to_cluster(cotangent)
    next(stage)
    pieces = [quarter] + [at.send(quarter, da=d) for d in range(1, at.a_size)]
    *w_heads, w_pad, vectors = pad_weights(
        at, sources, heads, groups, parts[1:]
    )
    moves = [(d, None, 0, (at.a - d) % at.a_size) for d in range(at.a_size)]
    quarter = shuffle(pieces, [((at.a_size, *quarter.shape), BF16)], moves)[0]
    others = {(0, 0, 0): quarter, (0, 0, 1): at.send(quarter, dc=1)}
    for db in range(1, at.b_size):
        others[(0, db, 0)] = at.send(quarter, db=db)
    if at.x_split == 2:
        others[(1, 0, 0)] = at.send(quarter, dx=1)
    vectors = vectors.T.astype(F32)
    g_attn, g_mlp, b_query, b_value = vectors[0], vectors[1], vectors[2], vectors[3]

    other_lengths = at.send(doc_lengths, dc=1)
    lengths = pick(jnp.where(at.c == at.a // seqs, doc_lengths, other_lengths), at.a % seqs)
    ends = jnp.cumsum(lengths)
    places = jnp.arange(length, dtype=jnp.int32)
    starts = jnp.max(jnp.where(ends[None, :] <= places[:, None], ends[None, :], 0), axis=1)
    starts_row = jnp.broadcast_to(starts[None, :], (8, length))
    starts_col = jnp.broadcast_to(starts[:, None], (length, LANES))
    info = jnp.concatenate([starts[::block] // block, jnp.stack([at.b, at.c])]).astype(jnp.int32)

    scale_dim = LOG_BASE / math.sqrt(HEAD_DIM) * jax.nn.softplus(dim_scale)
    scale_pad = jnp.tile(jnp.pad(scale_dim, (0, LANES - HEAD_DIM)), heads)
    lane = jnp.arange(LANES)
    ones_key = ((lane >= HEAD_DIM) & (lane < HEAD_DIM + 3)).astype(F32)
    ones_value = ((lane >= HEAD_DIM) & (lane < HEAD_DIM + 2)).astype(F32)

    def pad_heads(vec):
        part = lax.dynamic_slice_in_dim(vec, mine * width, width, 0).reshape(heads, HEAD_DIM)
        return jnp.pad(part, ((0, 0), (0, LANES - HEAD_DIM))).reshape(wide)

    bias_pad = jnp.concatenate(
        [
            pad_heads(b_query),
            jnp.tile(ones_key, heads),
            pad_heads(b_value) + jnp.tile(ones_value, heads),
        ]
    )
    times = jnp.concatenate([scale_pad, jnp.ones((2 * wide,), F32)])
    qkv, normed = project(at, parts, g_attn[None], w_pad, bias_pad[None], times[None])

    part_heads = heads // groups
    part_width = part_heads * HEAD_DIM
    stage.send([others[(0, db, 0)] for db in range(1, at.b_size)] + [others[(0, 0, 1)]])
    soon = []
    if at.x_split == 2:
        for db in range(1, at.b_size):
            others[(1, db, 0)] = at.send(later(others[(0, db, 0)], qkv), dx=1)
            soon.append(others[(1, db, 0)])
        others[(1, 0, 1)] = at.send(later(others[(1, 0, 0)], qkv), dc=1)
        soon.append(others[(1, 0, 1)])
    mixed_rel, query_aug = attend_forward(at, info, starts_col, qkv, heads, block)
    parts = []
    for db, dc in at.peers():
        part = mixed_rel[db, dc].reshape(own_rows, width)
        parts.append(at.send(part, db=db, dc=dc) if db or dc else part)
    d_out = stage.send(soon).reshape(own_rows, model)
    last = []
    for dx, db, dc in list(others):
        if (dx, db, 1) not in others:
            others[(dx, db, 1)] = at.send(later(others[(dx, db, 0)], d_out), dc=1)
            last.append(others[(dx, db, 1)])
    mixed = concat(parts, last)
    tokens = chunks.reshape(own_rows, model)
    output, d_residual, d_proj, normed_mlp, activated, d_up, *d_parts = middle(
        at, mixed, tokens, d_out, g_mlp[None], others
    )

    grads = []
    for (db, dc), part in zip(at.peers(), d_parts):
        part = at.send(part, db=db, dc=dc) if db or dc else part
        grads.append(part.reshape(at.a_size, half, width))

    pairs = [(mixed, d_proj), (normed_mlp, d_up), (activated, d_out)]
    give = outer(at, pairs, 1 - at.c)[0]
    full = FullReduce(at, outer(at, pairs, at.c, at.send(give, dc=1), grads))

    scale_rows = jnp.broadcast_to(scale_pad[None, : part_heads * LANES], (8, part_heads * LANES))
    zeros = jnp.zeros((model,), F32)

    def backward(g):
        d_heads, scale_sum, bias_sum = attend_backward(
            at,
            info,
            starts_row,
            scale_rows,
            query_aug,
            qkv,
            grads,
            mixed_rel,
            part_heads,
            groups,
            g,
            block,
        )
        bias_sum = bias_sum[0].reshape(3, part_heads, LANES)[:, :, :HEAD_DIM]
        bias_sum = bias_sum.reshape(3, part_width)
        spot = (mine * groups + g) * part_width
        scale_sum = jnp.pad(scale_sum[0, :HEAD_DIM], (0, rows - HEAD_DIM))
        extra = [
            lax.dynamic_update_slice(zeros, bias_sum[0], (spot,)),
            lax.dynamic_update_slice(zeros, bias_sum[2], (spot,)),
            jnp.tile(scale_sum, shards),
        ]
        return d_heads, jnp.stack(extra, axis=1).astype(BF16)

    stage = at.from_cluster(output.reshape(at.a_size, half, model))
    next(stage)
    d_first, extra_first = backward(0)
    full.next()
    next(stage)
    reduce_first = HeadsReduce(at, heads_outer(at, normed, d_first, extra_first))
    output = next(stage)
    full.over_a()
    d_second, extra_second = backward(1)
    full_parts = full.end()
    reduce_first.over_a()

    d_heads = [d_first, d_second]
    gives = [back_project(at, d_heads, w_heads, half, which)[0] for which in range(2)]
    keeps = []
    for which in range(2):
        terms = back_project(at, d_heads, w_heads, half, which, at.send(gives[which], dc=1))
        keeps.append([terms[0]] + [at.send(terms[db], db=db) for db in range(1, at.b_size)])
    first = reduce_first.to_peers()
    reduce_second = HeadsReduce(at, heads_outer(at, normed, d_second, extra_second))
    residual_chunks = d_residual.reshape(at.a_size, half, model)
    received = []

    def back(which):
        sent = norm_back(at, keeps[which], chunks, residual_chunks, g_attn[None], which)
        for k, part in enumerate(sent):
            received.append(at.send_back(part, which * len(sent) + k))

    back(0)
    *grads_full, grad_gain_mlp = finish_full(at, full_parts, up_weight, gain_mlp, first[0][1:])
    back(1)
    reduce_second.over_a()
    input_grad = at.place_back(received)
    second = reduce_second.to_peers()
    weights = (query_weight, key_weight, value_weight)
    *grads_heads, grad_gain_attn, few = finish_heads(at, [first, second], weights, gain_attn, 3)
    grad_scale = few[:HEAD_DIM, 2] / scale_dim * (LOG_BASE / math.sqrt(HEAD_DIM))
    grad_scale = grad_scale * jax.nn.sigmoid(dim_scale)
    return (
        output,
        input_grad,
        grad_gain_attn[:, 0],
        grads_heads[0],
        few[:, 0],
        grads_heads[1],
        grads_heads[2],
        few[:, 1],
        grad_scale,
        grads_full[0],
        grad_gain_mlp[:, 0],
        grads_full[1],
        grads_full[2],
    )


def solution(mesh):
    in_specs = (
        P("rep", "shard", None),
        P("rep", "shard", None),
        P("rep", None),
        P("shard"),
        P("shard", None),
        P("shard"),
        P("shard", None),
        P("shard", None),
        P("shard"),
        P(),
        P("shard", None),
        P("shard"),
        P("shard", None),
        P("shard", None),
    )
    out_specs = (
        P("rep", "shard", None),
        P("rep", "shard", None),
        P("shard"),
        P("shard", None),
        P("shard"),
        P("shard", None),
        P("shard", None),
        P("shard"),
        P(),
        P("shard", None),
        P("shard"),
        P("shard", None),
        P("shard", None),
    )
    body = functools.partial(local, mesh.shape["rep"], mesh.shape["shard"])
    return jax.shard_map(body, mesh=mesh, in_specs=in_specs, out_specs=out_specs, check_vma=False)
```

```python
import functools
import math

import jax
import jax.numpy as jnp
from jax import lax
from jax.experimental import pallas as pl
from jax.experimental.pallas import tpu as pltpu
from jax.sharding import PartitionSpec as P

HEAD_DIM = 80
LANES = 128
CORES = 2
NORM_EPS = 1e-06
LOG_BASE = 1.442695041
MASK_FILL = -1e30
AXES = ("rep", "shard")
F32 = jnp.float32
BF16 = jnp.bfloat16


def dot(left, right, left_dim=1, right_dim=0):
    return lax.dot_general(
        left, right, (((left_dim,), (right_dim,)), ((), ())), preferred_element_type=F32
    )


class Place:
    def __init__(self, reps, shards, seqs):
        self.x_size = reps // CORES
        self.x_split = 2 if self.x_size == 2 else 1
        self.a_size = CORES * seqs
        self.b_size = shards // self.a_size
        self.even = self.x_size == 2 and self.b_size == 2
        self.peer_count = self.b_size * CORES
        self.seqs = seqs
        rep, shard = lax.axis_index("rep"), lax.axis_index("shard")
        self.x, self.c = rep // CORES, rep % CORES
        self.a, self.b = shard // self.b_size, shard % self.b_size
        self.shard = shard

    def route(self, move):
        pairs = []
        for x in range(self.x_size):
            for c in range(CORES):
                for a in range(self.a_size):
                    for b in range(self.b_size):
                        pairs.append((self.number(x, c, a, b), self.number(*move(x, c, a, b))))
        return pairs

    def number(self, x, c, a, b):
        return ((x * CORES + c) * self.a_size + a) * self.b_size + b

    def send(self, value, dx=0, dc=0, da=0, db=0):
        return lax.ppermute(
            value,
            AXES,
            self.route(
                lambda x, c, a, b: (
                    (x + dx) % self.x_size,
                    (c + dc) % CORES,
                    (a + da) % self.a_size,
                    (b + db) % self.b_size,
                )
            ),
        )

    def peers(self):
        return [(db, dc) for db in range(self.b_size) for dc in range(CORES)]

    def source(self, db, dc):
        return ((self.b - db) % self.b_size) * CORES + (self.c + dc) % CORES

    def to_cluster(self, tokens, after=()):
        seqs, count, width = tokens.shape
        half = count // CORES
        halves = tokens.reshape(seqs, CORES, half, width)
        shape = (seqs, half, width)
        moves = []
        for i in range(seqs):
            moves += [(0, (i, self.c), 0, i), (0, (i, 1 - self.c), 1, i)]
        own, give = shuffle([halves], [(shape, BF16)] * 2, moves, after)
        got = self.send(give, dc=1)
        after = yield
        parts = route_parts(self, own, got, after or ())
        received = [parts[0]] + [self.send(parts[d], da=d) for d in range(1, self.a_size)]
        moves = [(d, None, 0, (self.a - d) % self.a_size) for d in range(self.a_size)]
        after = yield
        yield shuffle(received, [((self.a_size, half, width), BF16)], moves, after or ())[0]

    def from_cluster(self, chunks):
        half, width = chunks.shape[1:]
        picks = [(0, (self.a + d) % self.a_size, d, None) for d in range(self.a_size)]
        parts = shuffle([chunks], [((half, width), BF16)] * self.a_size, picks)
        received = [parts[0]] + [self.send(parts[d], da=d) for d in range(1, self.a_size)]
        yield
        own, give = route_back(self, received)
        got = self.send(give, dc=1)
        moves = []
        for i in range(self.seqs):
            moves += [(0, i, 0, i * CORES + self.c), (1, i, 0, i * CORES + 1 - self.c)]
        yield
        whole = shuffle([own, got], [((self.a_size, half, width), BF16)], moves)[0]
        yield whole.reshape(self.seqs, CORES * half, width)

    def send_back(self, part, m):
        return lax.ppermute(part, AXES, [(j, i) for i, j in self.route(self._match(m))])

    def place_back(self, received):
        half, width = received[0].shape
        moves = []
        for m in range(self.a_size):
            t = m ^ self.a
            moves.append((m, None, 0, (t % self.seqs) * CORES + t // self.seqs))
        whole = shuffle(received, [((self.a_size, half, width), BF16)], moves)[0]
        return whole.reshape(self.seqs, CORES * half, width)

    def _match(self, m):
        def move(x, c, a, b):
            t = m ^ a
            return x, t // self.seqs, self.seqs * c + t % self.seqs, b

        return move


VMEM = pl.BlockSpec(memory_space=pltpu.VMEM)
ANY = pl.BlockSpec(memory_space=pl.ANY)


LAST = []
SCALE = 0.25
SIZE = {
    "project": 28,
    "attend_forward": 24,
    "middle": 48,
    "outer": 60,
    "outer_give": 60,
    "attend_backward": 24,
    "heads_outer": 24,
    "back_project": 20,
    "finish_heads": 16,
    "finish_full": 16,
}
COST = {
    "project": 14.5,
    "attend_forward": 12.0,
    "middle": 20.0,
    "outer": 7.0,
    "outer_give": 0.1,
    "attend_backward": 25.0,
    "heads_outer": 5.5,
    "back_project": 3.5,
    "pad_weights": 3.5,
    "norm_back": 3.0,
    "finish_heads": 4.0,
    "finish_full": 3.5,
}


def call(name, body, scalars, inputs, outputs, grid=(1,), scratch=(), after=(), vmem=0):
    deps = [*LAST[-1:], *after]
    count, skip = len(inputs), len(deps)

    def run(spots, *refs):
        body(spots, *refs[:count], *refs[count + skip :])

    results = pl.pallas_call(
        run,
        out_shape=[jax.ShapeDtypeStruct(shape, kind) for shape, kind, _ in outputs],
        grid_spec=pltpu.PrefetchScalarGridSpec(
            num_scalar_prefetch=1,
            grid=grid,
            in_specs=[spec for _, spec in inputs] + [ANY] * skip,
            out_specs=[spec for _, _, spec in outputs],
            scratch_shapes=list(scratch),
        ),
        cost_estimate=pl.CostEstimate(
            flops=int(COST.get(name, 1.5) * SCALE * 1.1e9),
            bytes_accessed=int(COST.get(name, 1.5) * SCALE * 3.3e6),
            transcendentals=0,
        ),
        compiler_params=pltpu.CompilerParams(vmem_limit_bytes=(vmem or SIZE.get(name, 12)) * 1024 * 1024),
        name=name,
    )(scalars_of(scalars), *[value for value, _ in inputs], *deps)
    LAST.append(results[0])
    return results


def scalars_of(values):
    if isinstance(values, (list, tuple)):
        return jnp.stack([jnp.asarray(v, jnp.int32) for v in values])
    return values


def shuffle_body(moves, counts, spots, *refs):
    sources, targets, sems = refs[: counts[0]], refs[counts[0] : -1], refs[-1]
    copies, n = [], 0
    for src, src_rank, dst, dst_rank in moves:
        ends = []
        for ref, rank in ((sources[src], src_rank), (targets[dst], dst_rank)):
            ends.append(ref.at[tuple(spots[n + k] for k in range(rank))] if rank else ref)
            n += rank
        copies.append(pltpu.make_async_copy(*ends, sems.at[len(copies)]))
    for copy in copies:
        copy.start()
    for copy in copies:
        copy.wait()


def shuffle(sources, shapes, moves, after=()):
    spots, shape_of = [], []
    for src, src_spot, dst, dst_spot in moves:
        ranks = []
        for spot in (src_spot, dst_spot):
            spot = () if spot is None else spot if isinstance(spot, tuple) else (spot,)
            ranks.append(len(spot))
            spots += spot
        shape_of.append((src, ranks[0], dst, ranks[1]))
    return call(
        "shuffle",
        functools.partial(shuffle_body, shape_of, (len(sources), len(shapes))),
        spots or [0],
        [(source, VMEM) for source in sources],
        [(*shape, ANY) for shape in shapes],
        scratch=[pltpu.SemaphoreType.DMA((len(moves),))],
        after=after,
    )


def route_parts_body(seqs, info, own, got, *outs):
    for d, out in enumerate(outs):
        target = info[1 + d]

        @pl.when(target // seqs == info[0])
        def near():
            out[...] = own[target % seqs]

        @pl.when(target // seqs != info[0])
        def far():
            out[...] = got[target % seqs]


def route_parts(at, own, got, after=()):
    return call(
        "route_parts",
        functools.partial(route_parts_body, at.seqs),
        [at.c, *ahead(at.a, at.a_size)],
        [(own, VMEM), (got, VMEM)],
        [(own.shape[1:], BF16, VMEM)] * at.a_size,
        after=after,
    )


def route_back_body(seqs, info, *refs):
    parts, own, give = refs[:-2], refs[-2], refs[-1]
    for d, part in enumerate(parts):
        source = info[1 + d]

        @pl.when(source // seqs == info[0])
        def near():
            own[source % seqs] = part[...]

        @pl.when(source // seqs != info[0])
        def far():
            give[source % seqs] = part[...]


def route_back(at, parts):
    shape = (at.seqs, *parts[0].shape)
    return call(
        "route_back",
        functools.partial(route_back_body, at.seqs),
        [at.c, *[(at.a - d) % at.a_size for d in range(at.a_size)]],
        [(part, VMEM) for part in parts],
        [(shape, BF16, VMEM)] * 2,
    )


def add_body(counts, spots, *refs):
    terms = sum(counts)
    ins, outs, n = refs[:terms], refs[terms:], 0
    for count, out in zip(counts, outs):
        total = ins[n][...].astype(F32)
        for k in range(1, count):
            total = total + ins[n + k][...].astype(F32)
        out[...] = total.reshape(out.shape).astype(out.dtype)
        n += count


def add_blocks(groups, after=()):
    spots, inputs, outputs = [], [], []
    for terms in groups:
        for value, dim, index in terms:
            block = [1 if k == dim else size for k, size in enumerate(value.shape)]

            def spot(i, s, dim=dim, n=len(spots), rank=value.ndim):
                return tuple(s[n] if k == dim else 0 for k in range(rank))

            spots.append(index)
            inputs.append((value, pl.BlockSpec(tuple(block), spot)))
        shape = tuple(size for k, size in enumerate(value.shape) if k != dim)
        outputs.append((shape, BF16, VMEM))
    return call(
        "add_blocks",
        functools.partial(add_body, [len(terms) for terms in groups]),
        spots,
        inputs,
        outputs,
        after=after,
    )


def later(value, *done):
    return lax.optimization_barrier((value, *done))[0]


def pick(stacked, index, axis=0):
    return lax.dynamic_index_in_dim(stacked, index, axis, keepdims=False)


def by_order(own, others, axis_size, spot):
    moves = [(d, None, 0, (spot - d) % axis_size) for d in range(axis_size)]
    return shuffle([own, *others], [((axis_size, *own.shape), own.dtype)], moves)[0]


def heads_part_body(count, groups, info, query, key, value, vectors, *outs):
    width = query.shape[1] // count // groups
    rows = outs[0].shape[0]
    down = pl.ds(pl.multiple_of(info[len(outs)] * rows, rows), rows)
    for n, out in enumerate(outs):
        for peer in range(count):

            @pl.when(info[n] == peer)
            def copy():
                for g in range(groups):
                    for k, source in enumerate((query, key, value)):
                        spot = (g * 3 + k) * width
                        first = (peer * groups + g) * width
                        out[:, spot : spot + width] = source[down, first : first + width]

        out[:, 3 * groups * width :] = vectors[down, :]


def heads_parts(at, weights, vectors, groups):
    rows, model = weights[0].shape
    count = at.peer_count
    shape = (rows // at.x_split, 3 * model // count + vectors.shape[1])
    targets = [((at.b + db) % at.b_size) * CORES + at.c for db in range(at.b_size)]
    return call(
        "heads_parts",
        functools.partial(heads_part_body, count, groups),
        [*targets, at.x if at.x_split == 2 else 0],
        [(w, VMEM) for w in (*weights, vectors)],
        [(shape, BF16, VMEM)] * at.b_size,
    )


def quarter_body(info, *refs):
    out, sem = refs[3], refs[4]
    rows, half = out.shape[1:]
    down = pl.ds(pl.multiple_of(info[0] * rows, rows), rows)
    right = pl.ds(pl.multiple_of(info[1] * half, half), half)
    copies = [pltpu.make_async_copy(refs[w].at[down, right], out.at[w], sem.at[w]) for w in range(3)]
    for copy in copies:
        copy.start()
    for copy in copies:
        copy.wait()


def quarter_of(at, weights, after):
    rows, model = weights[0].shape
    return call(
        "quarter",
        quarter_body,
        [at.x if at.x_split == 2 else 0, at.c],
        [(w, VMEM) for w in weights],
        [((3, rows // at.x_split, model // CORES), BF16, ANY)],
        scratch=[pltpu.SemaphoreType.DMA((3,))],
        after=after,
    )[0]


def pad_body(heads, groups, a_size, info, *refs):
    split = (len(refs) - groups - 2) // a_size
    sources, outs = refs[: split * a_size], refs[split * a_size :]
    compact, (padded, vectors) = outs[:groups], outs[groups:]
    b_size, rows, width = sources[0].shape
    used = 3 * heads * HEAD_DIM
    part = heads // groups
    padded[...] = jnp.zeros_like(padded)
    for n in range(split):
        for d in range(a_size):
            for b in range(b_size):
                piece = sources[n * a_size + d][b]
                spot = (info[1 + d] * b_size + b) * split
                spot = (spot + (info[0] ^ n if split == 2 else 0)) * rows
                spot = pl.ds(pl.multiple_of(spot, rows), rows)
                for g in range(groups):
                    step = used // groups
                    compact[g][spot, :] = piece[:, g * step : (g + 1) * step]
                vectors[spot, :] = piece[:, used:]
                for k in range(3):
                    for h in range(heads):
                        first = (((h // part) * 3 + k) * part + h % part) * HEAD_DIM
                        lane = (k * heads + h) * LANES
                        padded[spot, lane : lane + HEAD_DIM] = piece[:, first : first + HEAD_DIM]


def pad_weights(at, sources, heads, groups, after):
    b_size, rows, width = sources[0].shape
    total = len(sources) * b_size * rows
    used = 3 * heads * HEAD_DIM
    return call(
        "pad_weights",
        functools.partial(pad_body, heads, groups, at.a_size),
        [at.x, *[(at.a - d) % at.a_size for d in range(at.a_size)]],
        [(source, VMEM) for source in sources],
        [
            *[((total, used // groups), BF16, VMEM)] * groups,
            ((total, 3 * heads * LANES), BF16, VMEM),
            ((total, width - used), BF16, VMEM),
        ],
        after=after,
        vmem=16,
    )


def project_body(count, spots, *refs):
    tokens, (gain, weight, bias, times, qkv, normed) = refs[:count], refs[count:]
    rows = tokens[0].shape[1]
    for p in range(count):
        value = tokens[p][0].astype(F32)
        rate = lax.rsqrt(jnp.mean(value * value, axis=-1, keepdims=True) + NORM_EPS)
        spot = pl.multiple_of(spots[p] * rows, rows)
        normed[pl.ds(spot, rows), :] = (value * rate * gain[...]).astype(BF16)
    step = qkv.shape[1] // 3
    for k in range(3):
        lanes = slice(k * step, (k + 1) * step)
        acc = dot(normed[...], weight[:, lanes])
        qkv[:, lanes] = ((acc + bias[:, lanes]) * times[:, lanes]).astype(BF16)


def project(at, parts, gain, weight, bias, times):
    a_size, half, model = parts[0].shape
    count = len(parts)
    cols = weight.shape[1]
    fixed = lambda a, s: (0, 0)
    return call(
        "project",
        functools.partial(project_body, count),
        [at.source(db, dc) for db, dc in at.peers()],
        [(part, pl.BlockSpec((1, half, model), lambda a, s: (a, 0, 0))) for part in parts]
        + [
            (gain, pl.BlockSpec((1, model), fixed)),
            (weight, pl.BlockSpec((model, cols), fixed)),
            (bias, pl.BlockSpec((1, cols), fixed)),
            (times, pl.BlockSpec((1, cols), fixed)),
        ],
        [
            (
                (a_size * count * half, cols),
                BF16,
                pl.BlockSpec((count * half, cols), lambda a, s: (a, 0)),
            ),
            (
                (a_size * count * half, model),
                BF16,
                pl.BlockSpec((count * half, model), lambda a, s: (a, 0)),
            ),
        ],
        grid=(a_size,),
    )


def forward_body(heads, block, info, starts, query, key, value, mixed, query_aug, total, top):
    index = pl.program_id(0)
    half = block // CORES
    core = info[pl.num_programs(0) + 1]
    total[...] = jnp.zeros_like(total)
    top[...] = jnp.full_like(top, MASK_FILL)
    rows = index * block + lax.broadcasted_iota(jnp.int32, (block, block), 0)
    begin = starts[...][:, :1]

    def step(j, carry):
        spot = pl.multiple_of(j * block, block)
        columns = spot + lax.broadcasted_iota(jnp.int32, (block, block), 1)
        bias = jnp.where((columns >= begin) & (columns <= rows), 0.0, MASK_FILL)
        lanes = [slice(h * LANES, (h + 1) * LANES) for h in range(heads)]
        scores = [dot(query[:, l], key[pl.ds(spot, block), l], 1, 1) + bias for l in lanes]
        olds = [top[h] for h in range(heads)]
        news = [
            jnp.maximum(old, jnp.max(score, axis=1, keepdims=True))
            for old, score in zip(olds, scores)
        ]
        weights = [
            jnp.exp(score - jnp.concatenate([new] * (block // LANES), axis=1)).astype(BF16)
            for score, new in zip(scores, news)
        ]
        for h in range(heads):
            total[h] = total[h] * jnp.exp(olds[h] - news[h]) + dot(
                weights[h], value[pl.ds(spot, block), lanes[h]]
            )
            top[h] = news[h]
        return carry

    lax.fori_loop(info[index], index + 1, step, 0)
    lane = lax.broadcasted_iota(jnp.int32, (block, LANES), 1)
    for h in range(heads):
        lanes = slice(h * LANES, (h + 1) * LANES)
        acc = total[h]
        weight_sum = acc[:, HEAD_DIM : HEAD_DIM + 1]
        result = (acc / weight_sum)[:, :HEAD_DIM].astype(BF16)
        for k in range(CORES):
            mixed[0, core ^ k, 0, :, h * HEAD_DIM : (h + 1) * HEAD_DIM] = result[
                k * half : (k + 1) * half
            ]
        rest = -(top[h] + jnp.log(weight_sum))
        aug = query[:, lanes].astype(F32)
        for k in range(3):
            term = rest.astype(BF16).astype(F32)
            aug = jnp.where(lane == HEAD_DIM + k, term, aug)
            rest = rest - term
        query_aug[:, lanes] = aug.astype(BF16)


def attend_forward(at, info, starts, qkv, heads, block):
    length = qkv.shape[0]
    wide = heads * LANES
    width = heads * HEAD_DIM
    count = length // block
    b_size = at.b_size
    return call(
        "attend_forward",
        functools.partial(forward_body, heads, block),
        info,
        [
            (starts, pl.BlockSpec((block, LANES), lambda i, s: (i, 0))),
            (qkv, pl.BlockSpec((block, wide), lambda i, s: (i, 0))),
            (qkv, pl.BlockSpec((length, wide), lambda i, s: (0, 1))),
            (qkv, pl.BlockSpec((length, wide), lambda i, s: (0, 2))),
        ],
        [
            (
                (b_size, CORES, at.a_size, block // CORES, width),
                BF16,
                pl.BlockSpec(
                    (1, CORES, 1, block // CORES, width),
                    lambda i, s: ((i + b_size - s[count]) % b_size, 0, i // b_size, 0, 0),
                ),
            ),
            ((length, wide), BF16, pl.BlockSpec((block, wide), lambda i, s: (i, 0))),
        ],
        grid=(count,),
        scratch=[
            pltpu.VMEM((heads, block, LANES), F32),
            pltpu.VMEM((heads, block, LANES), F32),
        ],
    )


def backward_body(
    heads,
    first,
    block,
    count,
    info,
    starts,
    scale,
    query,
    key,
    value,
    mixed,
    *rest,
):
    grad_refs = rest[:count]
    grads, scale_sum, bias_sum, grad, grad_aug, d_query, d_key, d_value = rest[count:]
    index = pl.num_programs(0) - 1 - pl.program_id(0)
    b_own, core = info[pl.num_programs(0)], info[pl.num_programs(0) + 1]
    b_size = count // CORES
    width = heads * HEAD_DIM

    @pl.when(pl.program_id(0) == 0)
    def clear():
        d_key[...] = jnp.zeros_like(d_key)
        d_value[...] = jnp.zeros_like(d_value)
        scale_sum[...] = jnp.zeros_like(scale_sum)
        bias_sum[...] = jnp.zeros_like(bias_sum)

    half = block // CORES
    lane = lax.broadcasted_iota(jnp.int32, (half, LANES), 1)
    for k in range(CORES):
        peer = ((b_own + b_size - index % b_size) % b_size) * CORES + (core ^ k)
        for p in range(count):

            @pl.when(peer == p)
            def fetch():
                grad[...] = grad_refs[p][index // b_size]

        for h in range(heads):
            part = slice((first + h) * HEAD_DIM, (first + h + 1) * HEAD_DIM)
            grad_h = grad[:, part].astype(F32)
            mixed_h = mixed[0, core ^ k, 0, :, part].astype(F32)
            delta = jnp.sum(grad_h * mixed_h, axis=1, keepdims=True)
            aug = jnp.concatenate([grad_h, jnp.zeros((half, LANES - HEAD_DIM), F32)], axis=1)
            high = (-delta).astype(BF16).astype(F32)
            aug = jnp.where(lane == HEAD_DIM, high, aug)
            aug = jnp.where(lane == HEAD_DIM + 1, -delta - high, aug)
            grad_aug[k * half : (k + 1) * half, h * LANES : (h + 1) * LANES] = aug.astype(BF16)
    d_query[...] = jnp.zeros_like(d_query)
    columns = index * block + lax.broadcasted_iota(jnp.int32, (block, block), 1)
    begin = starts[0:1, :]

    def step(j, carry):
        spot = pl.multiple_of(j * block, block)
        rows = spot + lax.broadcasted_iota(jnp.int32, (block, block), 0)
        allowed = (rows >= begin) & (rows <= columns)
        lanes = [slice(h * LANES, (h + 1) * LANES) for h in range(heads)]
        keys = [key[pl.ds(spot, block), l] for l in lanes]
        queries = [query[:, l] for l in lanes]
        grads_of = [grad_aug[:, l] for l in lanes]
        scores = [dot(k, q, 1, 1) for k, q in zip(keys, queries)]
        d_probs = [
            dot(value[pl.ds(spot, block), l], g, 1, 1) for l, g in zip(lanes, grads_of)
        ]
        probs = [jnp.where(allowed, jnp.exp(score), 0.0) for score in scores]
        d_scores = [(prob * d_prob).astype(BF16) for prob, d_prob in zip(probs, d_probs)]
        for h, l in enumerate(lanes):
            d_value[pl.ds(spot, block), l] += dot(probs[h].astype(BF16), grads_of[h])
            d_key[pl.ds(spot, block), l] += dot(d_scores[h], queries[h])
            d_query[:, l] += dot(d_scores[h], keys[h], 0, 0)
        return carry

    lax.fori_loop(info[index], index + 1, step, 0)
    here = pl.ds(pl.multiple_of(index * block, block), block)
    for h in range(heads):
        lanes = slice(h * LANES, (h + 1) * LANES)
        d_scaled = d_query[:, lanes].astype(BF16).astype(F32)
        scale_sum[...] += jnp.sum(d_scaled * query[:, lanes].astype(F32), axis=0, keepdims=True)
        d_q = (d_scaled * scale[0:1, lanes]).astype(BF16)
        for k, term in enumerate((d_q, d_key[here, lanes], d_value[here, lanes])):
            spot = k * width + h * HEAD_DIM
            term = term.astype(BF16)
            grads[:, spot : spot + HEAD_DIM] = term[:, :HEAD_DIM]
            bias_sum[:, (k * heads + h) * LANES : (k * heads + h + 1) * LANES] += jnp.sum(
                term.astype(F32), axis=0, keepdims=True
            )


def attend_backward(
    at, info, starts, scale, query_aug, qkv, grads, mixed, heads, groups, group, block
):
    length = qkv.shape[0]
    wide = heads * LANES
    width = heads * HEAD_DIM
    count = length // block
    b_size = at.b_size
    half = block // CORES

    def mixed_spot(i, s):
        i = count - 1 - i
        return (i + b_size - s[count]) % b_size, 0, i // b_size, 0, 0

    fixed = lambda i, s: (0, 0)
    return call(
        "attend_backward",
        functools.partial(backward_body, heads, group * heads, block, len(grads)),
        info,
        [
            (starts, pl.BlockSpec((8, block), lambda i, s: (0, count - 1 - i))),
            (scale, pl.BlockSpec((8, wide), fixed)),
            (query_aug, pl.BlockSpec((block, wide), lambda i, s: (count - 1 - i, group))),
            (qkv, pl.BlockSpec((length, wide), lambda i, s: (0, groups + group))),
            (qkv, pl.BlockSpec((length, wide), lambda i, s: (0, 2 * groups + group))),
            (mixed, pl.BlockSpec((1, CORES, 1, half, mixed.shape[4]), mixed_spot)),
        ]
        + [(grad, VMEM) for grad in grads],
        [
            (
                (length, 3 * width),
                BF16,
                pl.BlockSpec((block, 3 * width), lambda i, s: (count - 1 - i, 0)),
            ),
            ((8, LANES), F32, pl.BlockSpec((8, LANES), fixed)),
            ((8, 3 * wide), F32, pl.BlockSpec((8, 3 * wide), fixed)),
        ],
        grid=(count,),
        scratch=[
            pltpu.VMEM((half, mixed.shape[4]), BF16),
            pltpu.VMEM((block, wide), BF16),
            pltpu.VMEM((block, wide), F32),
            pltpu.VMEM((length, wide), F32),
            pltpu.VMEM((length, wide), F32),
        ],
    )


def concat_body(info, *refs):
    parts, out = refs[:-1], refs[-1]
    width = parts[0].shape[1]
    for p, part in enumerate(parts):
        out[:, p * width : (p + 1) * width] = part[...]


def concat(parts, after):
    rows, width = parts[0].shape
    return call(
        "concat",
        concat_body,
        [0],
        [(part, VMEM) for part in parts],
        [((rows, width * len(parts)), BF16, VMEM)],
        after=after,
    )[0]


def middle_body(count, source_count, moves, info, *refs):
    mixed, tokens, d_out, gain = refs[:4]
    sources = refs[4 : 4 + source_count]
    outs = refs[4 + source_count :]
    output, d_residual, d_proj, normed, activated, d_up = outs[:6]
    d_parts = outs[6:-4]
    weights, sems = outs[-4:-1], outs[-1]
    w_out, w_up, w_down = weights
    rows, half = sources[0].shape[2:]
    width = d_parts[0].shape[1]

    def copies(w):
        for n, (src, s, k) in enumerate(moves):
            if k == w:
                down = pl.ds(pl.multiple_of(info[2 * n] * rows, rows), rows)
                right = pl.ds(pl.multiple_of(info[2 * n + 1] * half, half), half)
                yield pltpu.make_async_copy(
                    sources[src].at[s, w], weights[w].at[down, right], sems.at[n]
                )

    def arrived(w):
        @pl.when(pl.program_id(0) == 0)
        def wait():
            for copy in copies(w):
                copy.wait()

    @pl.when(pl.program_id(0) == 0)
    def start():
        for w in range(3):
            for copy in copies(w):
                copy.start()

    arrived(0)
    residual = tokens[...].astype(F32) + dot(mixed[...], w_out[...])
    rate = lax.rsqrt(jnp.mean(residual * residual, axis=-1, keepdims=True) + NORM_EPS)
    normed[...] = (residual * rate * gain[...]).astype(BF16)
    arrived(1)
    upward = dot(normed[...], w_up[...])
    gate = 1.0 / (1.0 + jnp.exp(-upward))
    activated[...] = (upward * gate).astype(BF16)
    arrived(2)
    output[...] = (residual + dot(activated[...], w_down[...])).astype(BF16)
    d_activated = dot(d_out[...], w_down[...], 1, 1)
    d_up[...] = (d_activated * gate * (1 + upward * (1 - gate))).astype(BF16)
    scaled = dot(d_up[...], w_up[...], 1, 1) * gain[...]
    inner = jnp.mean(residual * scaled, axis=-1, keepdims=True)
    d_norm = rate * scaled - residual * (rate * rate * rate * inner)
    d_total = d_out[...].astype(F32) + d_norm
    d_residual[...] = d_total
    d_proj[...] = d_total.astype(BF16)
    d_mixed = dot(d_proj[...], w_out[...], 1, 1).astype(BF16)
    for p in range(count):
        d_parts[p][...] = d_mixed[:, p * width : (p + 1) * width]


def middle(at, mixed, tokens, d_out, gain, sources):
    count = at.peer_count
    rows, model = tokens.shape
    width = model // count
    arrays = list(sources.values())
    a_size, _, piece, half = arrays[0].shape
    group = model // at.peer_count // piece
    moves, spots = [], []
    for n, (dx, db, dc) in enumerate(sources):
        for a in range(a_size):
            for w in range(3):
                row = a * at.b_size + (at.b - db) % at.b_size
                if at.x_split == 2:
                    row = row * 2 + (at.x + dx) % 2
                if w == 0:
                    peer, rest = row // group, row % group
                    far = (at.b - peer // CORES) % at.b_size
                    row = (far * CORES + ((peer % CORES) ^ at.c)) * group + rest
                moves.append((n, a, w))
                spots += [row, (at.c + dc) % CORES]
    block = min(256, rows)
    row = lambda i, s: (i, 0)
    rows_of = pl.BlockSpec((block, model), row)
    part = pl.BlockSpec((block, width), row)
    types = [BF16, F32, BF16, BF16, BF16, BF16]
    return call(
        "middle",
        functools.partial(middle_body, count, len(arrays), moves),
        spots,
        [(mixed, rows_of), (tokens, rows_of), (d_out, rows_of)]
        + [(gain, pl.BlockSpec(gain.shape, lambda i, s: (0, 0)))]
        + [(source, ANY) for source in arrays],
        [((rows, model), kind, rows_of) for kind in types]
        + [((rows, width), BF16, part)] * count,
        grid=(rows // block,),
        scratch=[pltpu.VMEM((model, model), BF16)] * 3
        + [pltpu.SemaphoreType.DMA((len(moves),))],
    )


def outer_body(count, split, add, info, *refs):
    pairs, rest = refs[:6], refs[6:]
    for w in range(3):

        @pl.when(pl.program_id(0) == w)
        def product():
            value = dot(pairs[2 * w][...], pairs[2 * w + 1][...], 0, 0)
            target = rest[-1] if split else rest[-1].at[0]
            width = value.shape[0] // count
            for p in range(count):
                spot = p * width
                if w == 0:
                    spot = pl.multiple_of(info[3 + p] * width, width)
                part = value[p * width : (p + 1) * width]
                if add:
                    part = part + rest[0][0, pl.ds(spot, width)].astype(F32)
                target[pl.ds(spot, width)] = part.astype(BF16)

    if split:
        keep_x, give_x, keep_b, give_b, total = rest[1:]
        pairs_a, b_size, rows = keep_x.shape[1:4]
        for k in range(pairs_a):
            for b in range(b_size):
                for half, out in ((info[1], keep_x), (1 - info[1], give_x)):
                    spot = pl.multiple_of((k * b_size + b) * 2 * rows + half * rows, rows)
                    out[0, k, b] = total[pl.ds(spot, rows)]
            for b, out in ((info[2], keep_b), (1 - info[2], give_b)):
                for half in range(2):
                    spot = (((k + pairs_a) * b_size) * 2 + half) * rows + b * 2 * rows
                    out[0, k, half] = total[pl.ds(pl.multiple_of(spot, rows), rows)]


def outer(at, pairs, cols, add=None, after=()):
    rows, model = pairs[0][0].shape
    half = model // CORES
    count = at.peer_count
    split = add is not None and at.even
    info = [cols, at.x if at.even else 0, at.b, *[at.source(db, dc) for db, dc in at.peers()]]
    inputs = []
    for left, right in pairs:
        inputs.append((left, pl.BlockSpec((rows, model), lambda w, s: (0, 0))))
        inputs.append((right, pl.BlockSpec((rows, half), lambda w, s: (0, s[0]))))
    block = pl.BlockSpec((1, model, half), lambda w, s: (w, 0, 0))
    outputs = [((3, model, half), BF16, block)]
    scratch = []
    if add is not None:
        inputs.append((add, block))
    if split:
        shape = (at.a_size // 2, 2, model // at.a_size // 4, half)
        part = pl.BlockSpec((1, *shape), lambda w, s: (w, 0, 0, 0, 0))
        outputs = [((3, *shape), BF16, part)] * 4
        scratch = [pltpu.VMEM((model, half), BF16)]
    return call(
        "outer_give" if add is None else "outer",
        functools.partial(outer_body, count, split, add is not None),
        info,
        inputs,
        outputs,
        grid=(3,),
        scratch=scratch,
        after=after,
    )


def give_body(groups, info, *refs):
    grads, weights, out = refs[:groups], refs[groups : 2 * groups], refs[-1]
    value = back_product(grads, weights)
    out[...] = value.astype(BF16).reshape(out.shape)


def back_product(grads, weights):
    total = 0.0
    for grad, weight in zip(grads, weights):
        total = total + dot(grad[...].reshape(-1, grad.shape[-1]), weight[...], 1, 1)
    return total


def keep_body(groups, info, *refs):
    grads, weights, got = refs[:groups], refs[groups : 2 * groups], refs[2 * groups]
    outs = refs[2 * groups + 1 :]
    pairs, b_size, half = got.shape[:3]
    value = back_product(grads, weights).reshape(got.shape) + got[...].astype(F32)
    for b in range(b_size):
        for n, out in enumerate(outs):

            @pl.when(info[2 + n] == b)
            def copy():
                out[...] = value[:, b].astype(out.dtype)


def back_project(at, grads, weights, half, which, got=None):
    model = weights[0].shape[0]
    pair = at.a_size // 2
    groups = len(grads)
    width = grads[0].shape[1]
    shape = (pair, at.b_size, half, model)
    grads = [g.reshape(at.a_size, at.b_size, CORES, half, width) for g in grads]
    block = pl.BlockSpec((pair, at.b_size, 1, half, width), lambda i, s: (s[0], 0, s[1], 0, 0))
    core = at.c if got is not None else 1 - at.c
    inputs = [(g, block) for g in grads]
    inputs += [(weight, VMEM) for weight in weights]
    if got is None:
        body, outputs = give_body, [(shape, BF16, VMEM)]
    else:
        body = keep_body
        inputs.append((got, VMEM))
        outputs = [((pair, half, model), F32 if db == 0 else BF16, VMEM) for db in range(at.b_size)]
    return call(
        "back_project",
        functools.partial(body, groups),
        [which ^ core, core, *ahead(at.b, at.b_size)],
        inputs,
        outputs,
    )


def norm_back_body(count, info, *refs):
    own, others = refs[0], refs[1:count]
    tokens, d_residual, gain = refs[count : count + 3]
    for n, out in enumerate(refs[count + 3 :]):
        k = info[1 + n]
        grad = own[k]
        for other in others:
            grad = grad + other[k].astype(F32)
        value = tokens[k].astype(F32)
        rate = lax.rsqrt(jnp.mean(value * value, axis=-1, keepdims=True) + NORM_EPS)
        scaled = grad * gain[...]
        inner = jnp.mean(value * scaled, axis=-1, keepdims=True)
        d_norm = rate * scaled - value * (rate * rate * rate * inner)
        out[...] = (d_residual[k] + d_norm).astype(BF16)


def norm_back(at, terms, chunks, d_residual, gain, which):
    pair, half, model = terms[0].shape
    block = pl.BlockSpec((pair, half, model), lambda i, s: (s[0], 0, 0))
    order = [k ^ (at.a % pair) for k in range(pair)]
    return call(
        "norm_back",
        functools.partial(norm_back_body, len(terms)),
        [which ^ at.c, *order],
        [(t, VMEM) for t in terms] + [(chunks, block), (d_residual, block), (gain, VMEM)],
        [((half, model), BF16, VMEM)] * pair,
    )


def heads_outer_body(steps, info, normed, grads, extra, *rest):
    outs, acc = rest[:-1], rest[-1]
    value = dot(normed[...], grads[...], 0, 0)

    @pl.when(pl.program_id(0) == 0)
    def first():
        acc[...] = value

    @pl.when(pl.program_id(0) != 0)
    def later():
        acc[...] += value

    @pl.when(pl.program_id(0) == steps - 1)
    def last():
        used = acc.shape[1]
        pairs, b_size, rows = outs[0].shape[:3]
        split = len(outs)
        for n, out in enumerate(outs):
            for s in range(pairs * b_size):
                spot = (s * split + (info[0] ^ n if split == 2 else 0)) * rows
                spot = pl.ds(pl.multiple_of(spot, rows), rows)
                out[s // b_size, s % b_size, :, :used] = acc[spot, :].astype(BF16)
                out[s // b_size, s % b_size, :, used:] = extra[spot, :]


def heads_outer(at, normed, grads, extra):
    length, model = normed.shape
    used = grads.shape[1]
    block = min(512, length)
    steps = length // block
    rows = model // at.a_size // at.b_size // at.x_split
    shape = (at.a_size, at.b_size, rows, used + extra.shape[1])
    return call(
        "heads_outer",
        functools.partial(heads_outer_body, steps),
        [at.x],
        [
            (normed, pl.BlockSpec((block, model), lambda i, s: (i, 0))),
            (grads, pl.BlockSpec((block, used), lambda i, s: (i, 0))),
            (extra, pl.BlockSpec(extra.shape, lambda i, s: (0, 0))),
        ],
        [(shape, BF16, pl.BlockSpec(shape, lambda i, s: (0, 0, 0, 0)))] * at.x_split,
        grid=(steps,),
        scratch=[pltpu.VMEM((model, used), F32)],
    )


def all_sum(at, value, axis, size):
    total = value
    for d in range(1, size):
        total = total + at.send(value, **{axis: d}).astype(value.dtype)
    return total


def ahead(spot, size):
    return [(spot + d) % size for d in range(size)]


def cat_body(info, first, first_got, second, second_got, *outs):
    pair = first.shape[1]
    for d, out in enumerate(outs):
        spot = info[d] % pair

        @pl.when(info[d] < pair)
        def low():
            out[...] = (first[:, spot].astype(F32) + first_got[:, spot].astype(F32)).astype(BF16)

        @pl.when(info[d] >= pair)
        def high():
            out[...] = (second[:, spot].astype(F32) + second_got[:, spot].astype(F32)).astype(BF16)


class FullReduce:
    def __init__(self, at, parts):
        self.at = at
        if at.even:
            keep_x, give_x, keep_b, give_b = parts
            self.first = keep_x, at.send(give_x, dx=1)
            self.second = keep_b, at.send(give_b, db=1)
        else:
            self.part = parts[0].reshape(3, at.a_size, at.b_size, -1, parts[0].shape[-1])

    def next(self):
        at = self.at
        if not at.even:
            return
        groups = [[(t, 2, b) for t in self.first] for b in ahead(at.b, 2)]
        groups += [[(t, 2, x) for t in self.second] for x in ahead(at.x, 2)]
        keep_b, give_b, keep_x, give_x = add_blocks(groups)
        self.first = keep_b, at.send(give_b, db=1)
        self.second = keep_x, at.send(give_x, dx=1)

    def over_a(self):
        at = self.at
        if at.even:
            shape = self.first[0].shape
            parts = call(
                "cat",
                cat_body,
                ahead(at.a, at.a_size),
                [(t, VMEM) for t in (*self.first, *self.second)],
                [((3, *shape[2:]), BF16, VMEM)] * at.a_size,
            )
        else:
            parts = add_blocks([[(self.part, 1, a)] for a in ahead(at.a, at.a_size)])
        self.got = [parts[0]] + [at.send(parts[d], da=d) for d in range(1, at.a_size)]

    def end(self):
        at = self.at
        if at.even:
            part = add_blocks([[(t[None], 0, 0) for t in self.got]])[0]
            far = at.send(part, dx=1)
            return [part, far, at.send(part, dc=1), at.send(far, dc=1)]
        parts = add_blocks([[(t, 1, b) for t in self.got] for b in ahead(at.b, at.b_size)])
        got = [parts[0]] + [at.send(parts[d], db=d) for d in range(1, at.b_size)]
        part = add_blocks([[(t[None], 0, 0) for t in got]])[0]
        part = all_sum(at, part, "dx", at.x_size)
        return [part, at.send(part, dc=1)]


class HeadsReduce:
    def __init__(self, at, parts):
        self.at = at
        self.got = [parts[0]]
        if at.x_split == 2:
            self.got.append(at.send(parts[1], dx=1))

    def over_a(self):
        at = self.at
        parts = add_blocks([[(t, 0, a) for t in self.got] for a in ahead(at.a, at.a_size)])
        self.got = [parts[0]] + [at.send(parts[d], da=d) for d in range(1, at.a_size)]
        return parts

    def by_b(self, after=()):
        at = self.at
        if at.x_split == 1:
            total = add_blocks([[(t[None], 0, 0) for t in self.got]])[0]
            self.got = [all_sum(at, total, "dx", at.x_size)]
        groups = [[(t, 0, b) for t in self.got] for b in ahead(at.b, at.b_size)]
        return add_blocks(groups, after)


def side_body(groups, info, *refs):
    for n, out in enumerate(refs[-(len(refs) // (groups + 1)) :]):
        for g in range(groups):
            out[g] = refs[n * groups + g][...]


def to_peers(at, groups):
    shape = (len(groups), *groups[0][0].shape)
    parts = call(
        "side",
        functools.partial(side_body, len(groups)),
        [0],
        [(group[b], VMEM) for b in range(at.b_size) for group in groups],
        [(shape, BF16, VMEM)] * at.b_size,
    )
    parts = [at.send(parts[db], db=db, dc=dc) if db or dc else parts[0] for db, dc in at.peers()]
    if at.x_split == 1:
        return [parts]
    return [parts, at.send(jnp.stack(parts), dx=1)]


def in_order(info, refs, split, half, core, spot):
    near = [r[spot] for r in refs]
    if split == 2:
        near = [jnp.where(info[0] == half, near[2 * k], near[2 * k + 1]) for k in range(2)]
    return jnp.where(info[1] == core, near[0], near[1])


def finish_full_body(split, info, *refs):
    count = CORES * split
    parts, (weight, gain), outs = refs[:count], refs[count : count + 2], refs[count + 2 :]
    rows, half = parts[0].shape[1:]
    for x in range(split):
        spot = slice(x * rows, (x + 1) * rows)
        for w in range(3):
            for c in range(CORES):
                outs[w][spot, c * half : (c + 1) * half] = in_order(
                    info, parts, split, x, c, w
                ).astype(F32)
    total = jnp.sum(outs[1][...] * weight[...].astype(F32), axis=1, keepdims=True)
    outs[3][...] = total / gain[...].astype(F32)


def finish_full(at, parts, weight, gain, after):
    rows, model = weight.shape
    return call(
        "finish_full",
        functools.partial(finish_full_body, 2 if at.even else 1),
        [at.x, at.c],
        [(p, VMEM) for p in parts] + [(weight, VMEM), (gain[:, None], VMEM)],
        [((rows, model), F32, VMEM)] * 3 + [((rows, 1), F32, VMEM)],
        after=after,
    )


def finish_heads_body(count, split, info, *refs):
    parts, refs = refs[:count], refs[count:]
    far, refs = refs[: split - 1], refs[split - 1 :]
    weights, gain, outs = refs[:3], refs[3], refs[4:]
    few = outs[4].shape[1]
    groups, rows, width = parts[0].shape
    width = (width - few) // 3
    for n in range(split):
        down = pl.ds(pl.multiple_of((info[count] ^ n if split == 2 else 0) * rows, rows), rows)
        total = jnp.zeros((rows, few), F32)
        for p in range(count):
            for g in range(groups):
                source = far[0].at[p, g] if n else parts[p].at[g]
                total = total + source[:, 3 * width :].astype(F32)
                for peer in range(count):

                    @pl.when(info[p] == peer)
                    def copy():
                        for k in range(3):
                            spot = (peer * groups + g) * width
                            piece = source[:, k * width : (k + 1) * width]
                            outs[k][down, spot : spot + width] = piece.astype(F32)

        outs[4][down, :] = total
    total = jnp.zeros(outs[3].shape, F32)
    for k in range(3):
        total = total + jnp.sum(outs[k][...] * weights[k][...].astype(F32), axis=1, keepdims=True)
    outs[3][...] = total / gain[...].astype(F32)


def finish_heads(at, parts, weights, gain, few):
    rows, model = weights[0].shape
    flat = [*parts[0], *parts[1:]]
    return call(
        "finish_heads",
        functools.partial(finish_heads_body, at.peer_count, at.x_split),
        [*[at.source(db, dc) for db, dc in at.peers()], at.x],
        [(p, VMEM) for p in flat] + [(w, VMEM) for w in weights] + [(gain[:, None], VMEM)],
        [((rows, model), F32, VMEM)] * 3 + [((rows, 1), F32, VMEM), ((rows, few), F32, VMEM)],
    )


def local(
    reps,
    shards,
    activations,
    cotangent,
    doc_lengths,
    gain_attn,
    query_weight,
    query_bias,
    key_weight,
    value_weight,
    value_bias,
    dim_scale,
    out_weight,
    gain_mlp,
    up_weight,
    down_weight,
):
    seqs, tok_count, model = activations.shape
    at = Place(reps, shards, seqs)
    half = tok_count // CORES
    length = tok_count * shards
    peer_count = at.peer_count
    heads = model // HEAD_DIM // peer_count
    width = heads * HEAD_DIM
    wide = heads * LANES
    own_rows = at.a_size * half
    rows = gain_attn.shape[0]
    groups = 2
    block = CORES * half
    mine = at.b * CORES + at.c

    LAST.clear()
    stage = at.to_cluster(activations)
    next(stage)
    vectors = jnp.stack([gain_attn, gain_mlp, query_bias, value_bias], axis=1)
    own, *sent = heads_parts(at, (query_weight, key_weight, value_weight), vectors, groups)
    sent = [at.send(part, db=db + 1) for db, part in enumerate(sent)]
    next(stage)
    near = by_order(own, sent, at.b_size, at.b)
    sources = [near] + [at.send(near, da=d) for d in range(1, at.a_size)]
    if at.x_split == 2:
        sources += [at.send(source, dx=1) for source in sources]
    chunks = next(stage)
    parts = []
    early = sources[1 : at.a_size]
    if at.x_split == 2:
        early = [sources[2], sources[at.a_size + 1], sources[at.a_size + 3]]
    for db in range(at.b_size):
        near = at.send(chunks, db=db) if db else chunks
        ready = later(near, *early) if db else near
        parts += [near, at.send(ready, dc=1)]
    stage = at.to_cluster(cotangent, sources[at.a_size : at.a_size + 1])
    next(stage)
    quarter = quarter_of(at, (out_weight, up_weight, down_weight), sources[1 : at.a_size])
    pieces = [quarter] + [at.send(quarter, da=d) for d in range(1, at.a_size)]
    *w_heads, w_pad, vectors = pad_weights(at, sources, heads, groups, parts[1:])
    vectors = vectors.T.astype(F32)
    g_attn, g_mlp, b_query, b_value = vectors[0], vectors[1], vectors[2], vectors[3]

    other_lengths = at.send(doc_lengths, dc=1)
    lengths = pick(jnp.where(at.c == at.a // seqs, doc_lengths, other_lengths), at.a % seqs)
    ends = jnp.cumsum(lengths)
    places = jnp.arange(length, dtype=jnp.int32)
    starts = jnp.max(jnp.where(ends[None, :] <= places[:, None], ends[None, :], 0), axis=1)
    starts_row = jnp.broadcast_to(starts[None, :], (8, length))
    starts_col = jnp.broadcast_to(starts[:, None], (length, LANES))
    info = jnp.concatenate([starts[::block] // block, jnp.stack([at.b, at.c])]).astype(jnp.int32)

    scale_dim = LOG_BASE / math.sqrt(HEAD_DIM) * jax.nn.softplus(dim_scale)
    scale_pad = jnp.tile(jnp.pad(scale_dim, (0, LANES - HEAD_DIM)), heads)
    lane = jnp.arange(LANES)
    ones_key = ((lane >= HEAD_DIM) & (lane < HEAD_DIM + 3)).astype(F32)
    ones_value = ((lane >= HEAD_DIM) & (lane < HEAD_DIM + 2)).astype(F32)

    def pad_heads(vec):
        part = lax.dynamic_slice_in_dim(vec, mine * width, width, 0).reshape(heads, HEAD_DIM)
        return jnp.pad(part, ((0, 0), (0, LANES - HEAD_DIM))).reshape(wide)

    bias_pad = jnp.concatenate(
        [
            pad_heads(b_query),
            jnp.tile(ones_key, heads),
            pad_heads(b_value) + jnp.tile(ones_value, heads),
        ]
    )
    times = jnp.concatenate([scale_pad, jnp.ones((2 * wide,), F32)])
    qkv, normed = project(at, parts, g_attn[None], w_pad, bias_pad[None], times[None])

    part_heads = heads // groups
    part_width = part_heads * HEAD_DIM
    moves = [(d, None, 0, (at.a - d) % at.a_size) for d in range(at.a_size)]
    quarter = shuffle(pieces, [((at.a_size, *quarter.shape), BF16)], moves)[0]
    others = {(0, 0, 0): quarter, (0, 0, 1): at.send(quarter, dc=1)}
    for db in range(1, at.b_size):
        others[(0, db, 0)] = at.send(quarter, db=db)
    if at.x_split == 2:
        others[(1, 0, 0)] = at.send(quarter, dx=1)
    stage.send([others[(0, 0, 1)]])
    mixed_rel, query_aug = attend_forward(at, info, starts_col, qkv, heads, block)
    d_out = next(stage).reshape(own_rows, model)
    if at.x_split == 2:
        for db in range(1, at.b_size):
            others[(1, db, 0)] = at.send(later(others[(0, db, 0)], d_out), dx=1)
    parts = []
    for db, dc in at.peers():
        part = later(mixed_rel[db, dc], d_out).reshape(own_rows, width)
        parts.append(at.send(part, db=db, dc=dc) if db or dc else part)
    mixed = concat(parts, [])
    for dx, db, dc in list(others):
        if (dx, db, 1) not in others:
            others[(dx, db, 1)] = at.send(later(others[(dx, db, 0)], mixed), dc=1)
    tokens = chunks.reshape(own_rows, model)
    output, d_residual, d_proj, normed_mlp, activated, d_up, *d_parts = middle(
        at, mixed, tokens, d_out, g_mlp[None], others
    )

    grads = []
    for (db, dc), part in zip(at.peers(), d_parts):
        part = at.send(part, db=db, dc=dc) if db or dc else part
        grads.append(part.reshape(at.a_size, half, width))

    pairs = [(mixed, d_proj), (normed_mlp, d_up), (activated, d_out)]
    give = outer(at, pairs, 1 - at.c)[0]
    full = FullReduce(at, outer(at, pairs, at.c, at.send(give, dc=1), grads))

    scale_rows = jnp.broadcast_to(scale_pad[None, : part_heads * LANES], (8, part_heads * LANES))
    zeros = jnp.zeros((model,), F32)

    def backward(g):
        d_heads, scale_sum, bias_sum = attend_backward(
            at,
            info,
            starts_row,
            scale_rows,
            query_aug,
            qkv,
            grads,
            mixed_rel,
            part_heads,
            groups,
            g,
            block,
        )
        bias_sum = bias_sum[0].reshape(3, part_heads, LANES)[:, :, :HEAD_DIM]
        bias_sum = bias_sum.reshape(3, part_width)
        spot = (mine * groups + g) * part_width
        scale_sum = jnp.pad(scale_sum[0, :HEAD_DIM], (0, rows - HEAD_DIM))
        extra = [
            lax.dynamic_update_slice(zeros, bias_sum[0], (spot,)),
            lax.dynamic_update_slice(zeros, bias_sum[2], (spot,)),
            jnp.tile(scale_sum, shards),
        ]
        return d_heads, jnp.stack(extra, axis=1).astype(BF16)

    stage = at.from_cluster(output.reshape(at.a_size, half, model))
    next(stage)
    d_first, extra_first = backward(0)
    next(stage)
    full.next()
    reduce_first = HeadsReduce(at, heads_outer(at, normed, d_first, extra_first))
    full.over_a()
    d_second, extra_second = backward(1)
    full_parts = full.end()
    reduce_first.over_a()

    d_heads = [d_first, d_second]
    keeps, received = [], []
    residual_chunks = d_residual.reshape(at.a_size, half, model)

    def give(which):
        return at.send(back_project(at, d_heads, w_heads, half, which)[0], dc=1)

    def keep(which, got):
        terms = back_project(at, d_heads, w_heads, half, which, got)
        keeps.append([terms[0]] + [at.send(terms[db], db=db) for db in range(1, at.b_size)])

    def back(which):
        sent = norm_back(at, keeps[which], chunks, residual_chunks, g_attn[None], which)
        for k, part in enumerate(sent):
            received.append(at.send_back(part, which * len(sent) + k))

    got = give(0)
    reduce_second = HeadsReduce(at, heads_outer(at, normed, d_second, extra_second))
    first = reduce_first.by_b(full_parts[1:2])
    keep(0, got)
    keep(1, give(1))
    reduce_second.over_a()
    back(0)
    parts = to_peers(at, [first, reduce_second.by_b()])
    back(1)
    *grads_full, grad_gain_mlp = finish_full(at, full_parts, up_weight, gain_mlp, [])
    output = next(stage)
    input_grad = at.place_back(received)
    weights = (query_weight, key_weight, value_weight)
    *grads_heads, grad_gain_attn, few = finish_heads(at, parts, weights, gain_attn, 3)
    grad_scale = few[:HEAD_DIM, 2] / scale_dim * (LOG_BASE / math.sqrt(HEAD_DIM))
    grad_scale = grad_scale * jax.nn.sigmoid(dim_scale)
    return (
        output,
        input_grad,
        grad_gain_attn[:, 0],
        grads_heads[0],
        few[:, 0],
        grads_heads[1],
        grads_heads[2],
        few[:, 1],
        grad_scale,
        grads_full[0],
        grad_gain_mlp[:, 0],
        grads_full[1],
        grads_full[2],
    )


def solution(mesh):
    in_specs = (
        P("rep", "shard", None),
        P("rep", "shard", None),
        P("rep", None),
        P("shard"),
        P("shard", None),
        P("shard"),
        P("shard", None),
        P("shard", None),
        P("shard"),
        P(),
        P("shard", None),
        P("shard"),
        P("shard", None),
        P("shard", None),
    )
    out_specs = (
        P("rep", "shard", None),
        P("rep", "shard", None),
        P("shard"),
        P("shard", None),
        P("shard"),
        P("shard", None),
        P("shard", None),
        P("shard"),
        P(),
        P("shard", None),
        P("shard"),
        P("shard", None),
        P("shard", None),
    )
    body = functools.partial(local, mesh.shape["rep"], mesh.shape["shard"])
    return jax.shard_map(body, mesh=mesh, in_specs=in_specs, out_specs=out_specs, check_vma=False)
```

```python
import functools
import math

import jax
import jax.numpy as jnp
from jax import lax
from jax.experimental import pallas as pl
from jax.experimental.pallas import tpu as pltpu
from jax.sharding import PartitionSpec as P

HEAD_DIM = 80
LANES = 128
CORES = 2
NORM_EPS = 1e-06
LOG_BASE = 1.442695041
MASK_FILL = -1e30
AXES = ("rep", "shard")
F32 = jnp.float32
BF16 = jnp.bfloat16


def dot(left, right, left_dim=1, right_dim=0):
    return lax.dot_general(
        left, right, (((left_dim,), (right_dim,)), ((), ())), preferred_element_type=F32
    )


class Place:
    def __init__(self, reps, shards, seqs):
        self.x_size = reps // CORES
        self.x_split = 2 if self.x_size == 2 else 1
        self.a_size = CORES * seqs
        self.b_size = shards // self.a_size
        self.even = self.x_size == 2 and self.b_size == 2
        self.peer_count = self.b_size * CORES
        self.seqs = seqs
        rep, shard = lax.axis_index("rep"), lax.axis_index("shard")
        self.x, self.c = rep // CORES, rep % CORES
        self.a, self.b = shard // self.b_size, shard % self.b_size
        self.shard = shard

    def route(self, move):
        pairs = []
        for x in range(self.x_size):
            for c in range(CORES):
                for a in range(self.a_size):
                    for b in range(self.b_size):
                        pairs.append((self.number(x, c, a, b), self.number(*move(x, c, a, b))))
        return pairs

    def number(self, x, c, a, b):
        return ((x * CORES + c) * self.a_size + a) * self.b_size + b

    def send(self, value, dx=0, dc=0, da=0, db=0):
        return lax.ppermute(
            value,
            AXES,
            self.route(
                lambda x, c, a, b: (
                    (x + dx) % self.x_size,
                    (c + dc) % CORES,
                    (a + da) % self.a_size,
                    (b + db) % self.b_size,
                )
            ),
        )

    def peers(self):
        return [(db, dc) for db in range(self.b_size) for dc in range(CORES)]

    def source(self, db, dc):
        return ((self.b - db) % self.b_size) * CORES + (self.c + dc) % CORES

    def to_cluster(self, tokens, after=()):
        seqs, count, width = tokens.shape
        half = count // CORES
        halves = tokens.reshape(seqs, CORES, half, width)
        shape = (seqs, half, width)
        moves = []
        for i in range(seqs):
            moves += [(0, (i, self.c), 0, i), (0, (i, 1 - self.c), 1, i)]
        own, give = shuffle([halves], [(shape, BF16)] * 2, moves, after)
        got = self.send(give, dc=1)
        after = yield
        parts = route_parts(self, own, got, after or ())
        received = [parts[0]] + [self.send(parts[d], da=d) for d in range(1, self.a_size)]
        moves = [(d, None, 0, (self.a - d) % self.a_size) for d in range(self.a_size)]
        after = yield
        yield shuffle(received, [((self.a_size, half, width), BF16)], moves, after or ())[0]

    def from_cluster(self, chunks):
        half, width = chunks.shape[1:]
        picks = [(0, (self.a + d) % self.a_size, d, None) for d in range(self.a_size)]
        parts = shuffle([chunks], [((half, width), BF16)] * self.a_size, picks)
        received = [parts[0]] + [self.send(parts[d], da=d) for d in range(1, self.a_size)]
        yield
        own, give = route_back(self, received)
        got = self.send(give, dc=1)
        moves = []
        for i in range(self.seqs):
            moves += [(0, i, 0, i * CORES + self.c), (1, i, 0, i * CORES + 1 - self.c)]
        yield
        whole = shuffle([own, got], [((self.a_size, half, width), BF16)], moves)[0]
        yield whole.reshape(self.seqs, CORES * half, width)

    def send_back(self, part, m):
        return lax.ppermute(part, AXES, [(j, i) for i, j in self.route(self._match(m))])

    def place_back(self, received):
        half, width = received[0].shape
        moves = []
        for m in range(self.a_size):
            t = m ^ self.a
            moves.append((m, None, 0, (t % self.seqs) * CORES + t // self.seqs))
        whole = shuffle(received, [((self.a_size, half, width), BF16)], moves)[0]
        return whole.reshape(self.seqs, CORES * half, width)

    def _match(self, m):
        def move(x, c, a, b):
            t = m ^ a
            return x, t // self.seqs, self.seqs * c + t % self.seqs, b

        return move


VMEM = pl.BlockSpec(memory_space=pltpu.VMEM)
ANY = pl.BlockSpec(memory_space=pl.ANY)


LAST = []
SCALE = 0.25
SIZE = {
    "project": 28,
    "attend_forward": 24,
    "middle": 48,
    "outer": 60,
    "outer_give": 60,
    "attend_backward": 24,
    "heads_outer": 24,
    "back_project": 20,
    "finish_heads": 16,
    "finish_full": 16,
}
COST = {
    "project": 14.5,
    "attend_forward": 12.0,
    "middle": 20.0,
    "outer": 7.0,
    "outer_give": 0.1,
    "attend_backward": 25.0,
    "heads_outer": 5.5,
    "back_project": 3.5,
    "pad_weights": 3.5,
    "norm_back": 3.0,
    "finish_heads": 4.0,
    "finish_full": 3.5,
}


def call(name, body, scalars, inputs, outputs, grid=(1,), scratch=(), after=(), vmem=0):
    deps = [*LAST[-1:], *after]
    count, skip = len(inputs), len(deps)

    def run(spots, *refs):
        body(spots, *refs[:count], *refs[count + skip :])

    results = pl.pallas_call(
        run,
        out_shape=[jax.ShapeDtypeStruct(shape, kind) for shape, kind, _ in outputs],
        grid_spec=pltpu.PrefetchScalarGridSpec(
            num_scalar_prefetch=1,
            grid=grid,
            in_specs=[spec for _, spec in inputs] + [ANY] * skip,
            out_specs=[spec for _, _, spec in outputs],
            scratch_shapes=list(scratch),
        ),
        cost_estimate=pl.CostEstimate(
            flops=int(COST.get(name, 1.5) * SCALE * 1.1e9),
            bytes_accessed=int(COST.get(name, 1.5) * SCALE * 3.3e6),
            transcendentals=0,
        ),
        compiler_params=pltpu.CompilerParams(vmem_limit_bytes=(vmem or SIZE.get(name, 12)) * 1024 * 1024),
        name=name,
    )(scalars_of(scalars), *[value for value, _ in inputs], *deps)
    LAST.append(results[0])
    return results


def scalars_of(values):
    if isinstance(values, (list, tuple)):
        return jnp.stack([jnp.asarray(v, jnp.int32) for v in values])
    return values


def shuffle_body(moves, counts, spots, *refs):
    sources, targets, sems = refs[: counts[0]], refs[counts[0] : -1], refs[-1]
    copies, n = [], 0
    for src, src_rank, dst, dst_rank in moves:
        ends = []
        for ref, rank in ((sources[src], src_rank), (targets[dst], dst_rank)):
            ends.append(ref.at[tuple(spots[n + k] for k in range(rank))] if rank else ref)
            n += rank
        copies.append(pltpu.make_async_copy(*ends, sems.at[len(copies)]))
    for copy in copies:
        copy.start()
    for copy in copies:
        copy.wait()


def shuffle(sources, shapes, moves, after=()):
    spots, shape_of = [], []
    for src, src_spot, dst, dst_spot in moves:
        ranks = []
        for spot in (src_spot, dst_spot):
            spot = () if spot is None else spot if isinstance(spot, tuple) else (spot,)
            ranks.append(len(spot))
            spots += spot
        shape_of.append((src, ranks[0], dst, ranks[1]))
    return call(
        "shuffle",
        functools.partial(shuffle_body, shape_of, (len(sources), len(shapes))),
        spots or [0],
        [(source, VMEM) for source in sources],
        [(*shape, ANY) for shape in shapes],
        scratch=[pltpu.SemaphoreType.DMA((len(moves),))],
        after=after,
    )


def route_parts_body(seqs, info, own, got, *outs):
    for d, out in enumerate(outs):
        target = info[1 + d]

        @pl.when(target // seqs == info[0])
        def near():
            out[...] = own[target % seqs]

        @pl.when(target // seqs != info[0])
        def far():
            out[...] = got[target % seqs]


def route_parts(at, own, got, after=()):
    return call(
        "route_parts",
        functools.partial(route_parts_body, at.seqs),
        [at.c, *ahead(at.a, at.a_size)],
        [(own, VMEM), (got, VMEM)],
        [(own.shape[1:], BF16, VMEM)] * at.a_size,
        after=after,
    )


def route_back_body(seqs, info, *refs):
    parts, own, give = refs[:-2], refs[-2], refs[-1]
    for d, part in enumerate(parts):
        source = info[1 + d]

        @pl.when(source // seqs == info[0])
        def near():
            own[source % seqs] = part[...]

        @pl.when(source // seqs != info[0])
        def far():
            give[source % seqs] = part[...]


def route_back(at, parts):
    shape = (at.seqs, *parts[0].shape)
    return call(
        "route_back",
        functools.partial(route_back_body, at.seqs),
        [at.c, *[(at.a - d) % at.a_size for d in range(at.a_size)]],
        [(part, VMEM) for part in parts],
        [(shape, BF16, VMEM)] * 2,
    )


def add_body(counts, spots, *refs):
    terms = sum(counts)
    ins, outs, n = refs[:terms], refs[terms:], 0
    for count, out in zip(counts, outs):
        total = ins[n][...].astype(F32)
        for k in range(1, count):
            total = total + ins[n + k][...].astype(F32)
        out[...] = total.reshape(out.shape).astype(out.dtype)
        n += count


def add_blocks(groups, after=()):
    spots, inputs, outputs = [], [], []
    for terms in groups:
        for value, dim, index in terms:
            block = [1 if k == dim else size for k, size in enumerate(value.shape)]

            def spot(i, s, dim=dim, n=len(spots), rank=value.ndim):
                return tuple(s[n] if k == dim else 0 for k in range(rank))

            spots.append(index)
            inputs.append((value, pl.BlockSpec(tuple(block), spot)))
        shape = tuple(size for k, size in enumerate(value.shape) if k != dim)
        outputs.append((shape, BF16, VMEM))
    return call(
        "add_blocks",
        functools.partial(add_body, [len(terms) for terms in groups]),
        spots,
        inputs,
        outputs,
        after=after,
    )


def later(value, *done):
    return lax.optimization_barrier((value, *done))[0]


def pick(stacked, index, axis=0):
    return lax.dynamic_index_in_dim(stacked, index, axis, keepdims=False)


def by_order(own, others, axis_size, spot):
    moves = [(d, None, 0, (spot - d) % axis_size) for d in range(axis_size)]
    return shuffle([own, *others], [((axis_size, *own.shape), own.dtype)], moves)[0]


def heads_part_body(count, groups, info, query, key, value, vectors, *outs):
    width = query.shape[1] // count // groups
    rows = outs[0].shape[0]
    down = pl.ds(pl.multiple_of(info[len(outs)] * rows, rows), rows)
    for n, out in enumerate(outs):
        for peer in range(count):

            @pl.when(info[n] == peer)
            def copy():
                for g in range(groups):
                    for k, source in enumerate((query, key, value)):
                        spot = (g * 3 + k) * width
                        first = (peer * groups + g) * width
                        out[:, spot : spot + width] = source[down, first : first + width]

        out[:, 3 * groups * width :] = vectors[down, :]


def heads_parts(at, weights, vectors, groups):
    rows, model = weights[0].shape
    count = at.peer_count
    shape = (rows // at.x_split, 3 * model // count + vectors.shape[1])
    targets = [((at.b + db) % at.b_size) * CORES + at.c for db in range(at.b_size)]
    return call(
        "heads_parts",
        functools.partial(heads_part_body, count, groups),
        [*targets, at.x if at.x_split == 2 else 0],
        [(w, VMEM) for w in (*weights, vectors)],
        [(shape, BF16, VMEM)] * at.b_size,
    )


def quarter_body(info, *refs):
    out, sem = refs[3], refs[4]
    rows, half = out.shape[1:]
    down = pl.ds(pl.multiple_of(info[0] * rows, rows), rows)
    right = pl.ds(pl.multiple_of(info[1] * half, half), half)
    copies = [pltpu.make_async_copy(refs[w].at[down, right], out.at[w], sem.at[w]) for w in range(3)]
    for copy in copies:
        copy.start()
    for copy in copies:
        copy.wait()


def quarter_of(at, weights, after):
    rows, model = weights[0].shape
    return call(
        "quarter",
        quarter_body,
        [at.x if at.x_split == 2 else 0, at.c],
        [(w, VMEM) for w in weights],
        [((3, rows // at.x_split, model // CORES), BF16, ANY)],
        scratch=[pltpu.SemaphoreType.DMA((3,))],
        after=after,
    )[0]


def pad_body(heads, groups, a_size, info, *refs):
    split = (len(refs) - groups - 2) // a_size
    sources, outs = refs[: split * a_size], refs[split * a_size :]
    compact, (padded, vectors) = outs[:groups], outs[groups:]
    b_size, rows, width = sources[0].shape
    used = 3 * heads * HEAD_DIM
    part = heads // groups
    padded[...] = jnp.zeros_like(padded)
    for n in range(split):
        for d in range(a_size):
            for b in range(b_size):
                piece = sources[n * a_size + d][b]
                spot = (info[1 + d] * b_size + b) * split
                spot = (spot + (info[0] ^ n if split == 2 else 0)) * rows
                spot = pl.ds(pl.multiple_of(spot, rows), rows)
                for g in range(groups):
                    step = used // groups
                    compact[g][spot, :] = piece[:, g * step : (g + 1) * step]
                vectors[spot, :] = piece[:, used:]
                for k in range(3):
                    for h in range(heads):
                        first = (((h // part) * 3 + k) * part + h % part) * HEAD_DIM
                        lane = (k * heads + h) * LANES
                        padded[spot, lane : lane + HEAD_DIM] = piece[:, first : first + HEAD_DIM]


def pad_weights(at, sources, heads, groups, after):
    b_size, rows, width = sources[0].shape
    total = len(sources) * b_size * rows
    used = 3 * heads * HEAD_DIM
    return call(
        "pad_weights",
        functools.partial(pad_body, heads, groups, at.a_size),
        [at.x, *[(at.a - d) % at.a_size for d in range(at.a_size)]],
        [(source, VMEM) for source in sources],
        [
            *[((total, used // groups), BF16, VMEM)] * groups,
            ((total, 3 * heads * LANES), BF16, VMEM),
            ((total, width - used), BF16, VMEM),
        ],
        after=after,
        vmem=16,
    )


def project_body(count, spots, *refs):
    tokens, (gain, weight, bias, times, qkv, normed) = refs[:count], refs[count:]
    rows = tokens[0].shape[1]
    for p in range(count):
        value = tokens[p][0].astype(F32)
        rate = lax.rsqrt(jnp.mean(value * value, axis=-1, keepdims=True) + NORM_EPS)
        spot = pl.multiple_of(spots[p] * rows, rows)
        normed[pl.ds(spot, rows), :] = (value * rate * gain[...]).astype(BF16)
    step = qkv.shape[1] // 3
    for k in range(3):
        lanes = slice(k * step, (k + 1) * step)
        acc = dot(normed[...], weight[:, lanes])
        qkv[:, lanes] = ((acc + bias[:, lanes]) * times[:, lanes]).astype(BF16)


def project(at, parts, gain, weight, bias, times):
    a_size, half, model = parts[0].shape
    count = len(parts)
    cols = weight.shape[1]
    fixed = lambda a, s: (0, 0)
    return call(
        "project",
        functools.partial(project_body, count),
        [at.source(db, dc) for db, dc in at.peers()],
        [(part, pl.BlockSpec((1, half, model), lambda a, s: (a, 0, 0))) for part in parts]
        + [
            (gain, pl.BlockSpec((1, model), fixed)),
            (weight, pl.BlockSpec((model, cols), fixed)),
            (bias, pl.BlockSpec((1, cols), fixed)),
            (times, pl.BlockSpec((1, cols), fixed)),
        ],
        [
            (
                (a_size * count * half, cols),
                BF16,
                pl.BlockSpec((count * half, cols), lambda a, s: (a, 0)),
            ),
            (
                (a_size * count * half, model),
                BF16,
                pl.BlockSpec((count * half, model), lambda a, s: (a, 0)),
            ),
        ],
        grid=(a_size,),
    )


def forward_body(heads, block, info, starts, query, key, value, mixed, query_aug, total, top):
    index = pl.program_id(0)
    half = block // CORES
    core = info[pl.num_programs(0) + 1]
    total[...] = jnp.zeros_like(total)
    top[...] = jnp.full_like(top, MASK_FILL)
    rows = index * block + lax.broadcasted_iota(jnp.int32, (block, block), 0)
    begin = starts[...][:, :1]

    def step(j, carry):
        spot = pl.multiple_of(j * block, block)
        columns = spot + lax.broadcasted_iota(jnp.int32, (block, block), 1)
        bias = jnp.where((columns >= begin) & (columns <= rows), 0.0, MASK_FILL)
        lanes = [slice(h * LANES, (h + 1) * LANES) for h in range(heads)]
        scores = [dot(query[:, l], key[pl.ds(spot, block), l], 1, 1) + bias for l in lanes]
        olds = [top[h] for h in range(heads)]
        news = [
            jnp.maximum(old, jnp.max(score, axis=1, keepdims=True))
            for old, score in zip(olds, scores)
        ]
        weights = [
            jnp.exp(score - jnp.concatenate([new] * (block // LANES), axis=1)).astype(BF16)
            for score, new in zip(scores, news)
        ]
        for h in range(heads):
            total[h] = total[h] * jnp.exp(olds[h] - news[h]) + dot(
                weights[h], value[pl.ds(spot, block), lanes[h]]
            )
            top[h] = news[h]
        return carry

    lax.fori_loop(info[index], index + 1, step, 0)
    lane = lax.broadcasted_iota(jnp.int32, (block, LANES), 1)
    for h in range(heads):
        lanes = slice(h * LANES, (h + 1) * LANES)
        acc = total[h]
        weight_sum = acc[:, HEAD_DIM : HEAD_DIM + 1]
        result = (acc / weight_sum)[:, :HEAD_DIM].astype(BF16)
        for k in range(CORES):
            mixed[0, core ^ k, 0, :, h * HEAD_DIM : (h + 1) * HEAD_DIM] = result[
                k * half : (k + 1) * half
            ]
        rest = -(top[h] + jnp.log(weight_sum))
        aug = query[:, lanes].astype(F32)
        for k in range(3):
            term = rest.astype(BF16).astype(F32)
            aug = jnp.where(lane == HEAD_DIM + k, term, aug)
            rest = rest - term
        query_aug[:, lanes] = aug.astype(BF16)


def attend_forward(at, info, starts, qkv, heads, block):
    length = qkv.shape[0]
    wide = heads * LANES
    width = heads * HEAD_DIM
    count = length // block
    b_size = at.b_size
    return call(
        "attend_forward",
        functools.partial(forward_body, heads, block),
        info,
        [
            (starts, pl.BlockSpec((block, LANES), lambda i, s: (i, 0))),
            (qkv, pl.BlockSpec((block, wide), lambda i, s: (i, 0))),
            (qkv, pl.BlockSpec((length, wide), lambda i, s: (0, 1))),
            (qkv, pl.BlockSpec((length, wide), lambda i, s: (0, 2))),
        ],
        [
            (
                (b_size, CORES, at.a_size, block // CORES, width),
                BF16,
                pl.BlockSpec(
                    (1, CORES, 1, block // CORES, width),
                    lambda i, s: ((i + b_size - s[count]) % b_size, 0, i // b_size, 0, 0),
                ),
            ),
            ((length, wide), BF16, pl.BlockSpec((block, wide), lambda i, s: (i, 0))),
        ],
        grid=(count,),
        scratch=[
            pltpu.VMEM((heads, block, LANES), F32),
            pltpu.VMEM((heads, block, LANES), F32),
        ],
    )


def backward_body(
    heads,
    first,
    block,
    count,
    info,
    starts,
    scale,
    query,
    key,
    value,
    mixed,
    *rest,
):
    grad_refs = rest[:count]
    grads, scale_sum, bias_sum, grad, grad_aug, d_query, d_key, d_value = rest[count:]
    index = pl.num_programs(0) - 1 - pl.program_id(0)
    b_own, core = info[pl.num_programs(0)], info[pl.num_programs(0) + 1]
    b_size = count // CORES
    width = heads * HEAD_DIM

    @pl.when(pl.program_id(0) == 0)
    def clear():
        d_key[...] = jnp.zeros_like(d_key)
        d_value[...] = jnp.zeros_like(d_value)
        scale_sum[...] = jnp.zeros_like(scale_sum)
        bias_sum[...] = jnp.zeros_like(bias_sum)

    half = block // CORES
    lane = lax.broadcasted_iota(jnp.int32, (half, LANES), 1)
    for k in range(CORES):
        peer = ((b_own + b_size - index % b_size) % b_size) * CORES + (core ^ k)
        for p in range(count):

            @pl.when(peer == p)
            def fetch():
                grad[...] = grad_refs[p][index // b_size]

        for h in range(heads):
            part = slice((first + h) * HEAD_DIM, (first + h + 1) * HEAD_DIM)
            grad_h = grad[:, part].astype(F32)
            mixed_h = mixed[0, core ^ k, 0, :, part].astype(F32)
            delta = jnp.sum(grad_h * mixed_h, axis=1, keepdims=True)
            aug = jnp.concatenate([grad_h, jnp.zeros((half, LANES - HEAD_DIM), F32)], axis=1)
            high = (-delta).astype(BF16).astype(F32)
            aug = jnp.where(lane == HEAD_DIM, high, aug)
            aug = jnp.where(lane == HEAD_DIM + 1, -delta - high, aug)
            grad_aug[k * half : (k + 1) * half, h * LANES : (h + 1) * LANES] = aug.astype(BF16)
    d_query[...] = jnp.zeros_like(d_query)
    columns = index * block + lax.broadcasted_iota(jnp.int32, (block, block), 1)
    begin = starts[0:1, :]

    def step(j, carry):
        spot = pl.multiple_of(j * block, block)
        rows = spot + lax.broadcasted_iota(jnp.int32, (block, block), 0)
        allowed = (rows >= begin) & (rows <= columns)
        lanes = [slice(h * LANES, (h + 1) * LANES) for h in range(heads)]
        keys = [key[pl.ds(spot, block), l] for l in lanes]
        queries = [query[:, l] for l in lanes]
        grads_of = [grad_aug[:, l] for l in lanes]
        scores = [dot(k, q, 1, 1) for k, q in zip(keys, queries)]
        d_probs = [
            dot(value[pl.ds(spot, block), l], g, 1, 1) for l, g in zip(lanes, grads_of)
        ]
        probs = [jnp.where(allowed, jnp.exp(score), 0.0) for score in scores]
        d_scores = [(prob * d_prob).astype(BF16) for prob, d_prob in zip(probs, d_probs)]
        for h, l in enumerate(lanes):
            d_value[pl.ds(spot, block), l] += dot(probs[h].astype(BF16), grads_of[h])
            d_key[pl.ds(spot, block), l] += dot(d_scores[h], queries[h])
            d_query[:, l] += dot(d_scores[h], keys[h], 0, 0)
        return carry

    lax.fori_loop(info[index], index + 1, step, 0)
    here = pl.ds(pl.multiple_of(index * block, block), block)
    for h in range(heads):
        lanes = slice(h * LANES, (h + 1) * LANES)
        d_scaled = d_query[:, lanes].astype(BF16).astype(F32)
        scale_sum[...] += jnp.sum(d_scaled * query[:, lanes].astype(F32), axis=0, keepdims=True)
        d_q = (d_scaled * scale[0:1, lanes]).astype(BF16)
        for k, term in enumerate((d_q, d_key[here, lanes], d_value[here, lanes])):
            spot = k * width + h * HEAD_DIM
            term = term.astype(BF16)
            grads[:, spot : spot + HEAD_DIM] = term[:, :HEAD_DIM]
            bias_sum[:, (k * heads + h) * LANES : (k * heads + h + 1) * LANES] += jnp.sum(
                term.astype(F32), axis=0, keepdims=True
            )


def attend_backward(
    at, info, starts, scale, query_aug, qkv, grads, mixed, heads, groups, group, block
):
    length = qkv.shape[0]
    wide = heads * LANES
    width = heads * HEAD_DIM
    count = length // block
    b_size = at.b_size
    half = block // CORES

    def mixed_spot(i, s):
        i = count - 1 - i
        return (i + b_size - s[count]) % b_size, 0, i // b_size, 0, 0

    fixed = lambda i, s: (0, 0)
    return call(
        "attend_backward",
        functools.partial(backward_body, heads, group * heads, block, len(grads)),
        info,
        [
            (starts, pl.BlockSpec((8, block), lambda i, s: (0, count - 1 - i))),
            (scale, pl.BlockSpec((8, wide), fixed)),
            (query_aug, pl.BlockSpec((block, wide), lambda i, s: (count - 1 - i, group))),
            (qkv, pl.BlockSpec((length, wide), lambda i, s: (0, groups + group))),
            (qkv, pl.BlockSpec((length, wide), lambda i, s: (0, 2 * groups + group))),
            (mixed, pl.BlockSpec((1, CORES, 1, half, mixed.shape[4]), mixed_spot)),
        ]
        + [(grad, VMEM) for grad in grads],
        [
            (
                (length, 3 * width),
                BF16,
                pl.BlockSpec((block, 3 * width), lambda i, s: (count - 1 - i, 0)),
            ),
            ((8, LANES), F32, pl.BlockSpec((8, LANES), fixed)),
            ((8, 3 * wide), F32, pl.BlockSpec((8, 3 * wide), fixed)),
        ],
        grid=(count,),
        scratch=[
            pltpu.VMEM((half, mixed.shape[4]), BF16),
            pltpu.VMEM((block, wide), BF16),
            pltpu.VMEM((block, wide), F32),
            pltpu.VMEM((length, wide), F32),
            pltpu.VMEM((length, wide), F32),
        ],
    )


def concat_body(info, *refs):
    parts, out = refs[:-1], refs[-1]
    width = parts[0].shape[1]
    for p, part in enumerate(parts):
        out[:, p * width : (p + 1) * width] = part[...]


def concat(parts, after):
    rows, width = parts[0].shape
    return call(
        "concat",
        concat_body,
        [0],
        [(part, VMEM) for part in parts],
        [((rows, width * len(parts)), BF16, VMEM)],
        after=after,
    )[0]


def middle_body(count, source_count, moves, info, *refs):
    mixed, tokens, d_out, gain = refs[:4]
    sources = refs[4 : 4 + source_count]
    outs = refs[4 + source_count :]
    output, d_residual, d_proj, normed, activated, d_up = outs[:6]
    d_parts = outs[6:-4]
    weights, sems = outs[-4:-1], outs[-1]
    w_out, w_up, w_down = weights
    rows, half = sources[0].shape[2:]
    width = d_parts[0].shape[1]

    def copies(w):
        for n, (src, s, k) in enumerate(moves):
            if k == w:
                down = pl.ds(pl.multiple_of(info[2 * n] * rows, rows), rows)
                right = pl.ds(pl.multiple_of(info[2 * n + 1] * half, half), half)
                yield pltpu.make_async_copy(
                    sources[src].at[s, w], weights[w].at[down, right], sems.at[n]
                )

    def arrived(w):
        @pl.when(pl.program_id(0) == 0)
        def wait():
            for copy in copies(w):
                copy.wait()

    @pl.when(pl.program_id(0) == 0)
    def start():
        for w in range(3):
            for copy in copies(w):
                copy.start()

    arrived(0)
    residual = tokens[...].astype(F32) + dot(mixed[...], w_out[...])
    rate = lax.rsqrt(jnp.mean(residual * residual, axis=-1, keepdims=True) + NORM_EPS)
    normed[...] = (residual * rate * gain[...]).astype(BF16)
    arrived(1)
    upward = dot(normed[...], w_up[...])
    gate = 1.0 / (1.0 + jnp.exp(-upward))
    activated[...] = (upward * gate).astype(BF16)
    arrived(2)
    output[...] = (residual + dot(activated[...], w_down[...])).astype(BF16)
    d_activated = dot(d_out[...], w_down[...], 1, 1)
    d_up[...] = (d_activated * gate * (1 + upward * (1 - gate))).astype(BF16)
    scaled = dot(d_up[...], w_up[...], 1, 1) * gain[...]
    inner = jnp.mean(residual * scaled, axis=-1, keepdims=True)
    d_norm = rate * scaled - residual * (rate * rate * rate * inner)
    d_total = d_out[...].astype(F32) + d_norm
    d_residual[...] = d_total
    d_proj[...] = d_total.astype(BF16)
    d_mixed = dot(d_proj[...], w_out[...], 1, 1).astype(BF16)
    for p in range(count):
        d_parts[p][...] = d_mixed[:, p * width : (p + 1) * width]


def middle(at, mixed, tokens, d_out, gain, sources):
    count = at.peer_count
    rows, model = tokens.shape
    width = model // count
    arrays = list(sources.values())
    a_size, _, piece, half = arrays[0].shape
    group = model // at.peer_count // piece
    moves, spots = [], []
    for n, (dx, db, dc) in enumerate(sources):
        for a in range(a_size):
            for w in range(3):
                row = a * at.b_size + (at.b - db) % at.b_size
                if at.x_split == 2:
                    row = row * 2 + (at.x + dx) % 2
                if w == 0:
                    peer, rest = row // group, row % group
                    far = (at.b - peer // CORES) % at.b_size
                    row = (far * CORES + ((peer % CORES) ^ at.c)) * group + rest
                moves.append((n, a, w))
                spots += [row, (at.c + dc) % CORES]
    block = min(256, rows)
    row = lambda i, s: (i, 0)
    rows_of = pl.BlockSpec((block, model), row)
    part = pl.BlockSpec((block, width), row)
    types = [BF16, F32, BF16, BF16, BF16, BF16]
    return call(
        "middle",
        functools.partial(middle_body, count, len(arrays), moves),
        spots,
        [(mixed, rows_of), (tokens, rows_of), (d_out, rows_of)]
        + [(gain, pl.BlockSpec(gain.shape, lambda i, s: (0, 0)))]
        + [(source, ANY) for source in arrays],
        [((rows, model), kind, rows_of) for kind in types]
        + [((rows, width), BF16, part)] * count,
        grid=(rows // block,),
        scratch=[pltpu.VMEM((model, model), BF16)] * 3
        + [pltpu.SemaphoreType.DMA((len(moves),))],
    )


def outer_body(count, split, add, info, *refs):
    pairs, rest = refs[:6], refs[6:]
    for w in range(3):

        @pl.when(pl.program_id(0) == w)
        def product():
            value = dot(pairs[2 * w][...], pairs[2 * w + 1][...], 0, 0)
            target = rest[-1] if split else rest[-1].at[0]
            width = value.shape[0] // count
            for p in range(count):
                spot = p * width
                if w == 0:
                    spot = pl.multiple_of(info[3 + p] * width, width)
                part = value[p * width : (p + 1) * width]
                if add:
                    part = part + rest[0][0, pl.ds(spot, width)].astype(F32)
                target[pl.ds(spot, width)] = part.astype(BF16)

    if split:
        keep_x, give_x, keep_b, give_b, total = rest[1:]
        pairs_a, b_size, rows = keep_x.shape[1:4]
        for k in range(pairs_a):
            for b in range(b_size):
                for half, out in ((info[1], keep_x), (1 - info[1], give_x)):
                    spot = pl.multiple_of((k * b_size + b) * 2 * rows + half * rows, rows)
                    out[0, k, b] = total[pl.ds(spot, rows)]
            for b, out in ((info[2], keep_b), (1 - info[2], give_b)):
                for half in range(2):
                    spot = (((k + pairs_a) * b_size) * 2 + half) * rows + b * 2 * rows
                    out[0, k, half] = total[pl.ds(pl.multiple_of(spot, rows), rows)]


def outer(at, pairs, cols, add=None, after=()):
    rows, model = pairs[0][0].shape
    half = model // CORES
    count = at.peer_count
    split = add is not None and at.even
    info = [cols, at.x if at.even else 0, at.b, *[at.source(db, dc) for db, dc in at.peers()]]
    inputs = []
    for left, right in pairs:
        inputs.append((left, pl.BlockSpec((rows, model), lambda w, s: (0, 0))))
        inputs.append((right, pl.BlockSpec((rows, half), lambda w, s: (0, s[0]))))
    block = pl.BlockSpec((1, model, half), lambda w, s: (w, 0, 0))
    outputs = [((3, model, half), BF16, block)]
    scratch = []
    if add is not None:
        inputs.append((add, block))
    if split:
        shape = (at.a_size // 2, 2, model // at.a_size // 4, half)
        part = pl.BlockSpec((1, *shape), lambda w, s: (w, 0, 0, 0, 0))
        outputs = [((3, *shape), BF16, part)] * 4
        scratch = [pltpu.VMEM((model, half), BF16)]
    return call(
        "outer_give" if add is None else "outer",
        functools.partial(outer_body, count, split, add is not None),
        info,
        inputs,
        outputs,
        grid=(3,),
        scratch=scratch,
        after=after,
    )


def give_body(groups, info, *refs):
    grads, weights, out = refs[:groups], refs[groups : 2 * groups], refs[-1]
    value = back_product(grads, weights)
    out[...] = value.astype(BF16).reshape(out.shape)


def back_product(grads, weights):
    total = 0.0
    for grad, weight in zip(grads, weights):
        total = total + dot(grad[...].reshape(-1, grad.shape[-1]), weight[...], 1, 1)
    return total


def keep_body(groups, info, *refs):
    grads, weights, got = refs[:groups], refs[groups : 2 * groups], refs[2 * groups]
    outs = refs[2 * groups + 1 :]
    pairs, b_size, half = got.shape[:3]
    value = back_product(grads, weights).reshape(got.shape) + got[...].astype(F32)
    for b in range(b_size):
        for n, out in enumerate(outs):

            @pl.when(info[2 + n] == b)
            def copy():
                out[...] = value[:, b].astype(out.dtype)


def back_project(at, grads, weights, half, which, got=None):
    model = weights[0].shape[0]
    pair = at.a_size // 2
    groups = len(grads)
    width = grads[0].shape[1]
    shape = (pair, at.b_size, half, model)
    grads = [g.reshape(at.a_size, at.b_size, CORES, half, width) for g in grads]
    block = pl.BlockSpec((pair, at.b_size, 1, half, width), lambda i, s: (s[0], 0, s[1], 0, 0))
    core = at.c if got is not None else 1 - at.c
    inputs = [(g, block) for g in grads]
    inputs += [(weight, VMEM) for weight in weights]
    if got is None:
        body, outputs = give_body, [(shape, BF16, VMEM)]
    else:
        body = keep_body
        inputs.append((got, VMEM))
        outputs = [((pair, half, model), F32 if db == 0 else BF16, VMEM) for db in range(at.b_size)]
    return call(
        "back_project",
        functools.partial(body, groups),
        [which ^ core, core, *ahead(at.b, at.b_size)],
        inputs,
        outputs,
    )


def norm_back_body(count, info, *refs):
    own, others = refs[0], refs[1:count]
    tokens, d_residual, gain = refs[count : count + 3]
    for n, out in enumerate(refs[count + 3 :]):
        k = info[1 + n]
        grad = own[k]
        for other in others:
            grad = grad + other[k].astype(F32)
        value = tokens[k].astype(F32)
        rate = lax.rsqrt(jnp.mean(value * value, axis=-1, keepdims=True) + NORM_EPS)
        scaled = grad * gain[...]
        inner = jnp.mean(value * scaled, axis=-1, keepdims=True)
        d_norm = rate * scaled - value * (rate * rate * rate * inner)
        out[...] = (d_residual[k] + d_norm).astype(BF16)


def norm_back(at, terms, chunks, d_residual, gain, which, after):
    pair, half, model = terms[0].shape
    block = pl.BlockSpec((pair, half, model), lambda i, s: (s[0], 0, 0))
    order = [k ^ (at.a % pair) for k in range(pair)]
    return call(
        "norm_back",
        functools.partial(norm_back_body, len(terms)),
        [which ^ at.c, *order],
        [(t, VMEM) for t in terms] + [(chunks, block), (d_residual, block), (gain, VMEM)],
        [((half, model), BF16, VMEM)] * pair,
        after=after,
    )


def heads_outer_body(steps, info, normed, grads, extra, *rest):
    outs, acc = rest[:-1], rest[-1]
    value = dot(normed[...], grads[...], 0, 0)

    @pl.when(pl.program_id(0) == 0)
    def first():
        acc[...] = value

    @pl.when(pl.program_id(0) != 0)
    def later():
        acc[...] += value

    @pl.when(pl.program_id(0) == steps - 1)
    def last():
        used = acc.shape[1]
        pairs, b_size, rows = outs[0].shape[:3]
        split = len(outs)
        for n, out in enumerate(outs):
            for s in range(pairs * b_size):
                spot = (s * split + (info[0] ^ n if split == 2 else 0)) * rows
                spot = pl.ds(pl.multiple_of(spot, rows), rows)
                out[s // b_size, s % b_size, :, :used] = acc[spot, :].astype(BF16)
                out[s // b_size, s % b_size, :, used:] = extra[spot, :]


def heads_outer(at, normed, grads, extra):
    length, model = normed.shape
    used = grads.shape[1]
    block = min(512, length)
    steps = length // block
    rows = model // at.a_size // at.b_size // at.x_split
    shape = (at.a_size, at.b_size, rows, used + extra.shape[1])
    return call(
        "heads_outer",
        functools.partial(heads_outer_body, steps),
        [at.x],
        [
            (normed, pl.BlockSpec((block, model), lambda i, s: (i, 0))),
            (grads, pl.BlockSpec((block, used), lambda i, s: (i, 0))),
            (extra, pl.BlockSpec(extra.shape, lambda i, s: (0, 0))),
        ],
        [(shape, BF16, pl.BlockSpec(shape, lambda i, s: (0, 0, 0, 0)))] * at.x_split,
        grid=(steps,),
        scratch=[pltpu.VMEM((model, used), F32)],
    )


def all_sum(at, value, axis, size):
    total = value
    for d in range(1, size):
        total = total + at.send(value, **{axis: d}).astype(value.dtype)
    return total


def ahead(spot, size):
    return [(spot + d) % size for d in range(size)]


def cat_body(info, first, first_got, second, second_got, *outs):
    pair = first.shape[1]
    for d, out in enumerate(outs):
        spot = info[d] % pair

        @pl.when(info[d] < pair)
        def low():
            out[...] = (first[:, spot].astype(F32) + first_got[:, spot].astype(F32)).astype(BF16)

        @pl.when(info[d] >= pair)
        def high():
            out[...] = (second[:, spot].astype(F32) + second_got[:, spot].astype(F32)).astype(BF16)


class FullReduce:
    def __init__(self, at, parts):
        self.at = at
        if at.even:
            keep_x, give_x, keep_b, give_b = parts
            self.first = keep_x, at.send(give_x, dx=1)
            self.second = keep_b, at.send(give_b, db=1)
        else:
            self.part = parts[0].reshape(3, at.a_size, at.b_size, -1, parts[0].shape[-1])

    def next(self):
        at = self.at
        if not at.even:
            return
        groups = [[(t, 2, b) for t in self.first] for b in ahead(at.b, 2)]
        groups += [[(t, 2, x) for t in self.second] for x in ahead(at.x, 2)]
        keep_b, give_b, keep_x, give_x = add_blocks(groups)
        self.first = keep_b, at.send(give_b, db=1)
        self.second = keep_x, at.send(give_x, dx=1)

    def over_a(self):
        at = self.at
        if at.even:
            shape = self.first[0].shape
            parts = call(
                "cat",
                cat_body,
                ahead(at.a, at.a_size),
                [(t, VMEM) for t in (*self.first, *self.second)],
                [((3, *shape[2:]), BF16, VMEM)] * at.a_size,
            )
        else:
            parts = add_blocks([[(self.part, 1, a)] for a in ahead(at.a, at.a_size)])
        self.got = [parts[0]] + [at.send(parts[d], da=d) for d in range(1, at.a_size)]

    def end(self):
        at = self.at
        if at.even:
            part = add_blocks([[(t[None], 0, 0) for t in self.got]])[0]
            far = at.send(part, dx=1)
            return [part, far, at.send(part, dc=1), at.send(far, dc=1)]
        parts = add_blocks([[(t, 1, b) for t in self.got] for b in ahead(at.b, at.b_size)])
        got = [parts[0]] + [at.send(parts[d], db=d) for d in range(1, at.b_size)]
        part = add_blocks([[(t[None], 0, 0) for t in got]])[0]
        part = all_sum(at, part, "dx", at.x_size)
        return [part, at.send(part, dc=1)]


class HeadsReduce:
    def __init__(self, at, parts):
        self.at = at
        self.got = [parts[0]]
        if at.x_split == 2:
            self.got.append(at.send(parts[1], dx=1))

    def over_a(self):
        at = self.at
        parts = add_blocks([[(t, 0, a) for t in self.got] for a in ahead(at.a, at.a_size)])
        self.got = [parts[0]] + [at.send(parts[d], da=d) for d in range(1, at.a_size)]
        return parts

    def by_b(self, after=()):
        at = self.at
        if at.x_split == 1:
            total = add_blocks([[(t[None], 0, 0) for t in self.got]])[0]
            self.got = [all_sum(at, total, "dx", at.x_size)]
        groups = [[(t, 0, b) for t in self.got] for b in ahead(at.b, at.b_size)]
        return add_blocks(groups, after)


def side_body(groups, info, *refs):
    for n, out in enumerate(refs[-(len(refs) // (groups + 1)) :]):
        for g in range(groups):
            out[g] = refs[n * groups + g][...]


def to_peers(at, groups):
    shape = (len(groups), *groups[0][0].shape)
    parts = call(
        "side",
        functools.partial(side_body, len(groups)),
        [0],
        [(group[b], VMEM) for b in range(at.b_size) for group in groups],
        [(shape, BF16, VMEM)] * at.b_size,
    )
    parts = [at.send(parts[db], db=db, dc=dc) if db or dc else parts[0] for db, dc in at.peers()]
    if at.x_split == 1:
        return [parts]
    return [parts, at.send(jnp.stack(parts), dx=1)]


def in_order(info, refs, split, half, core, spot):
    near = [r[spot] for r in refs]
    if split == 2:
        near = [jnp.where(info[0] == half, near[2 * k], near[2 * k + 1]) for k in range(2)]
    return jnp.where(info[1] == core, near[0], near[1])


def finish_full_body(split, info, *refs):
    count = CORES * split
    parts, (weight, gain), outs = refs[:count], refs[count : count + 2], refs[count + 2 :]
    rows, half = parts[0].shape[1:]
    for x in range(split):
        spot = slice(x * rows, (x + 1) * rows)
        for w in range(3):
            for c in range(CORES):
                outs[w][spot, c * half : (c + 1) * half] = in_order(
                    info, parts, split, x, c, w
                ).astype(F32)
    total = jnp.sum(outs[1][...] * weight[...].astype(F32), axis=1, keepdims=True)
    outs[3][...] = total / gain[...].astype(F32)


def finish_full(at, parts, weight, gain, after):
    rows, model = weight.shape
    return call(
        "finish_full",
        functools.partial(finish_full_body, 2 if at.even else 1),
        [at.x, at.c],
        [(p, VMEM) for p in parts] + [(weight, VMEM), (gain[:, None], VMEM)],
        [((rows, model), F32, VMEM)] * 3 + [((rows, 1), F32, VMEM)],
        after=after,
    )


def finish_heads_body(count, split, info, *refs):
    parts, refs = refs[:count], refs[count:]
    far, refs = refs[: split - 1], refs[split - 1 :]
    weights, gain, outs = refs[:3], refs[3], refs[4:]
    few = outs[4].shape[1]
    groups, rows, width = parts[0].shape
    width = (width - few) // 3
    for n in range(split):
        down = pl.ds(pl.multiple_of((info[count] ^ n if split == 2 else 0) * rows, rows), rows)
        total = jnp.zeros((rows, few), F32)
        for p in range(count):
            for g in range(groups):
                source = far[0].at[p, g] if n else parts[p].at[g]
                total = total + source[:, 3 * width :].astype(F32)
                for peer in range(count):

                    @pl.when(info[p] == peer)
                    def copy():
                        for k in range(3):
                            spot = (peer * groups + g) * width
                            piece = source[:, k * width : (k + 1) * width]
                            outs[k][down, spot : spot + width] = piece.astype(F32)

        outs[4][down, :] = total
    total = jnp.zeros(outs[3].shape, F32)
    for k in range(3):
        total = total + jnp.sum(outs[k][...] * weights[k][...].astype(F32), axis=1, keepdims=True)
    outs[3][...] = total / gain[...].astype(F32)


def finish_heads(at, parts, weights, gain, few):
    rows, model = weights[0].shape
    flat = [*parts[0], *parts[1:]]
    return call(
        "finish_heads",
        functools.partial(finish_heads_body, at.peer_count, at.x_split),
        [*[at.source(db, dc) for db, dc in at.peers()], at.x],
        [(p, VMEM) for p in flat] + [(w, VMEM) for w in weights] + [(gain[:, None], VMEM)],
        [((rows, model), F32, VMEM)] * 3 + [((rows, 1), F32, VMEM), ((rows, few), F32, VMEM)],
    )


def local(
    reps,
    shards,
    activations,
    cotangent,
    doc_lengths,
    gain_attn,
    query_weight,
    query_bias,
    key_weight,
    value_weight,
    value_bias,
    dim_scale,
    out_weight,
    gain_mlp,
    up_weight,
    down_weight,
):
    seqs, tok_count, model = activations.shape
    at = Place(reps, shards, seqs)
    half = tok_count // CORES
    length = tok_count * shards
    peer_count = at.peer_count
    heads = model // HEAD_DIM // peer_count
    width = heads * HEAD_DIM
    wide = heads * LANES
    own_rows = at.a_size * half
    rows = gain_attn.shape[0]
    groups = 2
    block = CORES * half
    mine = at.b * CORES + at.c

    LAST.clear()
    stage = at.to_cluster(activations)
    next(stage)
    vectors = jnp.stack([gain_attn, gain_mlp, query_bias, value_bias], axis=1)
    own, *sent = heads_parts(at, (query_weight, key_weight, value_weight), vectors, groups)
    sent = [at.send(part, db=db + 1) for db, part in enumerate(sent)]
    next(stage)
    near = by_order(own, sent, at.b_size, at.b)
    sources = [near] + [at.send(near, da=d) for d in range(1, at.a_size)]
    if at.x_split == 2:
        sources += [at.send(source, dx=1) for source in sources]
    chunks = next(stage)
    parts = []
    early = sources[1 : at.a_size]
    if at.x_split == 2:
        early = [sources[2], sources[at.a_size + 1], sources[at.a_size + 3]]
    for db in range(at.b_size):
        near = at.send(chunks, db=db) if db else chunks
        ready = later(near, *early) if db else near
        parts += [near, at.send(ready, dc=1)]
    stage = at.to_cluster(cotangent, sources[at.a_size : at.a_size + 1])
    next(stage)
    quarter = quarter_of(at, (out_weight, up_weight, down_weight), sources[1 : at.a_size])
    pieces = [quarter] + [at.send(quarter, da=d) for d in range(1, at.a_size)]
    *w_heads, w_pad, vectors = pad_weights(at, sources, heads, groups, parts[1:])
    vectors = vectors.T.astype(F32)
    g_attn, g_mlp, b_query, b_value = vectors[0], vectors[1], vectors[2], vectors[3]

    other_lengths = at.send(doc_lengths, dc=1)
    lengths = pick(jnp.where(at.c == at.a // seqs, doc_lengths, other_lengths), at.a % seqs)
    ends = jnp.cumsum(lengths)
    places = jnp.arange(length, dtype=jnp.int32)
    starts = jnp.max(jnp.where(ends[None, :] <= places[:, None], ends[None, :], 0), axis=1)
    starts_row = jnp.broadcast_to(starts[None, :], (8, length))
    starts_col = jnp.broadcast_to(starts[:, None], (length, LANES))
    info = jnp.concatenate([starts[::block] // block, jnp.stack([at.b, at.c])]).astype(jnp.int32)

    scale_dim = LOG_BASE / math.sqrt(HEAD_DIM) * jax.nn.softplus(dim_scale)
    scale_pad = jnp.tile(jnp.pad(scale_dim, (0, LANES - HEAD_DIM)), heads)
    lane = jnp.arange(LANES)
    ones_key = ((lane >= HEAD_DIM) & (lane < HEAD_DIM + 3)).astype(F32)
    ones_value = ((lane >= HEAD_DIM) & (lane < HEAD_DIM + 2)).astype(F32)

    def pad_heads(vec):
        part = lax.dynamic_slice_in_dim(vec, mine * width, width, 0).reshape(heads, HEAD_DIM)
        return jnp.pad(part, ((0, 0), (0, LANES - HEAD_DIM))).reshape(wide)

    bias_pad = jnp.concatenate(
        [
            pad_heads(b_query),
            jnp.tile(ones_key, heads),
            pad_heads(b_value) + jnp.tile(ones_value, heads),
        ]
    )
    times = jnp.concatenate([scale_pad, jnp.ones((2 * wide,), F32)])
    qkv, normed = project(at, parts, g_attn[None], w_pad, bias_pad[None], times[None])

    part_heads = heads // groups
    part_width = part_heads * HEAD_DIM
    moves = [(d, None, 0, (at.a - d) % at.a_size) for d in range(at.a_size)]
    quarter = shuffle(pieces, [((at.a_size, *quarter.shape), BF16)], moves)[0]
    others = {(0, 0, 0): quarter, (0, 0, 1): at.send(quarter, dc=1)}
    for db in range(1, at.b_size):
        others[(0, db, 0)] = at.send(quarter, db=db)
    if at.x_split == 2:
        others[(1, 0, 0)] = at.send(quarter, dx=1)
    stage.send([others[(0, 0, 1)]])
    mixed_rel, query_aug = attend_forward(at, info, starts_col, qkv, heads, block)
    d_out = next(stage).reshape(own_rows, model)
    if at.x_split == 2:
        for db in range(1, at.b_size):
            others[(1, db, 0)] = at.send(later(others[(0, db, 0)], d_out), dx=1)
    parts = []
    for db, dc in at.peers():
        part = later(mixed_rel[db, dc], d_out).reshape(own_rows, width)
        parts.append(at.send(part, db=db, dc=dc) if db or dc else part)
    mixed = concat(parts, [])
    for dx, db, dc in list(others):
        if (dx, db, 1) not in others:
            others[(dx, db, 1)] = at.send(later(others[(dx, db, 0)], mixed), dc=1)
    tokens = chunks.reshape(own_rows, model)
    output, d_residual, d_proj, normed_mlp, activated, d_up, *d_parts = middle(
        at, mixed, tokens, d_out, g_mlp[None], others
    )

    grads = []
    for (db, dc), part in zip(at.peers(), d_parts):
        part = at.send(part, db=db, dc=dc) if db or dc else part
        grads.append(part.reshape(at.a_size, half, width))

    pairs = [(mixed, d_proj), (normed_mlp, d_up), (activated, d_out)]
    give = outer(at, pairs, 1 - at.c)[0]
    full = FullReduce(at, outer(at, pairs, at.c, at.send(give, dc=1), grads))

    scale_rows = jnp.broadcast_to(scale_pad[None, : part_heads * LANES], (8, part_heads * LANES))
    zeros = jnp.zeros((model,), F32)

    def backward(g):
        d_heads, scale_sum, bias_sum = attend_backward(
            at,
            info,
            starts_row,
            scale_rows,
            query_aug,
            qkv,
            grads,
            mixed_rel,
            part_heads,
            groups,
            g,
            block,
        )
        bias_sum = bias_sum[0].reshape(3, part_heads, LANES)[:, :, :HEAD_DIM]
        bias_sum = bias_sum.reshape(3, part_width)
        spot = (mine * groups + g) * part_width
        scale_sum = jnp.pad(scale_sum[0, :HEAD_DIM], (0, rows - HEAD_DIM))
        extra = [
            lax.dynamic_update_slice(zeros, bias_sum[0], (spot,)),
            lax.dynamic_update_slice(zeros, bias_sum[2], (spot,)),
            jnp.tile(scale_sum, shards),
        ]
        return d_heads, jnp.stack(extra, axis=1).astype(BF16)

    stage = at.from_cluster(output.reshape(at.a_size, half, model))
    next(stage)
    d_first, extra_first = backward(0)
    next(stage)
    full.next()
    reduce_first = HeadsReduce(at, heads_outer(at, normed, d_first, extra_first))
    full.over_a()
    d_second, extra_second = backward(1)
    full_parts = full.end()
    reduce_first.over_a()

    d_heads = [d_first, d_second]
    keeps, received = [], []
    residual_chunks = d_residual.reshape(at.a_size, half, model)

    def give(which):
        return at.send(back_project(at, d_heads, w_heads, half, which)[0], dc=1)

    def keep(which, got):
        terms = back_project(at, d_heads, w_heads, half, which, got)
        keeps.append([terms[0]] + [at.send(terms[db], db=db) for db in range(1, at.b_size)])

    def back(which):
        sent = norm_back(
            at, keeps[which], chunks, residual_chunks, g_attn[None], which, received[:]
        )
        for k, part in enumerate(sent):
            received.append(at.send_back(part, which * len(sent) + k))

    got = give(0)
    reduce_second = HeadsReduce(at, heads_outer(at, normed, d_second, extra_second))
    first = reduce_first.by_b(full_parts[1:2])
    keep(0, got)
    keep(1, give(1))
    *grads_full, grad_gain_mlp = finish_full(at, full_parts, up_weight, gain_mlp, [])
    output = next(stage)
    reduce_second.over_a()
    back(0)
    second = reduce_second.by_b(keeps[1][1:])
    back(1)
    parts = to_peers(at, [first, second])
    weights = (query_weight, key_weight, value_weight)
    *grads_heads, grad_gain_attn, few = finish_heads(at, parts, weights, gain_attn, 3)
    input_grad = at.place_back(received)
    grad_scale = few[:HEAD_DIM, 2] / scale_dim * (LOG_BASE / math.sqrt(HEAD_DIM))
    grad_scale = grad_scale * jax.nn.sigmoid(dim_scale)
    return (
        output,
        input_grad,
        grad_gain_attn[:, 0],
        grads_heads[0],
        few[:, 0],
        grads_heads[1],
        grads_heads[2],
        few[:, 1],
        grad_scale,
        grads_full[0],
        grad_gain_mlp[:, 0],
        grads_full[1],
        grads_full[2],
    )


def solution(mesh):
    in_specs = (
        P("rep", "shard", None),
        P("rep", "shard", None),
        P("rep", None),
        P("shard"),
        P("shard", None),
        P("shard"),
        P("shard", None),
        P("shard", None),
        P("shard"),
        P(),
        P("shard", None),
        P("shard"),
        P("shard", None),
        P("shard", None),
    )
    out_specs = (
        P("rep", "shard", None),
        P("rep", "shard", None),
        P("shard"),
        P("shard", None),
        P("shard"),
        P("shard", None),
        P("shard", None),
        P("shard"),
        P(),
        P("shard", None),
        P("shard"),
        P("shard", None),
        P("shard", None),
    )
    body = functools.partial(local, mesh.shape["rep"], mesh.shape["shard"])
    return jax.shard_map(body, mesh=mesh, in_specs=in_specs, out_specs=out_specs, check_vma=False)
```

```python
import functools
import math

import jax
import jax.numpy as jnp
from jax import lax
from jax.experimental import pallas as pl
from jax.experimental.pallas import tpu as pltpu
from jax.sharding import PartitionSpec as P

HEAD_DIM = 80
LANES = 128
CORES = 2
NORM_EPS = 1e-06
LOG_BASE = 1.442695041
MASK_FILL = -1e30
AXES = ("rep", "shard")
F32 = jnp.float32
BF16 = jnp.bfloat16


def dot(left, right, left_dim=1, right_dim=0):
    return lax.dot_general(
        left, right, (((left_dim,), (right_dim,)), ((), ())), preferred_element_type=F32
    )


class Place:
    def __init__(self, reps, shards, seqs):
        self.x_size = reps // CORES
        self.x_split = 2 if self.x_size == 2 else 1
        self.a_size = CORES * seqs
        self.b_size = shards // self.a_size
        self.even = self.x_size == 2 and self.b_size == 2
        self.peer_count = self.b_size * CORES
        self.seqs = seqs
        rep, shard = lax.axis_index("rep"), lax.axis_index("shard")
        self.x, self.c = rep // CORES, rep % CORES
        self.a, self.b = shard // self.b_size, shard % self.b_size
        self.shard = shard

    def route(self, move):
        pairs = []
        for x in range(self.x_size):
            for c in range(CORES):
                for a in range(self.a_size):
                    for b in range(self.b_size):
                        pairs.append((self.number(x, c, a, b), self.number(*move(x, c, a, b))))
        return pairs

    def number(self, x, c, a, b):
        return ((x * CORES + c) * self.a_size + a) * self.b_size + b

    def send(self, value, dx=0, dc=0, da=0, db=0):
        return lax.ppermute(
            value,
            AXES,
            self.route(
                lambda x, c, a, b: (
                    (x + dx) % self.x_size,
                    (c + dc) % CORES,
                    (a + da) % self.a_size,
                    (b + db) % self.b_size,
                )
            ),
        )

    def peers(self):
        return [(db, dc) for db in range(self.b_size) for dc in range(CORES)]

    def source(self, db, dc):
        return ((self.b - db) % self.b_size) * CORES + (self.c + dc) % CORES

    def to_cluster(self, tokens, after=()):
        seqs, count, width = tokens.shape
        half = count // CORES
        halves = tokens.reshape(seqs, CORES, half, width)
        shape = (seqs, half, width)
        moves = []
        for i in range(seqs):
            moves += [(0, (i, self.c), 0, i), (0, (i, 1 - self.c), 1, i)]
        own, give = shuffle([halves], [(shape, BF16)] * 2, moves, after)
        got = self.send(give, dc=1)
        after = yield got
        parts = route_parts(self, own, got, after or ())
        received = [parts[0]] + [self.send(parts[d], da=d) for d in range(1, self.a_size)]
        moves = [(d, None, 0, (self.a - d) % self.a_size) for d in range(self.a_size)]
        after = yield
        yield shuffle(received, [((self.a_size, half, width), BF16)], moves, after or ())[0]

    def from_cluster(self, chunks):
        half, width = chunks.shape[1:]
        picks = [(0, (self.a + d) % self.a_size, d, None) for d in range(self.a_size)]
        parts = shuffle([chunks], [((half, width), BF16)] * self.a_size, picks)
        received = [parts[0]] + [self.send(parts[d], da=d) for d in range(1, self.a_size)]
        yield
        own, give = route_back(self, received)
        got = self.send(give, dc=1)
        moves = []
        for i in range(self.seqs):
            moves += [(0, i, 0, i * CORES + self.c), (1, i, 0, i * CORES + 1 - self.c)]
        yield
        whole = shuffle([own, got], [((self.a_size, half, width), BF16)], moves)[0]
        yield whole.reshape(self.seqs, CORES * half, width)

    def send_back(self, part, m):
        return lax.ppermute(part, AXES, [(j, i) for i, j in self.route(self._match(m))])

    def place_back(self, received):
        half, width = received[0].shape
        moves = []
        for m in range(self.a_size):
            t = m ^ self.a
            moves.append((m, None, 0, (t % self.seqs) * CORES + t // self.seqs))
        whole = shuffle(received, [((self.a_size, half, width), BF16)], moves)[0]
        return whole.reshape(self.seqs, CORES * half, width)

    def _match(self, m):
        def move(x, c, a, b):
            t = m ^ a
            return x, t // self.seqs, self.seqs * c + t % self.seqs, b

        return move


VMEM = pl.BlockSpec(memory_space=pltpu.VMEM)
ANY = pl.BlockSpec(memory_space=pl.ANY)


LAST = []
SCALE = 0.25
SIZE = {
    "project": 28,
    "attend_forward": 24,
    "middle": 48,
    "outer": 60,
    "outer_give": 60,
    "attend_backward": 24,
    "heads_outer": 24,
    "back_project": 20,
    "finish_heads": 16,
    "finish_full": 16,
}
COST = {
    "project": 14.5,
    "attend_forward": 12.0,
    "middle": 20.0,
    "outer": 7.0,
    "outer_give": 0.1,
    "attend_backward": 25.0,
    "heads_outer": 5.5,
    "back_project": 3.5,
    "pad_weights": 3.5,
    "norm_back": 3.0,
    "finish_heads": 4.0,
    "finish_full": 3.5,
}


def call(name, body, scalars, inputs, outputs, grid=(1,), scratch=(), after=(), vmem=0):
    deps = [*LAST[-1:], *after]
    count, skip = len(inputs), len(deps)

    def run(spots, *refs):
        body(spots, *refs[:count], *refs[count + skip :])

    results = pl.pallas_call(
        run,
        out_shape=[jax.ShapeDtypeStruct(shape, kind) for shape, kind, _ in outputs],
        grid_spec=pltpu.PrefetchScalarGridSpec(
            num_scalar_prefetch=1,
            grid=grid,
            in_specs=[spec for _, spec in inputs] + [ANY] * skip,
            out_specs=[spec for _, _, spec in outputs],
            scratch_shapes=list(scratch),
        ),
        cost_estimate=pl.CostEstimate(
            flops=int(COST.get(name, 1.5) * SCALE * 1.1e9),
            bytes_accessed=int(COST.get(name, 1.5) * SCALE * 3.3e6),
            transcendentals=0,
        ),
        compiler_params=pltpu.CompilerParams(vmem_limit_bytes=(vmem or SIZE.get(name, 12)) * 1024 * 1024),
        name=name,
    )(scalars_of(scalars), *[value for value, _ in inputs], *deps)
    LAST.append(results[0])
    return results


def scalars_of(values):
    if isinstance(values, (list, tuple)):
        return jnp.stack([jnp.asarray(v, jnp.int32) for v in values])
    return values


def shuffle_body(moves, counts, spots, *refs):
    sources, targets, sems = refs[: counts[0]], refs[counts[0] : -1], refs[-1]
    copies, n = [], 0
    for src, src_rank, dst, dst_rank in moves:
        ends = []
        for ref, rank in ((sources[src], src_rank), (targets[dst], dst_rank)):
            ends.append(ref.at[tuple(spots[n + k] for k in range(rank))] if rank else ref)
            n += rank
        copies.append(pltpu.make_async_copy(*ends, sems.at[len(copies)]))
    for copy in copies:
        copy.start()
    for copy in copies:
        copy.wait()


def shuffle(sources, shapes, moves, after=()):
    spots, shape_of = [], []
    for src, src_spot, dst, dst_spot in moves:
        ranks = []
        for spot in (src_spot, dst_spot):
            spot = () if spot is None else spot if isinstance(spot, tuple) else (spot,)
            ranks.append(len(spot))
            spots += spot
        shape_of.append((src, ranks[0], dst, ranks[1]))
    return call(
        "shuffle",
        functools.partial(shuffle_body, shape_of, (len(sources), len(shapes))),
        spots or [0],
        [(source, VMEM) for source in sources],
        [(*shape, ANY) for shape in shapes],
        scratch=[pltpu.SemaphoreType.DMA((len(moves),))],
        after=after,
    )


def route_parts_body(seqs, info, own, got, *outs):
    for d, out in enumerate(outs):
        target = info[1 + d]

        @pl.when(target // seqs == info[0])
        def near():
            out[...] = own[target % seqs]

        @pl.when(target // seqs != info[0])
        def far():
            out[...] = got[target % seqs]


def route_parts(at, own, got, after=()):
    return call(
        "route_parts",
        functools.partial(route_parts_body, at.seqs),
        [at.c, *ahead(at.a, at.a_size)],
        [(own, VMEM), (got, VMEM)],
        [(own.shape[1:], BF16, VMEM)] * at.a_size,
        after=after,
    )


def route_back_body(seqs, info, *refs):
    parts, own, give = refs[:-2], refs[-2], refs[-1]
    for d, part in enumerate(parts):
        source = info[1 + d]

        @pl.when(source // seqs == info[0])
        def near():
            own[source % seqs] = part[...]

        @pl.when(source // seqs != info[0])
        def far():
            give[source % seqs] = part[...]


def route_back(at, parts):
    shape = (at.seqs, *parts[0].shape)
    return call(
        "route_back",
        functools.partial(route_back_body, at.seqs),
        [at.c, *[(at.a - d) % at.a_size for d in range(at.a_size)]],
        [(part, VMEM) for part in parts],
        [(shape, BF16, VMEM)] * 2,
    )


def add_body(counts, spots, *refs):
    terms = sum(counts)
    ins, outs, n = refs[:terms], refs[terms:], 0
    for count, out in zip(counts, outs):
        total = ins[n][...].astype(F32)
        for k in range(1, count):
            total = total + ins[n + k][...].astype(F32)
        out[...] = total.reshape(out.shape).astype(out.dtype)
        n += count


def add_blocks(groups, after=()):
    spots, inputs, outputs = [], [], []
    for terms in groups:
        for value, dim, index in terms:
            block = [1 if k == dim else size for k, size in enumerate(value.shape)]

            def spot(i, s, dim=dim, n=len(spots), rank=value.ndim):
                return tuple(s[n] if k == dim else 0 for k in range(rank))

            spots.append(index)
            inputs.append((value, pl.BlockSpec(tuple(block), spot)))
        shape = tuple(size for k, size in enumerate(value.shape) if k != dim)
        outputs.append((shape, BF16, VMEM))
    return call(
        "add_blocks",
        functools.partial(add_body, [len(terms) for terms in groups]),
        spots,
        inputs,
        outputs,
        after=after,
    )


def later(value, *done):
    return lax.optimization_barrier((value, *done))[0]


def pick(stacked, index, axis=0):
    return lax.dynamic_index_in_dim(stacked, index, axis, keepdims=False)


def by_order(own, others, axis_size, spot):
    moves = [(d, None, 0, (spot - d) % axis_size) for d in range(axis_size)]
    return shuffle([own, *others], [((axis_size, *own.shape), own.dtype)], moves)[0]


def heads_part_body(count, groups, info, query, key, value, vectors, *outs):
    width = query.shape[1] // count // groups
    rows = outs[0].shape[0]
    down = pl.ds(pl.multiple_of(info[len(outs)] * rows, rows), rows)
    for n, out in enumerate(outs):
        for peer in range(count):

            @pl.when(info[n] == peer)
            def copy():
                for g in range(groups):
                    for k, source in enumerate((query, key, value)):
                        spot = (g * 3 + k) * width
                        first = (peer * groups + g) * width
                        out[:, spot : spot + width] = source[down, first : first + width]

        out[:, 3 * groups * width :] = vectors[down, :]


def heads_parts(at, weights, vectors, groups):
    rows, model = weights[0].shape
    count = at.peer_count
    shape = (rows // at.x_split, 3 * model // count + vectors.shape[1])
    targets = [((at.b + db) % at.b_size) * CORES + at.c for db in range(at.b_size)]
    return call(
        "heads_parts",
        functools.partial(heads_part_body, count, groups),
        [*targets, at.x if at.x_split == 2 else 0],
        [(w, VMEM) for w in (*weights, vectors)],
        [(shape, BF16, VMEM)] * at.b_size,
    )


def quarter_body(info, *refs):
    out, sem = refs[3], refs[4]
    rows, half = out.shape[1:]
    down = pl.ds(pl.multiple_of(info[0] * rows, rows), rows)
    right = pl.ds(pl.multiple_of(info[1] * half, half), half)
    copies = [pltpu.make_async_copy(refs[w].at[down, right], out.at[w], sem.at[w]) for w in range(3)]
    for copy in copies:
        copy.start()
    for copy in copies:
        copy.wait()


def quarter_of(at, weights, after):
    rows, model = weights[0].shape
    return call(
        "quarter",
        quarter_body,
        [at.x if at.x_split == 2 else 0, at.c],
        [(w, VMEM) for w in weights],
        [((3, rows // at.x_split, model // CORES), BF16, ANY)],
        scratch=[pltpu.SemaphoreType.DMA((3,))],
        after=after,
    )[0]


def pad_body(heads, groups, a_size, info, *refs):
    split = (len(refs) - groups - 2) // a_size
    sources, outs = refs[: split * a_size], refs[split * a_size :]
    compact, (padded, vectors) = outs[:groups], outs[groups:]
    b_size, rows, width = sources[0].shape
    used = 3 * heads * HEAD_DIM
    part = heads // groups
    padded[...] = jnp.zeros_like(padded)
    for n in range(split):
        for d in range(a_size):
            for b in range(b_size):
                piece = sources[n * a_size + d][b]
                spot = (info[1 + d] * b_size + b) * split
                spot = (spot + (info[0] ^ n if split == 2 else 0)) * rows
                spot = pl.ds(pl.multiple_of(spot, rows), rows)
                for g in range(groups):
                    step = used // groups
                    compact[g][spot, :] = piece[:, g * step : (g + 1) * step]
                vectors[spot, :] = piece[:, used:]
                for k in range(3):
                    for h in range(heads):
                        first = (((h // part) * 3 + k) * part + h % part) * HEAD_DIM
                        lane = (k * heads + h) * LANES
                        padded[spot, lane : lane + HEAD_DIM] = piece[:, first : first + HEAD_DIM]


def pad_weights(at, sources, heads, groups, after):
    b_size, rows, width = sources[0].shape
    total = len(sources) * b_size * rows
    used = 3 * heads * HEAD_DIM
    return call(
        "pad_weights",
        functools.partial(pad_body, heads, groups, at.a_size),
        [at.x, *[(at.a - d) % at.a_size for d in range(at.a_size)]],
        [(source, VMEM) for source in sources],
        [
            *[((total, used // groups), BF16, VMEM)] * groups,
            ((total, 3 * heads * LANES), BF16, VMEM),
            ((total, width - used), BF16, VMEM),
        ],
        after=after,
        vmem=16,
    )


def project_body(count, spots, *refs):
    tokens, (gain, weight, bias, times, qkv, normed) = refs[:count], refs[count:]
    rows = tokens[0].shape[1]
    for p in range(count):
        value = tokens[p][0].astype(F32)
        rate = lax.rsqrt(jnp.mean(value * value, axis=-1, keepdims=True) + NORM_EPS)
        spot = pl.multiple_of(spots[p] * rows, rows)
        normed[pl.ds(spot, rows), :] = (value * rate * gain[...]).astype(BF16)
    step = qkv.shape[1] // 3
    for k in range(3):
        lanes = slice(k * step, (k + 1) * step)
        acc = dot(normed[...], weight[:, lanes])
        qkv[:, lanes] = ((acc + bias[:, lanes]) * times[:, lanes]).astype(BF16)


def project(at, parts, gain, weight, bias, times):
    a_size, half, model = parts[0].shape
    count = len(parts)
    cols = weight.shape[1]
    fixed = lambda a, s: (0, 0)
    return call(
        "project",
        functools.partial(project_body, count),
        [at.source(db, dc) for db, dc in at.peers()],
        [(part, pl.BlockSpec((1, half, model), lambda a, s: (a, 0, 0))) for part in parts]
        + [
            (gain, pl.BlockSpec((1, model), fixed)),
            (weight, pl.BlockSpec((model, cols), fixed)),
            (bias, pl.BlockSpec((1, cols), fixed)),
            (times, pl.BlockSpec((1, cols), fixed)),
        ],
        [
            (
                (a_size * count * half, cols),
                BF16,
                pl.BlockSpec((count * half, cols), lambda a, s: (a, 0)),
            ),
            (
                (a_size * count * half, model),
                BF16,
                pl.BlockSpec((count * half, model), lambda a, s: (a, 0)),
            ),
        ],
        grid=(a_size,),
    )


def forward_body(heads, block, info, starts, query, key, value, mixed, query_aug, total, top):
    index = pl.program_id(0)
    half = block // CORES
    core = info[pl.num_programs(0) + 1]
    total[...] = jnp.zeros_like(total)
    top[...] = jnp.full_like(top, MASK_FILL)
    rows = index * block + lax.broadcasted_iota(jnp.int32, (block, block), 0)
    begin = starts[...][:, :1]

    def step(j, carry):
        spot = pl.multiple_of(j * block, block)
        columns = spot + lax.broadcasted_iota(jnp.int32, (block, block), 1)
        bias = jnp.where((columns >= begin) & (columns <= rows), 0.0, MASK_FILL)
        lanes = [slice(h * LANES, (h + 1) * LANES) for h in range(heads)]
        scores = [dot(query[:, l], key[pl.ds(spot, block), l], 1, 1) + bias for l in lanes]
        olds = [top[h] for h in range(heads)]
        news = [
            jnp.maximum(old, jnp.max(score, axis=1, keepdims=True))
            for old, score in zip(olds, scores)
        ]
        weights = [
            jnp.exp(score - jnp.concatenate([new] * (block // LANES), axis=1)).astype(BF16)
            for score, new in zip(scores, news)
        ]
        for h in range(heads):
            total[h] = total[h] * jnp.exp(olds[h] - news[h]) + dot(
                weights[h], value[pl.ds(spot, block), lanes[h]]
            )
            top[h] = news[h]
        return carry

    lax.fori_loop(info[index], index + 1, step, 0)
    lane = lax.broadcasted_iota(jnp.int32, (block, LANES), 1)
    for h in range(heads):
        lanes = slice(h * LANES, (h + 1) * LANES)
        acc = total[h]
        weight_sum = acc[:, HEAD_DIM : HEAD_DIM + 1]
        result = (acc / weight_sum)[:, :HEAD_DIM].astype(BF16)
        for k in range(CORES):
            mixed[0, core ^ k, 0, :, h * HEAD_DIM : (h + 1) * HEAD_DIM] = result[
                k * half : (k + 1) * half
            ]
        rest = -(top[h] + jnp.log(weight_sum))
        aug = query[:, lanes].astype(F32)
        for k in range(3):
            term = rest.astype(BF16).astype(F32)
            aug = jnp.where(lane == HEAD_DIM + k, term, aug)
            rest = rest - term
        query_aug[:, lanes] = aug.astype(BF16)


def attend_forward(at, info, starts, qkv, heads, block):
    length = qkv.shape[0]
    wide = heads * LANES
    width = heads * HEAD_DIM
    count = length // block
    b_size = at.b_size
    return call(
        "attend_forward",
        functools.partial(forward_body, heads, block),
        info,
        [
            (starts, pl.BlockSpec((block, LANES), lambda i, s: (i, 0))),
            (qkv, pl.BlockSpec((block, wide), lambda i, s: (i, 0))),
            (qkv, pl.BlockSpec((length, wide), lambda i, s: (0, 1))),
            (qkv, pl.BlockSpec((length, wide), lambda i, s: (0, 2))),
        ],
        [
            (
                (b_size, CORES, at.a_size, block // CORES, width),
                BF16,
                pl.BlockSpec(
                    (1, CORES, 1, block // CORES, width),
                    lambda i, s: ((i + b_size - s[count]) % b_size, 0, i // b_size, 0, 0),
                ),
            ),
            ((length, wide), BF16, pl.BlockSpec((block, wide), lambda i, s: (i, 0))),
        ],
        grid=(count,),
        scratch=[
            pltpu.VMEM((heads, block, LANES), F32),
            pltpu.VMEM((heads, block, LANES), F32),
        ],
    )


def backward_body(
    heads,
    first,
    block,
    count,
    info,
    starts,
    scale,
    query,
    key,
    value,
    mixed,
    *rest,
):
    grad_refs = rest[:count]
    grads, scale_sum, bias_sum, grad, grad_aug, d_query, d_key, d_value = rest[count:]
    index = pl.num_programs(0) - 1 - pl.program_id(0)
    b_own, core = info[pl.num_programs(0)], info[pl.num_programs(0) + 1]
    b_size = count // CORES
    width = heads * HEAD_DIM

    @pl.when(pl.program_id(0) == 0)
    def clear():
        d_key[...] = jnp.zeros_like(d_key)
        d_value[...] = jnp.zeros_like(d_value)
        scale_sum[...] = jnp.zeros_like(scale_sum)
        bias_sum[...] = jnp.zeros_like(bias_sum)

    half = block // CORES
    lane = lax.broadcasted_iota(jnp.int32, (half, LANES), 1)
    for k in range(CORES):
        peer = ((b_own + b_size - index % b_size) % b_size) * CORES + (core ^ k)
        for p in range(count):

            @pl.when(peer == p)
            def fetch():
                grad[...] = grad_refs[p][index // b_size]

        for h in range(heads):
            part = slice((first + h) * HEAD_DIM, (first + h + 1) * HEAD_DIM)
            grad_h = grad[:, part].astype(F32)
            mixed_h = mixed[0, core ^ k, 0, :, part].astype(F32)
            delta = jnp.sum(grad_h * mixed_h, axis=1, keepdims=True)
            aug = jnp.concatenate([grad_h, jnp.zeros((half, LANES - HEAD_DIM), F32)], axis=1)
            high = (-delta).astype(BF16).astype(F32)
            aug = jnp.where(lane == HEAD_DIM, high, aug)
            aug = jnp.where(lane == HEAD_DIM + 1, -delta - high, aug)
            grad_aug[k * half : (k + 1) * half, h * LANES : (h + 1) * LANES] = aug.astype(BF16)
    d_query[...] = jnp.zeros_like(d_query)
    columns = index * block + lax.broadcasted_iota(jnp.int32, (block, block), 1)
    begin = starts[0:1, :]

    def step(j, carry):
        spot = pl.multiple_of(j * block, block)
        rows = spot + lax.broadcasted_iota(jnp.int32, (block, block), 0)
        allowed = (rows >= begin) & (rows <= columns)
        lanes = [slice(h * LANES, (h + 1) * LANES) for h in range(heads)]
        keys = [key[pl.ds(spot, block), l] for l in lanes]
        queries = [query[:, l] for l in lanes]
        grads_of = [grad_aug[:, l] for l in lanes]
        scores = [dot(k, q, 1, 1) for k, q in zip(keys, queries)]
        d_probs = [
            dot(value[pl.ds(spot, block), l], g, 1, 1) for l, g in zip(lanes, grads_of)
        ]
        probs = [jnp.where(allowed, jnp.exp(score), 0.0) for score in scores]
        d_scores = [(prob * d_prob).astype(BF16) for prob, d_prob in zip(probs, d_probs)]
        for h, l in enumerate(lanes):
            d_value[pl.ds(spot, block), l] += dot(probs[h].astype(BF16), grads_of[h])
            d_key[pl.ds(spot, block), l] += dot(d_scores[h], queries[h])
            d_query[:, l] += dot(d_scores[h], keys[h], 0, 0)
        return carry

    lax.fori_loop(info[index], index + 1, step, 0)
    here = pl.ds(pl.multiple_of(index * block, block), block)
    for h in range(heads):
        lanes = slice(h * LANES, (h + 1) * LANES)
        d_scaled = d_query[:, lanes].astype(BF16).astype(F32)
        scale_sum[...] += jnp.sum(d_scaled * query[:, lanes].astype(F32), axis=0, keepdims=True)
        d_q = (d_scaled * scale[0:1, lanes]).astype(BF16)
        for k, term in enumerate((d_q, d_key[here, lanes], d_value[here, lanes])):
            spot = k * width + h * HEAD_DIM
            term = term.astype(BF16)
            grads[:, spot : spot + HEAD_DIM] = term[:, :HEAD_DIM]
            bias_sum[:, (k * heads + h) * LANES : (k * heads + h + 1) * LANES] += jnp.sum(
                term.astype(F32), axis=0, keepdims=True
            )


def attend_backward(
    at, info, starts, scale, query_aug, qkv, grads, mixed, heads, groups, group, block
):
    length = qkv.shape[0]
    wide = heads * LANES
    width = heads * HEAD_DIM
    count = length // block
    b_size = at.b_size
    half = block // CORES

    def mixed_spot(i, s):
        i = count - 1 - i
        return (i + b_size - s[count]) % b_size, 0, i // b_size, 0, 0

    fixed = lambda i, s: (0, 0)
    return call(
        "attend_backward",
        functools.partial(backward_body, heads, group * heads, block, len(grads)),
        info,
        [
            (starts, pl.BlockSpec((8, block), lambda i, s: (0, count - 1 - i))),
            (scale, pl.BlockSpec((8, wide), fixed)),
            (query_aug, pl.BlockSpec((block, wide), lambda i, s: (count - 1 - i, group))),
            (qkv, pl.BlockSpec((length, wide), lambda i, s: (0, groups + group))),
            (qkv, pl.BlockSpec((length, wide), lambda i, s: (0, 2 * groups + group))),
            (mixed, pl.BlockSpec((1, CORES, 1, half, mixed.shape[4]), mixed_spot)),
        ]
        + [(grad, VMEM) for grad in grads],
        [
            (
                (length, 3 * width),
                BF16,
                pl.BlockSpec((block, 3 * width), lambda i, s: (count - 1 - i, 0)),
            ),
            ((8, LANES), F32, pl.BlockSpec((8, LANES), fixed)),
            ((8, 3 * wide), F32, pl.BlockSpec((8, 3 * wide), fixed)),
        ],
        grid=(count,),
        scratch=[
            pltpu.VMEM((half, mixed.shape[4]), BF16),
            pltpu.VMEM((block, wide), BF16),
            pltpu.VMEM((block, wide), F32),
            pltpu.VMEM((length, wide), F32),
            pltpu.VMEM((length, wide), F32),
        ],
    )


def concat_body(info, *refs):
    parts, out = refs[:-1], refs[-1]
    width = parts[0].shape[1]
    for p, part in enumerate(parts):
        out[:, p * width : (p + 1) * width] = part[...]


def concat(parts, after):
    rows, width = parts[0].shape
    return call(
        "concat",
        concat_body,
        [0],
        [(part, VMEM) for part in parts],
        [((rows, width * len(parts)), BF16, VMEM)],
        after=after,
    )[0]


def middle_body(count, source_count, moves, info, *refs):
    mixed, tokens, d_out, gain = refs[:4]
    sources = refs[4 : 4 + source_count]
    outs = refs[4 + source_count :]
    output, d_residual, d_proj, normed, activated, d_up = outs[:6]
    d_parts = outs[6:-4]
    weights, sems = outs[-4:-1], outs[-1]
    w_out, w_up, w_down = weights
    rows, half = sources[0].shape[2:]
    width = d_parts[0].shape[1]

    def copies(w):
        for n, (src, s, k) in enumerate(moves):
            if k == w:
                down = pl.ds(pl.multiple_of(info[2 * n] * rows, rows), rows)
                right = pl.ds(pl.multiple_of(info[2 * n + 1] * half, half), half)
                yield pltpu.make_async_copy(
                    sources[src].at[s, w], weights[w].at[down, right], sems.at[n]
                )

    def arrived(w):
        @pl.when(pl.program_id(0) == 0)
        def wait():
            for copy in copies(w):
                copy.wait()

    @pl.when(pl.program_id(0) == 0)
    def start():
        for w in range(3):
            for copy in copies(w):
                copy.start()

    arrived(0)
    residual = tokens[...].astype(F32) + dot(mixed[...], w_out[...])
    rate = lax.rsqrt(jnp.mean(residual * residual, axis=-1, keepdims=True) + NORM_EPS)
    normed[...] = (residual * rate * gain[...]).astype(BF16)
    arrived(1)
    upward = dot(normed[...], w_up[...])
    gate = 1.0 / (1.0 + jnp.exp(-upward))
    activated[...] = (upward * gate).astype(BF16)
    arrived(2)
    output[...] = (residual + dot(activated[...], w_down[...])).astype(BF16)
    d_activated = dot(d_out[...], w_down[...], 1, 1)
    d_up[...] = (d_activated * gate * (1 + upward * (1 - gate))).astype(BF16)
    scaled = dot(d_up[...], w_up[...], 1, 1) * gain[...]
    inner = jnp.mean(residual * scaled, axis=-1, keepdims=True)
    d_norm = rate * scaled - residual * (rate * rate * rate * inner)
    d_total = d_out[...].astype(F32) + d_norm
    d_residual[...] = d_total
    d_proj[...] = d_total.astype(BF16)
    d_mixed = dot(d_proj[...], w_out[...], 1, 1).astype(BF16)
    for p in range(count):
        d_parts[p][...] = d_mixed[:, p * width : (p + 1) * width]


def middle(at, mixed, tokens, d_out, gain, sources):
    count = at.peer_count
    rows, model = tokens.shape
    width = model // count
    arrays = list(sources.values())
    a_size, _, piece, half = arrays[0].shape
    group = model // at.peer_count // piece
    moves, spots = [], []
    for n, (dx, db, dc) in enumerate(sources):
        for a in range(a_size):
            for w in range(3):
                row = a * at.b_size + (at.b - db) % at.b_size
                if at.x_split == 2:
                    row = row * 2 + (at.x + dx) % 2
                if w == 0:
                    peer, rest = row // group, row % group
                    far = (at.b - peer // CORES) % at.b_size
                    row = (far * CORES + ((peer % CORES) ^ at.c)) * group + rest
                moves.append((n, a, w))
                spots += [row, (at.c + dc) % CORES]
    block = min(256, rows)
    row = lambda i, s: (i, 0)
    rows_of = pl.BlockSpec((block, model), row)
    part = pl.BlockSpec((block, width), row)
    types = [BF16, F32, BF16, BF16, BF16, BF16]
    return call(
        "middle",
        functools.partial(middle_body, count, len(arrays), moves),
        spots,
        [(mixed, rows_of), (tokens, rows_of), (d_out, rows_of)]
        + [(gain, pl.BlockSpec(gain.shape, lambda i, s: (0, 0)))]
        + [(source, ANY) for source in arrays],
        [((rows, model), kind, rows_of) for kind in types]
        + [((rows, width), BF16, part)] * count,
        grid=(rows // block,),
        scratch=[pltpu.VMEM((model, model), BF16)] * 3
        + [pltpu.SemaphoreType.DMA((len(moves),))],
    )


def outer_body(count, split, add, info, *refs):
    pairs, rest = refs[:6], refs[6:]
    for w in range(3):

        @pl.when(pl.program_id(0) == w)
        def product():
            value = dot(pairs[2 * w][...], pairs[2 * w + 1][...], 0, 0)
            target = rest[-1] if split else rest[-1].at[0]
            width = value.shape[0] // count
            for p in range(count):
                spot = p * width
                if w == 0:
                    spot = pl.multiple_of(info[3 + p] * width, width)
                part = value[p * width : (p + 1) * width]
                if add:
                    part = part + rest[0][0, pl.ds(spot, width)].astype(F32)
                target[pl.ds(spot, width)] = part.astype(BF16)

    if split:
        keep_x, give_x, keep_b, give_b, total = rest[1:]
        pairs_a, b_size, rows = keep_x.shape[1:4]
        for k in range(pairs_a):
            for b in range(b_size):
                for half, out in ((info[1], keep_x), (1 - info[1], give_x)):
                    spot = pl.multiple_of((k * b_size + b) * 2 * rows + half * rows, rows)
                    out[0, k, b] = total[pl.ds(spot, rows)]
            for b, out in ((info[2], keep_b), (1 - info[2], give_b)):
                for half in range(2):
                    spot = (((k + pairs_a) * b_size) * 2 + half) * rows + b * 2 * rows
                    out[0, k, half] = total[pl.ds(pl.multiple_of(spot, rows), rows)]


def outer(at, pairs, cols, add=None, after=()):
    rows, model = pairs[0][0].shape
    half = model // CORES
    count = at.peer_count
    split = add is not None and at.even
    info = [cols, at.x if at.even else 0, at.b, *[at.source(db, dc) for db, dc in at.peers()]]
    inputs = []
    for left, right in pairs:
        inputs.append((left, pl.BlockSpec((rows, model), lambda w, s: (0, 0))))
        inputs.append((right, pl.BlockSpec((rows, half), lambda w, s: (0, s[0]))))
    block = pl.BlockSpec((1, model, half), lambda w, s: (w, 0, 0))
    outputs = [((3, model, half), BF16, block)]
    scratch = []
    if add is not None:
        inputs.append((add, block))
    if split:
        shape = (at.a_size // 2, 2, model // at.a_size // 4, half)
        part = pl.BlockSpec((1, *shape), lambda w, s: (w, 0, 0, 0, 0))
        outputs = [((3, *shape), BF16, part)] * 4
        scratch = [pltpu.VMEM((model, half), BF16)]
    return call(
        "outer_give" if add is None else "outer",
        functools.partial(outer_body, count, split, add is not None),
        info,
        inputs,
        outputs,
        grid=(3,),
        scratch=scratch,
        after=after,
    )


def give_body(groups, info, *refs):
    grads, weights, out = refs[:groups], refs[groups : 2 * groups], refs[-1]
    value = back_product(grads, weights)
    out[...] = value.astype(BF16).reshape(out.shape)


def back_product(grads, weights):
    total = 0.0
    for grad, weight in zip(grads, weights):
        total = total + dot(grad[...].reshape(-1, grad.shape[-1]), weight[...], 1, 1)
    return total


def keep_body(groups, info, *refs):
    grads, weights, got = refs[:groups], refs[groups : 2 * groups], refs[2 * groups]
    outs = refs[2 * groups + 1 :]
    pairs, b_size, half = got.shape[:3]
    value = back_product(grads, weights).reshape(got.shape) + got[...].astype(F32)
    for b in range(b_size):
        for n, out in enumerate(outs):

            @pl.when(info[2 + n] == b)
            def copy():
                out[...] = value[:, b].astype(out.dtype)


def back_project(at, grads, weights, half, which, got=None):
    model = weights[0].shape[0]
    pair = at.a_size // 2
    groups = len(grads)
    width = grads[0].shape[1]
    shape = (pair, at.b_size, half, model)
    grads = [g.reshape(at.a_size, at.b_size, CORES, half, width) for g in grads]
    block = pl.BlockSpec((pair, at.b_size, 1, half, width), lambda i, s: (s[0], 0, s[1], 0, 0))
    core = at.c if got is not None else 1 - at.c
    inputs = [(g, block) for g in grads]
    inputs += [(weight, VMEM) for weight in weights]
    if got is None:
        body, outputs = give_body, [(shape, BF16, VMEM)]
    else:
        body = keep_body
        inputs.append((got, VMEM))
        outputs = [((pair, half, model), F32 if db == 0 else BF16, VMEM) for db in range(at.b_size)]
    return call(
        "back_project",
        functools.partial(body, groups),
        [which ^ core, core, *ahead(at.b, at.b_size)],
        inputs,
        outputs,
    )


def norm_back_body(count, info, *refs):
    own, others = refs[0], refs[1:count]
    tokens, d_residual, gain = refs[count : count + 3]
    for n, out in enumerate(refs[count + 3 :]):
        k = info[1 + n]
        grad = own[k]
        for other in others:
            grad = grad + other[k].astype(F32)
        value = tokens[k].astype(F32)
        rate = lax.rsqrt(jnp.mean(value * value, axis=-1, keepdims=True) + NORM_EPS)
        scaled = grad * gain[...]
        inner = jnp.mean(value * scaled, axis=-1, keepdims=True)
        d_norm = rate * scaled - value * (rate * rate * rate * inner)
        out[...] = (d_residual[k] + d_norm).astype(BF16)


def norm_back(at, terms, chunks, d_residual, gain, which):
    pair, half, model = terms[0].shape
    block = pl.BlockSpec((pair, half, model), lambda i, s: (s[0], 0, 0))
    order = [k ^ (at.a % pair) for k in range(pair)]
    return call(
        "norm_back",
        functools.partial(norm_back_body, len(terms)),
        [which ^ at.c, *order],
        [(t, VMEM) for t in terms] + [(chunks, block), (d_residual, block), (gain, VMEM)],
        [((half, model), BF16, VMEM)] * pair,
    )


def heads_outer_body(steps, info, normed, grads, extra, *rest):
    outs, acc = rest[:-1], rest[-1]
    value = dot(normed[...], grads[...], 0, 0)

    @pl.when(pl.program_id(0) == 0)
    def first():
        acc[...] = value

    @pl.when(pl.program_id(0) != 0)
    def later():
        acc[...] += value

    @pl.when(pl.program_id(0) == steps - 1)
    def last():
        used = acc.shape[1]
        pairs, b_size, rows = outs[0].shape[:3]
        split = len(outs)
        for n, out in enumerate(outs):
            for s in range(pairs * b_size):
                spot = (s * split + (info[0] ^ n if split == 2 else 0)) * rows
                spot = pl.ds(pl.multiple_of(spot, rows), rows)
                out[s // b_size, s % b_size, :, :used] = acc[spot, :].astype(BF16)
                out[s // b_size, s % b_size, :, used:] = extra[spot, :]


def heads_outer(at, normed, grads, extra):
    length, model = normed.shape
    used = grads.shape[1]
    block = min(512, length)
    steps = length // block
    rows = model // at.a_size // at.b_size // at.x_split
    shape = (at.a_size, at.b_size, rows, used + extra.shape[1])
    return call(
        "heads_outer",
        functools.partial(heads_outer_body, steps),
        [at.x],
        [
            (normed, pl.BlockSpec((block, model), lambda i, s: (i, 0))),
            (grads, pl.BlockSpec((block, used), lambda i, s: (i, 0))),
            (extra, pl.BlockSpec(extra.shape, lambda i, s: (0, 0))),
        ],
        [(shape, BF16, pl.BlockSpec(shape, lambda i, s: (0, 0, 0, 0)))] * at.x_split,
        grid=(steps,),
        scratch=[pltpu.VMEM((model, used), F32)],
    )


def all_sum(at, value, axis, size):
    total = value
    for d in range(1, size):
        total = total + at.send(value, **{axis: d}).astype(value.dtype)
    return total


def ahead(spot, size):
    return [(spot + d) % size for d in range(size)]


def cat_body(info, first, first_got, second, second_got, *outs):
    pair = first.shape[1]
    for d, out in enumerate(outs):
        spot = info[d] % pair

        @pl.when(info[d] < pair)
        def low():
            out[...] = (first[:, spot].astype(F32) + first_got[:, spot].astype(F32)).astype(BF16)

        @pl.when(info[d] >= pair)
        def high():
            out[...] = (second[:, spot].astype(F32) + second_got[:, spot].astype(F32)).astype(BF16)


class FullReduce:
    def __init__(self, at, parts):
        self.at = at
        if at.even:
            keep_x, give_x, keep_b, give_b = parts
            self.first = keep_x, at.send(give_x, dx=1)
            self.second = keep_b, at.send(give_b, db=1)
        else:
            self.part = parts[0].reshape(3, at.a_size, at.b_size, -1, parts[0].shape[-1])

    def next(self):
        at = self.at
        if not at.even:
            return
        groups = [[(t, 2, b) for t in self.first] for b in ahead(at.b, 2)]
        groups += [[(t, 2, x) for t in self.second] for x in ahead(at.x, 2)]
        keep_b, give_b, keep_x, give_x = add_blocks(groups)
        self.first = keep_b, at.send(give_b, db=1)
        self.second = keep_x, at.send(give_x, dx=1)

    def over_a(self):
        at = self.at
        if at.even:
            shape = self.first[0].shape
            parts = call(
                "cat",
                cat_body,
                ahead(at.a, at.a_size),
                [(t, VMEM) for t in (*self.first, *self.second)],
                [((3, *shape[2:]), BF16, VMEM)] * at.a_size,
            )
        else:
            parts = add_blocks([[(self.part, 1, a)] for a in ahead(at.a, at.a_size)])
        self.got = [parts[0]] + [at.send(parts[d], da=d) for d in range(1, at.a_size)]

    def end(self):
        at = self.at
        if at.even:
            part = add_blocks([[(t[None], 0, 0) for t in self.got]])[0]
            far = at.send(part, dx=1)
            return [part, far, at.send(part, dc=1), at.send(far, dc=1)]
        parts = add_blocks([[(t, 1, b) for t in self.got] for b in ahead(at.b, at.b_size)])
        got = [parts[0]] + [at.send(parts[d], db=d) for d in range(1, at.b_size)]
        part = add_blocks([[(t[None], 0, 0) for t in got]])[0]
        part = all_sum(at, part, "dx", at.x_size)
        return [part, at.send(part, dc=1)]


class HeadsReduce:
    def __init__(self, at, parts):
        self.at = at
        self.got = [parts[0]]
        if at.x_split == 2:
            self.got.append(at.send(parts[1], dx=1))

    def over_a(self):
        at = self.at
        parts = add_blocks([[(t, 0, a) for t in self.got] for a in ahead(at.a, at.a_size)])
        self.got = [parts[0]] + [at.send(parts[d], da=d) for d in range(1, at.a_size)]
        return parts

    def by_b(self, after=()):
        at = self.at
        if at.x_split == 1:
            total = add_blocks([[(t[None], 0, 0) for t in self.got]])[0]
            self.got = [all_sum(at, total, "dx", at.x_size)]
        groups = [[(t, 0, b) for t in self.got] for b in ahead(at.b, at.b_size)]
        return add_blocks(groups, after)


def side_body(groups, info, *refs):
    for n, out in enumerate(refs[-(len(refs) // (groups + 1)) :]):
        for g in range(groups):
            out[g] = refs[n * groups + g][...]


def to_peers(at, groups):
    shape = (len(groups), *groups[0][0].shape)
    parts = call(
        "side",
        functools.partial(side_body, len(groups)),
        [0],
        [(group[b], VMEM) for b in range(at.b_size) for group in groups],
        [(shape, BF16, VMEM)] * at.b_size,
    )
    parts = [at.send(parts[db], db=db, dc=dc) if db or dc else parts[0] for db, dc in at.peers()]
    if at.x_split == 1:
        return [parts]
    return [parts, at.send(jnp.stack(parts), dx=1)]


def in_order(info, refs, split, half, core, spot):
    near = [r[spot] for r in refs]
    if split == 2:
        near = [jnp.where(info[0] == half, near[2 * k], near[2 * k + 1]) for k in range(2)]
    return jnp.where(info[1] == core, near[0], near[1])


def finish_full_body(split, info, *refs):
    count = CORES * split
    parts, (weight, gain), outs = refs[:count], refs[count : count + 2], refs[count + 2 :]
    rows, half = parts[0].shape[1:]
    for x in range(split):
        spot = slice(x * rows, (x + 1) * rows)
        for w in range(3):
            for c in range(CORES):
                outs[w][spot, c * half : (c + 1) * half] = in_order(
                    info, parts, split, x, c, w
                ).astype(F32)
    total = jnp.sum(outs[1][...] * weight[...].astype(F32), axis=1, keepdims=True)
    outs[3][...] = total / gain[...].astype(F32)


def finish_full(at, parts, weight, gain, after):
    rows, model = weight.shape
    return call(
        "finish_full",
        functools.partial(finish_full_body, 2 if at.even else 1),
        [at.x, at.c],
        [(p, VMEM) for p in parts] + [(weight, VMEM), (gain[:, None], VMEM)],
        [((rows, model), F32, VMEM)] * 3 + [((rows, 1), F32, VMEM)],
        after=after,
    )


def finish_heads_body(count, split, info, *refs):
    parts, refs = refs[:count], refs[count:]
    far, refs = refs[: split - 1], refs[split - 1 :]
    weights, gain, outs = refs[:3], refs[3], refs[4:]
    few = outs[4].shape[1]
    groups, rows, width = parts[0].shape
    width = (width - few) // 3
    for n in range(split):
        down = pl.ds(pl.multiple_of((info[count] ^ n if split == 2 else 0) * rows, rows), rows)
        total = jnp.zeros((rows, few), F32)
        for p in range(count):
            for g in range(groups):
                source = far[0].at[p, g] if n else parts[p].at[g]
                total = total + source[:, 3 * width :].astype(F32)
                for peer in range(count):

                    @pl.when(info[p] == peer)
                    def copy():
                        for k in range(3):
                            spot = (peer * groups + g) * width
                            piece = source[:, k * width : (k + 1) * width]
                            outs[k][down, spot : spot + width] = piece.astype(F32)

        outs[4][down, :] = total
    total = jnp.zeros(outs[3].shape, F32)
    for k in range(3):
        total = total + jnp.sum(outs[k][...] * weights[k][...].astype(F32), axis=1, keepdims=True)
    outs[3][...] = total / gain[...].astype(F32)


def finish_heads(at, parts, weights, gain, few):
    rows, model = weights[0].shape
    flat = [*parts[0], *parts[1:]]
    return call(
        "finish_heads",
        functools.partial(finish_heads_body, at.peer_count, at.x_split),
        [*[at.source(db, dc) for db, dc in at.peers()], at.x],
        [(p, VMEM) for p in flat] + [(w, VMEM) for w in weights] + [(gain[:, None], VMEM)],
        [((rows, model), F32, VMEM)] * 3 + [((rows, 1), F32, VMEM), ((rows, few), F32, VMEM)],
    )


def local(
    reps,
    shards,
    activations,
    cotangent,
    doc_lengths,
    gain_attn,
    query_weight,
    query_bias,
    key_weight,
    value_weight,
    value_bias,
    dim_scale,
    out_weight,
    gain_mlp,
    up_weight,
    down_weight,
):
    seqs, tok_count, model = activations.shape
    at = Place(reps, shards, seqs)
    half = tok_count // CORES
    length = tok_count * shards
    peer_count = at.peer_count
    heads = model // HEAD_DIM // peer_count
    width = heads * HEAD_DIM
    wide = heads * LANES
    own_rows = at.a_size * half
    rows = gain_attn.shape[0]
    groups = 2
    block = CORES * half
    mine = at.b * CORES + at.c

    LAST.clear()
    stage = at.to_cluster(activations)
    next(stage)
    vectors = jnp.stack([gain_attn, gain_mlp, query_bias, value_bias], axis=1)
    own, *sent = heads_parts(at, (query_weight, key_weight, value_weight), vectors, groups)
    sent = [at.send(part, db=db + 1) for db, part in enumerate(sent)]
    next(stage)
    near = by_order(own, sent, at.b_size, at.b)
    sources = [near] + [at.send(near, da=d) for d in range(1, at.a_size)]
    if at.x_split == 2:
        sources += [at.send(source, dx=1) for source in sources]
    chunks = next(stage)
    parts = []
    early = sources[1 : at.a_size]
    if at.x_split == 2:
        early = [sources[2], sources[at.a_size + 1], sources[at.a_size + 3]]
    for db in range(at.b_size):
        near = at.send(chunks, db=db) if db else chunks
        ready = later(near, *early) if db else near
        parts += [near, at.send(ready, dc=1)]
    stage = at.to_cluster(cotangent)
    soon = [next(stage), at.send(doc_lengths, dc=1)]
    quarter = quarter_of(at, (out_weight, up_weight, down_weight), sources[1 : at.a_size])
    pieces = [quarter] + [at.send(quarter, da=d) for d in range(1, at.a_size)]
    *w_heads, w_pad, vectors = pad_weights(
        at, sources, heads, groups, [*parts[1:], *soon]
    )
    vectors = vectors.T.astype(F32)
    g_attn, g_mlp, b_query, b_value = vectors[0], vectors[1], vectors[2], vectors[3]

    other_lengths = soon[1]
    lengths = pick(jnp.where(at.c == at.a // seqs, doc_lengths, other_lengths), at.a % seqs)
    ends = jnp.cumsum(lengths)
    places = jnp.arange(length, dtype=jnp.int32)
    starts = jnp.max(jnp.where(ends[None, :] <= places[:, None], ends[None, :], 0), axis=1)
    starts_row = jnp.broadcast_to(starts[None, :], (8, length))
    starts_col = jnp.broadcast_to(starts[:, None], (length, LANES))
    info = jnp.concatenate([starts[::block] // block, jnp.stack([at.b, at.c])]).astype(jnp.int32)

    scale_dim = LOG_BASE / math.sqrt(HEAD_DIM) * jax.nn.softplus(dim_scale)
    scale_pad = jnp.tile(jnp.pad(scale_dim, (0, LANES - HEAD_DIM)), heads)
    lane = jnp.arange(LANES)
    ones_key = ((lane >= HEAD_DIM) & (lane < HEAD_DIM + 3)).astype(F32)
    ones_value = ((lane >= HEAD_DIM) & (lane < HEAD_DIM + 2)).astype(F32)

    def pad_heads(vec):
        part = lax.dynamic_slice_in_dim(vec, mine * width, width, 0).reshape(heads, HEAD_DIM)
        return jnp.pad(part, ((0, 0), (0, LANES - HEAD_DIM))).reshape(wide)

    bias_pad = jnp.concatenate(
        [
            pad_heads(b_query),
            jnp.tile(ones_key, heads),
            pad_heads(b_value) + jnp.tile(ones_value, heads),
        ]
    )
    times = jnp.concatenate([scale_pad, jnp.ones((2 * wide,), F32)])
    qkv, normed = project(at, parts, g_attn[None], w_pad, bias_pad[None], times[None])

    part_heads = heads // groups
    part_width = part_heads * HEAD_DIM
    moves = [(d, None, 0, (at.a - d) % at.a_size) for d in range(at.a_size)]
    quarter = shuffle(pieces, [((at.a_size, *quarter.shape), BF16)], moves)[0]
    others = {(0, 0, 0): quarter, (0, 0, 1): at.send(quarter, dc=1)}
    for db in range(1, at.b_size):
        others[(0, db, 0)] = at.send(quarter, db=db)
    if at.x_split == 2:
        others[(1, 0, 0)] = at.send(quarter, dx=1)
    stage.send([others[(0, 0, 1)]])
    mixed_rel, query_aug = attend_forward(at, info, starts_col, qkv, heads, block)
    d_out = next(stage).reshape(own_rows, model)
    if at.x_split == 2:
        for db in range(1, at.b_size):
            others[(1, db, 0)] = at.send(later(others[(0, db, 0)], d_out), dx=1)
    parts = []
    for db, dc in at.peers():
        part = later(mixed_rel[db, dc], d_out).reshape(own_rows, width)
        parts.append(at.send(part, db=db, dc=dc) if db or dc else part)
    mixed = concat(parts, [])
    for dx, db, dc in list(others):
        if (dx, db, 1) not in others:
            others[(dx, db, 1)] = at.send(later(others[(dx, db, 0)], mixed), dc=1)
    tokens = chunks.reshape(own_rows, model)
    output, d_residual, d_proj, normed_mlp, activated, d_up, *d_parts = middle(
        at, mixed, tokens, d_out, g_mlp[None], others
    )

    grads = []
    for (db, dc), part in zip(at.peers(), d_parts):
        part = at.send(part, db=db, dc=dc) if db or dc else part
        grads.append(part.reshape(at.a_size, half, width))

    pairs = [(mixed, d_proj), (normed_mlp, d_up), (activated, d_out)]
    give = outer(at, pairs, 1 - at.c)[0]
    full = FullReduce(at, outer(at, pairs, at.c, at.send(give, dc=1), grads))

    scale_rows = jnp.broadcast_to(scale_pad[None, : part_heads * LANES], (8, part_heads * LANES))
    zeros = jnp.zeros((model,), F32)

    def backward(g):
        d_heads, scale_sum, bias_sum = attend_backward(
            at,
            info,
            starts_row,
            scale_rows,
            query_aug,
            qkv,
            grads,
            mixed_rel,
            part_heads,
            groups,
            g,
            block,
        )
        bias_sum = bias_sum[0].reshape(3, part_heads, LANES)[:, :, :HEAD_DIM]
        bias_sum = bias_sum.reshape(3, part_width)
        spot = (mine * groups + g) * part_width
        scale_sum = jnp.pad(scale_sum[0, :HEAD_DIM], (0, rows - HEAD_DIM))
        extra = [
            lax.dynamic_update_slice(zeros, bias_sum[0], (spot,)),
            lax.dynamic_update_slice(zeros, bias_sum[2], (spot,)),
            jnp.tile(scale_sum, shards),
        ]
        return d_heads, jnp.stack(extra, axis=1).astype(BF16)

    stage = at.from_cluster(output.reshape(at.a_size, half, model))
    next(stage)
    d_first, extra_first = backward(0)
    next(stage)
    full.next()
    reduce_first = HeadsReduce(at, heads_outer(at, normed, d_first, extra_first))
    full.over_a()
    d_second, extra_second = backward(1)
    full_parts = full.end()
    reduce_first.over_a()

    d_heads = [d_first, d_second]
    keeps, received = [], []
    residual_chunks = d_residual.reshape(at.a_size, half, model)

    def give(which):
        return at.send(back_project(at, d_heads, w_heads, half, which)[0], dc=1)

    def keep(which, got):
        terms = back_project(at, d_heads, w_heads, half, which, got)
        keeps.append([terms[0]] + [at.send(terms[db], db=db) for db in range(1, at.b_size)])

    def back(which):
        sent = norm_back(at, keeps[which], chunks, residual_chunks, g_attn[None], which)
        for k, part in enumerate(sent):
            received.append(at.send_back(part, which * len(sent) + k))

    got = give(0)
    reduce_second = HeadsReduce(at, heads_outer(at, normed, d_second, extra_second))
    first = reduce_first.by_b(full_parts[1:2])
    keep(0, got)
    keep(1, give(1))
    reduce_second.over_a()
    back(0)
    parts = to_peers(at, [first, reduce_second.by_b(keeps[1][1:])])
    back(1)
    *grads_full, grad_gain_mlp = finish_full(at, full_parts, up_weight, gain_mlp, [])
    output = next(stage)
    weights = (query_weight, key_weight, value_weight)
    *grads_heads, grad_gain_attn, few = finish_heads(at, parts, weights, gain_attn, 3)
    input_grad = at.place_back(received)
    grad_scale = few[:HEAD_DIM, 2] / scale_dim * (LOG_BASE / math.sqrt(HEAD_DIM))
    grad_scale = grad_scale * jax.nn.sigmoid(dim_scale)
    return (
        output,
        input_grad,
        grad_gain_attn[:, 0],
        grads_heads[0],
        few[:, 0],
        grads_heads[1],
        grads_heads[2],
        few[:, 1],
        grad_scale,
        grads_full[0],
        grad_gain_mlp[:, 0],
        grads_full[1],
        grads_full[2],
    )


def solution(mesh):
    in_specs = (
        P("rep", "shard", None),
        P("rep", "shard", None),
        P("rep", None),
        P("shard"),
        P("shard", None),
        P("shard"),
        P("shard", None),
        P("shard", None),
        P("shard"),
        P(),
        P("shard", None),
        P("shard"),
        P("shard", None),
        P("shard", None),
    )
    out_specs = (
        P("rep", "shard", None),
        P("rep", "shard", None),
        P("shard"),
        P("shard", None),
        P("shard"),
        P("shard", None),
        P("shard", None),
        P("shard"),
        P(),
        P("shard", None),
        P("shard"),
        P("shard", None),
        P("shard", None),
    )
    body = functools.partial(local, mesh.shape["rep"], mesh.shape["shard"])
    return jax.shard_map(body, mesh=mesh, in_specs=in_specs, out_specs=out_specs, check_vma=False)
```

```python
import functools
import math

import jax
import jax.numpy as jnp
from jax import lax
from jax.experimental import pallas as pl
from jax.experimental.pallas import tpu as pltpu
from jax.sharding import PartitionSpec as P

HEAD_DIM = 80
LANES = 128
CORES = 2
NORM_EPS = 1e-06
LOG_BASE = 1.442695041
MASK_FILL = -1e30
AXES = ("rep", "shard")
F32 = jnp.float32
BF16 = jnp.bfloat16


def dot(left, right, left_dim=1, right_dim=0):
    return lax.dot_general(
        left, right, (((left_dim,), (right_dim,)), ((), ())), preferred_element_type=F32
    )


class Place:
    def __init__(self, reps, shards, seqs):
        self.x_size = reps // CORES
        self.x_split = 2 if self.x_size == 2 else 1
        self.a_size = CORES * seqs
        self.b_size = shards // self.a_size
        self.even = self.x_size == 2 and self.b_size == 2
        self.peer_count = self.b_size * CORES
        self.seqs = seqs
        rep, shard = lax.axis_index("rep"), lax.axis_index("shard")
        self.x, self.c = rep // CORES, rep % CORES
        self.a, self.b = shard // self.b_size, shard % self.b_size
        self.shard = shard

    def route(self, move):
        pairs = []
        for x in range(self.x_size):
            for c in range(CORES):
                for a in range(self.a_size):
                    for b in range(self.b_size):
                        pairs.append((self.number(x, c, a, b), self.number(*move(x, c, a, b))))
        return pairs

    def number(self, x, c, a, b):
        return ((x * CORES + c) * self.a_size + a) * self.b_size + b

    def send(self, value, dx=0, dc=0, da=0, db=0):
        return lax.ppermute(
            value,
            AXES,
            self.route(
                lambda x, c, a, b: (
                    (x + dx) % self.x_size,
                    (c + dc) % CORES,
                    (a + da) % self.a_size,
                    (b + db) % self.b_size,
                )
            ),
        )

    def peers(self):
        return [(db, dc) for db in range(self.b_size) for dc in range(CORES)]

    def source(self, db, dc):
        return ((self.b - db) % self.b_size) * CORES + (self.c + dc) % CORES

    def to_cluster(self, tokens, after=()):
        seqs, count, width = tokens.shape
        half = count // CORES
        halves = tokens.reshape(seqs, CORES, half, width)
        shape = (seqs, half, width)
        moves = []
        for i in range(seqs):
            moves += [(0, (i, self.c), 0, i), (0, (i, 1 - self.c), 1, i)]
        own, give = shuffle([halves], [(shape, BF16)] * 2, moves, after)
        got = self.send(give, dc=1)
        after = yield got
        parts = route_parts(self, own, got, after or ())
        received = [parts[0]] + [self.send(parts[d], da=d) for d in range(1, self.a_size)]
        moves = [(d, None, 0, (self.a - d) % self.a_size) for d in range(self.a_size)]
        after = yield
        yield shuffle(received, [((self.a_size, half, width), BF16)], moves, after or ())[0]

    def from_cluster(self, chunks):
        half, width = chunks.shape[1:]
        picks = [(0, (self.a + d) % self.a_size, d, None) for d in range(self.a_size)]
        parts = shuffle([chunks], [((half, width), BF16)] * self.a_size, picks)
        received = [parts[0]] + [self.send(parts[d], da=d) for d in range(1, self.a_size)]
        yield
        own, give = route_back(self, received)
        got = self.send(give, dc=1)
        moves = []
        for i in range(self.seqs):
            moves += [(0, i, 0, i * CORES + self.c), (1, i, 0, i * CORES + 1 - self.c)]
        yield
        whole = shuffle([own, got], [((self.a_size, half, width), BF16)], moves)[0]
        yield whole.reshape(self.seqs, CORES * half, width)

    def send_back(self, part, m):
        return lax.ppermute(part, AXES, [(j, i) for i, j in self.route(self._match(m))])

    def place_back(self, received):
        half, width = received[0].shape
        moves = []
        for m in range(self.a_size):
            t = m ^ self.a
            moves.append((m, None, 0, (t % self.seqs) * CORES + t // self.seqs))
        whole = shuffle(received, [((self.a_size, half, width), BF16)], moves)[0]
        return whole.reshape(self.seqs, CORES * half, width)

    def _match(self, m):
        def move(x, c, a, b):
            t = m ^ a
            return x, t // self.seqs, self.seqs * c + t % self.seqs, b

        return move


VMEM = pl.BlockSpec(memory_space=pltpu.VMEM)
ANY = pl.BlockSpec(memory_space=pl.ANY)


LAST = []
SCALE = 0.25
SIZE = {
    "project": 28,
    "attend_forward": 24,
    "middle": 48,
    "outer": 60,
    "outer_give": 60,
    "attend_backward": 24,
    "heads_outer": 24,
    "back_project": 20,
    "finish_heads": 16,
    "finish_full": 16,
}
COST = {
    "project": 14.5,
    "attend_forward": 12.0,
    "middle": 20.0,
    "outer": 7.0,
    "outer_give": 0.1,
    "attend_backward": 25.0,
    "heads_outer": 5.5,
    "back_project": 3.5,
    "pad_weights": 3.5,
    "norm_back": 3.0,
    "finish_heads": 4.0,
    "finish_full": 3.5,
}


def call(name, body, scalars, inputs, outputs, grid=(1,), scratch=(), after=(), vmem=0):
    deps = [*LAST[-1:], *after]
    count, skip = len(inputs), len(deps)

    def run(spots, *refs):
        body(spots, *refs[:count], *refs[count + skip :])

    results = pl.pallas_call(
        run,
        out_shape=[jax.ShapeDtypeStruct(shape, kind) for shape, kind, _ in outputs],
        grid_spec=pltpu.PrefetchScalarGridSpec(
            num_scalar_prefetch=1,
            grid=grid,
            in_specs=[spec for _, spec in inputs] + [ANY] * skip,
            out_specs=[spec for _, _, spec in outputs],
            scratch_shapes=list(scratch),
        ),
        cost_estimate=pl.CostEstimate(
            flops=int(COST.get(name, 1.5) * SCALE * 1.1e9),
            bytes_accessed=int(COST.get(name, 1.5) * SCALE * 3.3e6),
            transcendentals=0,
        ),
        compiler_params=pltpu.CompilerParams(vmem_limit_bytes=(vmem or SIZE.get(name, 12)) * 1024 * 1024),
        name=name,
    )(scalars_of(scalars), *[value for value, _ in inputs], *deps)
    LAST.append(results[0])
    return results


def scalars_of(values):
    if isinstance(values, (list, tuple)):
        return jnp.stack([jnp.asarray(v, jnp.int32) for v in values])
    return values


def shuffle_body(moves, counts, spots, *refs):
    sources, targets, sems = refs[: counts[0]], refs[counts[0] : -1], refs[-1]
    copies, n = [], 0
    for src, src_rank, dst, dst_rank in moves:
        ends = []
        for ref, rank in ((sources[src], src_rank), (targets[dst], dst_rank)):
            ends.append(ref.at[tuple(spots[n + k] for k in range(rank))] if rank else ref)
            n += rank
        copies.append(pltpu.make_async_copy(*ends, sems.at[len(copies)]))
    for copy in copies:
        copy.start()
    for copy in copies:
        copy.wait()


def shuffle(sources, shapes, moves, after=()):
    spots, shape_of = [], []
    for src, src_spot, dst, dst_spot in moves:
        ranks = []
        for spot in (src_spot, dst_spot):
            spot = () if spot is None else spot if isinstance(spot, tuple) else (spot,)
            ranks.append(len(spot))
            spots += spot
        shape_of.append((src, ranks[0], dst, ranks[1]))
    return call(
        "shuffle",
        functools.partial(shuffle_body, shape_of, (len(sources), len(shapes))),
        spots or [0],
        [(source, VMEM) for source in sources],
        [(*shape, ANY) for shape in shapes],
        scratch=[pltpu.SemaphoreType.DMA((len(moves),))],
        after=after,
    )


def route_parts_body(seqs, info, own, got, *outs):
    for d, out in enumerate(outs):
        target = info[1 + d]

        @pl.when(target // seqs == info[0])
        def near():
            out[...] = own[target % seqs]

        @pl.when(target // seqs != info[0])
        def far():
            out[...] = got[target % seqs]


def route_parts(at, own, got, after=()):
    return call(
        "route_parts",
        functools.partial(route_parts_body, at.seqs),
        [at.c, *ahead(at.a, at.a_size)],
        [(own, VMEM), (got, VMEM)],
        [(own.shape[1:], BF16, VMEM)] * at.a_size,
        after=after,
    )


def route_back_body(seqs, info, *refs):
    parts, own, give = refs[:-2], refs[-2], refs[-1]
    for d, part in enumerate(parts):
        source = info[1 + d]

        @pl.when(source // seqs == info[0])
        def near():
            own[source % seqs] = part[...]

        @pl.when(source // seqs != info[0])
        def far():
            give[source % seqs] = part[...]


def route_back(at, parts):
    shape = (at.seqs, *parts[0].shape)
    return call(
        "route_back",
        functools.partial(route_back_body, at.seqs),
        [at.c, *[(at.a - d) % at.a_size for d in range(at.a_size)]],
        [(part, VMEM) for part in parts],
        [(shape, BF16, VMEM)] * 2,
    )


def add_body(counts, spots, *refs):
    terms = sum(counts)
    ins, outs, n = refs[:terms], refs[terms:], 0
    for count, out in zip(counts, outs):
        total = ins[n][...].astype(F32)
        for k in range(1, count):
            total = total + ins[n + k][...].astype(F32)
        out[...] = total.reshape(out.shape).astype(out.dtype)
        n += count


def add_blocks(groups, after=()):
    spots, inputs, outputs = [], [], []
    for terms in groups:
        for value, dim, index in terms:
            block = [1 if k == dim else size for k, size in enumerate(value.shape)]

            def spot(i, s, dim=dim, n=len(spots), rank=value.ndim):
                return tuple(s[n] if k == dim else 0 for k in range(rank))

            spots.append(index)
            inputs.append((value, pl.BlockSpec(tuple(block), spot)))
        shape = tuple(size for k, size in enumerate(value.shape) if k != dim)
        outputs.append((shape, BF16, VMEM))
    return call(
        "add_blocks",
        functools.partial(add_body, [len(terms) for terms in groups]),
        spots,
        inputs,
        outputs,
        after=after,
    )


def later(value, *done):
    return lax.optimization_barrier((value, *done))[0]


def pick(stacked, index, axis=0):
    return lax.dynamic_index_in_dim(stacked, index, axis, keepdims=False)


def by_order(own, others, axis_size, spot):
    moves = [(d, None, 0, (spot - d) % axis_size) for d in range(axis_size)]
    return shuffle([own, *others], [((axis_size, *own.shape), own.dtype)], moves)[0]


def heads_part_body(count, groups, info, query, key, value, vectors, *outs):
    width = query.shape[1] // count // groups
    rows = outs[0].shape[0]
    down = pl.ds(pl.multiple_of(info[len(outs)] * rows, rows), rows)
    for n, out in enumerate(outs):
        for peer in range(count):

            @pl.when(info[n] == peer)
            def copy():
                for g in range(groups):
                    for k, source in enumerate((query, key, value)):
                        spot = (g * 3 + k) * width
                        first = (peer * groups + g) * width
                        out[:, spot : spot + width] = source[down, first : first + width]

        out[:, 3 * groups * width :] = vectors[down, :]


def heads_parts(at, weights, vectors, groups):
    rows, model = weights[0].shape
    count = at.peer_count
    shape = (rows // at.x_split, 3 * model // count + vectors.shape[1])
    targets = [((at.b + db) % at.b_size) * CORES + at.c for db in range(at.b_size)]
    return call(
        "heads_parts",
        functools.partial(heads_part_body, count, groups),
        [*targets, at.x if at.x_split == 2 else 0],
        [(w, VMEM) for w in (*weights, vectors)],
        [(shape, BF16, VMEM)] * at.b_size,
    )


def quarter_body(info, *refs):
    out, sem = refs[3], refs[4]
    rows, half = out.shape[1:]
    down = pl.ds(pl.multiple_of(info[0] * rows, rows), rows)
    right = pl.ds(pl.multiple_of(info[1] * half, half), half)
    copies = [pltpu.make_async_copy(refs[w].at[down, right], out.at[w], sem.at[w]) for w in range(3)]
    for copy in copies:
        copy.start()
    for copy in copies:
        copy.wait()


def quarter_of(at, weights, after):
    rows, model = weights[0].shape
    return call(
        "quarter",
        quarter_body,
        [at.x if at.x_split == 2 else 0, at.c],
        [(w, VMEM) for w in weights],
        [((3, rows // at.x_split, model // CORES), BF16, ANY)],
        scratch=[pltpu.SemaphoreType.DMA((3,))],
        after=after,
    )[0]


def pad_body(heads, groups, a_size, info, *refs):
    split = (len(refs) - groups - 2) // a_size
    sources, outs = refs[: split * a_size], refs[split * a_size :]
    compact, (padded, vectors) = outs[:groups], outs[groups:]
    b_size, rows, width = sources[0].shape
    used = 3 * heads * HEAD_DIM
    part = heads // groups
    padded[...] = jnp.zeros_like(padded)
    for n in range(split):
        for d in range(a_size):
            for b in range(b_size):
                piece = sources[n * a_size + d][b]
                spot = (info[1 + d] * b_size + b) * split
                spot = (spot + (info[0] ^ n if split == 2 else 0)) * rows
                spot = pl.ds(pl.multiple_of(spot, rows), rows)
                for g in range(groups):
                    step = used // groups
                    compact[g][spot, :] = piece[:, g * step : (g + 1) * step]
                vectors[spot, :] = piece[:, used:]
                for k in range(3):
                    for h in range(heads):
                        first = (((h // part) * 3 + k) * part + h % part) * HEAD_DIM
                        lane = (k * heads + h) * LANES
                        padded[spot, lane : lane + HEAD_DIM] = piece[:, first : first + HEAD_DIM]


def pad_weights(at, sources, heads, groups, after):
    b_size, rows, width = sources[0].shape
    total = len(sources) * b_size * rows
    used = 3 * heads * HEAD_DIM
    return call(
        "pad_weights",
        functools.partial(pad_body, heads, groups, at.a_size),
        [at.x, *[(at.a - d) % at.a_size for d in range(at.a_size)]],
        [(source, VMEM) for source in sources],
        [
            *[((total, used // groups), BF16, VMEM)] * groups,
            ((total, 3 * heads * LANES), BF16, VMEM),
            ((total, width - used), BF16, VMEM),
        ],
        after=after,
        vmem=16,
    )


def project_body(count, spots, *refs):
    tokens, (gain, weight, bias, times, qkv, normed) = refs[:count], refs[count:]
    rows = tokens[0].shape[1]
    for p in range(count):
        value = tokens[p][0].astype(F32)
        rate = lax.rsqrt(jnp.mean(value * value, axis=-1, keepdims=True) + NORM_EPS)
        spot = pl.multiple_of(spots[p] * rows, rows)
        normed[pl.ds(spot, rows), :] = (value * rate * gain[...]).astype(BF16)
    step = qkv.shape[1] // 3
    for k in range(3):
        lanes = slice(k * step, (k + 1) * step)
        acc = dot(normed[...], weight[:, lanes])
        qkv[:, lanes] = ((acc + bias[:, lanes]) * times[:, lanes]).astype(BF16)


def project(at, parts, gain, weight, bias, times):
    a_size, half, model = parts[0].shape
    count = len(parts)
    cols = weight.shape[1]
    fixed = lambda a, s: (0, 0)
    return call(
        "project",
        functools.partial(project_body, count),
        [at.source(db, dc) for db, dc in at.peers()],
        [(part, pl.BlockSpec((1, half, model), lambda a, s: (a, 0, 0))) for part in parts]
        + [
            (gain, pl.BlockSpec((1, model), fixed)),
            (weight, pl.BlockSpec((model, cols), fixed)),
            (bias, pl.BlockSpec((1, cols), fixed)),
            (times, pl.BlockSpec((1, cols), fixed)),
        ],
        [
            (
                (a_size * count * half, cols),
                BF16,
                pl.BlockSpec((count * half, cols), lambda a, s: (a, 0)),
            ),
            (
                (a_size * count * half, model),
                BF16,
                pl.BlockSpec((count * half, model), lambda a, s: (a, 0)),
            ),
        ],
        grid=(a_size,),
    )


def forward_body(heads, block, info, starts, query, key, value, mixed, query_aug, total, top):
    index = pl.program_id(0)
    half = block // CORES
    core = info[pl.num_programs(0) + 1]
    total[...] = jnp.zeros_like(total)
    top[...] = jnp.full_like(top, MASK_FILL)
    rows = index * block + lax.broadcasted_iota(jnp.int32, (block, block), 0)
    begin = starts[...][:, :1]

    def step(j, carry):
        spot = pl.multiple_of(j * block, block)
        columns = spot + lax.broadcasted_iota(jnp.int32, (block, block), 1)
        bias = jnp.where((columns >= begin) & (columns <= rows), 0.0, MASK_FILL)
        lanes = [slice(h * LANES, (h + 1) * LANES) for h in range(heads)]
        scores = [dot(query[:, l], key[pl.ds(spot, block), l], 1, 1) + bias for l in lanes]
        olds = [top[h] for h in range(heads)]
        news = [
            jnp.maximum(old, jnp.max(score, axis=1, keepdims=True))
            for old, score in zip(olds, scores)
        ]
        weights = [
            jnp.exp(score - jnp.concatenate([new] * (block // LANES), axis=1)).astype(BF16)
            for score, new in zip(scores, news)
        ]
        for h in range(heads):
            total[h] = total[h] * jnp.exp(olds[h] - news[h]) + dot(
                weights[h], value[pl.ds(spot, block), lanes[h]]
            )
            top[h] = news[h]
        return carry

    lax.fori_loop(info[index], index + 1, step, 0)
    lane = lax.broadcasted_iota(jnp.int32, (block, LANES), 1)
    for h in range(heads):
        lanes = slice(h * LANES, (h + 1) * LANES)
        acc = total[h]
        weight_sum = acc[:, HEAD_DIM : HEAD_DIM + 1]
        result = (acc / weight_sum)[:, :HEAD_DIM].astype(BF16)
        for k in range(CORES):
            mixed[0, core ^ k, 0, :, h * HEAD_DIM : (h + 1) * HEAD_DIM] = result[
                k * half : (k + 1) * half
            ]
        rest = -(top[h] + jnp.log(weight_sum))
        aug = query[:, lanes].astype(F32)
        for k in range(3):
            term = rest.astype(BF16).astype(F32)
            aug = jnp.where(lane == HEAD_DIM + k, term, aug)
            rest = rest - term
        query_aug[:, lanes] = aug.astype(BF16)


def attend_forward(at, info, starts, qkv, heads, block):
    length = qkv.shape[0]
    wide = heads * LANES
    width = heads * HEAD_DIM
    count = length // block
    b_size = at.b_size
    return call(
        "attend_forward",
        functools.partial(forward_body, heads, block),
        info,
        [
            (starts, pl.BlockSpec((block, LANES), lambda i, s: (i, 0))),
            (qkv, pl.BlockSpec((block, wide), lambda i, s: (i, 0))),
            (qkv, pl.BlockSpec((length, wide), lambda i, s: (0, 1))),
            (qkv, pl.BlockSpec((length, wide), lambda i, s: (0, 2))),
        ],
        [
            (
                (b_size, CORES, at.a_size, block // CORES, width),
                BF16,
                pl.BlockSpec(
                    (1, CORES, 1, block // CORES, width),
                    lambda i, s: ((i + b_size - s[count]) % b_size, 0, i // b_size, 0, 0),
                ),
            ),
            ((length, wide), BF16, pl.BlockSpec((block, wide), lambda i, s: (i, 0))),
        ],
        grid=(count,),
        scratch=[
            pltpu.VMEM((heads, block, LANES), F32),
            pltpu.VMEM((heads, block, LANES), F32),
        ],
    )


def backward_body(
    heads,
    first,
    block,
    count,
    info,
    starts,
    scale,
    query,
    key,
    value,
    mixed,
    *rest,
):
    grad_refs = rest[:count]
    grads, scale_sum, bias_sum, grad, grad_aug, d_query, d_key, d_value = rest[count:]
    index = pl.num_programs(0) - 1 - pl.program_id(0)
    b_own, core = info[pl.num_programs(0)], info[pl.num_programs(0) + 1]
    b_size = count // CORES
    width = heads * HEAD_DIM

    @pl.when(pl.program_id(0) == 0)
    def clear():
        d_key[...] = jnp.zeros_like(d_key)
        d_value[...] = jnp.zeros_like(d_value)
        scale_sum[...] = jnp.zeros_like(scale_sum)
        bias_sum[...] = jnp.zeros_like(bias_sum)

    half = block // CORES
    lane = lax.broadcasted_iota(jnp.int32, (half, LANES), 1)
    for k in range(CORES):
        peer = ((b_own + b_size - index % b_size) % b_size) * CORES + (core ^ k)
        for p in range(count):

            @pl.when(peer == p)
            def fetch():
                grad[...] = grad_refs[p][index // b_size]

        for h in range(heads):
            part = slice((first + h) * HEAD_DIM, (first + h + 1) * HEAD_DIM)
            grad_h = grad[:, part].astype(F32)
            mixed_h = mixed[0, core ^ k, 0, :, part].astype(F32)
            delta = jnp.sum(grad_h * mixed_h, axis=1, keepdims=True)
            aug = jnp.concatenate([grad_h, jnp.zeros((half, LANES - HEAD_DIM), F32)], axis=1)
            high = (-delta).astype(BF16).astype(F32)
            aug = jnp.where(lane == HEAD_DIM, high, aug)
            aug = jnp.where(lane == HEAD_DIM + 1, -delta - high, aug)
            grad_aug[k * half : (k + 1) * half, h * LANES : (h + 1) * LANES] = aug.astype(BF16)
    d_query[...] = jnp.zeros_like(d_query)
    columns = index * block + lax.broadcasted_iota(jnp.int32, (block, block), 1)
    begin = starts[0:1, :]

    def step(j, carry):
        spot = pl.multiple_of(j * block, block)
        rows = spot + lax.broadcasted_iota(jnp.int32, (block, block), 0)
        allowed = (rows >= begin) & (rows <= columns)
        lanes = [slice(h * LANES, (h + 1) * LANES) for h in range(heads)]
        keys = [key[pl.ds(spot, block), l] for l in lanes]
        queries = [query[:, l] for l in lanes]
        grads_of = [grad_aug[:, l] for l in lanes]
        scores = [dot(k, q, 1, 1) for k, q in zip(keys, queries)]
        d_probs = [
            dot(value[pl.ds(spot, block), l], g, 1, 1) for l, g in zip(lanes, grads_of)
        ]
        probs = [jnp.where(allowed, jnp.exp(score), 0.0) for score in scores]
        d_scores = [(prob * d_prob).astype(BF16) for prob, d_prob in zip(probs, d_probs)]
        for h, l in enumerate(lanes):
            d_value[pl.ds(spot, block), l] += dot(probs[h].astype(BF16), grads_of[h])
            d_key[pl.ds(spot, block), l] += dot(d_scores[h], queries[h])
            d_query[:, l] += dot(d_scores[h], keys[h], 0, 0)
        return carry

    lax.fori_loop(info[index], index + 1, step, 0)
    here = pl.ds(pl.multiple_of(index * block, block), block)
    for h in range(heads):
        lanes = slice(h * LANES, (h + 1) * LANES)
        d_scaled = d_query[:, lanes].astype(BF16).astype(F32)
        scale_sum[...] += jnp.sum(d_scaled * query[:, lanes].astype(F32), axis=0, keepdims=True)
        d_q = (d_scaled * scale[0:1, lanes]).astype(BF16)
        for k, term in enumerate((d_q, d_key[here, lanes], d_value[here, lanes])):
            spot = k * width + h * HEAD_DIM
            term = term.astype(BF16)
            grads[:, spot : spot + HEAD_DIM] = term[:, :HEAD_DIM]
            bias_sum[:, (k * heads + h) * LANES : (k * heads + h + 1) * LANES] += jnp.sum(
                term.astype(F32), axis=0, keepdims=True
            )


def attend_backward(
    at, info, starts, scale, query_aug, qkv, grads, mixed, heads, groups, group, block
):
    length = qkv.shape[0]
    wide = heads * LANES
    width = heads * HEAD_DIM
    count = length // block
    b_size = at.b_size
    half = block // CORES

    def mixed_spot(i, s):
        i = count - 1 - i
        return (i + b_size - s[count]) % b_size, 0, i // b_size, 0, 0

    fixed = lambda i, s: (0, 0)
    return call(
        "attend_backward",
        functools.partial(backward_body, heads, group * heads, block, len(grads)),
        info,
        [
            (starts, pl.BlockSpec((8, block), lambda i, s: (0, count - 1 - i))),
            (scale, pl.BlockSpec((8, wide), fixed)),
            (query_aug, pl.BlockSpec((block, wide), lambda i, s: (count - 1 - i, group))),
            (qkv, pl.BlockSpec((length, wide), lambda i, s: (0, groups + group))),
            (qkv, pl.BlockSpec((length, wide), lambda i, s: (0, 2 * groups + group))),
            (mixed, pl.BlockSpec((1, CORES, 1, half, mixed.shape[4]), mixed_spot)),
        ]
        + [(grad, VMEM) for grad in grads],
        [
            (
                (length, 3 * width),
                BF16,
                pl.BlockSpec((block, 3 * width), lambda i, s: (count - 1 - i, 0)),
            ),
            ((8, LANES), F32, pl.BlockSpec((8, LANES), fixed)),
            ((8, 3 * wide), F32, pl.BlockSpec((8, 3 * wide), fixed)),
        ],
        grid=(count,),
        scratch=[
            pltpu.VMEM((half, mixed.shape[4]), BF16),
            pltpu.VMEM((block, wide), BF16),
            pltpu.VMEM((block, wide), F32),
            pltpu.VMEM((length, wide), F32),
            pltpu.VMEM((length, wide), F32),
        ],
    )


def concat_body(info, *refs):
    parts, out = refs[:-1], refs[-1]
    width = parts[0].shape[1]
    for p, part in enumerate(parts):
        out[:, p * width : (p + 1) * width] = part[...]


def concat(parts, after):
    rows, width = parts[0].shape
    return call(
        "concat",
        concat_body,
        [0],
        [(part, VMEM) for part in parts],
        [((rows, width * len(parts)), BF16, VMEM)],
        after=after,
    )[0]


def middle_body(count, source_count, moves, info, *refs):
    mixed, tokens, d_out, gain = refs[:4]
    sources = refs[4 : 4 + source_count]
    outs = refs[4 + source_count :]
    output, d_residual, d_proj, normed, activated, d_up = outs[:6]
    d_parts = outs[6:-4]
    weights, sems = outs[-4:-1], outs[-1]
    w_out, w_up, w_down = weights
    rows, half = sources[0].shape[2:]
    width = d_parts[0].shape[1]

    def copies(w):
        for n, (src, s, k) in enumerate(moves):
            if k == w:
                down = pl.ds(pl.multiple_of(info[2 * n] * rows, rows), rows)
                right = pl.ds(pl.multiple_of(info[2 * n + 1] * half, half), half)
                yield pltpu.make_async_copy(
                    sources[src].at[s, w], weights[w].at[down, right], sems.at[n]
                )

    def arrived(w):
        @pl.when(pl.program_id(0) == 0)
        def wait():
            for copy in copies(w):
                copy.wait()

    @pl.when(pl.program_id(0) == 0)
    def start():
        for w in range(3):
            for copy in copies(w):
                copy.start()

    arrived(0)
    residual = tokens[...].astype(F32) + dot(mixed[...], w_out[...])
    rate = lax.rsqrt(jnp.mean(residual * residual, axis=-1, keepdims=True) + NORM_EPS)
    normed[...] = (residual * rate * gain[...]).astype(BF16)
    arrived(1)
    upward = dot(normed[...], w_up[...])
    gate = 1.0 / (1.0 + jnp.exp(-upward))
    activated[...] = (upward * gate).astype(BF16)
    arrived(2)
    output[...] = (residual + dot(activated[...], w_down[...])).astype(BF16)
    d_activated = dot(d_out[...], w_down[...], 1, 1)
    d_up[...] = (d_activated * gate * (1 + upward * (1 - gate))).astype(BF16)
    scaled = dot(d_up[...], w_up[...], 1, 1) * gain[...]
    inner = jnp.mean(residual * scaled, axis=-1, keepdims=True)
    d_norm = rate * scaled - residual * (rate * rate * rate * inner)
    d_total = d_out[...].astype(F32) + d_norm
    d_residual[...] = d_total
    d_proj[...] = d_total.astype(BF16)
    d_mixed = dot(d_proj[...], w_out[...], 1, 1).astype(BF16)
    for p in range(count):
        d_parts[p][...] = d_mixed[:, p * width : (p + 1) * width]


def middle(at, mixed, tokens, d_out, gain, sources):
    count = at.peer_count
    rows, model = tokens.shape
    width = model // count
    arrays = list(sources.values())
    a_size, _, piece, half = arrays[0].shape
    group = model // at.peer_count // piece
    moves, spots = [], []
    for n, (dx, db, dc) in enumerate(sources):
        for a in range(a_size):
            for w in range(3):
                row = a * at.b_size + (at.b - db) % at.b_size
                if at.x_split == 2:
                    row = row * 2 + (at.x + dx) % 2
                if w == 0:
                    peer, rest = row // group, row % group
                    far = (at.b - peer // CORES) % at.b_size
                    row = (far * CORES + ((peer % CORES) ^ at.c)) * group + rest
                moves.append((n, a, w))
                spots += [row, (at.c + dc) % CORES]
    block = min(256, rows)
    row = lambda i, s: (i, 0)
    rows_of = pl.BlockSpec((block, model), row)
    part = pl.BlockSpec((block, width), row)
    types = [BF16, F32, BF16, BF16, BF16, BF16]
    return call(
        "middle",
        functools.partial(middle_body, count, len(arrays), moves),
        spots,
        [(mixed, rows_of), (tokens, rows_of), (d_out, rows_of)]
        + [(gain, pl.BlockSpec(gain.shape, lambda i, s: (0, 0)))]
        + [(source, ANY) for source in arrays],
        [((rows, model), kind, rows_of) for kind in types]
        + [((rows, width), BF16, part)] * count,
        grid=(rows // block,),
        scratch=[pltpu.VMEM((model, model), BF16)] * 3
        + [pltpu.SemaphoreType.DMA((len(moves),))],
    )


def outer_body(count, split, add, info, *refs):
    pairs, rest = refs[:6], refs[6:]
    for w in range(3):

        @pl.when(pl.program_id(0) == w)
        def product():
            value = dot(pairs[2 * w][...], pairs[2 * w + 1][...], 0, 0)
            target = rest[-1] if split else rest[-1].at[0]
            width = value.shape[0] // count
            for p in range(count):
                spot = p * width
                if w == 0:
                    spot = pl.multiple_of(info[3 + p] * width, width)
                part = value[p * width : (p + 1) * width]
                if add:
                    part = part + rest[0][0, pl.ds(spot, width)].astype(F32)
                target[pl.ds(spot, width)] = part.astype(BF16)

    if split:
        keep_x, give_x, keep_b, give_b, total = rest[1:]
        pairs_a, b_size, rows = keep_x.shape[1:4]
        for k in range(pairs_a):
            for b in range(b_size):
                for half, out in ((info[1], keep_x), (1 - info[1], give_x)):
                    spot = pl.multiple_of((k * b_size + b) * 2 * rows + half * rows, rows)
                    out[0, k, b] = total[pl.ds(spot, rows)]
            for b, out in ((info[2], keep_b), (1 - info[2], give_b)):
                for half in range(2):
                    spot = (((k + pairs_a) * b_size) * 2 + half) * rows + b * 2 * rows
                    out[0, k, half] = total[pl.ds(pl.multiple_of(spot, rows), rows)]


def outer(at, pairs, cols, add=None, after=()):
    rows, model = pairs[0][0].shape
    half = model // CORES
    count = at.peer_count
    split = add is not None and at.even
    info = [cols, at.x if at.even else 0, at.b, *[at.source(db, dc) for db, dc in at.peers()]]
    inputs = []
    for left, right in pairs:
        inputs.append((left, pl.BlockSpec((rows, model), lambda w, s: (0, 0))))
        inputs.append((right, pl.BlockSpec((rows, half), lambda w, s: (0, s[0]))))
    block = pl.BlockSpec((1, model, half), lambda w, s: (w, 0, 0))
    outputs = [((3, model, half), BF16, block)]
    scratch = []
    if add is not None:
        inputs.append((add, block))
    if split:
        shape = (at.a_size // 2, 2, model // at.a_size // 4, half)
        part = pl.BlockSpec((1, *shape), lambda w, s: (w, 0, 0, 0, 0))
        outputs = [((3, *shape), BF16, part)] * 4
        scratch = [pltpu.VMEM((model, half), BF16)]
    return call(
        "outer_give" if add is None else "outer",
        functools.partial(outer_body, count, split, add is not None),
        info,
        inputs,
        outputs,
        grid=(3,),
        scratch=scratch,
        after=after,
    )


def give_body(groups, info, *refs):
    grads, weights, out = refs[:groups], refs[groups : 2 * groups], refs[-1]
    value = back_product(grads, weights)
    out[0] = value.astype(BF16).reshape(out.shape[1:])


def back_product(grads, weights):
    total = 0.0
    for grad, weight in zip(grads, weights):
        total = total + dot(grad[...].reshape(-1, grad.shape[-1]), weight[...], 1, 1)
    return total


def keep_body(groups, info, *refs):
    grads, weights, got = refs[:groups], refs[groups : 2 * groups], refs[2 * groups]
    outs = refs[2 * groups + 1 :]
    b_size = got.shape[2]
    value = back_product(grads, weights).reshape(got.shape[1:]) + got[0].astype(F32)
    for b in range(b_size):
        for n, out in enumerate(outs):

            @pl.when(info[2 + n] == b)
            def copy():
                out[...] = value[:, b].astype(out.dtype)


def back_project_give(at, grads, weights, half):
    model = weights[0].shape[0]
    pair = at.a_size // 2
    width = grads[0].shape[1]
    shape = (pair, at.b_size, half, model)
    grads = [g.reshape(at.a_size, at.b_size, CORES, half, width) for g in grads]
    block = pl.BlockSpec((pair, at.b_size, 1, half, width), lambda i, s: (s[i], 0, s[2], 0, 0))
    core = 1 - at.c
    return call(
        "back_project",
        functools.partial(give_body, len(grads)),
        [core, 1 ^ core, core],
        [(g, block) for g in grads] + [(weight, VMEM) for weight in weights],
        [((2, *shape), BF16, pl.BlockSpec((1, *shape), lambda i, s: (i, 0, 0, 0, 0)))],
        grid=(2,),
    )[0]


def back_project_keep(at, grads, weights, half, which, got):
    model = weights[0].shape[0]
    pair = at.a_size // 2
    width = grads[0].shape[1]
    shape = (pair, at.b_size, half, model)
    grads = [g.reshape(at.a_size, at.b_size, CORES, half, width) for g in grads]
    block = pl.BlockSpec((pair, at.b_size, 1, half, width), lambda i, s: (s[0], 0, s[1], 0, 0))
    return call(
        "back_project",
        functools.partial(keep_body, len(grads)),
        [which ^ at.c, at.c, *ahead(at.b, at.b_size)],
        [(g, block) for g in grads]
        + [(weight, VMEM) for weight in weights]
        + [(got, pl.BlockSpec((1, *shape), lambda i, s: (which, 0, 0, 0, 0)))],
        [((pair, half, model), F32 if db == 0 else BF16, VMEM) for db in range(at.b_size)],
    )


def norm_back_body(count, info, *refs):
    own, others = refs[0], refs[1:count]
    tokens, d_residual, gain = refs[count : count + 3]
    for n, out in enumerate(refs[count + 3 :]):
        k = info[1 + n]
        grad = own[k]
        for other in others:
            grad = grad + other[k].astype(F32)
        value = tokens[k].astype(F32)
        rate = lax.rsqrt(jnp.mean(value * value, axis=-1, keepdims=True) + NORM_EPS)
        scaled = grad * gain[...]
        inner = jnp.mean(value * scaled, axis=-1, keepdims=True)
        d_norm = rate * scaled - value * (rate * rate * rate * inner)
        out[...] = (d_residual[k] + d_norm).astype(BF16)


def norm_back(at, terms, chunks, d_residual, gain, which):
    pair, half, model = terms[0].shape
    block = pl.BlockSpec((pair, half, model), lambda i, s: (s[0], 0, 0))
    order = [k ^ (at.a % pair) for k in range(pair)]
    return call(
        "norm_back",
        functools.partial(norm_back_body, len(terms)),
        [which ^ at.c, *order],
        [(t, VMEM) for t in terms] + [(chunks, block), (d_residual, block), (gain, VMEM)],
        [((half, model), BF16, VMEM)] * pair,
    )


def heads_outer_body(steps, info, normed, grads, extra, *rest):
    outs, acc = rest[:-1], rest[-1]
    value = dot(normed[...], grads[...], 0, 0)

    @pl.when(pl.program_id(0) == 0)
    def first():
        acc[...] = value

    @pl.when(pl.program_id(0) != 0)
    def later():
        acc[...] += value

    @pl.when(pl.program_id(0) == steps - 1)
    def last():
        used = acc.shape[1]
        pairs, b_size, rows = outs[0].shape[:3]
        split = len(outs)
        for n, out in enumerate(outs):
            for s in range(pairs * b_size):
                spot = (s * split + (info[0] ^ n if split == 2 else 0)) * rows
                spot = pl.ds(pl.multiple_of(spot, rows), rows)
                out[s // b_size, s % b_size, :, :used] = acc[spot, :].astype(BF16)
                out[s // b_size, s % b_size, :, used:] = extra[spot, :]


def heads_outer(at, normed, grads, extra):
    length, model = normed.shape
    used = grads.shape[1]
    block = min(512, length)
    steps = length // block
    rows = model // at.a_size // at.b_size // at.x_split
    shape = (at.a_size, at.b_size, rows, used + extra.shape[1])
    return call(
        "heads_outer",
        functools.partial(heads_outer_body, steps),
        [at.x],
        [
            (normed, pl.BlockSpec((block, model), lambda i, s: (i, 0))),
            (grads, pl.BlockSpec((block, used), lambda i, s: (i, 0))),
            (extra, pl.BlockSpec(extra.shape, lambda i, s: (0, 0))),
        ],
        [(shape, BF16, pl.BlockSpec(shape, lambda i, s: (0, 0, 0, 0)))] * at.x_split,
        grid=(steps,),
        scratch=[pltpu.VMEM((model, used), F32)],
    )


def all_sum(at, value, axis, size):
    total = value
    for d in range(1, size):
        total = total + at.send(value, **{axis: d}).astype(value.dtype)
    return total


def ahead(spot, size):
    return [(spot + d) % size for d in range(size)]


def cat_body(info, first, first_got, second, second_got, *outs):
    pair = first.shape[1]
    for d, out in enumerate(outs):
        spot = info[d] % pair

        @pl.when(info[d] < pair)
        def low():
            out[...] = (first[:, spot].astype(F32) + first_got[:, spot].astype(F32)).astype(BF16)

        @pl.when(info[d] >= pair)
        def high():
            out[...] = (second[:, spot].astype(F32) + second_got[:, spot].astype(F32)).astype(BF16)


class FullReduce:
    def __init__(self, at, parts):
        self.at = at
        if at.even:
            keep_x, give_x, keep_b, give_b = parts
            self.first = keep_x, at.send(give_x, dx=1)
            self.second = keep_b, at.send(give_b, db=1)
        else:
            self.part = parts[0].reshape(3, at.a_size, at.b_size, -1, parts[0].shape[-1])

    def next(self):
        at = self.at
        if not at.even:
            return
        groups = [[(t, 2, b) for t in self.first] for b in ahead(at.b, 2)]
        groups += [[(t, 2, x) for t in self.second] for x in ahead(at.x, 2)]
        keep_b, give_b, keep_x, give_x = add_blocks(groups)
        self.first = keep_b, at.send(give_b, db=1)
        self.second = keep_x, at.send(give_x, dx=1)

    def over_a(self):
        at = self.at
        if at.even:
            shape = self.first[0].shape
            parts = call(
                "cat",
                cat_body,
                ahead(at.a, at.a_size),
                [(t, VMEM) for t in (*self.first, *self.second)],
                [((3, *shape[2:]), BF16, VMEM)] * at.a_size,
            )
        else:
            parts = add_blocks([[(self.part, 1, a)] for a in ahead(at.a, at.a_size)])
        self.got = [parts[0]] + [at.send(parts[d], da=d) for d in range(1, at.a_size)]

    def end(self):
        at = self.at
        if at.even:
            part = add_blocks([[(t[None], 0, 0) for t in self.got]])[0]
            far = at.send(part, dx=1)
            return [part, far, at.send(part, dc=1), at.send(far, dc=1)]
        parts = add_blocks([[(t, 1, b) for t in self.got] for b in ahead(at.b, at.b_size)])
        got = [parts[0]] + [at.send(parts[d], db=d) for d in range(1, at.b_size)]
        part = add_blocks([[(t[None], 0, 0) for t in got]])[0]
        part = all_sum(at, part, "dx", at.x_size)
        return [part, at.send(part, dc=1)]


class HeadsReduce:
    def __init__(self, at, parts):
        self.at = at
        self.got = [parts[0]]
        if at.x_split == 2:
            self.got.append(at.send(parts[1], dx=1))

    def over_a(self):
        at = self.at
        parts = add_blocks([[(t, 0, a) for t in self.got] for a in ahead(at.a, at.a_size)])
        self.got = [parts[0]] + [at.send(parts[d], da=d) for d in range(1, at.a_size)]
        return parts

    def by_b(self, after=()):
        at = self.at
        if at.x_split == 1:
            total = add_blocks([[(t[None], 0, 0) for t in self.got]])[0]
            self.got = [all_sum(at, total, "dx", at.x_size)]
        groups = [[(t, 0, b) for t in self.got] for b in ahead(at.b, at.b_size)]
        return add_blocks(groups, after)


def side_body(groups, info, *refs):
    for n, out in enumerate(refs[-(len(refs) // (groups + 1)) :]):
        for g in range(groups):
            out[g] = refs[n * groups + g][...]


def to_peers(at, groups):
    shape = (len(groups), *groups[0][0].shape)
    parts = call(
        "side",
        functools.partial(side_body, len(groups)),
        [0],
        [(group[b], VMEM) for b in range(at.b_size) for group in groups],
        [(shape, BF16, VMEM)] * at.b_size,
    )
    parts = [at.send(parts[db], db=db, dc=dc) if db or dc else parts[0] for db, dc in at.peers()]
    return parts


def in_order(info, refs, split, half, core, spot):
    near = [r[spot] for r in refs]
    if split == 2:
        near = [jnp.where(info[0] == half, near[2 * k], near[2 * k + 1]) for k in range(2)]
    return jnp.where(info[1] == core, near[0], near[1])


def finish_full_body(split, info, *refs):
    count = CORES * split
    parts, (weight, gain), outs = refs[:count], refs[count : count + 2], refs[count + 2 :]
    rows, half = parts[0].shape[1:]
    for x in range(split):
        spot = slice(x * rows, (x + 1) * rows)
        for w in range(3):
            for c in range(CORES):
                outs[w][spot, c * half : (c + 1) * half] = in_order(
                    info, parts, split, x, c, w
                ).astype(F32)
    total = jnp.sum(outs[1][...] * weight[...].astype(F32), axis=1, keepdims=True)
    outs[3][...] = total / gain[...].astype(F32)


def finish_full(at, parts, weight, gain, after):
    rows, model = weight.shape
    return call(
        "finish_full",
        functools.partial(finish_full_body, 2 if at.even else 1),
        [at.x, at.c],
        [(p, VMEM) for p in parts] + [(weight, VMEM), (gain[:, None], VMEM)],
        [((rows, model), F32, VMEM)] * 3 + [((rows, 1), F32, VMEM)],
        after=after,
    )


def finish_heads_body(count, split, info, *refs):
    parts, refs = refs[:count], refs[count:]
    far, refs = refs[: split - 1], refs[split - 1 :]
    weights, gain, outs = refs[:3], refs[3], refs[4:]
    few = outs[4].shape[1]
    groups, rows, width = parts[0].shape
    width = (width - few) // 3
    for n in range(split):
        down = pl.ds(pl.multiple_of((info[count] ^ n if split == 2 else 0) * rows, rows), rows)
        total = jnp.zeros((rows, few), F32)
        for p in range(count):
            for g in range(groups):
                source = far[0].at[p, g] if n else parts[p].at[g]
                total = total + source[:, 3 * width :].astype(F32)
                for peer in range(count):

                    @pl.when(info[p] == peer)
                    def copy():
                        for k in range(3):
                            spot = (peer * groups + g) * width
                            piece = source[:, k * width : (k + 1) * width]
                            outs[k][down, spot : spot + width] = piece.astype(F32)

        outs[4][down, :] = total
    total = jnp.zeros(outs[3].shape, F32)
    for k in range(3):
        total = total + jnp.sum(outs[k][...] * weights[k][...].astype(F32), axis=1, keepdims=True)
    outs[3][...] = total / gain[...].astype(F32)


def finish_heads(at, parts, weights, gain, few):
    rows, model = weights[0].shape
    flat = [*parts[0], *parts[1:]]
    return call(
        "finish_heads",
        functools.partial(finish_heads_body, at.peer_count, at.x_split),
        [*[at.source(db, dc) for db, dc in at.peers()], at.x],
        [(p, VMEM) for p in flat] + [(w, VMEM) for w in weights] + [(gain[:, None], VMEM)],
        [((rows, model), F32, VMEM)] * 3 + [((rows, 1), F32, VMEM), ((rows, few), F32, VMEM)],
    )


def local(
    reps,
    shards,
    activations,
    cotangent,
    doc_lengths,
    gain_attn,
    query_weight,
    query_bias,
    key_weight,
    value_weight,
    value_bias,
    dim_scale,
    out_weight,
    gain_mlp,
    up_weight,
    down_weight,
):
    seqs, tok_count, model = activations.shape
    at = Place(reps, shards, seqs)
    half = tok_count // CORES
    length = tok_count * shards
    peer_count = at.peer_count
    heads = model // HEAD_DIM // peer_count
    width = heads * HEAD_DIM
    wide = heads * LANES
    own_rows = at.a_size * half
    rows = gain_attn.shape[0]
    groups = 2
    block = CORES * half
    mine = at.b * CORES + at.c

    LAST.clear()
    stage = at.to_cluster(activations)
    next(stage)
    vectors = jnp.stack([gain_attn, gain_mlp, query_bias, value_bias], axis=1)
    own, *sent = heads_parts(at, (query_weight, key_weight, value_weight), vectors, groups)
    sent = [at.send(part, db=db + 1) for db, part in enumerate(sent)]
    next(stage)
    near = by_order(own, sent, at.b_size, at.b)
    sources = [near] + [at.send(near, da=d) for d in range(1, at.a_size)]
    if at.x_split == 2:
        sources += [at.send(source, dx=1) for source in sources]
    chunks = next(stage)
    parts = []
    early = sources[1 : at.a_size]
    if at.x_split == 2:
        early = [sources[2], sources[at.a_size + 1], sources[at.a_size + 3]]
    for db in range(at.b_size):
        near = at.send(chunks, db=db) if db else chunks
        ready = later(near, *early) if db else near
        parts += [near, at.send(ready, dc=1)]
    stage = at.to_cluster(cotangent)
    soon = [next(stage), at.send(doc_lengths, dc=1)]
    quarter = quarter_of(at, (out_weight, up_weight, down_weight), sources[1 : at.a_size])
    pieces = [quarter] + [at.send(quarter, da=d) for d in range(1, at.a_size)]
    *w_heads, w_pad, vectors = pad_weights(
        at, sources, heads, groups, [*parts[1:], *soon]
    )
    vectors = vectors.T.astype(F32)
    g_attn, g_mlp, b_query, b_value = vectors[0], vectors[1], vectors[2], vectors[3]

    other_lengths = soon[1]
    lengths = pick(jnp.where(at.c == at.a // seqs, doc_lengths, other_lengths), at.a % seqs)
    ends = jnp.cumsum(lengths)
    places = jnp.arange(length, dtype=jnp.int32)
    starts = jnp.max(jnp.where(ends[None, :] <= places[:, None], ends[None, :], 0), axis=1)
    starts_row = jnp.broadcast_to(starts[None, :], (8, length))
    starts_col = jnp.broadcast_to(starts[:, None], (length, LANES))
    info = jnp.concatenate([starts[::block] // block, jnp.stack([at.b, at.c])]).astype(jnp.int32)

    scale_dim = LOG_BASE / math.sqrt(HEAD_DIM) * jax.nn.softplus(dim_scale)
    scale_pad = jnp.tile(jnp.pad(scale_dim, (0, LANES - HEAD_DIM)), heads)
    lane = jnp.arange(LANES)
    ones_key = ((lane >= HEAD_DIM) & (lane < HEAD_DIM + 3)).astype(F32)
    ones_value = ((lane >= HEAD_DIM) & (lane < HEAD_DIM + 2)).astype(F32)

    def pad_heads(vec):
        part = lax.dynamic_slice_in_dim(vec, mine * width, width, 0).reshape(heads, HEAD_DIM)
        return jnp.pad(part, ((0, 0), (0, LANES - HEAD_DIM))).reshape(wide)

    bias_pad = jnp.concatenate(
        [
            pad_heads(b_query),
            jnp.tile(ones_key, heads),
            pad_heads(b_value) + jnp.tile(ones_value, heads),
        ]
    )
    times = jnp.concatenate([scale_pad, jnp.ones((2 * wide,), F32)])
    qkv, normed = project(at, parts, g_attn[None], w_pad, bias_pad[None], times[None])

    part_heads = heads // groups
    part_width = part_heads * HEAD_DIM
    moves = [(d, None, 0, (at.a - d) % at.a_size) for d in range(at.a_size)]
    quarter = shuffle(pieces, [((at.a_size, *quarter.shape), BF16)], moves)[0]
    others = {(0, 0, 0): quarter, (0, 0, 1): at.send(quarter, dc=1)}
    for db in range(1, at.b_size):
        others[(0, db, 0)] = at.send(quarter, db=db)
    if at.x_split == 2:
        others[(1, 0, 0)] = at.send(quarter, dx=1)
    stage.send([others[(0, 0, 1)]])
    mixed_rel, query_aug = attend_forward(at, info, starts_col, qkv, heads, block)
    d_out = next(stage).reshape(own_rows, model)
    if at.x_split == 2:
        for db in range(1, at.b_size):
            others[(1, db, 0)] = at.send(later(others[(0, db, 0)], d_out), dx=1)
    parts = []
    for db, dc in at.peers():
        part = later(mixed_rel[db, dc], d_out).reshape(own_rows, width)
        parts.append(at.send(part, db=db, dc=dc) if db or dc else part)
    mixed = concat(parts, [])
    for dx, db, dc in list(others):
        if (dx, db, 1) not in others:
            others[(dx, db, 1)] = at.send(later(others[(dx, db, 0)], mixed), dc=1)
    tokens = chunks.reshape(own_rows, model)
    output, d_residual, d_proj, normed_mlp, activated, d_up, *d_parts = middle(
        at, mixed, tokens, d_out, g_mlp[None], others
    )

    grads = []
    for (db, dc), part in zip(at.peers(), d_parts):
        part = at.send(part, db=db, dc=dc) if db or dc else part
        grads.append(part.reshape(at.a_size, half, width))

    pairs = [(mixed, d_proj), (normed_mlp, d_up), (activated, d_out)]
    give = outer(at, pairs, 1 - at.c)[0]
    full = FullReduce(at, outer(at, pairs, at.c, at.send(give, dc=1), grads))

    scale_rows = jnp.broadcast_to(scale_pad[None, : part_heads * LANES], (8, part_heads * LANES))
    zeros = jnp.zeros((model,), F32)

    def backward(g):
        d_heads, scale_sum, bias_sum = attend_backward(
            at,
            info,
            starts_row,
            scale_rows,
            query_aug,
            qkv,
            grads,
            mixed_rel,
            part_heads,
            groups,
            g,
            block,
        )
        bias_sum = bias_sum[0].reshape(3, part_heads, LANES)[:, :, :HEAD_DIM]
        bias_sum = bias_sum.reshape(3, part_width)
        spot = (mine * groups + g) * part_width
        scale_sum = jnp.pad(scale_sum[0, :HEAD_DIM], (0, rows - HEAD_DIM))
        extra = [
            lax.dynamic_update_slice(zeros, bias_sum[0], (spot,)),
            lax.dynamic_update_slice(zeros, bias_sum[2], (spot,)),
            jnp.tile(scale_sum, shards),
        ]
        return d_heads, jnp.stack(extra, axis=1).astype(BF16)

    stage = at.from_cluster(output.reshape(at.a_size, half, model))
    next(stage)
    d_first, extra_first = backward(0)
    next(stage)
    full.next()
    reduce_first = HeadsReduce(at, heads_outer(at, normed, d_first, extra_first))
    full.over_a()
    d_second, extra_second = backward(1)
    full_parts = full.end()
    reduce_first.over_a()

    d_heads = [d_first, d_second]
    keeps, received = [], []
    residual_chunks = d_residual.reshape(at.a_size, half, model)

    def keep(which, got):
        terms = back_project_keep(at, d_heads, w_heads, half, which, got)
        keeps.append([terms[0]] + [at.send(terms[db], db=db) for db in range(1, at.b_size)])

    def back(which):
        sent = norm_back(at, keeps[which], chunks, residual_chunks, g_attn[None], which)
        for k, part in enumerate(sent):
            received.append(at.send_back(part, which * len(sent) + k))
        return sent

    got = at.send(back_project_give(at, d_heads, w_heads, half), dc=1)
    reduce_second = HeadsReduce(at, heads_outer(at, normed, d_second, extra_second))
    first = reduce_first.by_b(full_parts[1:2])
    keep(0, got)
    keep(1, got)
    reduce_second.over_a()
    back(0)
    parts = [to_peers(at, [first, reduce_second.by_b(keeps[1][1:])])]
    sent = back(1)
    if at.x_split == 2:
        parts.append(at.send(later(jnp.stack(parts[0]), sent[0]), dx=1))
    *grads_full, grad_gain_mlp = finish_full(at, full_parts, up_weight, gain_mlp, [])
    output = next(stage)
    weights = (query_weight, key_weight, value_weight)
    *grads_heads, grad_gain_attn, few = finish_heads(at, parts, weights, gain_attn, 3)
    input_grad = at.place_back(received)
    grad_scale = few[:HEAD_DIM, 2] / scale_dim * (LOG_BASE / math.sqrt(HEAD_DIM))
    grad_scale = grad_scale * jax.nn.sigmoid(dim_scale)
    return (
        output,
        input_grad,
        grad_gain_attn[:, 0],
        grads_heads[0],
        few[:, 0],
        grads_heads[1],
        grads_heads[2],
        few[:, 1],
        grad_scale,
        grads_full[0],
        grad_gain_mlp[:, 0],
        grads_full[1],
        grads_full[2],
    )


def solution(mesh):
    in_specs = (
        P("rep", "shard", None),
        P("rep", "shard", None),
        P("rep", None),
        P("shard"),
        P("shard", None),
        P("shard"),
        P("shard", None),
        P("shard", None),
        P("shard"),
        P(),
        P("shard", None),
        P("shard"),
        P("shard", None),
        P("shard", None),
    )
    out_specs = (
        P("rep", "shard", None),
        P("rep", "shard", None),
        P("shard"),
        P("shard", None),
        P("shard"),
        P("shard", None),
        P("shard", None),
        P("shard"),
        P(),
        P("shard", None),
        P("shard"),
        P("shard", None),
        P("shard", None),
    )
    body = functools.partial(local, mesh.shape["rep"], mesh.shape["shard"])
    return jax.shard_map(body, mesh=mesh, in_specs=in_specs, out_specs=out_specs, check_vma=False)
```

```python
import functools
import math

import jax
import jax.numpy as jnp
from jax import lax
from jax.experimental import pallas as pl
from jax.experimental.pallas import tpu as pltpu
from jax.sharding import PartitionSpec as P

HEAD_DIM = 80
LANES = 128
CORES = 2
NORM_EPS = 1e-06
LOG_BASE = 1.442695041
MASK_FILL = -1e30
AXES = ("rep", "shard")
F32 = jnp.float32
BF16 = jnp.bfloat16


def dot(left, right, left_dim=1, right_dim=0):
    return lax.dot_general(
        left, right, (((left_dim,), (right_dim,)), ((), ())), preferred_element_type=F32
    )


class Place:
    def __init__(self, reps, shards, seqs):
        self.x_size = reps // CORES
        self.x_split = 2 if self.x_size == 2 else 1
        self.a_size = CORES * seqs
        self.b_size = shards // self.a_size
        self.even = self.x_size == 2 and self.b_size == 2
        self.peer_count = self.b_size * CORES
        self.seqs = seqs
        rep, shard = lax.axis_index("rep"), lax.axis_index("shard")
        self.x, self.c = rep // CORES, rep % CORES
        self.a, self.b = shard // self.b_size, shard % self.b_size
        self.shard = shard

    def route(self, move):
        pairs = []
        for x in range(self.x_size):
            for c in range(CORES):
                for a in range(self.a_size):
                    for b in range(self.b_size):
                        pairs.append((self.number(x, c, a, b), self.number(*move(x, c, a, b))))
        return pairs

    def number(self, x, c, a, b):
        return ((x * CORES + c) * self.a_size + a) * self.b_size + b

    def send(self, value, dx=0, dc=0, da=0, db=0):
        return lax.ppermute(
            value,
            AXES,
            self.route(
                lambda x, c, a, b: (
                    (x + dx) % self.x_size,
                    (c + dc) % CORES,
                    (a + da) % self.a_size,
                    (b + db) % self.b_size,
                )
            ),
        )

    def peers(self):
        return [(db, dc) for db in range(self.b_size) for dc in range(CORES)]

    def source(self, db, dc):
        return ((self.b - db) % self.b_size) * CORES + (self.c + dc) % CORES

    def to_cluster(self, tokens, after=()):
        seqs, count, width = tokens.shape
        half = count // CORES
        halves = tokens.reshape(seqs, CORES, half, width)
        shape = (seqs, half, width)
        moves = []
        for i in range(seqs):
            moves += [(0, (i, self.c), 0, i), (0, (i, 1 - self.c), 1, i)]
        own, give = shuffle([halves], [(shape, BF16)] * 2, moves, after)
        got = self.send(give, dc=1)
        after = yield got
        parts = route_parts(self, own, got, after or ())
        received = [parts[0]] + [self.send(parts[d], da=d) for d in range(1, self.a_size)]
        moves = [(d, None, 0, (self.a - d) % self.a_size) for d in range(self.a_size)]
        after = yield
        yield shuffle(received, [((self.a_size, half, width), BF16)], moves, after or ())[0]

    def from_cluster(self, chunks):
        half, width = chunks.shape[1:]
        picks = [(0, (self.a + d) % self.a_size, d, None) for d in range(self.a_size)]
        parts = shuffle([chunks], [((half, width), BF16)] * self.a_size, picks)
        received = [parts[0]] + [self.send(parts[d], da=d) for d in range(1, self.a_size)]
        yield
        own, give = route_back(self, received)
        got = self.send(give, dc=1)
        moves = []
        for i in range(self.seqs):
            moves += [(0, i, 0, i * CORES + self.c), (1, i, 0, i * CORES + 1 - self.c)]
        yield got
        whole = shuffle([own, got], [((self.a_size, half, width), BF16)], moves)[0]
        yield whole.reshape(self.seqs, CORES * half, width)

    def send_back(self, part, m):
        return lax.ppermute(part, AXES, [(j, i) for i, j in self.route(self._match(m))])

    def place_back(self, received):
        half, width = received[0].shape
        moves = []
        for m in range(self.a_size):
            t = m ^ self.a
            moves.append((m, None, 0, (t % self.seqs) * CORES + t // self.seqs))
        whole = shuffle(received, [((self.a_size, half, width), BF16)], moves)[0]
        return whole.reshape(self.seqs, CORES * half, width)

    def _match(self, m):
        def move(x, c, a, b):
            t = m ^ a
            return x, t // self.seqs, self.seqs * c + t % self.seqs, b

        return move


VMEM = pl.BlockSpec(memory_space=pltpu.VMEM)
ANY = pl.BlockSpec(memory_space=pl.ANY)


LAST = []
SCALE = 0.25
SIZE = {
    "project": 28,
    "attend_forward": 24,
    "middle": 48,
    "outer": 60,
    "outer_give": 60,
    "attend_backward": 24,
    "heads_outer": 24,
    "back_project": 20,
    "finish_heads": 16,
    "finish_full": 16,
}
COST = {
    "project": 14.5,
    "attend_forward": 12.0,
    "middle": 20.0,
    "outer": 7.0,
    "outer_give": 0.1,
    "attend_backward": 25.0,
    "heads_outer": 5.5,
    "back_project": 3.5,
    "pad_weights": 3.5,
    "norm_back": 3.0,
    "finish_heads": 4.0,
    "finish_full": 3.5,
}


def call(name, body, scalars, inputs, outputs, grid=(1,), scratch=(), after=(), vmem=0):
    deps = [*LAST[-1:], *after]
    count, skip = len(inputs), len(deps)

    def run(spots, *refs):
        body(spots, *refs[:count], *refs[count + skip :])

    results = pl.pallas_call(
        run,
        out_shape=[jax.ShapeDtypeStruct(shape, kind) for shape, kind, _ in outputs],
        grid_spec=pltpu.PrefetchScalarGridSpec(
            num_scalar_prefetch=1,
            grid=grid,
            in_specs=[spec for _, spec in inputs] + [ANY] * skip,
            out_specs=[spec for _, _, spec in outputs],
            scratch_shapes=list(scratch),
        ),
        cost_estimate=pl.CostEstimate(
            flops=int(COST.get(name, 1.5) * SCALE * 1.1e9),
            bytes_accessed=int(COST.get(name, 1.5) * SCALE * 3.3e6),
            transcendentals=0,
        ),
        compiler_params=pltpu.CompilerParams(vmem_limit_bytes=(vmem or SIZE.get(name, 12)) * 1024 * 1024),
        name=name,
    )(scalars_of(scalars), *[value for value, _ in inputs], *deps)
    LAST.append(results[0])
    return results


def scalars_of(values):
    if isinstance(values, (list, tuple)):
        return jnp.stack([jnp.asarray(v, jnp.int32) for v in values])
    return values


def shuffle_body(moves, counts, spots, *refs):
    sources, targets, sems = refs[: counts[0]], refs[counts[0] : -1], refs[-1]
    copies, n = [], 0
    for src, src_rank, dst, dst_rank in moves:
        ends = []
        for ref, rank in ((sources[src], src_rank), (targets[dst], dst_rank)):
            ends.append(ref.at[tuple(spots[n + k] for k in range(rank))] if rank else ref)
            n += rank
        copies.append(pltpu.make_async_copy(*ends, sems.at[len(copies)]))
    for copy in copies:
        copy.start()
    for copy in copies:
        copy.wait()


def shuffle(sources, shapes, moves, after=()):
    spots, shape_of = [], []
    for src, src_spot, dst, dst_spot in moves:
        ranks = []
        for spot in (src_spot, dst_spot):
            spot = () if spot is None else spot if isinstance(spot, tuple) else (spot,)
            ranks.append(len(spot))
            spots += spot
        shape_of.append((src, ranks[0], dst, ranks[1]))
    return call(
        "shuffle",
        functools.partial(shuffle_body, shape_of, (len(sources), len(shapes))),
        spots or [0],
        [(source, VMEM) for source in sources],
        [(*shape, ANY) for shape in shapes],
        scratch=[pltpu.SemaphoreType.DMA((len(moves),))],
        after=after,
    )


def route_parts_body(seqs, info, own, got, *outs):
    for d, out in enumerate(outs):
        target = info[1 + d]

        @pl.when(target // seqs == info[0])
        def near():
            out[...] = own[target % seqs]

        @pl.when(target // seqs != info[0])
        def far():
            out[...] = got[target % seqs]


def route_parts(at, own, got, after=()):
    return call(
        "route_parts",
        functools.partial(route_parts_body, at.seqs),
        [at.c, *ahead(at.a, at.a_size)],
        [(own, VMEM), (got, VMEM)],
        [(own.shape[1:], BF16, VMEM)] * at.a_size,
        after=after,
    )


def route_back_body(seqs, info, *refs):
    parts, own, give = refs[:-2], refs[-2], refs[-1]
    for d, part in enumerate(parts):
        source = info[1 + d]

        @pl.when(source // seqs == info[0])
        def near():
            own[source % seqs] = part[...]

        @pl.when(source // seqs != info[0])
        def far():
            give[source % seqs] = part[...]


def route_back(at, parts):
    shape = (at.seqs, *parts[0].shape)
    return call(
        "route_back",
        functools.partial(route_back_body, at.seqs),
        [at.c, *[(at.a - d) % at.a_size for d in range(at.a_size)]],
        [(part, VMEM) for part in parts],
        [(shape, BF16, VMEM)] * 2,
    )


def add_body(counts, spots, *refs):
    terms = sum(counts)
    ins, outs, n = refs[:terms], refs[terms:], 0
    for count, out in zip(counts, outs):
        total = ins[n][...].astype(F32)
        for k in range(1, count):
            total = total + ins[n + k][...].astype(F32)
        out[...] = total.reshape(out.shape).astype(out.dtype)
        n += count


def add_blocks(groups, after=()):
    spots, inputs, outputs = [], [], []
    for terms in groups:
        for value, dim, index in terms:
            block = [1 if k == dim else size for k, size in enumerate(value.shape)]

            def spot(i, s, dim=dim, n=len(spots), rank=value.ndim):
                return tuple(s[n] if k == dim else 0 for k in range(rank))

            spots.append(index)
            inputs.append((value, pl.BlockSpec(tuple(block), spot)))
        shape = tuple(size for k, size in enumerate(value.shape) if k != dim)
        outputs.append((shape, BF16, VMEM))
    return call(
        "add_blocks",
        functools.partial(add_body, [len(terms) for terms in groups]),
        spots,
        inputs,
        outputs,
        after=after,
    )


def later(value, *done):
    return lax.optimization_barrier((value, *done))[0]


def pick(stacked, index, axis=0):
    return lax.dynamic_index_in_dim(stacked, index, axis, keepdims=False)


def by_order(own, others, axis_size, spot):
    moves = [(d, None, 0, (spot - d) % axis_size) for d in range(axis_size)]
    return shuffle([own, *others], [((axis_size, *own.shape), own.dtype)], moves)[0]


def heads_part_body(count, groups, info, query, key, value, vectors, *outs):
    width = query.shape[1] // count // groups
    rows = outs[0].shape[0]
    down = pl.ds(pl.multiple_of(info[len(outs)] * rows, rows), rows)
    for n, out in enumerate(outs):
        for peer in range(count):

            @pl.when(info[n] == peer)
            def copy():
                for g in range(groups):
                    for k, source in enumerate((query, key, value)):
                        spot = (g * 3 + k) * width
                        first = (peer * groups + g) * width
                        out[:, spot : spot + width] = source[down, first : first + width]

        out[:, 3 * groups * width :] = vectors[down, :]


def heads_parts(at, weights, vectors, groups):
    rows, model = weights[0].shape
    count = at.peer_count
    shape = (rows // at.x_split, 3 * model // count + vectors.shape[1])
    targets = [((at.b + db) % at.b_size) * CORES + at.c for db in range(at.b_size)]
    return call(
        "heads_parts",
        functools.partial(heads_part_body, count, groups),
        [*targets, at.x if at.x_split == 2 else 0],
        [(w, VMEM) for w in (*weights, vectors)],
        [(shape, BF16, VMEM)] * at.b_size,
    )


def quarter_body(info, *refs):
    out, sem = refs[3], refs[4]
    rows, half = out.shape[1:]
    down = pl.ds(pl.multiple_of(info[0] * rows, rows), rows)
    right = pl.ds(pl.multiple_of(info[1] * half, half), half)
    copies = [pltpu.make_async_copy(refs[w].at[down, right], out.at[w], sem.at[w]) for w in range(3)]
    for copy in copies:
        copy.start()
    for copy in copies:
        copy.wait()


def quarter_of(at, weights, after):
    rows, model = weights[0].shape
    return call(
        "quarter",
        quarter_body,
        [at.x if at.x_split == 2 else 0, at.c],
        [(w, VMEM) for w in weights],
        [((3, rows // at.x_split, model // CORES), BF16, ANY)],
        scratch=[pltpu.SemaphoreType.DMA((3,))],
        after=after,
    )[0]


def pad_body(heads, groups, a_size, info, *refs):
    split = (len(refs) - groups - 2) // a_size
    sources, outs = refs[: split * a_size], refs[split * a_size :]
    compact, (padded, vectors) = outs[:groups], outs[groups:]
    b_size, rows, width = sources[0].shape
    used = 3 * heads * HEAD_DIM
    part = heads // groups
    padded[...] = jnp.zeros_like(padded)
    for n in range(split):
        for d in range(a_size):
            for b in range(b_size):
                piece = sources[n * a_size + d][b]
                spot = (info[1 + d] * b_size + b) * split
                spot = (spot + (info[0] ^ n if split == 2 else 0)) * rows
                spot = pl.ds(pl.multiple_of(spot, rows), rows)
                for g in range(groups):
                    step = used // groups
                    compact[g][spot, :] = piece[:, g * step : (g + 1) * step]
                vectors[spot, :] = piece[:, used:]
                for k in range(3):
                    for h in range(heads):
                        first = (((h // part) * 3 + k) * part + h % part) * HEAD_DIM
                        lane = (k * heads + h) * LANES
                        padded[spot, lane : lane + HEAD_DIM] = piece[:, first : first + HEAD_DIM]


def pad_weights(at, sources, heads, groups, after):
    b_size, rows, width = sources[0].shape
    total = len(sources) * b_size * rows
    used = 3 * heads * HEAD_DIM
    return call(
        "pad_weights",
        functools.partial(pad_body, heads, groups, at.a_size),
        [at.x, *[(at.a - d) % at.a_size for d in range(at.a_size)]],
        [(source, VMEM) for source in sources],
        [
            *[((total, used // groups), BF16, VMEM)] * groups,
            ((total, 3 * heads * LANES), BF16, VMEM),
            ((total, width - used), BF16, VMEM),
        ],
        after=after,
        vmem=16,
    )


def project_body(count, spots, *refs):
    tokens, (gain, weight, bias, times, qkv, normed) = refs[:count], refs[count:]
    rows = tokens[0].shape[1]
    for p in range(count):
        value = tokens[p][0].astype(F32)
        rate = lax.rsqrt(jnp.mean(value * value, axis=-1, keepdims=True) + NORM_EPS)
        spot = pl.multiple_of(spots[p] * rows, rows)
        normed[pl.ds(spot, rows), :] = (value * rate * gain[...]).astype(BF16)
    step = qkv.shape[1] // 3
    for k in range(3):
        lanes = slice(k * step, (k + 1) * step)
        acc = dot(normed[...], weight[:, lanes])
        qkv[:, lanes] = ((acc + bias[:, lanes]) * times[:, lanes]).astype(BF16)


def project(at, parts, gain, weight, bias, times):
    a_size, half, model = parts[0].shape
    count = len(parts)
    cols = weight.shape[1]
    fixed = lambda a, s: (0, 0)
    return call(
        "project",
        functools.partial(project_body, count),
        [at.source(db, dc) for db, dc in at.peers()],
        [(part, pl.BlockSpec((1, half, model), lambda a, s: (a, 0, 0))) for part in parts]
        + [
            (gain, pl.BlockSpec((1, model), fixed)),
            (weight, pl.BlockSpec((model, cols), fixed)),
            (bias, pl.BlockSpec((1, cols), fixed)),
            (times, pl.BlockSpec((1, cols), fixed)),
        ],
        [
            (
                (a_size * count * half, cols),
                BF16,
                pl.BlockSpec((count * half, cols), lambda a, s: (a, 0)),
            ),
            (
                (a_size * count * half, model),
                BF16,
                pl.BlockSpec((count * half, model), lambda a, s: (a, 0)),
            ),
        ],
        grid=(a_size,),
    )


def forward_body(heads, block, info, starts, query, key, value, mixed, query_aug, total, top):
    index = pl.program_id(0)
    half = block // CORES
    core = info[pl.num_programs(0) + 1]
    total[...] = jnp.zeros_like(total)
    top[...] = jnp.full_like(top, MASK_FILL)
    rows = index * block + lax.broadcasted_iota(jnp.int32, (block, block), 0)
    begin = starts[...][:, :1]

    def step(j, carry):
        spot = pl.multiple_of(j * block, block)
        columns = spot + lax.broadcasted_iota(jnp.int32, (block, block), 1)
        bias = jnp.where((columns >= begin) & (columns <= rows), 0.0, MASK_FILL)
        lanes = [slice(h * LANES, (h + 1) * LANES) for h in range(heads)]
        scores = [dot(query[:, l], key[pl.ds(spot, block), l], 1, 1) + bias for l in lanes]
        olds = [top[h] for h in range(heads)]
        news = [
            jnp.maximum(old, jnp.max(score, axis=1, keepdims=True))
            for old, score in zip(olds, scores)
        ]
        weights = [
            jnp.exp(score - jnp.concatenate([new] * (block // LANES), axis=1)).astype(BF16)
            for score, new in zip(scores, news)
        ]
        for h in range(heads):
            total[h] = total[h] * jnp.exp(olds[h] - news[h]) + dot(
                weights[h], value[pl.ds(spot, block), lanes[h]]
            )
            top[h] = news[h]
        return carry

    lax.fori_loop(info[index], index + 1, step, 0)
    lane = lax.broadcasted_iota(jnp.int32, (block, LANES), 1)
    for h in range(heads):
        lanes = slice(h * LANES, (h + 1) * LANES)
        acc = total[h]
        weight_sum = acc[:, HEAD_DIM : HEAD_DIM + 1]
        result = (acc / weight_sum)[:, :HEAD_DIM].astype(BF16)
        for k in range(CORES):
            mixed[0, core ^ k, 0, :, h * HEAD_DIM : (h + 1) * HEAD_DIM] = result[
                k * half : (k + 1) * half
            ]
        rest = -(top[h] + jnp.log(weight_sum))
        aug = query[:, lanes].astype(F32)
        for k in range(3):
            term = rest.astype(BF16).astype(F32)
            aug = jnp.where(lane == HEAD_DIM + k, term, aug)
            rest = rest - term
        query_aug[:, lanes] = aug.astype(BF16)


def attend_forward(at, info, starts, qkv, heads, block):
    length = qkv.shape[0]
    wide = heads * LANES
    width = heads * HEAD_DIM
    count = length // block
    b_size = at.b_size
    return call(
        "attend_forward",
        functools.partial(forward_body, heads, block),
        info,
        [
            (starts, pl.BlockSpec((block, LANES), lambda i, s: (i, 0))),
            (qkv, pl.BlockSpec((block, wide), lambda i, s: (i, 0))),
            (qkv, pl.BlockSpec((length, wide), lambda i, s: (0, 1))),
            (qkv, pl.BlockSpec((length, wide), lambda i, s: (0, 2))),
        ],
        [
            (
                (b_size, CORES, at.a_size, block // CORES, width),
                BF16,
                pl.BlockSpec(
                    (1, CORES, 1, block // CORES, width),
                    lambda i, s: ((i + b_size - s[count]) % b_size, 0, i // b_size, 0, 0),
                ),
            ),
            ((length, wide), BF16, pl.BlockSpec((block, wide), lambda i, s: (i, 0))),
        ],
        grid=(count,),
        scratch=[
            pltpu.VMEM((heads, block, LANES), F32),
            pltpu.VMEM((heads, block, LANES), F32),
        ],
    )


def backward_body(
    heads,
    first,
    block,
    count,
    info,
    starts,
    scale,
    query,
    key,
    value,
    mixed,
    *rest,
):
    grad_refs = rest[:count]
    grads, scale_sum, bias_sum, grad, grad_aug, d_query, d_key, d_value = rest[count:]
    index = pl.num_programs(0) - 1 - pl.program_id(0)
    b_own, core = info[pl.num_programs(0)], info[pl.num_programs(0) + 1]
    b_size = count // CORES
    width = heads * HEAD_DIM

    @pl.when(pl.program_id(0) == 0)
    def clear():
        d_key[...] = jnp.zeros_like(d_key)
        d_value[...] = jnp.zeros_like(d_value)
        scale_sum[...] = jnp.zeros_like(scale_sum)
        bias_sum[...] = jnp.zeros_like(bias_sum)

    half = block // CORES
    lane = lax.broadcasted_iota(jnp.int32, (half, LANES), 1)
    for k in range(CORES):
        peer = ((b_own + b_size - index % b_size) % b_size) * CORES + (core ^ k)
        for p in range(count):

            @pl.when(peer == p)
            def fetch():
                grad[...] = grad_refs[p][index // b_size]

        for h in range(heads):
            part = slice((first + h) * HEAD_DIM, (first + h + 1) * HEAD_DIM)
            grad_h = grad[:, part].astype(F32)
            mixed_h = mixed[0, core ^ k, 0, :, part].astype(F32)
            delta = jnp.sum(grad_h * mixed_h, axis=1, keepdims=True)
            aug = jnp.concatenate([grad_h, jnp.zeros((half, LANES - HEAD_DIM), F32)], axis=1)
            high = (-delta).astype(BF16).astype(F32)
            aug = jnp.where(lane == HEAD_DIM, high, aug)
            aug = jnp.where(lane == HEAD_DIM + 1, -delta - high, aug)
            grad_aug[k * half : (k + 1) * half, h * LANES : (h + 1) * LANES] = aug.astype(BF16)
    d_query[...] = jnp.zeros_like(d_query)
    columns = index * block + lax.broadcasted_iota(jnp.int32, (block, block), 1)
    begin = starts[0:1, :]

    def step(j, carry):
        spot = pl.multiple_of(j * block, block)
        rows = spot + lax.broadcasted_iota(jnp.int32, (block, block), 0)
        allowed = (rows >= begin) & (rows <= columns)
        lanes = [slice(h * LANES, (h + 1) * LANES) for h in range(heads)]
        keys = [key[pl.ds(spot, block), l] for l in lanes]
        queries = [query[:, l] for l in lanes]
        grads_of = [grad_aug[:, l] for l in lanes]
        scores = [dot(k, q, 1, 1) for k, q in zip(keys, queries)]
        d_probs = [
            dot(value[pl.ds(spot, block), l], g, 1, 1) for l, g in zip(lanes, grads_of)
        ]
        probs = [jnp.where(allowed, jnp.exp(score), 0.0) for score in scores]
        d_scores = [(prob * d_prob).astype(BF16) for prob, d_prob in zip(probs, d_probs)]
        for h, l in enumerate(lanes):
            d_value[pl.ds(spot, block), l] += dot(probs[h].astype(BF16), grads_of[h])
            d_key[pl.ds(spot, block), l] += dot(d_scores[h], queries[h])
            d_query[:, l] += dot(d_scores[h], keys[h], 0, 0)
        return carry

    lax.fori_loop(info[index], index + 1, step, 0)
    here = pl.ds(pl.multiple_of(index * block, block), block)
    for h in range(heads):
        lanes = slice(h * LANES, (h + 1) * LANES)
        d_scaled = d_query[:, lanes].astype(BF16).astype(F32)
        scale_sum[...] += jnp.sum(d_scaled * query[:, lanes].astype(F32), axis=0, keepdims=True)
        d_q = (d_scaled * scale[0:1, lanes]).astype(BF16)
        for k, term in enumerate((d_q, d_key[here, lanes], d_value[here, lanes])):
            spot = k * width + h * HEAD_DIM
            term = term.astype(BF16)
            grads[:, spot : spot + HEAD_DIM] = term[:, :HEAD_DIM]
            bias_sum[:, (k * heads + h) * LANES : (k * heads + h + 1) * LANES] += jnp.sum(
                term.astype(F32), axis=0, keepdims=True
            )


def attend_backward(
    at, info, starts, scale, query_aug, qkv, grads, mixed, heads, groups, group, block
):
    length = qkv.shape[0]
    wide = heads * LANES
    width = heads * HEAD_DIM
    count = length // block
    b_size = at.b_size
    half = block // CORES

    def mixed_spot(i, s):
        i = count - 1 - i
        return (i + b_size - s[count]) % b_size, 0, i // b_size, 0, 0

    fixed = lambda i, s: (0, 0)
    return call(
        "attend_backward",
        functools.partial(backward_body, heads, group * heads, block, len(grads)),
        info,
        [
            (starts, pl.BlockSpec((8, block), lambda i, s: (0, count - 1 - i))),
            (scale, pl.BlockSpec((8, wide), fixed)),
            (query_aug, pl.BlockSpec((block, wide), lambda i, s: (count - 1 - i, group))),
            (qkv, pl.BlockSpec((length, wide), lambda i, s: (0, groups + group))),
            (qkv, pl.BlockSpec((length, wide), lambda i, s: (0, 2 * groups + group))),
            (mixed, pl.BlockSpec((1, CORES, 1, half, mixed.shape[4]), mixed_spot)),
        ]
        + [(grad, VMEM) for grad in grads],
        [
            (
                (length, 3 * width),
                BF16,
                pl.BlockSpec((block, 3 * width), lambda i, s: (count - 1 - i, 0)),
            ),
            ((8, LANES), F32, pl.BlockSpec((8, LANES), fixed)),
            ((8, 3 * wide), F32, pl.BlockSpec((8, 3 * wide), fixed)),
        ],
        grid=(count,),
        scratch=[
            pltpu.VMEM((half, mixed.shape[4]), BF16),
            pltpu.VMEM((block, wide), BF16),
            pltpu.VMEM((block, wide), F32),
            pltpu.VMEM((length, wide), F32),
            pltpu.VMEM((length, wide), F32),
        ],
    )


def concat_body(info, *refs):
    parts, out = refs[:-1], refs[-1]
    width = parts[0].shape[1]
    for p, part in enumerate(parts):
        out[:, p * width : (p + 1) * width] = part[...]


def concat(parts, after):
    rows, width = parts[0].shape
    return call(
        "concat",
        concat_body,
        [0],
        [(part, VMEM) for part in parts],
        [((rows, width * len(parts)), BF16, VMEM)],
        after=after,
    )[0]


def middle_body(count, source_count, moves, info, *refs):
    mixed, tokens, d_out, gain = refs[:4]
    sources = refs[4 : 4 + source_count]
    outs = refs[4 + source_count :]
    output, d_residual, d_proj, normed, activated, d_up = outs[:6]
    d_parts = outs[6:-4]
    weights, sems = outs[-4:-1], outs[-1]
    w_out, w_up, w_down = weights
    rows, half = sources[0].shape[2:]
    width = d_parts[0].shape[1]

    def copies(w):
        for n, (src, s, k) in enumerate(moves):
            if k == w:
                down = pl.ds(pl.multiple_of(info[2 * n] * rows, rows), rows)
                right = pl.ds(pl.multiple_of(info[2 * n + 1] * half, half), half)
                yield pltpu.make_async_copy(
                    sources[src].at[s, w], weights[w].at[down, right], sems.at[n]
                )

    def arrived(w):
        @pl.when(pl.program_id(0) == 0)
        def wait():
            for copy in copies(w):
                copy.wait()

    @pl.when(pl.program_id(0) == 0)
    def start():
        for w in range(3):
            for copy in copies(w):
                copy.start()

    arrived(0)
    residual = tokens[...].astype(F32) + dot(mixed[...], w_out[...])
    rate = lax.rsqrt(jnp.mean(residual * residual, axis=-1, keepdims=True) + NORM_EPS)
    normed[...] = (residual * rate * gain[...]).astype(BF16)
    arrived(1)
    upward = dot(normed[...], w_up[...])
    gate = 1.0 / (1.0 + jnp.exp(-upward))
    activated[...] = (upward * gate).astype(BF16)
    arrived(2)
    output[...] = (residual + dot(activated[...], w_down[...])).astype(BF16)
    d_activated = dot(d_out[...], w_down[...], 1, 1)
    d_up[...] = (d_activated * gate * (1 + upward * (1 - gate))).astype(BF16)
    scaled = dot(d_up[...], w_up[...], 1, 1) * gain[...]
    inner = jnp.mean(residual * scaled, axis=-1, keepdims=True)
    d_norm = rate * scaled - residual * (rate * rate * rate * inner)
    d_total = d_out[...].astype(F32) + d_norm
    d_residual[...] = d_total
    d_proj[...] = d_total.astype(BF16)
    d_mixed = dot(d_proj[...], w_out[...], 1, 1).astype(BF16)
    for p in range(count):
        d_parts[p][...] = d_mixed[:, p * width : (p + 1) * width]


def middle(at, mixed, tokens, d_out, gain, sources):
    count = at.peer_count
    rows, model = tokens.shape
    width = model // count
    arrays = list(sources.values())
    a_size, _, piece, half = arrays[0].shape
    group = model // at.peer_count // piece
    moves, spots = [], []
    for n, (dx, db, dc) in enumerate(sources):
        for a in range(a_size):
            for w in range(3):
                row = a * at.b_size + (at.b - db) % at.b_size
                if at.x_split == 2:
                    row = row * 2 + (at.x + dx) % 2
                if w == 0:
                    peer, rest = row // group, row % group
                    far = (at.b - peer // CORES) % at.b_size
                    row = (far * CORES + ((peer % CORES) ^ at.c)) * group + rest
                moves.append((n, a, w))
                spots += [row, (at.c + dc) % CORES]
    block = min(256, rows)
    row = lambda i, s: (i, 0)
    rows_of = pl.BlockSpec((block, model), row)
    part = pl.BlockSpec((block, width), row)
    types = [BF16, F32, BF16, BF16, BF16, BF16]
    return call(
        "middle",
        functools.partial(middle_body, count, len(arrays), moves),
        spots,
        [(mixed, rows_of), (tokens, rows_of), (d_out, rows_of)]
        + [(gain, pl.BlockSpec(gain.shape, lambda i, s: (0, 0)))]
        + [(source, ANY) for source in arrays],
        [((rows, model), kind, rows_of) for kind in types]
        + [((rows, width), BF16, part)] * count,
        grid=(rows // block,),
        scratch=[pltpu.VMEM((model, model), BF16)] * 3
        + [pltpu.SemaphoreType.DMA((len(moves),))],
    )


def outer_body(count, split, add, info, *refs):
    pairs, rest = refs[:6], refs[6:]
    for w in range(3):

        @pl.when(pl.program_id(0) == w)
        def product():
            value = dot(pairs[2 * w][...], pairs[2 * w + 1][...], 0, 0)
            target = rest[-1] if split else rest[-1].at[0]
            width = value.shape[0] // count
            for p in range(count):
                spot = p * width
                if w == 0:
                    spot = pl.multiple_of(info[3 + p] * width, width)
                part = value[p * width : (p + 1) * width]
                if add:
                    part = part + rest[0][0, pl.ds(spot, width)].astype(F32)
                target[pl.ds(spot, width)] = part.astype(BF16)

    if split:
        keep_x, give_x, keep_b, give_b, total = rest[1:]
        pairs_a, b_size, rows = keep_x.shape[1:4]
        for k in range(pairs_a):
            for b in range(b_size):
                for half, out in ((info[1], keep_x), (1 - info[1], give_x)):
                    spot = pl.multiple_of((k * b_size + b) * 2 * rows + half * rows, rows)
                    out[0, k, b] = total[pl.ds(spot, rows)]
            for b, out in ((info[2], keep_b), (1 - info[2], give_b)):
                for half in range(2):
                    spot = (((k + pairs_a) * b_size) * 2 + half) * rows + b * 2 * rows
                    out[0, k, half] = total[pl.ds(pl.multiple_of(spot, rows), rows)]


def outer(at, pairs, cols, add=None, after=()):
    rows, model = pairs[0][0].shape
    half = model // CORES
    count = at.peer_count
    split = add is not None and at.even
    info = [cols, at.x if at.even else 0, at.b, *[at.source(db, dc) for db, dc in at.peers()]]
    inputs = []
    for left, right in pairs:
        inputs.append((left, pl.BlockSpec((rows, model), lambda w, s: (0, 0))))
        inputs.append((right, pl.BlockSpec((rows, half), lambda w, s: (0, s[0]))))
    block = pl.BlockSpec((1, model, half), lambda w, s: (w, 0, 0))
    outputs = [((3, model, half), BF16, block)]
    scratch = []
    if add is not None:
        inputs.append((add, block))
    if split:
        shape = (at.a_size // 2, 2, model // at.a_size // 4, half)
        part = pl.BlockSpec((1, *shape), lambda w, s: (w, 0, 0, 0, 0))
        outputs = [((3, *shape), BF16, part)] * 4
        scratch = [pltpu.VMEM((model, half), BF16)]
    return call(
        "outer_give" if add is None else "outer",
        functools.partial(outer_body, count, split, add is not None),
        info,
        inputs,
        outputs,
        grid=(3,),
        scratch=scratch,
        after=after,
    )


def give_body(groups, info, *refs):
    grads, weights, out = refs[:groups], refs[groups : 2 * groups], refs[-1]
    value = back_product(grads, weights)
    out[0] = value.astype(BF16).reshape(out.shape[1:])


def back_product(grads, weights):
    total = 0.0
    for grad, weight in zip(grads, weights):
        total = total + dot(grad[...].reshape(-1, grad.shape[-1]), weight[...], 1, 1)
    return total


def keep_body(groups, info, *refs):
    grads, weights, got = refs[:groups], refs[groups : 2 * groups], refs[2 * groups]
    outs = refs[2 * groups + 1 :]
    b_size = got.shape[2]
    value = back_product(grads, weights).reshape(got.shape[1:]) + got[0].astype(F32)
    for b in range(b_size):
        for n, out in enumerate(outs):

            @pl.when(info[2 + n] == b)
            def copy():
                out[...] = value[:, b].astype(out.dtype)


def back_project_give(at, grads, weights, half):
    model = weights[0].shape[0]
    pair = at.a_size // 2
    width = grads[0].shape[1]
    shape = (pair, at.b_size, half, model)
    grads = [g.reshape(at.a_size, at.b_size, CORES, half, width) for g in grads]
    block = pl.BlockSpec((pair, at.b_size, 1, half, width), lambda i, s: (s[i], 0, s[2], 0, 0))
    core = 1 - at.c
    return call(
        "back_project",
        functools.partial(give_body, len(grads)),
        [core, 1 ^ core, core],
        [(g, block) for g in grads] + [(weight, VMEM) for weight in weights],
        [((2, *shape), BF16, pl.BlockSpec((1, *shape), lambda i, s: (i, 0, 0, 0, 0)))],
        grid=(2,),
    )[0]


def back_project_keep(at, grads, weights, half, which, got):
    model = weights[0].shape[0]
    pair = at.a_size // 2
    width = grads[0].shape[1]
    shape = (pair, at.b_size, half, model)
    grads = [g.reshape(at.a_size, at.b_size, CORES, half, width) for g in grads]
    block = pl.BlockSpec((pair, at.b_size, 1, half, width), lambda i, s: (s[0], 0, s[1], 0, 0))
    return call(
        "back_project",
        functools.partial(keep_body, len(grads)),
        [which ^ at.c, at.c, *ahead(at.b, at.b_size)],
        [(g, block) for g in grads]
        + [(weight, VMEM) for weight in weights]
        + [(got, pl.BlockSpec((1, *shape), lambda i, s: (which, 0, 0, 0, 0)))],
        [((pair, half, model), F32 if db == 0 else BF16, VMEM) for db in range(at.b_size)],
    )


def norm_back_body(count, info, *refs):
    own, others = refs[0], refs[1:count]
    tokens, d_residual, gain = refs[count : count + 3]
    for n, out in enumerate(refs[count + 3 :]):
        k = info[1 + n]
        grad = own[k]
        for other in others:
            grad = grad + other[k].astype(F32)
        value = tokens[k].astype(F32)
        rate = lax.rsqrt(jnp.mean(value * value, axis=-1, keepdims=True) + NORM_EPS)
        scaled = grad * gain[...]
        inner = jnp.mean(value * scaled, axis=-1, keepdims=True)
        d_norm = rate * scaled - value * (rate * rate * rate * inner)
        out[...] = (d_residual[k] + d_norm).astype(BF16)


def norm_back(at, terms, chunks, d_residual, gain, which):
    pair, half, model = terms[0].shape
    block = pl.BlockSpec((pair, half, model), lambda i, s: (s[0], 0, 0))
    order = [k ^ (at.a % pair) for k in range(pair)]
    return call(
        "norm_back",
        functools.partial(norm_back_body, len(terms)),
        [which ^ at.c, *order],
        [(t, VMEM) for t in terms] + [(chunks, block), (d_residual, block), (gain, VMEM)],
        [((half, model), BF16, VMEM)] * pair,
    )


def heads_outer_body(steps, info, normed, grads, extra, *rest):
    outs, acc = rest[:-1], rest[-1]
    value = dot(normed[...], grads[...], 0, 0)

    @pl.when(pl.program_id(0) == 0)
    def first():
        acc[...] = value

    @pl.when(pl.program_id(0) != 0)
    def later():
        acc[...] += value

    @pl.when(pl.program_id(0) == steps - 1)
    def last():
        used = acc.shape[1]
        pairs, b_size, rows = outs[0].shape[:3]
        split = len(outs)
        for n, out in enumerate(outs):
            for s in range(pairs * b_size):
                spot = (s * split + (info[0] ^ n if split == 2 else 0)) * rows
                spot = pl.ds(pl.multiple_of(spot, rows), rows)
                out[s // b_size, s % b_size, :, :used] = acc[spot, :].astype(BF16)
                out[s // b_size, s % b_size, :, used:] = extra[spot, :]


def heads_outer(at, normed, grads, extra):
    length, model = normed.shape
    used = grads.shape[1]
    block = min(512, length)
    steps = length // block
    rows = model // at.a_size // at.b_size // at.x_split
    shape = (at.a_size, at.b_size, rows, used + extra.shape[1])
    return call(
        "heads_outer",
        functools.partial(heads_outer_body, steps),
        [at.x],
        [
            (normed, pl.BlockSpec((block, model), lambda i, s: (i, 0))),
            (grads, pl.BlockSpec((block, used), lambda i, s: (i, 0))),
            (extra, pl.BlockSpec(extra.shape, lambda i, s: (0, 0))),
        ],
        [(shape, BF16, pl.BlockSpec(shape, lambda i, s: (0, 0, 0, 0)))] * at.x_split,
        grid=(steps,),
        scratch=[pltpu.VMEM((model, used), F32)],
    )


def all_sum(at, value, axis, size):
    total = value
    for d in range(1, size):
        total = total + at.send(value, **{axis: d}).astype(value.dtype)
    return total


def ahead(spot, size):
    return [(spot + d) % size for d in range(size)]


def cat_body(info, first, first_got, second, second_got, *outs):
    pair = first.shape[1]
    for d, out in enumerate(outs):
        spot = info[d] % pair

        @pl.when(info[d] < pair)
        def low():
            out[...] = (first[:, spot].astype(F32) + first_got[:, spot].astype(F32)).astype(BF16)

        @pl.when(info[d] >= pair)
        def high():
            out[...] = (second[:, spot].astype(F32) + second_got[:, spot].astype(F32)).astype(BF16)


class FullReduce:
    def __init__(self, at, parts):
        self.at = at
        if at.even:
            keep_x, give_x, keep_b, give_b = parts
            self.first = keep_x, at.send(give_x, dx=1)
            self.second = keep_b, at.send(give_b, db=1)
        else:
            self.part = parts[0].reshape(3, at.a_size, at.b_size, -1, parts[0].shape[-1])

    def next(self):
        at = self.at
        if not at.even:
            return
        groups = [[(t, 2, b) for t in self.first] for b in ahead(at.b, 2)]
        groups += [[(t, 2, x) for t in self.second] for x in ahead(at.x, 2)]
        keep_b, give_b, keep_x, give_x = add_blocks(groups)
        self.first = keep_b, at.send(give_b, db=1)
        self.second = keep_x, at.send(give_x, dx=1)

    def over_a(self):
        at = self.at
        if at.even:
            shape = self.first[0].shape
            parts = call(
                "cat",
                cat_body,
                ahead(at.a, at.a_size),
                [(t, VMEM) for t in (*self.first, *self.second)],
                [((3, *shape[2:]), BF16, VMEM)] * at.a_size,
            )
        else:
            parts = add_blocks([[(self.part, 1, a)] for a in ahead(at.a, at.a_size)])
        self.got = [parts[0]] + [at.send(parts[d], da=d) for d in range(1, at.a_size)]

    def end(self):
        at = self.at
        if at.even:
            part = add_blocks([[(t[None], 0, 0) for t in self.got]])[0]
            far = at.send(part, dx=1)
            return [part, far, at.send(part, dc=1), at.send(far, dc=1)]
        parts = add_blocks([[(t, 1, b) for t in self.got] for b in ahead(at.b, at.b_size)])
        got = [parts[0]] + [at.send(parts[d], db=d) for d in range(1, at.b_size)]
        part = add_blocks([[(t[None], 0, 0) for t in got]])[0]
        part = all_sum(at, part, "dx", at.x_size)
        return [part, at.send(part, dc=1)]


class HeadsReduce:
    def __init__(self, at, parts):
        self.at = at
        self.got = [parts[0]]
        if at.x_split == 2:
            self.got.append(at.send(parts[1], dx=1))

    def over_a(self, after=()):
        at = self.at
        groups = [[(t, 0, a) for t in self.got] for a in ahead(at.a, at.a_size)]
        parts = add_blocks(groups, after)
        self.got = [parts[0]] + [at.send(parts[d], da=d) for d in range(1, at.a_size)]
        return parts

    def by_b(self, after=()):
        at = self.at
        if at.x_split == 1:
            total = add_blocks([[(t[None], 0, 0) for t in self.got]])[0]
            self.got = [all_sum(at, total, "dx", at.x_size)]
        groups = [[(t, 0, b) for t in self.got] for b in ahead(at.b, at.b_size)]
        return add_blocks(groups, after)


def side_body(groups, info, *refs):
    for n, out in enumerate(refs[-(len(refs) // (groups + 1)) :]):
        for g in range(groups):
            out[g] = refs[n * groups + g][...]


def to_peers(at, groups):
    shape = (len(groups), *groups[0][0].shape)
    parts = call(
        "side",
        functools.partial(side_body, len(groups)),
        [0],
        [(group[b], VMEM) for b in range(at.b_size) for group in groups],
        [(shape, BF16, VMEM)] * at.b_size,
    )
    parts = [at.send(parts[db], db=db, dc=dc) if db or dc else parts[0] for db, dc in at.peers()]
    return parts


def in_order(info, refs, split, half, core, spot):
    near = [r[spot] for r in refs]
    if split == 2:
        near = [jnp.where(info[0] == half, near[2 * k], near[2 * k + 1]) for k in range(2)]
    return jnp.where(info[1] == core, near[0], near[1])


def finish_full_body(split, info, *refs):
    count = CORES * split
    parts, (weight, gain), outs = refs[:count], refs[count : count + 2], refs[count + 2 :]
    rows, half = parts[0].shape[1:]
    for x in range(split):
        spot = slice(x * rows, (x + 1) * rows)
        for w in range(3):
            for c in range(CORES):
                outs[w][spot, c * half : (c + 1) * half] = in_order(
                    info, parts, split, x, c, w
                ).astype(F32)
    total = jnp.sum(outs[1][...] * weight[...].astype(F32), axis=1, keepdims=True)
    outs[3][...] = total / gain[...].astype(F32)


def finish_full(at, parts, weight, gain, after):
    rows, model = weight.shape
    return call(
        "finish_full",
        functools.partial(finish_full_body, 2 if at.even else 1),
        [at.x, at.c],
        [(p, VMEM) for p in parts] + [(weight, VMEM), (gain[:, None], VMEM)],
        [((rows, model), F32, VMEM)] * 3 + [((rows, 1), F32, VMEM)],
        after=after,
    )


def finish_heads_body(count, split, info, *refs):
    parts, refs = refs[:count], refs[count:]
    far, refs = refs[: split - 1], refs[split - 1 :]
    weights, gain, outs = refs[:3], refs[3], refs[4:]
    few = outs[4].shape[1]
    groups, rows, width = parts[0].shape
    width = (width - few) // 3
    for n in range(split):
        down = pl.ds(pl.multiple_of((info[count] ^ n if split == 2 else 0) * rows, rows), rows)
        total = jnp.zeros((rows, few), F32)
        for p in range(count):
            for g in range(groups):
                source = far[0].at[p, g] if n else parts[p].at[g]
                total = total + source[:, 3 * width :].astype(F32)
                for peer in range(count):

                    @pl.when(info[p] == peer)
                    def copy():
                        for k in range(3):
                            spot = (peer * groups + g) * width
                            piece = source[:, k * width : (k + 1) * width]
                            outs[k][down, spot : spot + width] = piece.astype(F32)

        outs[4][down, :] = total
    total = jnp.zeros(outs[3].shape, F32)
    for k in range(3):
        total = total + jnp.sum(outs[k][...] * weights[k][...].astype(F32), axis=1, keepdims=True)
    outs[3][...] = total / gain[...].astype(F32)


def finish_heads(at, parts, weights, gain, few):
    rows, model = weights[0].shape
    flat = [*parts[0], *parts[1:]]
    return call(
        "finish_heads",
        functools.partial(finish_heads_body, at.peer_count, at.x_split),
        [*[at.source(db, dc) for db, dc in at.peers()], at.x],
        [(p, VMEM) for p in flat] + [(w, VMEM) for w in weights] + [(gain[:, None], VMEM)],
        [((rows, model), F32, VMEM)] * 3 + [((rows, 1), F32, VMEM), ((rows, few), F32, VMEM)],
    )


def local(
    reps,
    shards,
    activations,
    cotangent,
    doc_lengths,
    gain_attn,
    query_weight,
    query_bias,
    key_weight,
    value_weight,
    value_bias,
    dim_scale,
    out_weight,
    gain_mlp,
    up_weight,
    down_weight,
):
    seqs, tok_count, model = activations.shape
    at = Place(reps, shards, seqs)
    half = tok_count // CORES
    length = tok_count * shards
    peer_count = at.peer_count
    heads = model // HEAD_DIM // peer_count
    width = heads * HEAD_DIM
    wide = heads * LANES
    own_rows = at.a_size * half
    rows = gain_attn.shape[0]
    groups = 2
    block = CORES * half
    mine = at.b * CORES + at.c

    LAST.clear()
    stage = at.to_cluster(activations)
    next(stage)
    vectors = jnp.stack([gain_attn, gain_mlp, query_bias, value_bias], axis=1)
    own, *sent = heads_parts(at, (query_weight, key_weight, value_weight), vectors, groups)
    sent = [at.send(part, db=db + 1) for db, part in enumerate(sent)]
    next(stage)
    near = by_order(own, sent, at.b_size, at.b)
    sources = [near] + [at.send(near, da=d) for d in range(1, at.a_size)]
    if at.x_split == 2:
        sources += [at.send(source, dx=1) for source in sources]
    chunks = next(stage)
    parts = []
    early = sources[1 : at.a_size]
    if at.x_split == 2:
        early = [sources[2], sources[at.a_size + 1], sources[at.a_size + 3]]
    for db in range(at.b_size):
        near = at.send(chunks, db=db) if db else chunks
        ready = later(near, *early) if db else near
        parts += [near, at.send(ready, dc=1)]
    stage = at.to_cluster(cotangent)
    soon = [next(stage), at.send(doc_lengths, dc=1)]
    quarter = quarter_of(at, (out_weight, up_weight, down_weight), sources[1 : at.a_size])
    pieces = [quarter] + [at.send(quarter, da=d) for d in range(1, at.a_size)]
    *w_heads, w_pad, vectors = pad_weights(
        at, sources, heads, groups, [*parts[1:], *soon]
    )
    vectors = vectors.T.astype(F32)
    g_attn, g_mlp, b_query, b_value = vectors[0], vectors[1], vectors[2], vectors[3]

    other_lengths = soon[1]
    lengths = pick(jnp.where(at.c == at.a // seqs, doc_lengths, other_lengths), at.a % seqs)
    ends = jnp.cumsum(lengths)
    places = jnp.arange(length, dtype=jnp.int32)
    starts = jnp.max(jnp.where(ends[None, :] <= places[:, None], ends[None, :], 0), axis=1)
    starts_row = jnp.broadcast_to(starts[None, :], (8, length))
    starts_col = jnp.broadcast_to(starts[:, None], (length, LANES))
    info = jnp.concatenate([starts[::block] // block, jnp.stack([at.b, at.c])]).astype(jnp.int32)

    scale_dim = LOG_BASE / math.sqrt(HEAD_DIM) * jax.nn.softplus(dim_scale)
    scale_pad = jnp.tile(jnp.pad(scale_dim, (0, LANES - HEAD_DIM)), heads)
    lane = jnp.arange(LANES)
    ones_key = ((lane >= HEAD_DIM) & (lane < HEAD_DIM + 3)).astype(F32)
    ones_value = ((lane >= HEAD_DIM) & (lane < HEAD_DIM + 2)).astype(F32)

    def pad_heads(vec):
        part = lax.dynamic_slice_in_dim(vec, mine * width, width, 0).reshape(heads, HEAD_DIM)
        return jnp.pad(part, ((0, 0), (0, LANES - HEAD_DIM))).reshape(wide)

    bias_pad = jnp.concatenate(
        [
            pad_heads(b_query),
            jnp.tile(ones_key, heads),
            pad_heads(b_value) + jnp.tile(ones_value, heads),
        ]
    )
    times = jnp.concatenate([scale_pad, jnp.ones((2 * wide,), F32)])
    qkv, normed = project(at, parts, g_attn[None], w_pad, bias_pad[None], times[None])

    part_heads = heads // groups
    part_width = part_heads * HEAD_DIM
    moves = [(d, None, 0, (at.a - d) % at.a_size) for d in range(at.a_size)]
    quarter = shuffle(pieces, [((at.a_size, *quarter.shape), BF16)], moves)[0]
    others = {(0, 0, 0): quarter, (0, 0, 1): at.send(quarter, dc=1)}
    for db in range(1, at.b_size):
        others[(0, db, 0)] = at.send(quarter, db=db)
    if at.x_split == 2:
        others[(1, 0, 0)] = at.send(quarter, dx=1)
    stage.send([others[(0, 0, 1)]])
    mixed_rel, query_aug = attend_forward(at, info, starts_col, qkv, heads, block)
    d_out = next(stage).reshape(own_rows, model)
    if at.x_split == 2:
        for db in range(1, at.b_size):
            others[(1, db, 0)] = at.send(later(others[(0, db, 0)], d_out), dx=1)
    parts = []
    for db, dc in at.peers():
        part = later(mixed_rel[db, dc], d_out).reshape(own_rows, width)
        parts.append(at.send(part, db=db, dc=dc) if db or dc else part)
    mixed = concat(parts, [])
    for dx, db, dc in list(others):
        if (dx, db, 1) not in others:
            others[(dx, db, 1)] = at.send(later(others[(dx, db, 0)], mixed), dc=1)
    tokens = chunks.reshape(own_rows, model)
    output, d_residual, d_proj, normed_mlp, activated, d_up, *d_parts = middle(
        at, mixed, tokens, d_out, g_mlp[None], others
    )

    grads = []
    for (db, dc), part in zip(at.peers(), d_parts):
        part = at.send(part, db=db, dc=dc) if db or dc else part
        grads.append(part.reshape(at.a_size, half, width))

    pairs = [(mixed, d_proj), (normed_mlp, d_up), (activated, d_out)]
    give = outer(at, pairs, 1 - at.c)[0]
    full = FullReduce(at, outer(at, pairs, at.c, at.send(give, dc=1), grads))

    scale_rows = jnp.broadcast_to(scale_pad[None, : part_heads * LANES], (8, part_heads * LANES))
    zeros = jnp.zeros((model,), F32)

    def backward(g):
        d_heads, scale_sum, bias_sum = attend_backward(
            at,
            info,
            starts_row,
            scale_rows,
            query_aug,
            qkv,
            grads,
            mixed_rel,
            part_heads,
            groups,
            g,
            block,
        )
        bias_sum = bias_sum[0].reshape(3, part_heads, LANES)[:, :, :HEAD_DIM]
        bias_sum = bias_sum.reshape(3, part_width)
        spot = (mine * groups + g) * part_width
        scale_sum = jnp.pad(scale_sum[0, :HEAD_DIM], (0, rows - HEAD_DIM))
        extra = [
            lax.dynamic_update_slice(zeros, bias_sum[0], (spot,)),
            lax.dynamic_update_slice(zeros, bias_sum[2], (spot,)),
            jnp.tile(scale_sum, shards),
        ]
        return d_heads, jnp.stack(extra, axis=1).astype(BF16)

    stage = at.from_cluster(output.reshape(at.a_size, half, model))
    next(stage)
    d_first, extra_first = backward(0)
    output_got = next(stage)
    full.next()
    reduce_first = HeadsReduce(at, heads_outer(at, normed, d_first, extra_first))
    full.over_a()
    d_second, extra_second = backward(1)
    full_parts = full.end()
    reduce_first.over_a()

    d_heads = [d_first, d_second]
    keeps, received = [], []
    residual_chunks = d_residual.reshape(at.a_size, half, model)

    def keep(which, got):
        terms = back_project_keep(at, d_heads, w_heads, half, which, got)
        keeps.append([terms[0]] + [at.send(terms[db], db=db) for db in range(1, at.b_size)])

    def back(which):
        sent = norm_back(at, keeps[which], chunks, residual_chunks, g_attn[None], which)
        for k, part in enumerate(sent):
            received.append(at.send_back(part, which * len(sent) + k))
        return sent

    got = at.send(back_project_give(at, d_heads, w_heads, half), dc=1)
    reduce_second = HeadsReduce(at, heads_outer(at, normed, d_second, extra_second))
    first = reduce_first.by_b([full_parts[1], output_got])
    keep(0, got)
    keep(1, got)
    reduce_second.over_a(full_parts[2:])
    back(0)
    parts = [to_peers(at, [first, reduce_second.by_b(keeps[1][1:])])]
    sent = back(1)
    if at.x_split == 2:
        parts.append(at.send(later(jnp.stack(parts[0]), sent[0]), dx=1))
    *grads_full, grad_gain_mlp = finish_full(at, full_parts, up_weight, gain_mlp, [])
    output = next(stage)
    weights = (query_weight, key_weight, value_weight)
    *grads_heads, grad_gain_attn, few = finish_heads(at, parts, weights, gain_attn, 3)
    input_grad = at.place_back(received)
    grad_scale = few[:HEAD_DIM, 2] / scale_dim * (LOG_BASE / math.sqrt(HEAD_DIM))
    grad_scale = grad_scale * jax.nn.sigmoid(dim_scale)
    return (
        output,
        input_grad,
        grad_gain_attn[:, 0],
        grads_heads[0],
        few[:, 0],
        grads_heads[1],
        grads_heads[2],
        few[:, 1],
        grad_scale,
        grads_full[0],
        grad_gain_mlp[:, 0],
        grads_full[1],
        grads_full[2],
    )


def solution(mesh):
    in_specs = (
        P("rep", "shard", None),
        P("rep", "shard", None),
        P("rep", None),
        P("shard"),
        P("shard", None),
        P("shard"),
        P("shard", None),
        P("shard", None),
        P("shard"),
        P(),
        P("shard", None),
        P("shard"),
        P("shard", None),
        P("shard", None),
    )
    out_specs = (
        P("rep", "shard", None),
        P("rep", "shard", None),
        P("shard"),
        P("shard", None),
        P("shard"),
        P("shard", None),
        P("shard", None),
        P("shard"),
        P(),
        P("shard", None),
        P("shard"),
        P("shard", None),
        P("shard", None),
    )
    body = functools.partial(local, mesh.shape["rep"], mesh.shape["shard"])
    return jax.shard_map(body, mesh=mesh, in_specs=in_specs, out_specs=out_specs, check_vma=False)
```

```python
import functools
import math

import jax
import jax.numpy as jnp
from jax import lax
from jax.experimental import pallas as pl
from jax.experimental.pallas import tpu as pltpu
from jax.sharding import PartitionSpec as P

HEAD_DIM = 80
LANES = 128
CORES = 2
NORM_EPS = 1e-06
LOG_BASE = 1.442695041
MASK_FILL = -1e30
AXES = ("rep", "shard")
F32 = jnp.float32
BF16 = jnp.bfloat16


def dot(left, right, left_dim=1, right_dim=0):
    return lax.dot_general(
        left, right, (((left_dim,), (right_dim,)), ((), ())), preferred_element_type=F32
    )


class Place:
    def __init__(self, reps, shards, seqs):
        self.x_size = reps // CORES
        self.x_split = 2 if self.x_size == 2 else 1
        self.a_size = CORES * seqs
        self.b_size = shards // self.a_size
        self.even = self.x_size == 2 and self.b_size == 2
        self.peer_count = self.b_size * CORES
        self.seqs = seqs
        rep, shard = lax.axis_index("rep"), lax.axis_index("shard")
        self.x, self.c = rep // CORES, rep % CORES
        self.a, self.b = shard // self.b_size, shard % self.b_size
        self.shard = shard

    def route(self, move):
        pairs = []
        for x in range(self.x_size):
            for c in range(CORES):
                for a in range(self.a_size):
                    for b in range(self.b_size):
                        pairs.append((self.number(x, c, a, b), self.number(*move(x, c, a, b))))
        return pairs

    def number(self, x, c, a, b):
        return ((x * CORES + c) * self.a_size + a) * self.b_size + b

    def send(self, value, dx=0, dc=0, da=0, db=0):
        return lax.ppermute(
            value,
            AXES,
            self.route(
                lambda x, c, a, b: (
                    (x + dx) % self.x_size,
                    (c + dc) % CORES,
                    (a + da) % self.a_size,
                    (b + db) % self.b_size,
                )
            ),
        )

    def peers(self):
        return [(db, dc) for db in range(self.b_size) for dc in range(CORES)]

    def source(self, db, dc):
        return ((self.b - db) % self.b_size) * CORES + (self.c + dc) % CORES

    def to_cluster(self, tokens, after=()):
        seqs, count, width = tokens.shape
        half = count // CORES
        halves = tokens.reshape(seqs, CORES, half, width)
        shape = (seqs, half, width)
        moves = []
        for i in range(seqs):
            moves += [(0, (i, self.c), 0, i), (0, (i, 1 - self.c), 1, i)]
        own, give = shuffle([halves], [(shape, BF16)] * 2, moves, after)
        got = self.send(give, dc=1)
        after = yield got
        parts = route_parts(self, own, got, after or ())
        received = [parts[0]] + [self.send(parts[d], da=d) for d in range(1, self.a_size)]
        moves = [(d, None, 0, (self.a - d) % self.a_size) for d in range(self.a_size)]
        after = yield
        yield shuffle(received, [((self.a_size, half, width), BF16)], moves, after or ())[0]

    def from_cluster(self, chunks):
        half, width = chunks.shape[1:]
        picks = [(0, (self.a + d) % self.a_size, d, None) for d in range(self.a_size)]
        parts = shuffle([chunks], [((half, width), BF16)] * self.a_size, picks)
        received = [parts[0]] + [self.send(parts[d], da=d) for d in range(1, self.a_size)]
        yield
        own, give = route_back(self, received)
        got = self.send(give, dc=1)
        moves = []
        for i in range(self.seqs):
            moves += [(0, i, 0, i * CORES + self.c), (1, i, 0, i * CORES + 1 - self.c)]
        yield
        whole = shuffle([own, got], [((self.a_size, half, width), BF16)], moves)[0]
        yield whole.reshape(self.seqs, CORES * half, width)

    def send_back(self, part, m):
        return lax.ppermute(part, AXES, [(j, i) for i, j in self.route(self._match(m))])

    def place_back(self, received):
        half, width = received[0].shape
        moves = []
        for m in range(self.a_size):
            t = m ^ self.a
            moves.append((m, None, 0, (t % self.seqs) * CORES + t // self.seqs))
        whole = shuffle(received, [((self.a_size, half, width), BF16)], moves)[0]
        return whole.reshape(self.seqs, CORES * half, width)

    def _match(self, m):
        def move(x, c, a, b):
            t = m ^ a
            return x, t // self.seqs, self.seqs * c + t % self.seqs, b

        return move


VMEM = pl.BlockSpec(memory_space=pltpu.VMEM)
ANY = pl.BlockSpec(memory_space=pl.ANY)


LAST = []
SCALE = 0.25
SIZE = {
    "project": 28,
    "attend_forward": 60,
    "middle": 48,
    "outer": 60,
    "outer_give": 60,
    "attend_backward": 60,
    "heads_outer": 24,
    "back_project": 20,
    "finish_heads": 16,
    "finish_full": 16,
}
COST = {
    "project": 14.5,
    "attend_forward": 12.0,
    "middle": 20.0,
    "outer": 7.0,
    "outer_give": 0.1,
    "attend_backward": 25.0,
    "heads_outer": 5.5,
    "back_project": 3.5,
    "pad_weights": 3.5,
    "norm_back": 3.0,
    "finish_heads": 4.0,
    "finish_full": 3.5,
}


def call(name, body, scalars, inputs, outputs, grid=(1,), scratch=(), after=(), vmem=0):
    deps = [*LAST[-1:], *after]
    count, skip = len(inputs), len(deps)

    def run(spots, *refs):
        body(spots, *refs[:count], *refs[count + skip :])

    results = pl.pallas_call(
        run,
        out_shape=[jax.ShapeDtypeStruct(shape, kind) for shape, kind, _ in outputs],
        grid_spec=pltpu.PrefetchScalarGridSpec(
            num_scalar_prefetch=1,
            grid=grid,
            in_specs=[spec for _, spec in inputs] + [ANY] * skip,
            out_specs=[spec for _, _, spec in outputs],
            scratch_shapes=list(scratch),
        ),
        cost_estimate=pl.CostEstimate(
            flops=int(COST.get(name, 1.5) * SCALE * 1.1e9),
            bytes_accessed=int(COST.get(name, 1.5) * SCALE * 3.3e6),
            transcendentals=0,
        ),
        compiler_params=pltpu.CompilerParams(vmem_limit_bytes=(vmem or SIZE.get(name, 12)) * 1024 * 1024),
        name=name,
    )(scalars_of(scalars), *[value for value, _ in inputs], *deps)
    LAST.append(results[0])
    return results


def scalars_of(values):
    if isinstance(values, (list, tuple)):
        return jnp.stack([jnp.asarray(v, jnp.int32) for v in values])
    return values


def shuffle_body(moves, counts, spots, *refs):
    sources, targets, sems = refs[: counts[0]], refs[counts[0] : -1], refs[-1]
    copies, n = [], 0
    for src, src_rank, dst, dst_rank in moves:
        ends = []
        for ref, rank in ((sources[src], src_rank), (targets[dst], dst_rank)):
            ends.append(ref.at[tuple(spots[n + k] for k in range(rank))] if rank else ref)
            n += rank
        copies.append(pltpu.make_async_copy(*ends, sems.at[len(copies)]))
    for copy in copies:
        copy.start()
    for copy in copies:
        copy.wait()


def shuffle(sources, shapes, moves, after=()):
    spots, shape_of = [], []
    for src, src_spot, dst, dst_spot in moves:
        ranks = []
        for spot in (src_spot, dst_spot):
            spot = () if spot is None else spot if isinstance(spot, tuple) else (spot,)
            ranks.append(len(spot))
            spots += spot
        shape_of.append((src, ranks[0], dst, ranks[1]))
    return call(
        "shuffle",
        functools.partial(shuffle_body, shape_of, (len(sources), len(shapes))),
        spots or [0],
        [(source, VMEM) for source in sources],
        [(*shape, ANY) for shape in shapes],
        scratch=[pltpu.SemaphoreType.DMA((len(moves),))],
        after=after,
    )


def route_parts_body(seqs, info, own, got, *outs):
    for d, out in enumerate(outs):
        target = info[1 + d]

        @pl.when(target // seqs == info[0])
        def near():
            out[...] = own[target % seqs]

        @pl.when(target // seqs != info[0])
        def far():
            out[...] = got[target % seqs]


def route_parts(at, own, got, after=()):
    return call(
        "route_parts",
        functools.partial(route_parts_body, at.seqs),
        [at.c, *ahead(at.a, at.a_size)],
        [(own, VMEM), (got, VMEM)],
        [(own.shape[1:], BF16, VMEM)] * at.a_size,
        after=after,
    )


def route_back_body(seqs, info, *refs):
    parts, own, give = refs[:-2], refs[-2], refs[-1]
    for d, part in enumerate(parts):
        source = info[1 + d]

        @pl.when(source // seqs == info[0])
        def near():
            own[source % seqs] = part[...]

        @pl.when(source // seqs != info[0])
        def far():
            give[source % seqs] = part[...]


def route_back(at, parts):
    shape = (at.seqs, *parts[0].shape)
    return call(
        "route_back",
        functools.partial(route_back_body, at.seqs),
        [at.c, *[(at.a - d) % at.a_size for d in range(at.a_size)]],
        [(part, VMEM) for part in parts],
        [(shape, BF16, VMEM)] * 2,
    )


def add_body(counts, spots, *refs):
    terms = sum(counts)
    ins, outs, n = refs[:terms], refs[terms:], 0
    for count, out in zip(counts, outs):
        total = ins[n][...].astype(F32)
        for k in range(1, count):
            total = total + ins[n + k][...].astype(F32)
        out[...] = total.reshape(out.shape).astype(out.dtype)
        n += count


def add_blocks(groups, after=()):
    spots, inputs, outputs = [], [], []
    for terms in groups:
        for value, dim, index in terms:
            block = [1 if k == dim else size for k, size in enumerate(value.shape)]

            def spot(i, s, dim=dim, n=len(spots), rank=value.ndim):
                return tuple(s[n] if k == dim else 0 for k in range(rank))

            spots.append(index)
            inputs.append((value, pl.BlockSpec(tuple(block), spot)))
        shape = tuple(size for k, size in enumerate(value.shape) if k != dim)
        outputs.append((shape, BF16, VMEM))
    return call(
        "add_blocks",
        functools.partial(add_body, [len(terms) for terms in groups]),
        spots,
        inputs,
        outputs,
        after=after,
    )


def later(value, *done):
    return lax.optimization_barrier((value, *done))[0]


def pick(stacked, index, axis=0):
    return lax.dynamic_index_in_dim(stacked, index, axis, keepdims=False)


def by_order(own, others, axis_size, spot):
    moves = [(d, None, 0, (spot - d) % axis_size) for d in range(axis_size)]
    return shuffle([own, *others], [((axis_size, *own.shape), own.dtype)], moves)[0]


def heads_part_body(count, groups, info, query, key, value, vectors, *outs):
    width = query.shape[1] // count // groups
    rows = outs[0].shape[0]
    down = pl.ds(pl.multiple_of(info[len(outs)] * rows, rows), rows)
    for n, out in enumerate(outs):
        for peer in range(count):

            @pl.when(info[n] == peer)
            def copy():
                for g in range(groups):
                    for k, source in enumerate((query, key, value)):
                        spot = (g * 3 + k) * width
                        first = (peer * groups + g) * width
                        out[:, spot : spot + width] = source[down, first : first + width]

        out[:, 3 * groups * width :] = vectors[down, :]


def heads_parts(at, weights, vectors, groups):
    rows, model = weights[0].shape
    count = at.peer_count
    shape = (rows // at.x_split, 3 * model // count + vectors.shape[1])
    targets = [((at.b + db) % at.b_size) * CORES + at.c for db in range(at.b_size)]
    return call(
        "heads_parts",
        functools.partial(heads_part_body, count, groups),
        [*targets, at.x if at.x_split == 2 else 0],
        [(w, VMEM) for w in (*weights, vectors)],
        [(shape, BF16, VMEM)] * at.b_size,
    )


def quarter_body(info, *refs):
    out, sem = refs[3], refs[4]
    rows, half = out.shape[1:]
    down = pl.ds(pl.multiple_of(info[0] * rows, rows), rows)
    right = pl.ds(pl.multiple_of(info[1] * half, half), half)
    copies = [pltpu.make_async_copy(refs[w].at[down, right], out.at[w], sem.at[w]) for w in range(3)]
    for copy in copies:
        copy.start()
    for copy in copies:
        copy.wait()


def quarter_of(at, weights, after):
    rows, model = weights[0].shape
    return call(
        "quarter",
        quarter_body,
        [at.x if at.x_split == 2 else 0, at.c],
        [(w, VMEM) for w in weights],
        [((3, rows // at.x_split, model // CORES), BF16, ANY)],
        scratch=[pltpu.SemaphoreType.DMA((3,))],
        after=after,
    )[0]


def pad_body(heads, groups, a_size, info, *refs):
    split = (len(refs) - groups - 2) // a_size
    sources, outs = refs[: split * a_size], refs[split * a_size :]
    compact, (padded, vectors) = outs[:groups], outs[groups:]
    b_size, rows, width = sources[0].shape
    used = 3 * heads * HEAD_DIM
    part = heads // groups
    padded[...] = jnp.zeros_like(padded)
    for n in range(split):
        for d in range(a_size):
            for b in range(b_size):
                piece = sources[n * a_size + d][b]
                spot = (info[1 + d] * b_size + b) * split
                spot = (spot + (info[0] ^ n if split == 2 else 0)) * rows
                spot = pl.ds(pl.multiple_of(spot, rows), rows)
                for g in range(groups):
                    step = used // groups
                    compact[g][spot, :] = piece[:, g * step : (g + 1) * step]
                vectors[spot, :] = piece[:, used:]
                for k in range(3):
                    for h in range(heads):
                        first = (((h // part) * 3 + k) * part + h % part) * HEAD_DIM
                        lane = (k * heads + h) * LANES
                        padded[spot, lane : lane + HEAD_DIM] = piece[:, first : first + HEAD_DIM]


def pad_weights(at, sources, heads, groups, after):
    b_size, rows, width = sources[0].shape
    total = len(sources) * b_size * rows
    used = 3 * heads * HEAD_DIM
    return call(
        "pad_weights",
        functools.partial(pad_body, heads, groups, at.a_size),
        [at.x, *[(at.a - d) % at.a_size for d in range(at.a_size)]],
        [(source, VMEM) for source in sources],
        [
            *[((total, used // groups), BF16, VMEM)] * groups,
            ((total, 3 * heads * LANES), BF16, VMEM),
            ((total, width - used), BF16, VMEM),
        ],
        after=after,
        vmem=16,
    )


def project_body(count, spots, *refs):
    tokens, (gain, weight, bias, times, qkv, normed) = refs[:count], refs[count:]
    rows = tokens[0].shape[1]
    for p in range(count):
        value = tokens[p][0].astype(F32)
        rate = lax.rsqrt(jnp.mean(value * value, axis=-1, keepdims=True) + NORM_EPS)
        spot = pl.multiple_of(spots[p] * rows, rows)
        normed[pl.ds(spot, rows), :] = (value * rate * gain[...]).astype(BF16)
    step = qkv.shape[1] // 3
    for k in range(3):
        lanes = slice(k * step, (k + 1) * step)
        acc = dot(normed[...], weight[:, lanes])
        qkv[:, lanes] = ((acc + bias[:, lanes]) * times[:, lanes]).astype(BF16)


def project(at, parts, gain, weight, bias, times):
    a_size, half, model = parts[0].shape
    count = len(parts)
    cols = weight.shape[1]
    fixed = lambda a, s: (0, 0)
    return call(
        "project",
        functools.partial(project_body, count),
        [at.source(db, dc) for db, dc in at.peers()],
        [(part, pl.BlockSpec((1, half, model), lambda a, s: (a, 0, 0))) for part in parts]
        + [
            (gain, pl.BlockSpec((1, model), fixed)),
            (weight, pl.BlockSpec((model, cols), fixed)),
            (bias, pl.BlockSpec((1, cols), fixed)),
            (times, pl.BlockSpec((1, cols), fixed)),
        ],
        [
            (
                (a_size * count * half, cols),
                BF16,
                pl.BlockSpec((count * half, cols), lambda a, s: (a, 0)),
            ),
            (
                (a_size * count * half, model),
                BF16,
                pl.BlockSpec((count * half, model), lambda a, s: (a, 0)),
            ),
        ],
        grid=(a_size,),
    )


def forward_body(heads, block, info, starts, query, key, value, mixed, query_aug, total, top):
    index = pl.program_id(0)
    half = block // CORES
    core = info[pl.num_programs(0) + 1]
    total[...] = jnp.zeros_like(total)
    top[...] = jnp.full_like(top, MASK_FILL)
    rows = index * block + lax.broadcasted_iota(jnp.int32, (block, block), 0)
    begin = starts[...][:, :1]

    def step(j, carry):
        spot = pl.multiple_of(j * block, block)
        columns = spot + lax.broadcasted_iota(jnp.int32, (block, block), 1)
        bias = jnp.where((columns >= begin) & (columns <= rows), 0.0, MASK_FILL)
        lanes = [slice(h * LANES, (h + 1) * LANES) for h in range(heads)]
        scores = [dot(query[:, l], key[pl.ds(spot, block), l], 1, 1) + bias for l in lanes]
        olds = [top[h] for h in range(heads)]
        news = [
            jnp.maximum(old, jnp.max(score, axis=1, keepdims=True))
            for old, score in zip(olds, scores)
        ]
        weights = [
            jnp.exp(score - jnp.concatenate([new] * (block // LANES), axis=1)).astype(BF16)
            for score, new in zip(scores, news)
        ]
        for h in range(heads):
            total[h] = total[h] * jnp.exp(olds[h] - news[h]) + dot(
                weights[h], value[pl.ds(spot, block), lanes[h]]
            )
            top[h] = news[h]
        return carry

    lax.fori_loop(info[index], index + 1, step, 0)
    lane = lax.broadcasted_iota(jnp.int32, (block, LANES), 1)
    for h in range(heads):
        lanes = slice(h * LANES, (h + 1) * LANES)
        acc = total[h]
        weight_sum = acc[:, HEAD_DIM : HEAD_DIM + 1]
        result = (acc / weight_sum)[:, :HEAD_DIM].astype(BF16)
        for k in range(CORES):
            mixed[0, core ^ k, 0, :, h * HEAD_DIM : (h + 1) * HEAD_DIM] = result[
                k * half : (k + 1) * half
            ]
        rest = -(top[h] + jnp.log(weight_sum))
        aug = query[:, lanes].astype(F32)
        for k in range(3):
            term = rest.astype(BF16).astype(F32)
            aug = jnp.where(lane == HEAD_DIM + k, term, aug)
            rest = rest - term
        query_aug[:, lanes] = aug.astype(BF16)


def attend_forward(at, info, starts, qkv, heads, block):
    length = qkv.shape[0]
    wide = heads * LANES
    width = heads * HEAD_DIM
    count = length // block
    b_size = at.b_size
    return call(
        "attend_forward",
        functools.partial(forward_body, heads, block),
        info,
        [
            (starts, pl.BlockSpec((block, LANES), lambda i, s: (i, 0))),
            (qkv, pl.BlockSpec((block, wide), lambda i, s: (i, 0))),
            (qkv, pl.BlockSpec((length, wide), lambda i, s: (0, 1))),
            (qkv, pl.BlockSpec((length, wide), lambda i, s: (0, 2))),
        ],
        [
            (
                (b_size, CORES, at.a_size, block // CORES, width),
                BF16,
                pl.BlockSpec(
                    (1, CORES, 1, block // CORES, width),
                    lambda i, s: ((i + b_size - s[count]) % b_size, 0, i // b_size, 0, 0),
                ),
            ),
            ((length, wide), BF16, pl.BlockSpec((block, wide), lambda i, s: (i, 0))),
        ],
        grid=(count,),
        scratch=[
            pltpu.VMEM((heads, block, LANES), F32),
            pltpu.VMEM((heads, block, LANES), F32),
        ],
    )


def backward_body(
    heads,
    first,
    block,
    count,
    info,
    starts,
    scale,
    query,
    key,
    value,
    mixed,
    *rest,
):
    grad_refs = rest[:count]
    grads, scale_sum, bias_sum, grad, grad_aug, d_query, d_key, d_value = rest[count:]
    index = pl.num_programs(0) - 1 - pl.program_id(0)
    b_own, core = info[pl.num_programs(0)], info[pl.num_programs(0) + 1]
    b_size = count // CORES
    width = heads * HEAD_DIM

    @pl.when(pl.program_id(0) == 0)
    def clear():
        d_key[...] = jnp.zeros_like(d_key)
        d_value[...] = jnp.zeros_like(d_value)
        scale_sum[...] = jnp.zeros_like(scale_sum)
        bias_sum[...] = jnp.zeros_like(bias_sum)

    half = block // CORES
    lane = lax.broadcasted_iota(jnp.int32, (half, LANES), 1)
    for k in range(CORES):
        peer = ((b_own + b_size - index % b_size) % b_size) * CORES + (core ^ k)
        for p in range(count):

            @pl.when(peer == p)
            def fetch():
                grad[...] = grad_refs[p][index // b_size]

        for h in range(heads):
            part = slice((first + h) * HEAD_DIM, (first + h + 1) * HEAD_DIM)
            grad_h = grad[:, part].astype(F32)
            mixed_h = mixed[0, core ^ k, 0, :, part].astype(F32)
            delta = jnp.sum(grad_h * mixed_h, axis=1, keepdims=True)
            aug = jnp.concatenate([grad_h, jnp.zeros((half, LANES - HEAD_DIM), F32)], axis=1)
            high = (-delta).astype(BF16).astype(F32)
            aug = jnp.where(lane == HEAD_DIM, high, aug)
            aug = jnp.where(lane == HEAD_DIM + 1, -delta - high, aug)
            grad_aug[k * half : (k + 1) * half, h * LANES : (h + 1) * LANES] = aug.astype(BF16)
    d_query[...] = jnp.zeros_like(d_query)
    columns = index * block + lax.broadcasted_iota(jnp.int32, (block, block), 1)
    begin = starts[0:1, :]

    def step(j, carry):
        spot = pl.multiple_of(j * block, block)
        rows = spot + lax.broadcasted_iota(jnp.int32, (block, block), 0)
        allowed = (rows >= begin) & (rows <= columns)
        lanes = [slice(h * LANES, (h + 1) * LANES) for h in range(heads)]
        keys = [key[pl.ds(spot, block), l] for l in lanes]
        queries = [query[:, l] for l in lanes]
        grads_of = [grad_aug[:, l] for l in lanes]
        scores = [dot(k, q, 1, 1) for k, q in zip(keys, queries)]
        d_probs = [
            dot(value[pl.ds(spot, block), l], g, 1, 1) for l, g in zip(lanes, grads_of)
        ]
        probs = [jnp.where(allowed, jnp.exp(score), 0.0) for score in scores]
        d_scores = [(prob * d_prob).astype(BF16) for prob, d_prob in zip(probs, d_probs)]
        for h, l in enumerate(lanes):
            d_value[pl.ds(spot, block), l] += dot(probs[h].astype(BF16), grads_of[h])
            d_key[pl.ds(spot, block), l] += dot(d_scores[h], queries[h])
            d_query[:, l] += dot(d_scores[h], keys[h], 0, 0)
        return carry

    lax.fori_loop(info[index], index + 1, step, 0)
    here = pl.ds(pl.multiple_of(index * block, block), block)
    for h in range(heads):
        lanes = slice(h * LANES, (h + 1) * LANES)
        d_scaled = d_query[:, lanes].astype(BF16).astype(F32)
        scale_sum[...] += jnp.sum(d_scaled * query[:, lanes].astype(F32), axis=0, keepdims=True)
        d_q = (d_scaled * scale[0:1, lanes]).astype(BF16)
        for k, term in enumerate((d_q, d_key[here, lanes], d_value[here, lanes])):
            spot = k * width + h * HEAD_DIM
            term = term.astype(BF16)
            grads[:, spot : spot + HEAD_DIM] = term[:, :HEAD_DIM]
            bias_sum[:, (k * heads + h) * LANES : (k * heads + h + 1) * LANES] += jnp.sum(
                term.astype(F32), axis=0, keepdims=True
            )


def attend_backward(
    at, info, starts, scale, query_aug, qkv, grads, mixed, heads, groups, group, block
):
    length = qkv.shape[0]
    wide = heads * LANES
    width = heads * HEAD_DIM
    count = length // block
    b_size = at.b_size
    half = block // CORES

    def mixed_spot(i, s):
        i = count - 1 - i
        return (i + b_size - s[count]) % b_size, 0, i // b_size, 0, 0

    fixed = lambda i, s: (0, 0)
    return call(
        "attend_backward",
        functools.partial(backward_body, heads, group * heads, block, len(grads)),
        info,
        [
            (starts, pl.BlockSpec((8, block), lambda i, s: (0, count - 1 - i))),
            (scale, pl.BlockSpec((8, wide), fixed)),
            (query_aug, pl.BlockSpec((block, wide), lambda i, s: (count - 1 - i, group))),
            (qkv, pl.BlockSpec((length, wide), lambda i, s: (0, groups + group))),
            (qkv, pl.BlockSpec((length, wide), lambda i, s: (0, 2 * groups + group))),
            (mixed, pl.BlockSpec((1, CORES, 1, half, mixed.shape[4]), mixed_spot)),
        ]
        + [(grad, VMEM) for grad in grads],
        [
            (
                (length, 3 * width),
                BF16,
                pl.BlockSpec((block, 3 * width), lambda i, s: (count - 1 - i, 0)),
            ),
            ((8, LANES), F32, pl.BlockSpec((8, LANES), fixed)),
            ((8, 3 * wide), F32, pl.BlockSpec((8, 3 * wide), fixed)),
        ],
        grid=(count,),
        scratch=[
            pltpu.VMEM((half, mixed.shape[4]), BF16),
            pltpu.VMEM((block, wide), BF16),
            pltpu.VMEM((block, wide), F32),
            pltpu.VMEM((length, wide), F32),
            pltpu.VMEM((length, wide), F32),
        ],
    )


def concat_body(info, *refs):
    parts, out = refs[:-1], refs[-1]
    width = parts[0].shape[1]
    for p, part in enumerate(parts):
        out[:, p * width : (p + 1) * width] = part[...]


def concat(parts, after):
    rows, width = parts[0].shape
    return call(
        "concat",
        concat_body,
        [0],
        [(part, VMEM) for part in parts],
        [((rows, width * len(parts)), BF16, VMEM)],
        after=after,
    )[0]


def middle_body(count, source_count, moves, info, *refs):
    mixed, tokens, d_out, gain = refs[:4]
    sources = refs[4 : 4 + source_count]
    outs = refs[4 + source_count :]
    output, d_residual, d_proj, normed, activated, d_up = outs[:6]
    d_parts = outs[6:-4]
    weights, sems = outs[-4:-1], outs[-1]
    w_out, w_up, w_down = weights
    rows, half = sources[0].shape[2:]
    width = d_parts[0].shape[1]

    def copies(w):
        for n, (src, s, k) in enumerate(moves):
            if k == w:
                down = pl.ds(pl.multiple_of(info[2 * n] * rows, rows), rows)
                right = pl.ds(pl.multiple_of(info[2 * n + 1] * half, half), half)
                yield pltpu.make_async_copy(
                    sources[src].at[s, w], weights[w].at[down, right], sems.at[n]
                )

    def arrived(w):
        @pl.when(pl.program_id(0) == 0)
        def wait():
            for copy in copies(w):
                copy.wait()

    @pl.when(pl.program_id(0) == 0)
    def start():
        for w in range(3):
            for copy in copies(w):
                copy.start()

    arrived(0)
    residual = tokens[...].astype(F32) + dot(mixed[...], w_out[...])
    rate = lax.rsqrt(jnp.mean(residual * residual, axis=-1, keepdims=True) + NORM_EPS)
    normed[...] = (residual * rate * gain[...]).astype(BF16)
    arrived(1)
    upward = dot(normed[...], w_up[...])
    gate = 1.0 / (1.0 + jnp.exp(-upward))
    activated[...] = (upward * gate).astype(BF16)
    arrived(2)
    output[...] = (residual + dot(activated[...], w_down[...])).astype(BF16)
    d_activated = dot(d_out[...], w_down[...], 1, 1)
    d_up[...] = (d_activated * gate * (1 + upward * (1 - gate))).astype(BF16)
    scaled = dot(d_up[...], w_up[...], 1, 1) * gain[...]
    inner = jnp.mean(residual * scaled, axis=-1, keepdims=True)
    d_norm = rate * scaled - residual * (rate * rate * rate * inner)
    d_total = d_out[...].astype(F32) + d_norm
    d_residual[...] = d_total
    d_proj[...] = d_total.astype(BF16)
    d_mixed = dot(d_proj[...], w_out[...], 1, 1).astype(BF16)
    for p in range(count):
        d_parts[p][...] = d_mixed[:, p * width : (p + 1) * width]


def middle(at, mixed, tokens, d_out, gain, sources):
    count = at.peer_count
    rows, model = tokens.shape
    width = model // count
    arrays = list(sources.values())
    a_size, _, piece, half = arrays[0].shape
    group = model // at.peer_count // piece
    moves, spots = [], []
    for n, (dx, db, dc) in enumerate(sources):
        for a in range(a_size):
            for w in range(3):
                row = a * at.b_size + (at.b - db) % at.b_size
                if at.x_split == 2:
                    row = row * 2 + (at.x + dx) % 2
                if w == 0:
                    peer, rest = row // group, row % group
                    far = (at.b - peer // CORES) % at.b_size
                    row = (far * CORES + ((peer % CORES) ^ at.c)) * group + rest
                moves.append((n, a, w))
                spots += [row, (at.c + dc) % CORES]
    block = min(256, rows)
    row = lambda i, s: (i, 0)
    rows_of = pl.BlockSpec((block, model), row)
    part = pl.BlockSpec((block, width), row)
    types = [BF16, F32, BF16, BF16, BF16, BF16]
    return call(
        "middle",
        functools.partial(middle_body, count, len(arrays), moves),
        spots,
        [(mixed, rows_of), (tokens, rows_of), (d_out, rows_of)]
        + [(gain, pl.BlockSpec(gain.shape, lambda i, s: (0, 0)))]
        + [(source, ANY) for source in arrays],
        [((rows, model), kind, rows_of) for kind in types]
        + [((rows, width), BF16, part)] * count,
        grid=(rows // block,),
        scratch=[pltpu.VMEM((model, model), BF16)] * 3
        + [pltpu.SemaphoreType.DMA((len(moves),))],
    )


def outer_body(count, split, add, info, *refs):
    pairs, rest = refs[:6], refs[6:]
    for w in range(3):

        @pl.when(pl.program_id(0) == w)
        def product():
            value = dot(pairs[2 * w][...], pairs[2 * w + 1][...], 0, 0)
            target = rest[-1] if split else rest[-1].at[0]
            width = value.shape[0] // count
            for p in range(count):
                spot = p * width
                if w == 0:
                    spot = pl.multiple_of(info[3 + p] * width, width)
                part = value[p * width : (p + 1) * width]
                if add:
                    part = part + rest[0][0, pl.ds(spot, width)].astype(F32)
                target[pl.ds(spot, width)] = part.astype(BF16)

    if split:
        keep_x, give_x, keep_b, give_b, total = rest[1:]
        pairs_a, b_size, rows = keep_x.shape[1:4]
        for k in range(pairs_a):
            for b in range(b_size):
                for half, out in ((info[1], keep_x), (1 - info[1], give_x)):
                    spot = pl.multiple_of((k * b_size + b) * 2 * rows + half * rows, rows)
                    out[0, k, b] = total[pl.ds(spot, rows)]
            for b, out in ((info[2], keep_b), (1 - info[2], give_b)):
                for half in range(2):
                    spot = (((k + pairs_a) * b_size) * 2 + half) * rows + b * 2 * rows
                    out[0, k, half] = total[pl.ds(pl.multiple_of(spot, rows), rows)]


def outer(at, pairs, cols, add=None, after=()):
    rows, model = pairs[0][0].shape
    half = model // CORES
    count = at.peer_count
    split = add is not None and at.even
    info = [cols, at.x if at.even else 0, at.b, *[at.source(db, dc) for db, dc in at.peers()]]
    inputs = []
    for left, right in pairs:
        inputs.append((left, pl.BlockSpec((rows, model), lambda w, s: (0, 0))))
        inputs.append((right, pl.BlockSpec((rows, half), lambda w, s: (0, s[0]))))
    block = pl.BlockSpec((1, model, half), lambda w, s: (w, 0, 0))
    outputs = [((3, model, half), BF16, block)]
    scratch = []
    if add is not None:
        inputs.append((add, block))
    if split:
        shape = (at.a_size // 2, 2, model // at.a_size // 4, half)
        part = pl.BlockSpec((1, *shape), lambda w, s: (w, 0, 0, 0, 0))
        outputs = [((3, *shape), BF16, part)] * 4
        scratch = [pltpu.VMEM((model, half), BF16)]
    return call(
        "outer_give" if add is None else "outer",
        functools.partial(outer_body, count, split, add is not None),
        info,
        inputs,
        outputs,
        grid=(3,),
        scratch=scratch,
        after=after,
    )


def give_body(groups, info, *refs):
    grads, weights, out = refs[:groups], refs[groups : 2 * groups], refs[-1]
    value = back_product(grads, weights)
    out[0] = value.astype(BF16).reshape(out.shape[1:])


def back_product(grads, weights):
    total = 0.0
    for grad, weight in zip(grads, weights):
        total = total + dot(grad[...].reshape(-1, grad.shape[-1]), weight[...], 1, 1)
    return total


def keep_body(groups, info, *refs):
    grads, weights, got = refs[:groups], refs[groups : 2 * groups], refs[2 * groups]
    outs = refs[2 * groups + 1 :]
    b_size = got.shape[2]
    value = back_product(grads, weights).reshape(got.shape[1:]) + got[0].astype(F32)
    for b in range(b_size):
        for n, out in enumerate(outs):

            @pl.when(info[2 + n] == b)
            def copy():
                out[...] = value[:, b].astype(out.dtype)


def back_project_give(at, grads, weights, half):
    model = weights[0].shape[0]
    pair = at.a_size // 2
    width = grads[0].shape[1]
    shape = (pair, at.b_size, half, model)
    grads = [g.reshape(at.a_size, at.b_size, CORES, half, width) for g in grads]
    block = pl.BlockSpec((pair, at.b_size, 1, half, width), lambda i, s: (s[i], 0, s[2], 0, 0))
    core = 1 - at.c
    return call(
        "back_project",
        functools.partial(give_body, len(grads)),
        [core, 1 ^ core, core],
        [(g, block) for g in grads] + [(weight, VMEM) for weight in weights],
        [((2, *shape), BF16, pl.BlockSpec((1, *shape), lambda i, s: (i, 0, 0, 0, 0)))],
        grid=(2,),
    )[0]


def back_project_keep(at, grads, weights, half, which, got):
    model = weights[0].shape[0]
    pair = at.a_size // 2
    width = grads[0].shape[1]
    shape = (pair, at.b_size, half, model)
    grads = [g.reshape(at.a_size, at.b_size, CORES, half, width) for g in grads]
    block = pl.BlockSpec((pair, at.b_size, 1, half, width), lambda i, s: (s[0], 0, s[1], 0, 0))
    return call(
        "back_project",
        functools.partial(keep_body, len(grads)),
        [which ^ at.c, at.c, *ahead(at.b, at.b_size)],
        [(g, block) for g in grads]
        + [(weight, VMEM) for weight in weights]
        + [(got, pl.BlockSpec((1, *shape), lambda i, s: (which, 0, 0, 0, 0)))],
        [((pair, half, model), F32 if db == 0 else BF16, VMEM) for db in range(at.b_size)],
    )


def norm_back_body(count, info, *refs):
    own, others = refs[0], refs[1:count]
    tokens, d_residual, gain = refs[count : count + 3]
    for n, out in enumerate(refs[count + 3 :]):
        k = info[1 + n]
        grad = own[k]
        for other in others:
            grad = grad + other[k].astype(F32)
        value = tokens[k].astype(F32)
        rate = lax.rsqrt(jnp.mean(value * value, axis=-1, keepdims=True) + NORM_EPS)
        scaled = grad * gain[...]
        inner = jnp.mean(value * scaled, axis=-1, keepdims=True)
        d_norm = rate * scaled - value * (rate * rate * rate * inner)
        out[...] = (d_residual[k] + d_norm).astype(BF16)


def norm_back(at, terms, chunks, d_residual, gain, which):
    pair, half, model = terms[0].shape
    block = pl.BlockSpec((pair, half, model), lambda i, s: (s[0], 0, 0))
    order = [k ^ (at.a % pair) for k in range(pair)]
    return call(
        "norm_back",
        functools.partial(norm_back_body, len(terms)),
        [which ^ at.c, *order],
        [(t, VMEM) for t in terms] + [(chunks, block), (d_residual, block), (gain, VMEM)],
        [((half, model), BF16, VMEM)] * pair,
    )


def heads_outer_body(steps, info, normed, grads, extra, *rest):
    outs, acc = rest[:-1], rest[-1]
    value = dot(normed[...], grads[...], 0, 0)

    @pl.when(pl.program_id(0) == 0)
    def first():
        acc[...] = value

    @pl.when(pl.program_id(0) != 0)
    def later():
        acc[...] += value

    @pl.when(pl.program_id(0) == steps - 1)
    def last():
        used = acc.shape[1]
        pairs, b_size, rows = outs[0].shape[:3]
        split = len(outs)
        for n, out in enumerate(outs):
            for s in range(pairs * b_size):
                spot = (s * split + (info[0] ^ n if split == 2 else 0)) * rows
                spot = pl.ds(pl.multiple_of(spot, rows), rows)
                out[s // b_size, s % b_size, :, :used] = acc[spot, :].astype(BF16)
                out[s // b_size, s % b_size, :, used:] = extra[spot, :]


def heads_outer(at, normed, grads, extra):
    length, model = normed.shape
    used = grads.shape[1]
    block = min(512, length)
    steps = length // block
    rows = model // at.a_size // at.b_size // at.x_split
    shape = (at.a_size, at.b_size, rows, used + extra.shape[1])
    return call(
        "heads_outer",
        functools.partial(heads_outer_body, steps),
        [at.x],
        [
            (normed, pl.BlockSpec((block, model), lambda i, s: (i, 0))),
            (grads, pl.BlockSpec((block, used), lambda i, s: (i, 0))),
            (extra, pl.BlockSpec(extra.shape, lambda i, s: (0, 0))),
        ],
        [(shape, BF16, pl.BlockSpec(shape, lambda i, s: (0, 0, 0, 0)))] * at.x_split,
        grid=(steps,),
        scratch=[pltpu.VMEM((model, used), F32)],
    )


def all_sum(at, value, axis, size):
    total = value
    for d in range(1, size):
        total = total + at.send(value, **{axis: d}).astype(value.dtype)
    return total


def ahead(spot, size):
    return [(spot + d) % size for d in range(size)]


def cat_body(info, first, first_got, second, second_got, *outs):
    pair = first.shape[1]
    for d, out in enumerate(outs):
        spot = info[d] % pair

        @pl.when(info[d] < pair)
        def low():
            out[...] = (first[:, spot].astype(F32) + first_got[:, spot].astype(F32)).astype(BF16)

        @pl.when(info[d] >= pair)
        def high():
            out[...] = (second[:, spot].astype(F32) + second_got[:, spot].astype(F32)).astype(BF16)


class FullReduce:
    def __init__(self, at, parts):
        self.at = at
        if at.even:
            keep_x, give_x, keep_b, give_b = parts
            self.first = keep_x, at.send(give_x, dx=1)
            self.second = keep_b, at.send(give_b, db=1)
        else:
            self.part = parts[0].reshape(3, at.a_size, at.b_size, -1, parts[0].shape[-1])

    def next(self):
        at = self.at
        if not at.even:
            return
        groups = [[(t, 2, b) for t in self.first] for b in ahead(at.b, 2)]
        groups += [[(t, 2, x) for t in self.second] for x in ahead(at.x, 2)]
        keep_b, give_b, keep_x, give_x = add_blocks(groups)
        self.first = keep_b, at.send(give_b, db=1)
        self.second = keep_x, at.send(give_x, dx=1)

    def over_a(self):
        at = self.at
        if at.even:
            shape = self.first[0].shape
            parts = call(
                "cat",
                cat_body,
                ahead(at.a, at.a_size),
                [(t, VMEM) for t in (*self.first, *self.second)],
                [((3, *shape[2:]), BF16, VMEM)] * at.a_size,
            )
        else:
            parts = add_blocks([[(self.part, 1, a)] for a in ahead(at.a, at.a_size)])
        self.got = [parts[0]] + [at.send(parts[d], da=d) for d in range(1, at.a_size)]

    def end(self):
        at = self.at
        if at.even:
            part = add_blocks([[(t[None], 0, 0) for t in self.got]])[0]
            far = at.send(part, dx=1)
            return [part, far, at.send(part, dc=1), at.send(far, dc=1)]
        parts = add_blocks([[(t, 1, b) for t in self.got] for b in ahead(at.b, at.b_size)])
        got = [parts[0]] + [at.send(parts[d], db=d) for d in range(1, at.b_size)]
        part = add_blocks([[(t[None], 0, 0) for t in got]])[0]
        part = all_sum(at, part, "dx", at.x_size)
        return [part, at.send(part, dc=1)]


class HeadsReduce:
    def __init__(self, at, parts):
        self.at = at
        self.got = [parts[0]]
        if at.x_split == 2:
            self.got.append(at.send(parts[1], dx=1))

    def over_a(self):
        at = self.at
        parts = add_blocks([[(t, 0, a) for t in self.got] for a in ahead(at.a, at.a_size)])
        self.got = [parts[0]] + [at.send(parts[d], da=d) for d in range(1, at.a_size)]
        return parts

    def by_b(self, after=()):
        at = self.at
        if at.x_split == 1:
            total = add_blocks([[(t[None], 0, 0) for t in self.got]])[0]
            self.got = [all_sum(at, total, "dx", at.x_size)]
        groups = [[(t, 0, b) for t in self.got] for b in ahead(at.b, at.b_size)]
        return add_blocks(groups, after)


def side_body(groups, info, *refs):
    for n, out in enumerate(refs[-(len(refs) // (groups + 1)) :]):
        for g in range(groups):
            out[g] = refs[n * groups + g][...]


def to_peers(at, groups):
    shape = (len(groups), *groups[0][0].shape)
    parts = call(
        "side",
        functools.partial(side_body, len(groups)),
        [0],
        [(group[b], VMEM) for b in range(at.b_size) for group in groups],
        [(shape, BF16, VMEM)] * at.b_size,
    )
    parts = [at.send(parts[db], db=db, dc=dc) if db or dc else parts[0] for db, dc in at.peers()]
    return parts


def in_order(info, refs, split, half, core, spot):
    near = [r[spot] for r in refs]
    if split == 2:
        near = [jnp.where(info[0] == half, near[2 * k], near[2 * k + 1]) for k in range(2)]
    return jnp.where(info[1] == core, near[0], near[1])


def finish_full_body(split, info, *refs):
    count = CORES * split
    parts, (weight, gain), outs = refs[:count], refs[count : count + 2], refs[count + 2 :]
    rows, half = parts[0].shape[1:]
    for x in range(split):
        spot = slice(x * rows, (x + 1) * rows)
        for w in range(3):
            for c in range(CORES):
                outs[w][spot, c * half : (c + 1) * half] = in_order(
                    info, parts, split, x, c, w
                ).astype(F32)
    total = jnp.sum(outs[1][...] * weight[...].astype(F32), axis=1, keepdims=True)
    outs[3][...] = total / gain[...].astype(F32)


def finish_full(at, parts, weight, gain, after):
    rows, model = weight.shape
    return call(
        "finish_full",
        functools.partial(finish_full_body, 2 if at.even else 1),
        [at.x, at.c],
        [(p, VMEM) for p in parts] + [(weight, VMEM), (gain[:, None], VMEM)],
        [((rows, model), F32, VMEM)] * 3 + [((rows, 1), F32, VMEM)],
        after=after,
    )


def finish_heads_body(count, split, info, *refs):
    parts, refs = refs[:count], refs[count:]
    far, refs = refs[: split - 1], refs[split - 1 :]
    weights, gain, outs = refs[:3], refs[3], refs[4:]
    few = outs[4].shape[1]
    groups, rows, width = parts[0].shape
    width = (width - few) // 3
    for n in range(split):
        down = pl.ds(pl.multiple_of((info[count] ^ n if split == 2 else 0) * rows, rows), rows)
        total = jnp.zeros((rows, few), F32)
        for p in range(count):
            for g in range(groups):
                source = far[0].at[p, g] if n else parts[p].at[g]
                total = total + source[:, 3 * width :].astype(F32)
                for peer in range(count):

                    @pl.when(info[p] == peer)
                    def copy():
                        for k in range(3):
                            spot = (peer * groups + g) * width
                            piece = source[:, k * width : (k + 1) * width]
                            outs[k][down, spot : spot + width] = piece.astype(F32)

        outs[4][down, :] = total
    total = jnp.zeros(outs[3].shape, F32)
    for k in range(3):
        total = total + jnp.sum(outs[k][...] * weights[k][...].astype(F32), axis=1, keepdims=True)
    outs[3][...] = total / gain[...].astype(F32)


def finish_heads(at, parts, weights, gain, few):
    rows, model = weights[0].shape
    flat = [*parts[0], *parts[1:]]
    return call(
        "finish_heads",
        functools.partial(finish_heads_body, at.peer_count, at.x_split),
        [*[at.source(db, dc) for db, dc in at.peers()], at.x],
        [(p, VMEM) for p in flat] + [(w, VMEM) for w in weights] + [(gain[:, None], VMEM)],
        [((rows, model), F32, VMEM)] * 3 + [((rows, 1), F32, VMEM), ((rows, few), F32, VMEM)],
    )


def local(
    reps,
    shards,
    activations,
    cotangent,
    doc_lengths,
    gain_attn,
    query_weight,
    query_bias,
    key_weight,
    value_weight,
    value_bias,
    dim_scale,
    out_weight,
    gain_mlp,
    up_weight,
    down_weight,
):
    seqs, tok_count, model = activations.shape
    at = Place(reps, shards, seqs)
    half = tok_count // CORES
    length = tok_count * shards
    peer_count = at.peer_count
    heads = model // HEAD_DIM // peer_count
    width = heads * HEAD_DIM
    wide = heads * LANES
    own_rows = at.a_size * half
    rows = gain_attn.shape[0]
    groups = 2
    block = CORES * half
    mine = at.b * CORES + at.c

    LAST.clear()
    stage = at.to_cluster(activations)
    next(stage)
    vectors = jnp.stack([gain_attn, gain_mlp, query_bias, value_bias], axis=1)
    own, *sent = heads_parts(at, (query_weight, key_weight, value_weight), vectors, groups)
    sent = [at.send(part, db=db + 1) for db, part in enumerate(sent)]
    next(stage)
    near = by_order(own, sent, at.b_size, at.b)
    sources = [near] + [at.send(near, da=d) for d in range(1, at.a_size)]
    if at.x_split == 2:
        sources += [at.send(source, dx=1) for source in sources]
    chunks = next(stage)
    parts = []
    early = sources[1 : at.a_size]
    if at.x_split == 2:
        early = [sources[2], sources[at.a_size + 1], sources[at.a_size + 3]]
    for db in range(at.b_size):
        near = at.send(chunks, db=db) if db else chunks
        ready = later(near, *early) if db else near
        parts += [near, at.send(ready, dc=1)]
    stage = at.to_cluster(cotangent)
    soon = [next(stage), at.send(doc_lengths, dc=1)]
    quarter = quarter_of(at, (out_weight, up_weight, down_weight), sources[1 : at.a_size])
    pieces = [quarter] + [at.send(quarter, da=d) for d in range(1, at.a_size)]
    *w_heads, w_pad, vectors = pad_weights(
        at, sources, heads, groups, [*parts[1:], *soon]
    )
    vectors = vectors.T.astype(F32)
    g_attn, g_mlp, b_query, b_value = vectors[0], vectors[1], vectors[2], vectors[3]

    other_lengths = soon[1]
    lengths = pick(jnp.where(at.c == at.a // seqs, doc_lengths, other_lengths), at.a % seqs)
    ends = jnp.cumsum(lengths)
    places = jnp.arange(length, dtype=jnp.int32)
    starts = jnp.max(jnp.where(ends[None, :] <= places[:, None], ends[None, :], 0), axis=1)
    starts_row = jnp.broadcast_to(starts[None, :], (8, length))
    starts_col = jnp.broadcast_to(starts[:, None], (length, LANES))
    info = jnp.concatenate([starts[::block] // block, jnp.stack([at.b, at.c])]).astype(jnp.int32)

    scale_dim = LOG_BASE / math.sqrt(HEAD_DIM) * jax.nn.softplus(dim_scale)
    scale_pad = jnp.tile(jnp.pad(scale_dim, (0, LANES - HEAD_DIM)), heads)
    lane = jnp.arange(LANES)
    ones_key = ((lane >= HEAD_DIM) & (lane < HEAD_DIM + 3)).astype(F32)
    ones_value = ((lane >= HEAD_DIM) & (lane < HEAD_DIM + 2)).astype(F32)

    def pad_heads(vec):
        part = lax.dynamic_slice_in_dim(vec, mine * width, width, 0).reshape(heads, HEAD_DIM)
        return jnp.pad(part, ((0, 0), (0, LANES - HEAD_DIM))).reshape(wide)

    bias_pad = jnp.concatenate(
        [
            pad_heads(b_query),
            jnp.tile(ones_key, heads),
            pad_heads(b_value) + jnp.tile(ones_value, heads),
        ]
    )
    times = jnp.concatenate([scale_pad, jnp.ones((2 * wide,), F32)])
    qkv, normed = project(at, parts, g_attn[None], w_pad, bias_pad[None], times[None])

    part_heads = heads // groups
    part_width = part_heads * HEAD_DIM
    moves = [(d, None, 0, (at.a - d) % at.a_size) for d in range(at.a_size)]
    quarter = shuffle(pieces, [((at.a_size, *quarter.shape), BF16)], moves)[0]
    others = {(0, 0, 0): quarter, (0, 0, 1): at.send(quarter, dc=1)}
    for db in range(1, at.b_size):
        others[(0, db, 0)] = at.send(quarter, db=db)
    if at.x_split == 2:
        others[(1, 0, 0)] = at.send(quarter, dx=1)
    stage.send([others[(0, 0, 1)]])
    mixed_rel, query_aug = attend_forward(at, info, starts_col, qkv, heads, block)
    d_out = next(stage).reshape(own_rows, model)
    if at.x_split == 2:
        for db in range(1, at.b_size):
            others[(1, db, 0)] = at.send(later(others[(0, db, 0)], d_out), dx=1)
    parts = []
    for db, dc in at.peers():
        part = later(mixed_rel[db, dc], d_out).reshape(own_rows, width)
        parts.append(at.send(part, db=db, dc=dc) if db or dc else part)
    mixed = concat(parts, [])
    for dx, db, dc in list(others):
        if (dx, db, 1) not in others:
            others[(dx, db, 1)] = at.send(later(others[(dx, db, 0)], mixed), dc=1)
    tokens = chunks.reshape(own_rows, model)
    output, d_residual, d_proj, normed_mlp, activated, d_up, *d_parts = middle(
        at, mixed, tokens, d_out, g_mlp[None], others
    )

    grads = []
    for (db, dc), part in zip(at.peers(), d_parts):
        part = at.send(part, db=db, dc=dc) if db or dc else part
        grads.append(part.reshape(at.a_size, half, width))

    pairs = [(mixed, d_proj), (normed_mlp, d_up), (activated, d_out)]
    give = outer(at, pairs, 1 - at.c)[0]
    full = FullReduce(at, outer(at, pairs, at.c, at.send(give, dc=1), grads))

    scale_rows = jnp.broadcast_to(scale_pad[None, : part_heads * LANES], (8, part_heads * LANES))
    zeros = jnp.zeros((model,), F32)

    def backward(g):
        d_heads, scale_sum, bias_sum = attend_backward(
            at,
            info,
            starts_row,
            scale_rows,
            query_aug,
            qkv,
            grads,
            mixed_rel,
            part_heads,
            groups,
            g,
            block,
        )
        bias_sum = bias_sum[0].reshape(3, part_heads, LANES)[:, :, :HEAD_DIM]
        bias_sum = bias_sum.reshape(3, part_width)
        spot = (mine * groups + g) * part_width
        scale_sum = jnp.pad(scale_sum[0, :HEAD_DIM], (0, rows - HEAD_DIM))
        extra = [
            lax.dynamic_update_slice(zeros, bias_sum[0], (spot,)),
            lax.dynamic_update_slice(zeros, bias_sum[2], (spot,)),
            jnp.tile(scale_sum, shards),
        ]
        return d_heads, jnp.stack(extra, axis=1).astype(BF16)

    stage = at.from_cluster(output.reshape(at.a_size, half, model))
    next(stage)
    d_first, extra_first = backward(0)
    next(stage)
    full.next()
    reduce_first = HeadsReduce(at, heads_outer(at, normed, d_first, extra_first))
    full.over_a()
    d_second, extra_second = backward(1)
    full_parts = full.end()
    reduce_first.over_a()

    d_heads = [d_first, d_second]
    keeps, received = [], []
    residual_chunks = d_residual.reshape(at.a_size, half, model)

    def keep(which, got):
        terms = back_project_keep(at, d_heads, w_heads, half, which, got)
        keeps.append([terms[0]] + [at.send(terms[db], db=db) for db in range(1, at.b_size)])

    def back(which):
        sent = norm_back(at, keeps[which], chunks, residual_chunks, g_attn[None], which)
        for k, part in enumerate(sent):
            received.append(at.send_back(part, which * len(sent) + k))
        return sent

    got = at.send(back_project_give(at, d_heads, w_heads, half), dc=1)
    reduce_second = HeadsReduce(at, heads_outer(at, normed, d_second, extra_second))
    first = reduce_first.by_b(full_parts[1:2])
    keep(0, got)
    keep(1, got)
    reduce_second.over_a()
    back(0)
    parts = [to_peers(at, [first, reduce_second.by_b(keeps[1][1:])])]
    sent = back(1)
    if at.x_split == 2:
        parts.append(at.send(later(jnp.stack(parts[0]), sent[0]), dx=1))
    *grads_full, grad_gain_mlp = finish_full(at, full_parts, up_weight, gain_mlp, [])
    output = next(stage)
    weights = (query_weight, key_weight, value_weight)
    *grads_heads, grad_gain_attn, few = finish_heads(at, parts, weights, gain_attn, 3)
    input_grad = at.place_back(received)
    grad_scale = few[:HEAD_DIM, 2] / scale_dim * (LOG_BASE / math.sqrt(HEAD_DIM))
    grad_scale = grad_scale * jax.nn.sigmoid(dim_scale)
    return (
        output,
        input_grad,
        grad_gain_attn[:, 0],
        grads_heads[0],
        few[:, 0],
        grads_heads[1],
        grads_heads[2],
        few[:, 1],
        grad_scale,
        grads_full[0],
        grad_gain_mlp[:, 0],
        grads_full[1],
        grads_full[2],
    )


def solution(mesh):
    in_specs = (
        P("rep", "shard", None),
        P("rep", "shard", None),
        P("rep", None),
        P("shard"),
        P("shard", None),
        P("shard"),
        P("shard", None),
        P("shard", None),
        P("shard"),
        P(),
        P("shard", None),
        P("shard"),
        P("shard", None),
        P("shard", None),
    )
    out_specs = (
        P("rep", "shard", None),
        P("rep", "shard", None),
        P("shard"),
        P("shard", None),
        P("shard"),
        P("shard", None),
        P("shard", None),
        P("shard"),
        P(),
        P("shard", None),
        P("shard"),
        P("shard", None),
        P("shard", None),
    )
    body = functools.partial(local, mesh.shape["rep"], mesh.shape["shard"])
    return jax.shard_map(body, mesh=mesh, in_specs=in_specs, out_specs=out_specs, check_vma=False)
```
